32 devices in a mesh: fsdp: 8 (over z, y), dp: 4 (over x, core).
Axes of the slice: x: 2, y: 2, z: 4, core: 2. Of those that a mesh axis runs over, the one named last changes fastest.
Arguments:
- images: bfloat16 [64, 14, 14, 2048], P(('fsdp', 'dp')), may hold values from -24 to 24
- valid: int32 [64], P(('fsdp', 'dp')), may hold values from 0 to 1, as said below
- cotangent: bfloat16 [64, 14, 14, 2048], P(('fsdp', 'dp')), may hold values from -24 to 24
- w_reduce: bfloat16 [2048, 1024], P('fsdp'), may hold values from -0.125 to 0.125
- gain_one: bfloat16 [1024], P('fsdp'), may hold values from 0.25 to 1.75
- shift_one: bfloat16 [1024], P('fsdp'), may hold values from -3 to 3
- w_group: bfloat16 [288, 1024], P('fsdp'), may hold values from -0.375 to 0.375
- gain_two: bfloat16 [1024], P('fsdp'), may hold values from 0.25 to 1.75
- shift_two: bfloat16 [1024], P('fsdp'), may hold values from -3 to 3
- w_expand: bfloat16 [1024, 2048], P('fsdp'), may hold values from -0.1875 to 0.1875
- gain_three: bfloat16 [2048], P('fsdp'), may hold values from 0.25 to 1.75
- shift_three: bfloat16 [2048], P('fsdp'), may hold values from -3 to 3
Outputs:
- output: bfloat16 [64, 14, 14, 2048], P(('fsdp', 'dp'))
- grad_input: bfloat16 [64, 14, 14, 2048], P(('fsdp', 'dp'))
- grad_w_reduce: float32 [2048, 1024], P('fsdp')
- grad_w_group: float32 [288, 1024], P('fsdp')
- grad_w_expand: float32 [1024, 2048], P('fsdp')
- grad_gain_one: float32 [1024], P('fsdp')
- grad_shift_one: float32 [1024], P('fsdp')
- grad_gain_two: float32 [1024], P('fsdp')
- grad_shift_two: float32 [1024], P('fsdp')
- grad_gain_three: float32 [2048], P('fsdp')
- grad_shift_three: float32 [2048], P('fsdp')
The draws below stay inside these ranges and needn't reach their ends.
Inputs may be any that keep to these rules, and one draw needn't show every extreme that they name: At least one slot of all is valid; each slot is valid with probability 9/10.
All inputs are finite; a program needn't handle non-finite values.
Results may differ from the reference program's by a relative error of at most 0.0075.
Values may be sent and summed in bfloat16 or wider, within the bound.
No kernel may reach another device: no remote copies, remote signals or barrier semaphores. Data moves between devices by JAX's collectives and lax.ppermute only.
A program may use at most 192 MiB of HBM per device.

```python
import jax
import jax.numpy as jnp
from jax import lax

CHANNELS = 2048
WIDTH = 1024
GROUPS = 32
SIDE = 14
GROUP_WIDTH = 32
IMAGES = 64


def image_ramp():
    return 1.0 + 2.0 * jnp.arange(IMAGES, dtype=jnp.float32) / max(IMAGES - 1, 1)


def rough_field(key):
    shape = (IMAGES, SIDE, SIDE, CHANNELS)
    keys = jax.random.split(key, 5)
    noise = jax.random.truncated_normal(keys[0], -3.0, 3.0, shape, jnp.float32)
    common = jax.random.truncated_normal(keys[1], -3.0, 3.0, (IMAGES, SIDE, SIDE, 1), jnp.float32)
    shifts = jax.random.truncated_normal(keys[2], -2.5, 2.5, (IMAGES, 1, 1, CHANNELS), jnp.float32)
    base = 0.5 * noise + 0.5 * common + 0.9 * shifts
    image_scale = jnp.exp(jax.random.uniform(keys[4], (IMAGES, 1, 1, 1), jnp.float32, -0.8, 0.2))
    return base * image_ramp().reshape(IMAGES, 1, 1, 1) * image_scale


def draw_images(key, part):
    key = jax.random.fold_in(key, 11)
    return rough_field(key).astype(jnp.bfloat16)


def draw_cotangent(key, part):
    key = jax.random.fold_in(key, 12)
    return rough_field(key).astype(jnp.bfloat16)


def draw_valid(key, part):
    key = jax.random.fold_in(key, 13)
    first, second = jax.random.split(key)
    coins = jax.random.randint(first, (IMAGES,), 0, 10)
    chosen = jax.random.randint(second, (), 0, IMAGES)
    slots = jnp.arange(IMAGES, dtype=jnp.int32)
    return jnp.where((coins < 9) | (slots == chosen), 1, 0).astype(jnp.int32)


def shard_levels(key, extent, cuts, low, largest):
    level, own = 1.0, jax.random.fold_in(key, 6)
    for axis_at, blocks in cuts:
        draws = jnp.exp(jax.random.uniform(jax.random.fold_in(own, axis_at), (blocks,), jnp.float32, low / len(cuts), largest / len(cuts)))
        level = level * jnp.repeat(draws, extent[axis_at] // blocks).reshape([-1 if axis == axis_at else 1 for axis in range(len(extent))])
    return level


def bell_draw(stream_key, dims, deviation, bound, cuts=(), held_as=jnp.bfloat16):
    result = jax.random.normal(stream_key, dims, jnp.float32) * deviation
    if len(cuts) > 0:
        result = shard_levels(stream_key, dims, cuts, -0.22, 0.18) * result
    return jnp.clip(result, min=-bound, max=bound).astype(held_as)


def setup_inputs(seed: int = 0) -> dict:
    seeds = jax.random.split(jax.random.key(seed), 13)
    return {
        "images": draw_images(jax.random.fold_in(seeds[12], 71), 0),
        "valid": draw_valid(jax.random.fold_in(seeds[12], 71), 0),
        "cotangent": draw_cotangent(jax.random.fold_in(seeds[12], 71), 0),
        "w_reduce": bell_draw(seeds[3], (CHANNELS, WIDTH), CHANNELS ** -0.5, 0.125, ((0, 8),)),
        "gain_one": jnp.clip(1.0 + 0.15 * jax.random.normal(seeds[4], (WIDTH,), jnp.float32), 0.25, 1.75).astype(jnp.bfloat16),
        "shift_one": bell_draw(seeds[5], (WIDTH,), 0.5, 3.0, ((0, 8),)),
        "w_group": bell_draw(seeds[6], (9 * GROUP_WIDTH, WIDTH), (9 * GROUP_WIDTH) ** -0.5, 0.375, ((0, 8),)),
        "gain_two": jnp.clip(1.0 + 0.15 * jax.random.normal(seeds[7], (WIDTH,), jnp.float32), 0.25, 1.75).astype(jnp.bfloat16),
        "shift_two": bell_draw(seeds[8], (WIDTH,), 0.5, 3.0, ((0, 8),)),
        "w_expand": bell_draw(seeds[9], (WIDTH, CHANNELS), WIDTH ** -0.5, 0.1875, ((0, 8),)),
        "gain_three": jnp.clip(1.0 + 0.15 * jax.random.normal(seeds[10], (CHANNELS,), jnp.float32), 0.25, 1.75).astype(jnp.bfloat16),
        "shift_three": bell_draw(seeds[11], (CHANNELS,), 0.5, 3.0, ((0, 8),)),
    }


@jax.custom_vjp
def low(v):
    return lax.optimization_barrier(v.astype(jnp.bfloat16)).astype(jnp.float32)

@jax.custom_vjp
def low_back(v):
    return v

def low_keep(v):
    return (low(v), None)

def low_pass(kept, grad):
    return (grad,)

def back_keep(v):
    return (v, None)

def back_low(kept, grad):
    return (low(grad),)
low.defvjp(low_keep, low_pass)
low_back.defvjp(back_keep, back_low)
epsilon = 1e-05

def reference(images, valid, cotangent, w_reduce, gain_one, shift_one, w_group, gain_two, shift_two, w_expand, gain_three, shift_three):
    pixel_mask = valid.astype(jnp.float32).reshape(IMAGES, 1, 1, 1)
    pixels = jnp.sum(valid.astype(jnp.float32)) * (SIDE * SIDE)

    def normalize(hidden, gain, shift):
        mean = lax.optimization_barrier(jnp.sum(pixel_mask * hidden, axis=(0, 1, 2))) / pixels
        square = lax.optimization_barrier(jnp.sum(pixel_mask * hidden * hidden, axis=(0, 1, 2))) / pixels
        inverse = lax.rsqrt(square - mean * mean + epsilon)
        return (hidden - mean) * inverse * gain + shift

    def forward(inputs, weight_a, gain_a, shift_a, weight_b, gain_b, shift_b, weight_c, gain_c, shift_c):
        reduced = jnp.dot(inputs.reshape(-1, CHANNELS), weight_a, precision=lax.Precision.HIGHEST, preferred_element_type=jnp.float32)
        reduced = low_back(reduced.reshape(IMAGES, SIDE, SIDE, WIDTH))
        act_one = low(jax.nn.silu(normalize(reduced, gain_a, shift_a)))
        kernel = weight_b.reshape(3, 3, WIDTH // GROUPS, WIDTH)
        grouped = lax.conv_general_dilated(act_one, kernel, (1, 1), 'SAME', dimension_numbers=('NHWC', 'HWIO', 'NHWC'), feature_group_count=GROUPS, precision=lax.Precision.HIGHEST)
        grouped = low_back(grouped)
        act_two = low(jax.nn.silu(normalize(grouped, gain_b, shift_b)))
        expanded = jnp.dot(act_two.reshape(-1, WIDTH), weight_c, precision=lax.Precision.HIGHEST, preferred_element_type=jnp.float32)
        expanded = low_back(expanded.reshape(IMAGES, SIDE, SIDE, CHANNELS))
        summed = normalize(expanded, gain_c, shift_c) + inputs
        return jax.nn.silu(summed) * pixel_mask
    primals = [a.astype(jnp.float32) for a in (images, w_reduce, gain_one, shift_one, w_group, gain_two, shift_two, w_expand, gain_three, shift_three)]
    output, pullback = jax.vjp(forward, *primals)
    grads = pullback(cotangent.astype(jnp.float32))
    return (output.astype(jnp.bfloat16), grads[0].astype(jnp.bfloat16), grads[1], grads[4], grads[7], grads[2], grads[3], grads[5], grads[6], grads[8], grads[9])
```

```python
import functools

import jax
import jax.numpy as jnp
from jax import lax
from jax.experimental import pallas as pl
from jax.experimental.pallas import tpu as pltpu
from jax.sharding import Mesh
from jax.sharding import PartitionSpec as P

GROUPS = 32
TAPS = 9
LINE = 16
BLOCK = 256
epsilon = 1e-05
BF16, F32 = jnp.bfloat16, jnp.float32
SWAP = [(0, 1), (1, 0)]


def sigmoid(values):
    return 0.5 * jnp.tanh(0.5 * values) + 0.5


def dsilu(values):
    sigma = sigmoid(values)
    return sigma * (1.0 + values * (1.0 - sigma))


def dot(a, b, contract=((1,), (0,))):
    return lax.dot_general(a, b, (contract, ((), ())), preferred_element_type=F32)


NT = ((1,), (1,))
TN = ((0,), (0,))


def call(kernel, outs, *args, scalars=0, scratch=(), vmem=40, name=None, flops=0):
    vm = pl.BlockSpec(memory_space=pltpu.VMEM)
    sm = pl.BlockSpec(memory_space=pltpu.SMEM)
    many = isinstance(outs, (list, tuple))
    return pl.pallas_call(
        kernel,
        out_shape=outs,
        in_specs=[sm] * scalars + [vm] * (len(args) - scalars),
        out_specs=[vm] * len(outs) if many else vm,
        scratch_shapes=list(scratch),
        compiler_params=pltpu.CompilerParams(vmem_limit_bytes=vmem << 20),
        cost_estimate=pl.CostEstimate(flops=flops, bytes_accessed=1 << 20, transcendentals=0),
        name=name,
    )(*args)


def shape(dims, dtype):
    return jax.ShapeDtypeStruct(dims, dtype)


def moments(total, pixels):
    mean = total[0:1, :] / pixels
    inverse = lax.rsqrt(total[1:2, :] / pixels - mean * mean + epsilon)
    return mean, inverse


def line_mask(columns):
    return lax.broadcasted_iota(jnp.int32, (LINE, columns), 0) < 14


def column_sums(ref_rows):
    return jnp.sum(ref_rows, axis=0, keepdims=True)


def reduce_kernel(slots, scalar, mask, x, *refs):
    weights, (red, stats) = refs[: 2 * slots], refs[2 * slots :]
    depth = weights[0].shape[0]
    half = weights[0].shape[1]
    for side in range(2):
        base = scalar[slots + side] * half
        for at in range(0, half, BLOCK):
            total = None
            for slot in range(slots):
                rows = pl.ds(pl.multiple_of(scalar[slot] * depth, 128), depth)
                term = dot(x[:, rows], weights[2 * slot + side][:, at : at + BLOCK])
                total = term if total is None else total + term
            columns = pl.ds(pl.multiple_of(base + at, BLOCK), BLOCK)
            red[:, columns] = total
            masked = total * mask[...]
            stats[0:1, columns] = column_sums(masked)
            stats[1:2, columns] = column_sums(masked * total)


def fill_pads(pads, image, line, values):
    rows = pl.ds(pl.multiple_of((line + 1) * LINE, LINE), LINE)
    pads[0, image, rows, :] = pltpu.roll(values, 1, 0).astype(BF16)
    pads[1, image, rows, :] = values.astype(BF16)
    pads[2, image, rows, :] = pltpu.roll(values, LINE - 1, 0).astype(BF16)


def clear_pads(pads):
    images, rows, columns = pads.shape[1:]
    zeros = jnp.zeros((3, images, LINE, columns), BF16)
    pads[:, :, 0:LINE, :] = zeros
    pads[:, :, rows - LINE : rows, :] = zeros


def group_kernel(side, mask, red, total, pixels, gain, shift, wide, pads, grouped, stats):
    images, padded, width = pads.shape[1:]
    rows = side * LINE
    mean, inverse = moments(total, pixels[...])
    scale = inverse * gain[...]
    clear_pads(pads)
    inside = line_mask(width)

    def body(step, carry):
        image, line = step // side, step % side
        at = pl.ds(pl.multiple_of(step * LINE, LINE), LINE)
        normal = (red[at, :] - mean) * scale + shift[...]
        fill_pads(pads, image, line, jnp.where(inside, normal * sigmoid(normal), 0.0))
        return carry

    lax.fori_loop(0, images * side, body, 0)
    for block in range(width // BLOCK):
        columns = slice(block * BLOCK, (block + 1) * BLOCK)
        sums = [0.0, 0.0]
        for image in range(images):
            value = None
            for tap in range(TAPS):
                top, left = divmod(tap, 3)
                term = dot(
                    pads[left, image, top * LINE : top * LINE + rows, columns], wide[tap, block]
                )
                value = term if value is None else value + term
            at = slice(image * rows, (image + 1) * rows)
            grouped[at, columns] = value
            masked = value * mask[at, :]
            sums = [sums[0] + column_sums(masked), sums[1] + column_sums(masked * value)]
        stats[0:1, columns] = sums[0]
        stats[1:2, columns] = sums[1]


def expand_kernel(scalar, mask, grouped, total, pixels, gain, shift, mine, other, act, expanded, stats):
    width = grouped.shape[1]
    mean, inverse = moments(total, pixels[...])
    scale = inverse * gain[...]
    inside = line_mask(width)

    def body(step, carry):
        at = pl.ds(pl.multiple_of(step * LINE, LINE), LINE)
        normal = (grouped[at, :] - mean) * scale + shift[...]
        act[at, :] = jnp.where(inside, normal * sigmoid(normal), 0.0).astype(BF16)
        return carry

    lax.fori_loop(0, grouped.shape[0] // LINE, body, 0)
    half = mine.shape[1]
    for side, weight in enumerate((mine, other)):
        base = scalar[side] * half
        for at in range(0, half, BLOCK):
            value = dot(act[...], weight[:, at : at + BLOCK])
            columns = pl.ds(pl.multiple_of(base + at, BLOCK), BLOCK)
            expanded[:, columns] = value
            masked = value * mask[...]
            stats[0:1, columns] = column_sums(masked)
            stats[1:2, columns] = column_sums(masked * value)


def output_kernel(side, valid, expanded, total, pixels, gain, shift, x, cotangent, output, grad, stats):
    mean, inverse = moments(total, pixels[0:1, 0:1])
    zero = jnp.zeros((8, expanded.shape[1]), F32)

    def body(step, carry):
        image, line = step // side, step % side
        at = pl.ds(pl.multiple_of(step * LINE, LINE), LINE)
        keep = valid[image].astype(F32)
        normed = (expanded[at, :] - mean) * inverse
        summed = normed * gain[...] + shift[...] + x[at, :].astype(F32)
        sigma = sigmoid(summed)
        output[image, line] = (summed * sigma * keep).astype(BF16)[0:side]
        here = cotangent[at, :].astype(F32) * keep * (sigma * (1.0 + summed * (1.0 - sigma)))
        grad[at, :] = here
        both = here * normed
        return carry[0] + here[0:8] + here[8:16], carry[1] + both[0:8] + both[8:16]

    first, second = lax.fori_loop(0, expanded.shape[0] // LINE, body, (zero, zero))
    stats[0:1, :] = column_sums(first)
    stats[1:2, :] = column_sums(second)


def back_expand_kernel(
    scalar, mask, grad, expanded, total, sums, pixels, gain, grouped, total_two, gain_two, shift_two, mine, other,
    flat, dz, stats,
):
    width = grouped.shape[1]
    mean, inverse = moments(total, pixels[0:1, 0:1])
    scale = inverse * gain[...]
    first, second = sums[0:1, :] / pixels[0:1, 0:1], sums[1:2, :] / pixels[0:1, 0:1]

    def body(step, carry):
        at = pl.ds(pl.multiple_of(step * LINE, LINE), LINE)
        normed = (expanded[at, :] - mean) * inverse
        flat[at, :] = (scale * (grad[at, :] - mask[at, :] * (first + normed * second))).astype(BF16)
        return carry

    lax.fori_loop(0, grouped.shape[0] // LINE, body, 0)
    half = mine.shape[1]
    for at in range(0, width, BLOCK):
        value = None
        for side, weight in enumerate((mine, other)):
            columns = pl.ds(pl.multiple_of(scalar[side] * half, 128), half)
            term = dot(flat[:, columns], weight[at : at + BLOCK, :], NT)
            value = term if value is None else value + term
        dz[:, at : at + BLOCK] = value
    mean_two, inverse_two = moments(total_two, pixels[...])
    zero = jnp.zeros((8, width), F32)

    def tail(step, carry):
        at = pl.ds(pl.multiple_of(step * LINE, LINE), LINE)
        normed = (grouped[at, :] - mean_two) * inverse_two
        here = dz[at, :] * dsilu(normed * gain_two[...] + shift_two[...])
        dz[at, :] = here
        both = here * normed
        return carry[0] + here[0:8] + here[8:16], carry[1] + both[0:8] + both[8:16]

    one, two = lax.fori_loop(0, grouped.shape[0] // LINE, tail, (zero, zero))
    stats[0:1, :] = column_sums(one)
    stats[1:2, :] = column_sums(two)


def weight_expand_kernel(scalar, act, flat, send, keep):
    half = send.shape[1]
    turned = act[...].T
    for side, out in enumerate((keep, send)):
        base = scalar[side] * half
        for at in range(0, half, BLOCK):
            columns = pl.ds(pl.multiple_of(base + at, BLOCK), BLOCK)
            out[:, at : at + BLOCK] = dot(turned, flat[:, columns]).astype(BF16)


def back_group_kernel(
    side, mask, dz, grouped, total, sums, pixels, gain, red, total_one, gain_one, shift_one, wide,
    flat, dz_one, stats, pads,
):
    images, padded, width = pads.shape[1:]
    rows = side * LINE
    mean, inverse = moments(total, pixels[...])
    scale = inverse * gain[...]
    first, second = sums[0:1, :] / pixels[...], sums[1:2, :] / pixels[...]
    clear_pads(pads)

    def body(step, carry):
        image, line = step // side, step % side
        at = pl.ds(pl.multiple_of(step * LINE, LINE), LINE)
        normed = (grouped[at, :] - mean) * inverse
        value = scale * (dz[at, :] - mask[at, :] * (first + normed * second))
        flat[at, :] = value.astype(BF16)
        fill_pads(pads, image, line, value)
        return carry

    lax.fori_loop(0, images * side, body, 0)
    for block in range(width // BLOCK):
        columns = slice(block * BLOCK, (block + 1) * BLOCK)
        for image in range(images):
            value = None
            for tap in range(TAPS):
                top, left = divmod(TAPS - 1 - tap, 3)
                term = dot(
                    pads[left, image, top * LINE : top * LINE + rows, columns], wide[tap, block], NT
                )
                value = term if value is None else value + term
            dz_one[image * rows : (image + 1) * rows, columns] = value
    mean_one, inverse_one = moments(total_one, pixels[...])
    inside = line_mask(width)
    zero = jnp.zeros((8, width), F32)

    def tail(step, carry):
        at = pl.ds(pl.multiple_of(step * LINE, LINE), LINE)
        normed = (red[at, :] - mean_one) * inverse_one
        here = dz_one[at, :] * dsilu(normed * gain_one[...] + shift_one[...])
        here = jnp.where(inside, here, 0.0)
        dz_one[at, :] = here
        both = here * normed
        return carry[0] + here[0:8] + here[8:16], carry[1] + both[0:8] + both[8:16]

    one, two = lax.fori_loop(0, images * side, tail, (zero, zero))
    stats[0:1, :] = column_sums(one)
    stats[1:2, :] = column_sums(two)


def weight_group_kernel(side, pads, flat, out):
    images, padded, width = pads.shape[1:]
    rows = side * LINE
    inner = width // GROUPS
    row = lax.broadcasted_iota(jnp.int32, (BLOCK, BLOCK), 0) // inner
    column = lax.broadcasted_iota(jnp.int32, (BLOCK, BLOCK), 1) // inner
    own = row == column
    fold_row = lax.broadcasted_iota(jnp.int32, (inner, BLOCK), 0)
    fold_column = lax.broadcasted_iota(jnp.int32, (inner, BLOCK), 1) % inner
    fold = jnp.where(fold_row == fold_column, 1.0, 0.0).astype(BF16)
    for block in range(width // BLOCK):
        columns = slice(block * BLOCK, (block + 1) * BLOCK)
        turned = [flat[image * rows : (image + 1) * rows, columns].T for image in range(images)]
        for tap in range(TAPS):
            top, left = divmod(tap, 3)
            value = None
            for image in range(images):
                term = dot(turned[image], pads[left, image, top * LINE : top * LINE + rows, columns])
                value = term if value is None else value + term
            kept = jnp.where(own, value, 0.0).astype(BF16)
            out[tap * inner : (tap + 1) * inner, columns] = dot(fold, kept, NT).astype(BF16)


def back_reduce_kernel(scalar, mask, dz, red, total, sums, pixels, gain, turned, flat, send, keep):
    mean, inverse = moments(total, pixels[...])
    scale = inverse * gain[...]
    first, second = sums[0:1, :] / pixels[...], sums[1:2, :] / pixels[...]

    def body(step, carry):
        at = pl.ds(pl.multiple_of(step * LINE, LINE), LINE)
        normed = (red[at, :] - mean) * inverse
        flat[at, :] = (scale * (dz[at, :] - mask[at, :] * (first + normed * second))).astype(BF16)
        return carry

    lax.fori_loop(0, red.shape[0] // LINE, body, 0)
    half = send.shape[1]
    for side, out in enumerate((keep, send)):
        base = scalar[side] * half
        for at in range(0, half, BLOCK):
            columns = pl.ds(pl.multiple_of(base + at, BLOCK), BLOCK)
            out[:, at : at + BLOCK] = dot(turned[...], flat[:, columns]).astype(BF16)


def grad_input_kernel(slots, side, scalar, flat, grad, *refs):
    weights, (out, held) = refs[: 2 * slots], refs[2 * slots :]
    depth, half = weights[0].shape
    for slot in range(slots):
        value = None
        for part in range(2):
            columns = pl.ds(pl.multiple_of(scalar[slots + part] * half, 128), half)
            term = dot(flat[:, columns], weights[2 * slot + part][...], NT)
            value = term if value is None else value + term
        columns = pl.ds(pl.multiple_of(scalar[slot] * depth, 128), depth)
        held[:, columns] = value + grad[:, columns]

    def body(step, carry):
        at = pl.ds(pl.multiple_of(step * LINE, LINE), LINE)
        out[step // side, step % side] = held[at, :].astype(BF16)[0:side]
        return carry

    lax.fori_loop(0, flat.shape[0] // LINE, body, 0)


def everywhere(values):
    values = values + lax.ppermute(values, "core", SWAP)
    chips = lax.axis_size("fsdp") * lax.axis_size("x")
    spread = jnp.broadcast_to(values[None], (chips,) + values.shape)
    return jnp.sum(lax.all_to_all(spread, ("fsdp", "x"), 0, 0, tiled=True), axis=0)


def swap_core(values):
    return lax.ppermute(values, "core", SWAP)


def around(values):
    return lax.ppermute(values, "fsdp", [(f, (f + 2) % 8) for f in range(8)])


def across(values):
    return lax.ppermute(values, "fsdp", [(f, f ^ 1) for f in range(8)])


def gather_reduce(half):
    position = lax.axis_index("fsdp")
    size = lax.axis_size("fsdp")
    if size != 8:
        return [lax.all_gather(half, "fsdp", axis=0, tiled=True)], jnp.zeros((1,), jnp.int32)
    blocks, owners, moving = [], [], half
    for step in range(4):
        if step > 0:
            moving = around(moving)
        owner = (position - 2 * step + 8) % 8
        blocks += [moving, across(moving)]
        owners += [owner, owner ^ 1]
    return blocks, jnp.stack(owners).astype(jnp.int32)


def scatter_reduce(part):
    position = lax.axis_index("fsdp")
    size = lax.axis_size("fsdp")
    if size != 8:
        flat = part.reshape(-1, part.shape[-1])
        own = lax.psum_scatter(flat, "fsdp", scatter_dimension=0, tiled=True)
        return lax.psum(own.astype(F32), "x")

    def block(owner):
        return lax.dynamic_index_in_dim(part, owner, 0, keepdims=False)

    total = None
    for step in range(1, 5):
        owner = (position - 2 * step + 8) % 8
        sent = across(block(owner ^ 1))
        here = block(owner).astype(F32) + sent.astype(F32)
        if total is not None:
            here = here + total.astype(F32)
        if step < 4:
            total = around(here.astype(BF16))
    return here + lax.ppermute(here.astype(BF16), "x", SWAP).astype(F32)


def halves(values, core):
    half = values.shape[1] // 2
    return lax.dynamic_slice_in_dim(values, core * half, half, 1)


def join(mine, other, core):
    first = jnp.where(core == 0, mine, other)
    second = jnp.where(core == 0, other, mine)
    return jnp.concatenate([first, second], axis=1)


def per_device(
    images,
    valid,
    cotangent,
    w_reduce,
    gain_one,
    shift_one,
    w_group,
    gain_two,
    shift_two,
    w_expand,
    gain_three,
    shift_three,
):
    count, side, _, channels = images.shape
    width = w_reduce.shape[1]
    inner = width // GROUPS
    size = lax.axis_size("fsdp")
    position, core = lax.axis_index("fsdp"), lax.axis_index("core").astype(jnp.int32)
    rows = count * side * LINE

    def padded(values):
        return jnp.pad(values, ((0, 0), (0, 0), (0, LINE - side), (0, 0))).reshape(rows, channels)

    x, cot = padded(images), padded(cotangent)
    turned = x.T
    pixel = jnp.arange(LINE) < side
    mask = (valid.astype(F32)[:, None, None] * pixel[None, None, :].astype(F32)) * jnp.ones((1, side, 1), F32)
    mask = mask.reshape(rows, 1)

    cores = jnp.stack([core, 1 - core])
    blocks, owners = gather_reduce(halves(w_reduce, core))
    weights = []
    for block in blocks:
        weights += [block, swap_core(block)]
    slots = jnp.concatenate([owners, cores])
    slot_count = len(blocks)
    vectors = jnp.concatenate([gain_one, shift_one, gain_two, shift_two, gain_three, shift_three])
    small = jnp.concatenate([w_group.reshape(-1), vectors])
    small = lax.all_gather(small.reshape(1, -1), "fsdp", axis=0, tiled=True)
    w_group_all = small[:, : w_group.size].reshape(TAPS, inner, width)
    vectors = small[:, w_group.size :].astype(F32)
    cut, per, outer = [], gain_one.shape[0], gain_three.shape[0]
    for begin, length in (
        (0, per), (per, per), (2 * per, per), (3 * per, per), (4 * per, outer), (4 * per + outer, outer)
    ):
        cut.append(vectors[:, begin : begin + length].reshape(1, -1))
    g1, s1, g2, s2, g3, s3 = cut
    per_block = BLOCK // inner
    tiled = jnp.broadcast_to(
        w_group_all.reshape(TAPS, 1, 1, inner, width // BLOCK, BLOCK),
        (TAPS, 1, per_block, inner, width // BLOCK, BLOCK),
    )
    tiled = tiled.reshape(TAPS, BLOCK, width // BLOCK, BLOCK).transpose(0, 2, 1, 3)
    own = (jnp.arange(BLOCK) // inner)[:, None] == (jnp.arange(BLOCK) // inner)[None, :]
    wide = jnp.where(own[None, None], tiled, jnp.zeros((), BF16))
    expand_mine = lax.all_gather(halves(w_expand, core), "fsdp", axis=0, tiled=True)
    expand_other = swap_core(expand_mine)

    red, part = call(
        functools.partial(reduce_kernel, slot_count),
        [shape((rows, width), F32), shape((2, width), F32)],
        slots, mask, x, *weights, scalars=1, name="reduce", flops=2 * rows * width * channels,
    )
    pixel_count = jnp.sum(valid.astype(F32)) * (side * side)
    part = jnp.concatenate([part, jnp.full((1, width), 1.0, F32) * pixel_count], axis=0)
    total = everywhere(part)
    total_one, pixels = total[0:2], total[2:3]
    pads, grouped, part = call(
        functools.partial(group_kernel, side),
        [
            shape((3, count, (side + 2) * LINE, width), BF16),
            shape((rows, width), F32),
            shape((2, width), F32),
        ],
        mask, red, total_one, pixels, g1, s1, wide, name="group", flops=2 * TAPS * rows * width * BLOCK,
    )
    total_two = everywhere(part)
    act_two, expanded, part = call(
        expand_kernel,
        [shape((rows, width), BF16), shape((rows, channels), F32), shape((2, channels), F32)],
        cores, mask, grouped, total_two, pixels, g2, s2, expand_mine, expand_other,
        scalars=1, name="expand", flops=2 * rows * width * channels,
    )
    total_three = everywhere(part)
    output, grad_summed, part = call(
        functools.partial(output_kernel, side),
        [shape(images.shape, BF16), shape((rows, channels), F32), shape((2, channels), F32)],
        valid, expanded, total_three, pixels, g3, s3, x, cot, scalars=1, name="output",
    )

    sums_three = everywhere(part)
    flat_three, dz_two, part = call(
        back_expand_kernel,
        [shape((rows, channels), BF16), shape((rows, width), F32), shape((2, width), F32)],
        cores, mask, grad_summed, expanded, total_three, sums_three, pixels, g3, grouped, total_two, g2, s2,
        expand_mine, expand_other, scalars=1, name="back_expand", flops=2 * rows * width * channels,
    )
    send, keep = call(
        weight_expand_kernel,
        [shape((width, channels // 2), BF16)] * 2,
        cores, act_two, flat_three, scalars=1, name="weight_expand", flops=2 * rows * width * channels,
    )
    chip = (keep.astype(F32) + swap_core(send).astype(F32)).astype(BF16)
    own_expand = lax.psum_scatter(chip, "fsdp", scatter_dimension=0, tiled=True)
    own_expand = own_expand.astype(F32)
    if lax.axis_size("x") == 2:
        own_expand = own_expand + lax.ppermute(own_expand.astype(BF16), "x", SWAP).astype(F32)
    else:
        own_expand = lax.psum(own_expand, "x")
    grad_w_expand = join(own_expand, swap_core(own_expand), core)

    sums_two = everywhere(part)
    flat_two, dz_one, part = call(
        functools.partial(back_group_kernel, side),
        [shape((rows, width), BF16), shape((rows, width), F32), shape((2, width), F32)],
        mask, dz_two, grouped, total_two, sums_two, pixels, g2, red, total_one, g1, s1, wide,
        scratch=[pltpu.VMEM((3, count, (side + 2) * LINE, width), BF16)],
        name="back_group", flops=2 * TAPS * rows * width * BLOCK,
    )
    group_term = call(
        functools.partial(weight_group_kernel, side),
        shape((TAPS * inner, width), BF16),
        pads, flat_two, name="weight_group", flops=2 * TAPS * rows * width * BLOCK,
    )
    own_group = lax.psum(group_term, ("fsdp", "x", "core"))
    shard = w_group.shape[0]
    grad_w_group = lax.dynamic_slice_in_dim(own_group, position * shard, shard, 0).astype(F32)

    sums_one = everywhere(part)
    flat_one, send, keep = call(
        back_reduce_kernel,
        [shape((rows, width), BF16)] + [shape((channels, width // 2), BF16)] * 2,
        cores, mask, dz_one, red, total_one, sums_one, pixels, g1, turned,
        scalars=1, name="back_reduce", flops=2 * rows * width * channels,
    )
    chip = (keep.astype(F32) + swap_core(send).astype(F32)).astype(BF16)
    own_reduce = scatter_reduce(chip.reshape(size, channels // size, width // 2))
    grad_w_reduce = join(own_reduce, swap_core(own_reduce), core)
    grad_input = call(
        functools.partial(grad_input_kernel, slot_count, side),
        shape(images.shape, BF16),
        slots, flat_one, grad_summed, *weights,
        scalars=1, scratch=[pltpu.VMEM((rows, channels), F32)], name="grad_input",
        flops=2 * rows * width * channels,
    )

    def own_shard(total, shard):
        return lax.dynamic_slice_in_dim(total, position * shard, shard, 0)

    return (
        output,
        grad_input,
        grad_w_reduce,
        grad_w_group,
        grad_w_expand,
        own_shard(sums_one[1], per),
        own_shard(sums_one[0], per),
        own_shard(sums_two[1], per),
        own_shard(sums_two[0], per),
        own_shard(sums_three[1], outer),
        own_shard(sums_three[0], outer),
    )


def solution(mesh):
    fsdp, dp = mesh.shape["fsdp"], mesh.shape["dp"]
    split = Mesh(mesh.devices.reshape(fsdp, dp // 2, 2), ("fsdp", "x", "core"))
    images, rows, vector = P(("fsdp", "x", "core"), None, None, None), P("fsdp", None), P("fsdp")
    return jax.shard_map(
        per_device,
        mesh=split,
        in_specs=(
            images, P(("fsdp", "x", "core")), images,
            rows, vector, vector, rows, vector, vector, rows, vector, vector,
        ),
        out_specs=(images, images, rows, rows, rows) + (vector,) * 6,
        check_vma=False,
    )
```

```python
import functools

import jax
import jax.numpy as jnp
from jax import lax
from jax.experimental import pallas as pl
from jax.experimental.pallas import tpu as pltpu
from jax.sharding import Mesh
from jax.sharding import PartitionSpec as P

GROUPS = 32
TAPS = 9
LINE = 16
BLOCK = 256
epsilon = 1e-05
BF16, F32 = jnp.bfloat16, jnp.float32
SWAP = [(0, 1), (1, 0)]


def sigmoid(values):
    return 0.5 * jnp.tanh(0.5 * values) + 0.5


def dsilu(values):
    sigma = sigmoid(values)
    return sigma * (1.0 + values * (1.0 - sigma))


def dot(a, b, contract=((1,), (0,))):
    return lax.dot_general(a, b, (contract, ((), ())), preferred_element_type=F32)


NT = ((1,), (1,))
TN = ((0,), (0,))


def call(kernel, outs, *args, scalars=0, scratch=(), vmem=8, name=None, flops=0):
    vm = pl.BlockSpec(memory_space=pltpu.VMEM)
    sm = pl.BlockSpec(memory_space=pltpu.SMEM)
    many = isinstance(outs, (list, tuple))
    return pl.pallas_call(
        kernel,
        out_shape=outs,
        in_specs=[sm] * scalars + [vm] * (len(args) - scalars),
        out_specs=[vm] * len(outs) if many else vm,
        scratch_shapes=list(scratch),
        compiler_params=pltpu.CompilerParams(vmem_limit_bytes=vmem << 20),
        cost_estimate=pl.CostEstimate(flops=flops, bytes_accessed=1 << 20, transcendentals=0),
        name=name,
    )(*args)


def shape(dims, dtype):
    return jax.ShapeDtypeStruct(dims, dtype)


def after(values, *others):
    return lax.optimization_barrier((values,) + others)[0]


def moments(total, pixels):
    mean = total[0:1, :] / pixels
    inverse = lax.rsqrt(total[1:2, :] / pixels - mean * mean + epsilon)
    return mean, inverse


def line_mask(columns):
    return lax.broadcasted_iota(jnp.int32, (LINE, columns), 0) < 14


def column_sums(ref_rows):
    return jnp.sum(ref_rows, axis=0, keepdims=True)


def reduce_kernel(slots, scalar, mask, x, *refs):
    weights, (red, stats) = refs[: 2 * slots], refs[2 * slots :]
    depth = weights[0].shape[0]
    half = weights[0].shape[1]
    for side in range(2):
        base = scalar[slots + side] * half
        for at in range(0, half, BLOCK):
            total = None
            for slot in range(slots):
                rows = pl.ds(pl.multiple_of(scalar[slot] * depth, 128), depth)
                term = dot(x[:, rows], weights[2 * slot + side][:, at : at + BLOCK])
                total = term if total is None else total + term
            columns = pl.ds(pl.multiple_of(base + at, BLOCK), BLOCK)
            red[:, columns] = total
            masked = total * mask[...]
            stats[0:1, columns] = column_sums(masked)
            stats[1:2, columns] = column_sums(masked * total)


def widen_kernel(weight, wide):
    taps, blocks = wide.shape[:2]
    inner = weight.shape[0] // taps
    row = lax.broadcasted_iota(jnp.int32, (BLOCK, BLOCK), 0) // inner
    column = lax.broadcasted_iota(jnp.int32, (BLOCK, BLOCK), 1) // inner
    own = row == column
    for tap in range(taps):
        for block in range(blocks):
            piece = weight[tap * inner : (tap + 1) * inner, block * BLOCK : (block + 1) * BLOCK]
            tall = jnp.concatenate([piece.astype(F32)] * (BLOCK // inner), axis=0)
            wide[tap, block] = jnp.where(own, tall, 0.0).astype(BF16)


def fill_pads(pads, image, line, values):
    rows = pl.ds(pl.multiple_of((line + 1) * LINE, LINE), LINE)
    pads[0, image, rows, :] = pltpu.roll(values, 1, 0).astype(BF16)
    pads[1, image, rows, :] = values.astype(BF16)
    pads[2, image, rows, :] = pltpu.roll(values, LINE - 1, 0).astype(BF16)


def clear_pads(pads):
    images, rows, columns = pads.shape[1:]
    zeros = jnp.zeros((3, images, LINE, columns), BF16)
    pads[:, :, 0:LINE, :] = zeros
    pads[:, :, rows - LINE : rows, :] = zeros


def group_kernel(side, mask, red, total, pixels, gain, shift, wide, pads, grouped, stats):
    images, padded, width = pads.shape[1:]
    rows = side * LINE
    mean, inverse = moments(total, pixels[...])
    scale = inverse * gain[...]
    clear_pads(pads)
    inside = line_mask(width)

    def body(step, carry):
        image, line = step // side, step % side
        at = pl.ds(pl.multiple_of(step * LINE, LINE), LINE)
        normal = (red[at, :] - mean) * scale + shift[...]
        fill_pads(pads, image, line, jnp.where(inside, normal * sigmoid(normal), 0.0))
        return carry

    lax.fori_loop(0, images * side, body, 0)
    for block in range(width // BLOCK):
        columns = slice(block * BLOCK, (block + 1) * BLOCK)
        sums = [0.0, 0.0]
        for image in range(images):
            value = None
            for tap in range(TAPS):
                top, left = divmod(tap, 3)
                term = dot(
                    pads[left, image, top * LINE : top * LINE + rows, columns], wide[tap, block]
                )
                value = term if value is None else value + term
            at = slice(image * rows, (image + 1) * rows)
            grouped[at, columns] = value
            masked = value * mask[at, :]
            sums = [sums[0] + column_sums(masked), sums[1] + column_sums(masked * value)]
        stats[0:1, columns] = sums[0]
        stats[1:2, columns] = sums[1]


def expand_kernel(scalar, mask, grouped, total, pixels, gain, shift, mine, other, act, expanded, stats):
    width = grouped.shape[1]
    mean, inverse = moments(total, pixels[...])
    scale = inverse * gain[...]
    inside = line_mask(width)

    def body(step, carry):
        at = pl.ds(pl.multiple_of(step * LINE, LINE), LINE)
        normal = (grouped[at, :] - mean) * scale + shift[...]
        act[at, :] = jnp.where(inside, normal * sigmoid(normal), 0.0).astype(BF16)
        return carry

    lax.fori_loop(0, grouped.shape[0] // LINE, body, 0)
    half = mine.shape[1]
    for side, weight in enumerate((mine, other)):
        base = scalar[side] * half
        for at in range(0, half, BLOCK):
            value = dot(act[...], weight[:, at : at + BLOCK])
            columns = pl.ds(pl.multiple_of(base + at, BLOCK), BLOCK)
            expanded[:, columns] = value
            masked = value * mask[...]
            stats[0:1, columns] = column_sums(masked)
            stats[1:2, columns] = column_sums(masked * value)


def output_kernel(side, valid, expanded, total, pixels, gain, shift, x, cotangent, output, grad, stats):
    mean, inverse = moments(total, pixels[0:1, 0:1])
    zero = jnp.zeros((8, expanded.shape[1]), F32)

    def body(step, carry):
        image, line = step // side, step % side
        at = pl.ds(pl.multiple_of(step * LINE, LINE), LINE)
        keep = valid[image].astype(F32)
        normed = (expanded[at, :] - mean) * inverse
        summed = normed * gain[...] + shift[...] + x[at, :].astype(F32)
        sigma = sigmoid(summed)
        output[image, line] = (summed * sigma * keep).astype(BF16)[0:side]
        here = cotangent[at, :].astype(F32) * keep * (sigma * (1.0 + summed * (1.0 - sigma)))
        grad[at, :] = here
        both = here * normed
        return carry[0] + here[0:8] + here[8:16], carry[1] + both[0:8] + both[8:16]

    first, second = lax.fori_loop(0, expanded.shape[0] // LINE, body, (zero, zero))
    stats[0:1, :] = column_sums(first)
    stats[1:2, :] = column_sums(second)


def back_expand_kernel(
    scalar, mask, grad, expanded, total, sums, pixels, gain, grouped, total_two, gain_two, shift_two, mine, other,
    flat, dz, stats,
):
    width = grouped.shape[1]
    mean, inverse = moments(total, pixels[0:1, 0:1])
    scale = inverse * gain[...]
    first, second = sums[0:1, :] / pixels[0:1, 0:1], sums[1:2, :] / pixels[0:1, 0:1]

    def body(step, carry):
        at = pl.ds(pl.multiple_of(step * LINE, LINE), LINE)
        normed = (expanded[at, :] - mean) * inverse
        flat[at, :] = (scale * (grad[at, :] - mask[at, :] * (first + normed * second))).astype(BF16)
        return carry

    lax.fori_loop(0, grouped.shape[0] // LINE, body, 0)
    half = mine.shape[1]
    for at in range(0, width, BLOCK):
        value = None
        for side, weight in enumerate((mine, other)):
            columns = pl.ds(pl.multiple_of(scalar[side] * half, 128), half)
            term = dot(flat[:, columns], weight[at : at + BLOCK, :], NT)
            value = term if value is None else value + term
        dz[:, at : at + BLOCK] = value
    mean_two, inverse_two = moments(total_two, pixels[...])
    zero = jnp.zeros((8, width), F32)

    def tail(step, carry):
        at = pl.ds(pl.multiple_of(step * LINE, LINE), LINE)
        normed = (grouped[at, :] - mean_two) * inverse_two
        here = dz[at, :] * dsilu(normed * gain_two[...] + shift_two[...])
        dz[at, :] = here
        both = here * normed
        return carry[0] + here[0:8] + here[8:16], carry[1] + both[0:8] + both[8:16]

    one, two = lax.fori_loop(0, grouped.shape[0] // LINE, tail, (zero, zero))
    stats[0:1, :] = column_sums(one)
    stats[1:2, :] = column_sums(two)


def weight_expand_kernel(scalar, act, flat, send, keep):
    half = send.shape[1]
    turned = act[...].T
    for side, out in enumerate((keep, send)):
        base = scalar[side] * half
        for at in range(0, half, BLOCK):
            columns = pl.ds(pl.multiple_of(base + at, BLOCK), BLOCK)
            out[:, at : at + BLOCK] = dot(turned, flat[:, columns]).astype(BF16)


def back_group_kernel(
    side, mask, dz, grouped, total, sums, pixels, gain, red, total_one, gain_one, shift_one, wide,
    flat, dz_one, stats, pads,
):
    images, padded, width = pads.shape[1:]
    rows = side * LINE
    mean, inverse = moments(total, pixels[...])
    scale = inverse * gain[...]
    first, second = sums[0:1, :] / pixels[...], sums[1:2, :] / pixels[...]
    clear_pads(pads)

    def body(step, carry):
        image, line = step // side, step % side
        at = pl.ds(pl.multiple_of(step * LINE, LINE), LINE)
        normed = (grouped[at, :] - mean) * inverse
        value = scale * (dz[at, :] - mask[at, :] * (first + normed * second))
        flat[at, :] = value.astype(BF16)
        fill_pads(pads, image, line, value)
        return carry

    lax.fori_loop(0, images * side, body, 0)
    for block in range(width // BLOCK):
        columns = slice(block * BLOCK, (block + 1) * BLOCK)
        for image in range(images):
            value = None
            for tap in range(TAPS):
                top, left = divmod(TAPS - 1 - tap, 3)
                term = dot(
                    pads[left, image, top * LINE : top * LINE + rows, columns], wide[tap, block], NT
                )
                value = term if value is None else value + term
            dz_one[image * rows : (image + 1) * rows, columns] = value
    mean_one, inverse_one = moments(total_one, pixels[...])
    inside = line_mask(width)
    zero = jnp.zeros((8, width), F32)

    def tail(step, carry):
        at = pl.ds(pl.multiple_of(step * LINE, LINE), LINE)
        normed = (red[at, :] - mean_one) * inverse_one
        here = dz_one[at, :] * dsilu(normed * gain_one[...] + shift_one[...])
        here = jnp.where(inside, here, 0.0)
        dz_one[at, :] = here
        both = here * normed
        return carry[0] + here[0:8] + here[8:16], carry[1] + both[0:8] + both[8:16]

    one, two = lax.fori_loop(0, images * side, tail, (zero, zero))
    stats[0:1, :] = column_sums(one)
    stats[1:2, :] = column_sums(two)


def weight_group_kernel(side, pads, flat, out):
    images, padded, width = pads.shape[1:]
    rows = side * LINE
    inner = width // GROUPS
    row = lax.broadcasted_iota(jnp.int32, (BLOCK, BLOCK), 0) // inner
    column = lax.broadcasted_iota(jnp.int32, (BLOCK, BLOCK), 1) // inner
    own = row == column
    fold_row = lax.broadcasted_iota(jnp.int32, (inner, BLOCK), 0)
    fold_column = lax.broadcasted_iota(jnp.int32, (inner, BLOCK), 1) % inner
    fold = jnp.where(fold_row == fold_column, 1.0, 0.0).astype(BF16)
    for block in range(width // BLOCK):
        columns = slice(block * BLOCK, (block + 1) * BLOCK)
        turned = [flat[image * rows : (image + 1) * rows, columns].T for image in range(images)]
        for tap in range(TAPS):
            top, left = divmod(tap, 3)
            value = None
            for image in range(images):
                term = dot(turned[image], pads[left, image, top * LINE : top * LINE + rows, columns])
                value = term if value is None else value + term
            kept = jnp.where(own, value, 0.0).astype(BF16)
            out[tap * inner : (tap + 1) * inner, columns] = dot(fold, kept, NT).astype(BF16)


def back_reduce_kernel(scalar, mask, dz, red, total, sums, pixels, gain, turned, group, flat, send):
    mean, inverse = moments(total, pixels[...])
    scale = inverse * gain[...]
    first, second = sums[0:1, :] / pixels[...], sums[1:2, :] / pixels[...]

    def body(step, carry):
        at = pl.ds(pl.multiple_of(step * LINE, LINE), LINE)
        normed = (red[at, :] - mean) * inverse
        flat[at, :] = (scale * (dz[at, :] - mask[at, :] * (first + normed * second))).astype(BF16)
        return carry

    lax.fori_loop(0, red.shape[0] // LINE, body, 0)
    blocks, tall, half = send.shape
    depth = tall - group.shape[1]
    columns = pl.ds(pl.multiple_of(scalar[blocks + 1] * half, 128), half)
    for block in range(blocks):
        rows = pl.ds(pl.multiple_of(scalar[block] * depth, 16), depth)
        send[block, 0:depth, :] = dot(turned[rows, :], flat[:, columns]).astype(BF16)
        send[block, depth:tall, :] = group[scalar[block], :, columns]


def block_sum_kernel(blocks, places, scalar, turned, group, flat, near, *refs):
    arrived, outs = refs[: len(refs) - len(places)], refs[len(refs) - len(places) :]
    tall, half = near.shape[1:]
    depth = tall - group.shape[1]
    columns = pl.ds(pl.multiple_of(scalar[blocks] * half, 128), half)
    for out, place in zip(outs, places):
        owner = scalar[place]
        rows = pl.ds(pl.multiple_of(owner * depth, 16), depth)
        value = dot(turned[rows, :], flat[:, columns]) + near[place, 0:depth, :].astype(F32)
        more = group[owner, :, columns].astype(F32) + near[place, depth:tall, :].astype(F32)
        for other in arrived:
            value = value + other[0:depth, :].astype(F32)
            more = more + other[depth:tall, :].astype(F32)
        out[0:depth, :] = value.astype(out.dtype)
        out[depth:tall, :] = more.astype(out.dtype)


def add_kernel(a, b, out):
    out[...] = a[...].astype(F32) + b[...].astype(F32)


def join_kernel(scalar, mine, other, *outs):
    half = mine.shape[1]
    at = 0
    for out in outs:
        rows = out.shape[0]
        for side, part in enumerate((mine, other)):
            columns = pl.ds(pl.multiple_of(scalar[side] * half, 128), half)
            out[:, columns] = part[at : at + rows, :]
        at += -(-rows // 16) * 16


def grad_input_kernel(slots, side, scalar, flat, grad, *refs):
    weights, (out, held) = refs[: 2 * slots], refs[2 * slots :]
    depth, half = weights[0].shape
    for slot in range(slots):
        value = None
        for part in range(2):
            columns = pl.ds(pl.multiple_of(scalar[slots + part] * half, 128), half)
            term = dot(flat[:, columns], weights[2 * slot + part][...], NT)
            value = term if value is None else value + term
        columns = pl.ds(pl.multiple_of(scalar[slot] * depth, 128), depth)
        held[:, columns] = value + grad[:, columns]

    def body(step, carry):
        at = pl.ds(pl.multiple_of(step * LINE, LINE), LINE)
        out[step // side, step % side] = held[at, :].astype(BF16)[0:side]
        return carry

    lax.fori_loop(0, flat.shape[0] // LINE, body, 0)


def everywhere(values):
    values = values + lax.ppermute(values, "core", SWAP)
    chips = lax.axis_size("fsdp") * lax.axis_size("x")
    spread = jnp.broadcast_to(values[None], (chips,) + values.shape)
    return jnp.sum(lax.all_to_all(spread, ("fsdp", "x"), 0, 0, tiled=True), axis=0)


def swap_core(values):
    return lax.ppermute(values, "core", SWAP)


def swap_x(values):
    size = lax.axis_size("x")
    if size == 2:
        return lax.ppermute(values, "x", SWAP)
    return (lax.psum(values.astype(F32), "x") - values.astype(F32)).astype(values.dtype)


def around(values):
    return lax.ppermute(values, "fsdp", [(f, (f + 2) % 8) for f in range(8)])


def across(values):
    return lax.ppermute(values, "fsdp", [(f, f ^ 1) for f in range(8)])


def gather_reduce(half):
    position = lax.axis_index("fsdp")
    size = lax.axis_size("fsdp")
    if size != 8:
        return [lax.all_gather(half, "fsdp", axis=0, tiled=True)], jnp.zeros((1,), jnp.int32)
    blocks, owners, moving = [], [], half
    for step in range(4):
        if step > 0:
            moving = around(moving)
        owner = (position - 2 * step + 8) % 8
        blocks += [moving, across(moving)]
        owners += [owner, owner ^ 1]
    return blocks, jnp.stack(owners).astype(jnp.int32)


def halves(values, core):
    half = values.shape[1] // 2
    return lax.dynamic_slice_in_dim(values, core * half, half, 1)


def per_device(
    images,
    valid,
    cotangent,
    w_reduce,
    gain_one,
    shift_one,
    w_group,
    gain_two,
    shift_two,
    w_expand,
    gain_three,
    shift_three,
):
    count, side, _, channels = images.shape
    width = w_reduce.shape[1]
    inner = width // GROUPS
    size = lax.axis_size("fsdp")
    position, core = lax.axis_index("fsdp"), lax.axis_index("core").astype(jnp.int32)
    rows = count * side * LINE

    def padded(values):
        return jnp.pad(values, ((0, 0), (0, 0), (0, LINE - side), (0, 0))).reshape(rows, channels)

    x, cot = padded(images), padded(cotangent)
    turned = x.T
    pixel = jnp.arange(LINE) < side
    mask = (valid.astype(F32)[:, None, None] * pixel[None, None, :].astype(F32)) * jnp.ones((1, side, 1), F32)
    mask = mask.reshape(rows, 1)

    cores = jnp.stack([core, 1 - core])
    blocks, owners = gather_reduce(halves(w_reduce, core))
    weights = []
    for block in blocks:
        weights += [block, swap_core(block)]
    slots = jnp.concatenate([owners, cores])
    slot_count = len(blocks)
    vectors = jnp.concatenate([gain_one, shift_one, gain_two, shift_two, gain_three, shift_three])
    vectors = jnp.pad(vectors, (0, width - vectors.size)).reshape(1, width)
    small = lax.all_gather(jnp.concatenate([w_group, vectors]), "fsdp", axis=0, tiled=False)
    w_group_all = small[:, : w_group.shape[0]].reshape(TAPS * inner, width)
    vectors = small[:, w_group.shape[0]].astype(F32)
    cut, per, outer = [], gain_one.shape[0], gain_three.shape[0]
    for begin, length in (
        (0, per), (per, per), (2 * per, per), (3 * per, per), (4 * per, outer), (4 * per + outer, outer)
    ):
        cut.append(vectors[:, begin : begin + length].reshape(1, -1))
    g1, s1, g2, s2, g3, s3 = cut
    half_expand = after(halves(w_expand, core), blocks[len(blocks) // 2])
    expand_mine = lax.all_gather(half_expand, "fsdp", axis=0, tiled=True)

    red, part = call(
        functools.partial(reduce_kernel, slot_count),
        [shape((rows, width), F32), shape((2, width), F32)],
        slots, mask, x, *weights, scalars=1, name="reduce", flops=2 * rows * width * channels,
    )
    pixel_count = jnp.sum(valid.astype(F32)) * (side * side)
    part = jnp.concatenate([part, jnp.full((1, width), 1.0, F32) * pixel_count], axis=0)
    wide = call(
        widen_kernel,
        shape((TAPS, width // BLOCK, BLOCK, BLOCK), BF16),
        after(w_group_all, part), name="widen", flops=1 << 30,
    )
    total = everywhere(part)
    total_one, pixels = total[0:2], total[2:3]
    pads, grouped, part = call(
        functools.partial(group_kernel, side),
        [
            shape((3, count, (side + 2) * LINE, width), BF16),
            shape((rows, width), F32),
            shape((2, width), F32),
        ],
        mask, red, total_one, pixels, g1, s1, wide, name="group", flops=2 * TAPS * rows * width * BLOCK,
    )
    total_two = everywhere(part)
    expand_other = swap_core(after(expand_mine, total_two))
    act_two, expanded, part = call(
        expand_kernel,
        [shape((rows, width), BF16), shape((rows, channels), F32), shape((2, channels), F32)],
        cores, mask, grouped, total_two, pixels, g2, s2, expand_mine, expand_other,
        scalars=1, name="expand", flops=2 * rows * width * channels,
    )
    total_three = everywhere(part)
    output, grad_summed, part = call(
        functools.partial(output_kernel, side),
        [shape(images.shape, BF16), shape((rows, channels), F32), shape((2, channels), F32)],
        valid, expanded, total_three, pixels, g3, s3, x, cot, scalars=1, name="output",
    )

    sums_three = everywhere(part)
    flat_three, dz_two, part = call(
        back_expand_kernel,
        [shape((rows, channels), BF16), shape((rows, width), F32), shape((2, width), F32)],
        cores, mask, grad_summed, expanded, total_three, sums_three, pixels, g3, grouped, total_two, g2, s2,
        expand_mine, expand_other, scalars=1, name="back_expand", flops=2 * rows * width * channels,
    )
    send, keep = call(
        weight_expand_kernel,
        [shape((width, channels // 2), BF16)] * 2,
        cores, act_two, flat_three, scalars=1, name="weight_expand", flops=2 * rows * width * channels,
    )
    chip = (keep.astype(F32) + swap_core(send).astype(F32)).astype(BF16)
    own_expand = lax.psum_scatter(chip, "fsdp", scatter_dimension=0, tiled=True)
    own_expand = call(add_kernel, shape(own_expand.shape, F32), own_expand, swap_x(own_expand), name="add")
    grad_w_expand = call(
        join_kernel, shape(w_expand.shape, F32), cores, own_expand, swap_core(own_expand), scalars=1, name="join"
    )

    sums_two = everywhere(part)
    flat_two, dz_one, part = call(
        functools.partial(back_group_kernel, side),
        [shape((rows, width), BF16), shape((rows, width), F32), shape((2, width), F32)],
        mask, dz_two, grouped, total_two, sums_two, pixels, g2, red, total_one, g1, s1, wide,
        scratch=[pltpu.VMEM((3, count, (side + 2) * LINE, width), BF16)],
        name="back_group", flops=2 * TAPS * rows * width * BLOCK,
    )
    group_term = call(
        functools.partial(weight_group_kernel, side),
        shape((TAPS * inner, width), BF16),
        pads, flat_two, name="weight_group", flops=2 * TAPS * rows * width * BLOCK,
    )
    shard = w_group.shape[0]
    tail = -(-shard // 16) * 16
    group_term = jnp.pad(group_term.reshape(size, shard, width), ((0, 0), (0, tail - shard), (0, 0)))

    sums_one = everywhere(part)
    depth, half = w_reduce.shape[0], width // 2
    if size == 8:
        order = jnp.concatenate([jnp.roll(owners.reshape(4, 2), -1, 0)[:, ::-1].T.reshape(-1), cores])
        parts = size
    else:
        order = jnp.concatenate([jnp.arange(size, dtype=jnp.int32), cores])
    flat_one, send = call(
        back_reduce_kernel,
        [shape((rows, width), BF16), shape((size, depth + tail, half), BF16)],
        order, mask, dz_one, red, total_one, sums_one, pixels, g1, turned, group_term,
        scalars=1, name="back_reduce", flops=rows * width * channels,
    )
    near = swap_core(send)

    def sums(places, arrived, dtype=BF16):
        return call(
            functools.partial(block_sum_kernel, size, places),
            [shape((depth + tail, half), dtype)] * len(places),
            order, turned, group_term, flat_one, near, *arrived,
            scalars=1, name="block_sum", flops=2 * rows * depth * half * len(places),
        )

    if size == 8:
        ahead = sums((0, 1, 2, 3), ())
        ahead = [across(block) for block in ahead]
        moving = []
        for step in range(3):
            (block,) = sums((4 + step,), [ahead[step]] + moving)
            moving = [around(block)]
        (own_reduce,) = sums((7,), [ahead[3]] + moving)
    else:
        whole = jnp.stack(sums(tuple(range(size)), ())).reshape(size * (depth + tail), half)
        own_reduce = lax.psum_scatter(whole, "fsdp", scatter_dimension=0, tiled=True)
    own_reduce = call(add_kernel, shape(own_reduce.shape, F32), own_reduce, swap_x(own_reduce), name="add")
    grad_w_reduce, grad_w_group = call(
        join_kernel,
        [shape(w_reduce.shape, F32), shape(w_group.shape, F32)],
        cores, own_reduce, swap_core(own_reduce), scalars=1, name="join",
    )
    grad_input = call(
        functools.partial(grad_input_kernel, slot_count, side),
        shape(images.shape, BF16),
        slots, flat_one, grad_summed, *weights,
        scalars=1, scratch=[pltpu.VMEM((rows, channels), F32)], name="grad_input",
        flops=2 * rows * width * channels,
    )

    def own_shard(total, shard):
        return lax.dynamic_slice_in_dim(total, position * shard, shard, 0)

    return (
        output,
        grad_input,
        grad_w_reduce,
        grad_w_group,
        grad_w_expand,
        own_shard(sums_one[1], per),
        own_shard(sums_one[0], per),
        own_shard(sums_two[1], per),
        own_shard(sums_two[0], per),
        own_shard(sums_three[1], outer),
        own_shard(sums_three[0], outer),
    )


def solution(mesh):
    fsdp, dp = mesh.shape["fsdp"], mesh.shape["dp"]
    split = Mesh(mesh.devices.reshape(fsdp, dp // 2, 2), ("fsdp", "x", "core"))
    images, rows, vector = P(("fsdp", "x", "core"), None, None, None), P("fsdp", None), P("fsdp")
    return jax.shard_map(
        per_device,
        mesh=split,
        in_specs=(
            images, P(("fsdp", "x", "core")), images,
            rows, vector, vector, rows, vector, vector, rows, vector, vector,
        ),
        out_specs=(images, images, rows, rows, rows) + (vector,) * 6,
        check_vma=False,
    )
```

```python
import functools

import jax
import jax.numpy as jnp
from jax import lax
from jax.experimental import pallas as pl
from jax.experimental.pallas import tpu as pltpu
from jax.sharding import Mesh
from jax.sharding import PartitionSpec as P

GROUPS = 32
TAPS = 9
LINE = 16
BLOCK = 256
epsilon = 1e-05
BF16, F32 = jnp.bfloat16, jnp.float32
SWAP = [(0, 1), (1, 0)]
NN, NT = ((1,), (0,)), ((1,), (1,))
CHIPS = ("fsdp", "x")


def sigmoid(values):
    return 0.5 * jnp.tanh(0.5 * values) + 0.5


def dsilu(values):
    sigma = sigmoid(values)
    return sigma * (1.0 + values * (1.0 - sigma))


def dot(a, b, contract=NN):
    return lax.dot_general(a, b, (contract, ((), ())), preferred_element_type=F32)


def after(values, *others):
    return lax.optimization_barrier((values,) + others)[0]


def shape(dims, dtype):
    return jax.ShapeDtypeStruct(dims, dtype)


def call(kernel, outs, args, scalars=0, scratch=(), vmem=8, name=None, flops=0):
    vm = pl.BlockSpec(memory_space=pltpu.VMEM)
    sm = pl.BlockSpec(memory_space=pltpu.SMEM)
    return pl.pallas_call(
        kernel,
        out_shape=outs,
        in_specs=[sm] * scalars + [vm] * (len(args) - scalars),
        out_specs=[vm] * len(outs),
        scratch_shapes=list(scratch),
        compiler_params=pltpu.CompilerParams(vmem_limit_bytes=vmem << 20),
        cost_estimate=pl.CostEstimate(flops=flops, bytes_accessed=1 << 20, transcendentals=0),
        name=name,
    )(*args)


def moments(total, pixels):
    mean = total[0:1, :] / pixels
    inverse = lax.rsqrt(total[1:2, :] / pixels - mean * mean + epsilon)
    return mean, inverse


def line_mask(columns, side):
    return lax.broadcasted_iota(jnp.int32, (LINE, columns), 0) < side


def column_sums(values):
    return jnp.sum(values, axis=0, keepdims=True)


def line_at(step):
    return pl.ds(pl.multiple_of(step * LINE, LINE), LINE)


def fold(values):
    return values[0:8] + values[8:16]


def part_at(part, half, at=0, length=None):
    core = lax.axis_index("core")
    side = core if part == 0 else 1 - core
    length = half if length is None else length
    return pl.ds(pl.multiple_of(side * half + at, 128), length)


def block_owner(slot):
    position = lax.axis_index("fsdp")
    way = 1 - 2 * lax.axis_index("x")
    step = (0, -way, way, 2)[slot % 4]
    owner = lax.rem(position + 2 * step + 8, 8)
    return owner if slot < 4 else owner + 1 - 2 * lax.rem(owner, 2)


def rows_of(owner, depth):
    return pl.ds(pl.multiple_of(owner * depth, 16), depth)


def reduce_kernel(slots, depth, side, valid, mask, x, *refs):
    weights, (red, stats) = refs[: 2 * slots], refs[2 * slots :]
    half = weights[0].shape[1]
    for part in range(2):
        for at in range(0, half, BLOCK):
            total = None
            for slot in range(slots):
                if slots == 1:
                    piece = x[...]
                else:
                    piece = x[:, pl.ds(pl.multiple_of(block_owner(slot) * depth, 128), depth)]
                term = dot(piece, weights[2 * slot + part][0:depth, at : at + BLOCK])
                total = term if total is None else total + term
            columns = part_at(part, half, at, BLOCK)
            red[:, columns] = total
            masked = total * mask[...]
            stats[0:1, columns] = column_sums(masked)
            stats[1:2, columns] = column_sums(masked * total)
    pixels = valid[0].astype(F32)
    for image in range(1, valid.shape[0]):
        pixels = pixels + valid[image].astype(F32)
    stats[2:3, :] = jnp.full((1, stats.shape[1]), 1.0, F32) * (pixels * (side * side))


def spread_kernel(slots, depth, *refs):
    blocks, (wide, inner_vectors, outer_vectors, held, rows) = refs[: 2 * slots], refs[2 * slots :]
    extra, half = held.shape[1], held.shape[2] // 2
    for slot in range(slots):
        for part in range(2):
            held[block_owner(slot), :, part_at(part, half)] = blocks[2 * slot + part][depth : depth + extra, :].astype(F32)
    shard = rows.shape[0] // slots
    per, outer = inner_vectors.shape[1] // slots, outer_vectors.shape[1] // slots
    for owner in range(slots):
        rows[owner * shard : (owner + 1) * shard, :] = held[owner, 0:shard, :]
        for row in range(4):
            inner_vectors[row : row + 1, owner * per : (owner + 1) * per] = held[
                owner, shard : shard + 1, row * per : (row + 1) * per
            ]
        for row in range(2):
            outer_vectors[row : row + 1, owner * outer : (owner + 1) * outer] = held[
                owner, shard : shard + 1, 4 * per + row * outer : 4 * per + (row + 1) * outer
            ]
    widen(rows, wide)


def widen_kernel(weight, wide, rows):
    rows[...] = weight[...].astype(F32)
    widen(rows, wide)


def widen(weight, wide):
    taps, blocks = wide.shape[:2]
    inner = weight.shape[0] // taps
    row = lax.broadcasted_iota(jnp.int32, (BLOCK, BLOCK), 0) // inner
    column = lax.broadcasted_iota(jnp.int32, (BLOCK, BLOCK), 1) // inner
    own = row == column
    for tap in range(taps):
        for block in range(blocks):
            piece = weight[tap * inner : (tap + 1) * inner, block * BLOCK : (block + 1) * BLOCK]
            tall = jnp.concatenate([piece] * (BLOCK // inner), axis=0)
            wide[tap, block] = jnp.where(own, tall, 0.0).astype(BF16)


def fill_pads(pads, image, line, values):
    rows = pl.ds(pl.multiple_of((line + 1) * LINE, LINE), LINE)
    pads[0, image, rows, :] = pltpu.roll(values, 1, 0).astype(BF16)
    pads[1, image, rows, :] = values.astype(BF16)
    pads[2, image, rows, :] = pltpu.roll(values, LINE - 1, 0).astype(BF16)


def clear_pads(pads):
    images, rows, columns = pads.shape[1:]
    zeros = jnp.zeros((3, images, LINE, columns), BF16)
    pads[:, :, 0:LINE, :] = zeros
    pads[:, :, rows - LINE : rows, :] = zeros


def convolve(pads, wide, image, block, rows, turned=False):
    columns = slice(block * BLOCK, (block + 1) * BLOCK)
    value = None
    for tap in range(TAPS):
        top, left = divmod(TAPS - 1 - tap if turned else tap, 3)
        piece = pads[left, image, top * LINE : top * LINE + rows, columns]
        term = dot(piece, wide[tap, block], NT if turned else NN)
        value = term if value is None else value + term
    return value


def group_kernel(side, mask, total, vectors, red, wide, pads, grouped, stats):
    images, padded, width = pads.shape[1:]
    rows = side * LINE
    mean, inverse = moments(total, total[2:3, :])
    scale, bias = inverse * vectors[0:1, :], vectors[1:2, :]
    clear_pads(pads)
    inside = line_mask(width, side)

    def body(step, carry):
        normal = (red[line_at(step), :] - mean) * scale + bias
        fill_pads(pads, step // side, step % side, jnp.where(inside, normal * sigmoid(normal), 0.0))
        return carry

    lax.fori_loop(0, images * side, body, 0)
    for block in range(width // BLOCK):
        columns = slice(block * BLOCK, (block + 1) * BLOCK)
        sums = [0.0, 0.0]
        for image in range(images):
            at = slice(image * rows, (image + 1) * rows)
            value = convolve(pads, wide, image, block, rows)
            grouped[at, columns] = value
            masked = value * mask[at, :]
            sums = [sums[0] + column_sums(masked), sums[1] + column_sums(masked * value)]
        stats[0:1, columns] = sums[0]
        stats[1:2, columns] = sums[1]


def expand_kernel(side, mask, total, first, vectors, grouped, mine, other, act, expanded, stats):
    rows, width = grouped.shape
    mean, inverse = moments(total, first[2:3, :])
    scale, bias = inverse * vectors[2:3, :], vectors[3:4, :]
    inside = line_mask(width, side)

    def body(step, carry):
        at = line_at(step)
        normal = (grouped[at, :] - mean) * scale + bias
        act[at, :] = jnp.where(inside, normal * sigmoid(normal), 0.0).astype(BF16)
        return carry

    lax.fori_loop(0, rows // LINE, body, 0)
    half = mine.shape[1]
    for part, weight in enumerate((mine, other)):
        for at in range(0, half, BLOCK):
            value = dot(act[...], weight[:, at : at + BLOCK])
            columns = part_at(part, half, at, BLOCK)
            expanded[:, columns] = value
            masked = value * mask[...]
            stats[0:1, columns] = column_sums(masked)
            stats[1:2, columns] = column_sums(masked * value)


def output_kernel(side, valid, total, first, vectors, expanded, x, cotangent, output, grad, stats):
    rows, channels = expanded.shape
    mean, inverse = moments(total, first[2:3, 0:1])
    gains, bias = vectors[0:1, :], vectors[1:2, :]
    zero = jnp.zeros((8, channels), F32)

    def body(step, carry):
        image, line = step // side, step % side
        at = line_at(step)
        keep = valid[image].astype(F32)
        normed = (expanded[at, :] - mean) * inverse
        summed = normed * gains + bias + x[at, :].astype(F32)
        sigma = sigmoid(summed)
        output[image, line] = (summed * sigma * keep).astype(BF16)[0:side]
        here = cotangent[at, :].astype(F32) * keep * (sigma * (1.0 + summed * (1.0 - sigma)))
        grad[at, :] = here
        return carry[0] + fold(here), carry[1] + fold(here * normed)

    one, two = lax.fori_loop(0, rows // LINE, body, (zero, zero))
    stats[0:1, :] = column_sums(one)
    stats[1:2, :] = column_sums(two)


def back_expand_kernel(
    mask, total, sums, first, vectors, total_two, vectors_two, grad, expanded, grouped, mine, other, flat, dz, stats
):
    rows, width = grouped.shape
    pixels = first[2:3, 0:1]
    mean, inverse = moments(total, pixels)
    scale = inverse * vectors[0:1, :]
    shifted, scaled = sums[0:1, :] / pixels, sums[1:2, :] / pixels

    def body(step, carry):
        at = line_at(step)
        normed = (expanded[at, :] - mean) * inverse
        flat[at, :] = (scale * (grad[at, :] - mask[at, :] * (shifted + normed * scaled))).astype(BF16)
        return carry

    lax.fori_loop(0, rows // LINE, body, 0)
    half = mine.shape[1]
    for at in range(0, width, BLOCK):
        value = None
        for part, weight in enumerate((mine, other)):
            term = dot(flat[:, part_at(part, half)], weight[at : at + BLOCK, :], NT)
            value = term if value is None else value + term
        dz[:, at : at + BLOCK] = value
    mean_two, inverse_two = moments(total_two, first[2:3, :])
    gains, bias = vectors_two[2:3, :], vectors_two[3:4, :]
    zero = jnp.zeros((8, width), F32)

    def tail(step, carry):
        at = line_at(step)
        normed = (grouped[at, :] - mean_two) * inverse_two
        here = dz[at, :] * dsilu(normed * gains + bias)
        dz[at, :] = here
        return carry[0] + fold(here), carry[1] + fold(here * normed)

    one, two = lax.fori_loop(0, rows // LINE, tail, (zero, zero))
    stats[0:1, :] = column_sums(one)
    stats[1:2, :] = column_sums(two)


def weight_expand_kernel(act, flat, send, keep):
    half = send.shape[1]
    turned = act[...].T
    for part, out in ((1, send), (0, keep)):
        for at in range(0, half, BLOCK):
            out[:, at : at + BLOCK] = dot(turned, flat[:, part_at(part, half, at, BLOCK)]).astype(BF16)


def back_group_kernel(
    side, mask, total, sums, first, vectors, dz, grouped, red, wide, flat, dz_one, stats, pads
):
    images, padded, width = pads.shape[1:]
    rows = side * LINE
    pixels = first[2:3, :]
    mean, inverse = moments(total, pixels)
    scale = inverse * vectors[2:3, :]
    shifted, scaled = sums[0:1, :] / pixels, sums[1:2, :] / pixels
    clear_pads(pads)

    def body(step, carry):
        at = line_at(step)
        normed = (grouped[at, :] - mean) * inverse
        value = scale * (dz[at, :] - mask[at, :] * (shifted + normed * scaled))
        flat[at, :] = value.astype(BF16)
        fill_pads(pads, step // side, step % side, value)
        return carry

    lax.fori_loop(0, images * side, body, 0)
    for block in range(width // BLOCK):
        columns = slice(block * BLOCK, (block + 1) * BLOCK)
        for image in range(images):
            dz_one[image * rows : (image + 1) * rows, columns] = convolve(pads, wide, image, block, rows, True)
    mean_one, inverse_one = moments(first, pixels)
    gains, bias = vectors[0:1, :], vectors[1:2, :]
    inside = line_mask(width, side)
    zero = jnp.zeros((8, width), F32)

    def tail(step, carry):
        at = line_at(step)
        normed = (red[at, :] - mean_one) * inverse_one
        here = jnp.where(inside, dz_one[at, :] * dsilu(normed * gains + bias), 0.0)
        dz_one[at, :] = here
        return carry[0] + fold(here), carry[1] + fold(here * normed)

    one, two = lax.fori_loop(0, images * side, tail, (zero, zero))
    stats[0:1, :] = column_sums(one)
    stats[1:2, :] = column_sums(two)


def weight_group_kernel(side, pads, flat, out):
    images, padded, width = pads.shape[1:]
    rows = side * LINE
    inner = width // GROUPS
    row = lax.broadcasted_iota(jnp.int32, (BLOCK, BLOCK), 0) // inner
    column = lax.broadcasted_iota(jnp.int32, (BLOCK, BLOCK), 1) // inner
    own = row == column
    lanes = 128 // inner
    pick_row = lax.broadcasted_iota(jnp.int32, (BLOCK, 128), 0) % inner
    pick_lane = lax.broadcasted_iota(jnp.int32, (BLOCK, 128), 1)
    picks = [
        jnp.where(pick_lane == pick_row + inner * lane, 1.0, 0.0).astype(BF16) for lane in range(lanes)
    ]
    for block in range(width // BLOCK):
        columns = slice(block * BLOCK, (block + 1) * BLOCK)
        turned = [flat[image * rows : (image + 1) * rows, columns].T for image in range(images)]
        for begin in range(0, TAPS, lanes):
            packed = None
            taps = range(begin, min(begin + lanes, TAPS))
            for tap in taps:
                top, left = divmod(tap, 3)
                value = None
                for image in range(images):
                    term = dot(turned[image], pads[left, image, top * LINE : top * LINE + rows, columns])
                    value = term if value is None else value + term
                term = dot(jnp.where(own, value, 0.0).astype(BF16), picks[tap - begin])
                packed = term if packed is None else packed + term
            length = len(taps) * inner
            out[begin * inner : begin * inner + length, columns] = packed.T[0:length].astype(BF16)


def back_reduce_kernel(blocks, small, mask, first, sums, vectors, dz, red, turned, group, flat, send):
    rows, width = red.shape
    pixels = first[2:3, :]
    mean, inverse = moments(first, pixels)
    scale = inverse * vectors[0:1, :]
    shifted, scaled = sums[0:1, :] / pixels, sums[1:2, :] / pixels

    def body(step, carry):
        at = line_at(step)
        normed = (red[at, :] - mean) * inverse
        flat[at, :] = (scale * (dz[at, :] - mask[at, :] * (shifted + normed * scaled))).astype(BF16)
        return carry

    lax.fori_loop(0, rows // LINE, body, 0)
    tall, half = send.shape[1:]
    depth = tall - group.shape[1]
    columns = part_at(1, half)
    for block in range(blocks):
        owner = block_owner(block) if small else block
        send[block, 0:depth, :] = dot(turned[rows_of(owner, depth), :], flat[:, columns]).astype(BF16)
        send[block, depth:tall, :] = group[owner, :, columns]


def block_sum_kernel(small, places, turned, group, flat, near, *refs):
    arrived, outs = refs[: len(refs) - len(places)], refs[len(refs) - len(places) :]
    tall, half = near.shape[1:]
    depth = tall - group.shape[1]
    columns = part_at(0, half)
    for out, (block, chosen) in zip(outs, places):
        owner = block_owner(block) if small else block
        value = dot(turned[rows_of(owner, depth), :], flat[:, columns]) + near[block, 0:depth, :].astype(F32)
        more = group[owner, :, columns].astype(F32) + near[block, depth:tall, :].astype(F32)
        for other in chosen:
            value = value + arrived[other][0:depth, :].astype(F32)
            more = more + arrived[other][depth:tall, :].astype(F32)
        out[0:depth, :] = value.astype(BF16)
        out[depth:tall, :] = more.astype(BF16)


def add_kernel(a, b, out):
    out[...] = (a[...].astype(F32) + b[...].astype(F32)).astype(out.dtype)


def join_kernel(mine, other, *outs):
    half = mine.shape[1]
    at = 0
    for out in outs:
        rows = out.shape[0]
        for part, values in enumerate((mine, other)):
            out[:, part_at(part, half)] = values[at : at + rows, :]
        at += -(-rows // 16) * 16


def own_kernel(*refs):
    number = len(refs) // 3
    position = lax.axis_index("fsdp")
    for at, total in enumerate(refs[:number]):
        for row, out in ((1, refs[number + 2 * at]), (0, refs[number + 2 * at + 1])):
            length = out.shape[1]
            out[...] = total[row : row + 1, pl.ds(pl.multiple_of(position * length, 128), length)]


def grad_input_kernel(slots, depth, side, flat, grad, *refs):
    weights, (out, held) = refs[: 2 * slots], refs[2 * slots :]
    half = weights[0].shape[1]
    for slot in range(slots):
        columns = pl.ds(pl.multiple_of(block_owner(slot) * depth, 128), depth) if slots > 1 else slice(None)
        value = grad[:, columns]
        for part in range(2):
            value = value + dot(flat[:, part_at(part, half)], weights[2 * slot + part][0:depth, :], NT)
        held[:, columns] = value

    def body(step, carry):
        out[step // side, step % side] = held[line_at(step), :].astype(BF16)[0:side]
        return carry

    lax.fori_loop(0, flat.shape[0] // LINE, body, 0)


def swap_core(values):
    return lax.ppermute(values, "core", SWAP)


def swap_x(values):
    if lax.axis_size("x") == 2:
        return lax.ppermute(values, "x", SWAP)
    return (lax.psum(values.astype(F32), "x") - values.astype(F32)).astype(values.dtype)


def sum_chips(values, flips):
    got = [lax.ppermute(values, CHIPS, [(at, at ^ flip) for at in range(16)]) for flip in flips]
    for other in got:
        values = values + other
    return values


def along(values, way):
    pairs = [(f * 2 + x, (f + 2 * way * (1 - 2 * x)) % 8 * 2 + x) for f in range(8) for x in range(2)]
    return lax.ppermute(values, CHIPS, pairs)


def across(values):
    return lax.ppermute(values, "fsdp", [(f, f ^ 1) for f in range(8)])


def gather_blocks(own):
    first = along(own, 1)
    other = across(own)
    first = after(first, other)
    passed, second, first_other = swap_x(first), along(first, 1), across(first)
    second = after(second, passed, first_other)
    first_other = after(first_other, second)
    passed_other, second_other = swap_x(first_other), across(second)
    return [own, first, passed, second, other, first_other, passed_other, second_other]


def halves(values, core):
    half = values.shape[1] // 2
    return lax.dynamic_slice_in_dim(values, core * half, half, 1)


def per_device(
    images,
    valid,
    cotangent,
    w_reduce,
    gain_one,
    shift_one,
    w_group,
    gain_two,
    shift_two,
    w_expand,
    gain_three,
    shift_three,
):
    count, side, _, channels = images.shape
    width = w_reduce.shape[1]
    inner = width // GROUPS
    size = lax.axis_size("fsdp")
    small = size == 8 and lax.axis_size("x") == 2
    position, core = lax.axis_index("fsdp"), lax.axis_index("core")
    rows = count * side * LINE
    per, outer, shard, depth = gain_one.shape[0], gain_three.shape[0], w_group.shape[0], w_reduce.shape[0]
    extra = -(-(shard + 1) // 16) * 16
    half = width // 2

    def everywhere(values, *meanwhile):
        if not small:
            return lax.psum(values, ("fsdp", "x", "core"))
        values = values + swap_core(values)
        return sum_chips(sum_chips(values, (1, 2, 3)), (4, 8, 12))

    def padded(values):
        return jnp.pad(values, ((0, 0), (0, 0), (0, LINE - side), (0, 0))).reshape(rows, channels)

    pixel = jnp.arange(LINE) < side
    mask = (valid.astype(F32)[:, None, None] * pixel[None, None, :].astype(F32)) * jnp.ones((1, side, 1), F32)
    mask = mask.reshape(rows, 1)
    x, cot = padded(images), padded(cotangent)
    turned = x.T

    expand_mine = lax.all_gather(halves(w_expand, core), "fsdp", axis=0, tiled=True)
    vectors = jnp.concatenate([gain_one, shift_one, gain_two, shift_two, gain_three, shift_three])
    vectors = jnp.pad(vectors, (0, width - vectors.size)).reshape(1, width)
    below = jnp.pad(jnp.concatenate([w_group, vectors]), ((0, extra - shard - 1), (0, 0)))
    own = halves(jnp.concatenate([w_reduce, below]), core)
    wide_shape = shape((TAPS, width // BLOCK, BLOCK, BLOCK), BF16)
    if small:
        weights = []
        for block in gather_blocks(own):
            weights += [block, swap_core(block)]
        slots, slot_depth = size, depth
    else:
        whole = lax.all_gather(own, "fsdp", axis=0, tiled=False)
        block = whole[:, :depth].reshape(channels, half)
        weights = [block, swap_core(block)]
        slots, slot_depth = 1, channels

    red, part = call(
        functools.partial(reduce_kernel, slots, slot_depth, side),
        [shape((rows, width), F32), shape((3, width), F32)],
        [valid, mask, x] + weights, scalars=1, name="reduce", flops=2 * rows * width * channels,
    )
    if small:
        wide, inner_vectors, outer_vectors = call(
            functools.partial(spread_kernel, slots, depth),
            [wide_shape, shape((4, width), F32), shape((2, channels), F32)],
            [after(weights[0], part)] + weights[1:],
            scratch=[pltpu.VMEM((size, extra, width), F32), pltpu.VMEM((size * shard, width), F32)],
            name="spread", flops=1 << 28,
        )
    else:
        mine = whole[:, depth:]
        other = swap_core(mine)
        packed = jnp.concatenate([jnp.where(core == 0, mine, other), jnp.where(core == 0, other, mine)], axis=2)
        (wide,) = call(
            widen_kernel, [wide_shape], [packed[:, :shard].reshape(size * shard, width)],
            scratch=[pltpu.VMEM((size * shard, width), F32)], name="widen",
        )
        line = packed[:, shard].astype(F32)
        inner_vectors = line[:, : 4 * per].reshape(size, 4, per).transpose(1, 0, 2).reshape(4, width)
        outer_vectors = line[:, 4 * per : 4 * per + 2 * outer].reshape(size, 2, outer)
        outer_vectors = outer_vectors.transpose(1, 0, 2).reshape(2, channels)
    first = everywhere(part)
    pad_shape = (3, count, (side + 2) * LINE, width)
    pads, grouped, part = call(
        functools.partial(group_kernel, side),
        [shape(pad_shape, BF16), shape((rows, width), F32), shape((2, width), F32)],
        [mask, first, inner_vectors, red, wide],
        name="group", flops=2 * TAPS * rows * width * BLOCK,
    )
    total_two = everywhere(part)
    expand_other = swap_core(after(expand_mine, part))
    act_two, expanded, part = call(
        functools.partial(expand_kernel, side),
        [shape((rows, width), BF16), shape((rows, channels), F32), shape((2, channels), F32)],
        [mask, total_two, first, inner_vectors, grouped, expand_mine, expand_other],
        name="expand", flops=2 * rows * width * channels,
    )
    total_three = everywhere(part)
    output, grad_summed, part = call(
        functools.partial(output_kernel, side),
        [shape(images.shape, BF16), shape((rows, channels), F32), shape((2, channels), F32)],
        [valid, total_three, first, outer_vectors, expanded, x, cot], scalars=1, name="output",
    )

    sums_three = everywhere(part)
    flat_three, dz_two, part = call(
        back_expand_kernel,
        [shape((rows, channels), BF16), shape((rows, width), F32), shape((2, width), F32)],
        [mask, total_three, sums_three, first, outer_vectors, total_two, inner_vectors, grad_summed, expanded, grouped,
         expand_mine, expand_other],
        name="back_expand", flops=2 * rows * width * channels,
    )
    sums_two = everywhere(part)
    send, keep = call(
        weight_expand_kernel,
        [shape((width, channels // 2), BF16)] * 2,
        [act_two, flat_three], name="weight_expand", flops=2 * rows * width * channels,
    )
    (chip,) = call(add_kernel, [shape(keep.shape, BF16)], [keep, swap_core(send)], name="add")
    own_expand = lax.psum_scatter(chip, "fsdp", scatter_dimension=0, tiled=True)
    (own_expand,) = call(add_kernel, [shape(own_expand.shape, F32)], [own_expand, swap_x(own_expand)], name="add")
    (grad_w_expand,) = call(join_kernel, [shape(w_expand.shape, F32)], [own_expand, swap_core(own_expand)], name="join")

    flat_two, dz_one, part = call(
        functools.partial(back_group_kernel, side),
        [shape((rows, width), BF16), shape((rows, width), F32), shape((2, width), F32)],
        [mask, total_two, sums_two, first, inner_vectors, dz_two, grouped, red, wide],
        scratch=[pltpu.VMEM(pad_shape, BF16)], name="back_group", flops=2 * TAPS * rows * width * BLOCK,
    )
    sums_one = everywhere(part)
    (group_term,) = call(
        functools.partial(weight_group_kernel, side),
        [shape((TAPS * inner, width), BF16)],
        [pads, flat_two], name="weight_group", flops=2 * TAPS * rows * width * BLOCK,
    )
    group_term = jnp.pad(group_term.reshape(size, shard, width), ((0, 0), (0, extra - shard), (0, 0)))
    tall = depth + extra
    flat_one, send = call(
        functools.partial(back_reduce_kernel, size, small),
        [shape((rows, width), BF16), shape((size, tall, half), BF16)],
        [mask, first, sums_one, inner_vectors, dz_one, red, turned, group_term],
        name="back_reduce", flops=rows * width * channels,
    )
    near = swap_core(send)

    def sums(places, arrived=()):
        return call(
            functools.partial(block_sum_kernel, small, places),
            [shape((tall, half), BF16)] * len(places),
            [turned, group_term, flat_one, near] + list(arrived),
            name="block_sum", flops=2 * rows * depth * half * len(places),
        )

    def back_input(flat):
        (out,) = call(
            functools.partial(grad_input_kernel, slots, slot_depth, side),
            [shape(images.shape, BF16)],
            [flat, grad_summed] + weights,
            scratch=[pltpu.VMEM((rows, channels), F32)], name="grad_input", flops=2 * rows * width * channels,
        )
        return out.transpose(1, 2, 0, 3)

    def own_shards(*totals):
        if not small:
            cut = []
            for total, length in zip(totals, (per, per, outer)):
                cut += [lax.dynamic_slice_in_dim(total[row], position * length, length, 0) for row in (1, 0)]
            return cut
        lengths = (per, per, per, per, outer, outer)
        return [out.reshape(-1) for out in call(own_kernel, [shape((1, n), F32) for n in lengths], totals, name="own")]

    if small:
        passed_other, second_other = sums(((6, ()), (7, ())))
        got_x, got_y = swap_x(passed_other), across(second_other)
        grad_input = back_input(after(flat_one, second_other))
        got_x = after(got_x, grad_input)
        first_other, passed, second = sums(((5, (0,)), (2, ()), (3, (1,))), (got_x, got_y))
        got = [swap_x(passed), along(second, -1), across(first_other)]
        shards = own_shards(after(sums_one, second), sums_two, sums_three)
        first_own, other = sums(((1, (0, 1, 2)), (4, ())), got)
        got = [along(first_own, -1), across(other)]
        (own_reduce,) = sums(((0, (0, 1)),), got)
    else:
        grad_input = back_input(flat_one)
        shards = own_shards(sums_one, sums_two, sums_three)
        whole = jnp.stack(sums(tuple((at, ()) for at in range(size)))).reshape(size * tall, half)
        own_reduce = lax.psum_scatter(whole, "fsdp", scatter_dimension=0, tiled=True)
    (own_reduce,) = call(add_kernel, [shape(own_reduce.shape, F32)], [own_reduce, swap_x(own_reduce)], name="add")
    grad_w_reduce, grad_w_group = call(
        join_kernel,
        [shape(w_reduce.shape, F32), shape(w_group.shape, F32)],
        [own_reduce, swap_core(own_reduce)], name="join",
    )
    return (output, grad_input.transpose(2, 0, 1, 3), grad_w_reduce, grad_w_group, grad_w_expand) + tuple(shards)


def solution(mesh):
    fsdp, dp = mesh.shape["fsdp"], mesh.shape["dp"]
    split = Mesh(mesh.devices.reshape(fsdp, dp // 2, 2), ("fsdp", "x", "core"))
    images, rows, vector = P(("fsdp", "x", "core"), None, None, None), P("fsdp", None), P("fsdp")
    return jax.shard_map(
        per_device,
        mesh=split,
        in_specs=(
            images, P(("fsdp", "x", "core")), images,
            rows, vector, vector, rows, vector, vector, rows, vector, vector,
        ),
        out_specs=(images, images, rows, rows, rows) + (vector,) * 6,
        check_vma=False,
    )
```

```python
import functools

import jax
import jax.numpy as jnp
from jax import lax
from jax.experimental import pallas as pl
from jax.experimental.pallas import tpu as pltpu
from jax.sharding import Mesh
from jax.sharding import PartitionSpec as P

GROUPS = 32
TAPS = 9
LINE = 16
BLOCK = 256
epsilon = 1e-05
BF16, F32 = jnp.bfloat16, jnp.float32
SWAP = [(0, 1), (1, 0)]
NN, NT = ((1,), (0,)), ((1,), (1,))
CHIPS = ("fsdp", "x")


def sigmoid(values):
    return 0.5 * jnp.tanh(0.5 * values) + 0.5


def dsilu(values):
    sigma = sigmoid(values)
    return sigma * (1.0 + values * (1.0 - sigma))


def dot(a, b, contract=NN):
    return lax.dot_general(a, b, (contract, ((), ())), preferred_element_type=F32)


def after(values, *others):
    return lax.optimization_barrier((values,) + others)[0]


def together(*values):
    return lax.optimization_barrier(values)


def shape(dims, dtype):
    return jax.ShapeDtypeStruct(dims, dtype)


def call(kernel, outs, args, scalars=0, scratch=(), vmem=8, name=None, flops=0):
    vm = pl.BlockSpec(memory_space=pltpu.VMEM)
    sm = pl.BlockSpec(memory_space=pltpu.SMEM)
    return pl.pallas_call(
        kernel,
        out_shape=outs,
        in_specs=[sm] * scalars + [vm] * (len(args) - scalars),
        out_specs=[vm] * len(outs),
        scratch_shapes=list(scratch),
        compiler_params=pltpu.CompilerParams(vmem_limit_bytes=vmem << 20),
        cost_estimate=pl.CostEstimate(flops=flops, bytes_accessed=1 << 20, transcendentals=0),
        name=name,
    )(*args)


def moments(total, pixels):
    mean = total[0:1, :] / pixels
    inverse = lax.rsqrt(total[1:2, :] / pixels - mean * mean + epsilon)
    return mean, inverse


def line_mask(columns, side):
    return lax.broadcasted_iota(jnp.int32, (LINE, columns), 0) < side


def column_sums(values):
    return jnp.sum(values, axis=0, keepdims=True)


def line_at(step):
    return pl.ds(pl.multiple_of(step * LINE, LINE), LINE)


def fold(values):
    return values[0:8] + values[8:16]


def part_at(part, half, at=0, length=None):
    core = lax.axis_index("core")
    side = core if part == 0 else 1 - core
    length = half if length is None else length
    return pl.ds(pl.multiple_of(side * half + at, 128), length)


def block_owner(slot):
    position = lax.axis_index("fsdp")
    way = 1 - 2 * lax.axis_index("x")
    step = (0, -way, way, 2)[slot % 4]
    owner = lax.rem(position + 2 * step + 8, 8)
    return owner if slot < 4 else owner + 1 - 2 * lax.rem(owner, 2)


def rows_of(owner, depth):
    return pl.ds(pl.multiple_of(owner * depth, 16), depth)


def pack_kernel(side, valid, weight, group, vectors, out, mask):
    depth, half = weight.shape[0], out.shape[1]
    shard, extra = group.shape[0], out.shape[0] - weight.shape[0]
    columns = part_at(0, half)
    out[0:depth, :] = weight[:, columns]
    below = [group[:, columns].astype(F32), vectors[:, columns].astype(F32)]
    if extra > shard + 1:
        below.append(jnp.zeros((extra - shard - 1, half), F32))
    out[depth : depth + extra, :] = jnp.concatenate(below, axis=0).astype(BF16)
    images = valid.shape[0]
    rows = mask.shape[0] // images
    inside = lax.broadcasted_iota(jnp.int32, (rows, 1), 0) % LINE < side
    for image in range(images):
        mask[image * rows : (image + 1) * rows, :] = jnp.where(inside, valid[image].astype(F32), 0.0)


def reduce_kernel(slots, depth, side, valid, mask, x, *refs):
    weights, (red, stats) = refs[: 2 * slots], refs[2 * slots :]
    half = weights[0].shape[1]
    for part in range(2):
        for at in range(0, half, BLOCK):
            total = None
            for slot in range(slots):
                if slots == 1:
                    piece = x[...]
                else:
                    piece = x[:, pl.ds(pl.multiple_of(block_owner(slot) * depth, 128), depth)]
                term = dot(piece, weights[2 * slot + part][0:depth, at : at + BLOCK])
                total = term if total is None else total + term
            columns = part_at(part, half, at, BLOCK)
            red[:, columns] = total
            masked = total * mask[...]
            stats[0:1, columns] = column_sums(masked)
            stats[1:2, columns] = column_sums(masked * total)
    pixels = valid[0].astype(F32)
    for image in range(1, valid.shape[0]):
        pixels = pixels + valid[image].astype(F32)
    stats[2:3, :] = jnp.full((1, stats.shape[1]), 1.0, F32) * (pixels * (side * side))


def spread_kernel(slots, depth, *refs):
    blocks, (wide, inner_vectors, outer_vectors, held, rows) = refs[: 2 * slots], refs[2 * slots :]
    extra, half = held.shape[1], held.shape[2] // 2
    for slot in range(slots):
        for part in range(2):
            held[block_owner(slot), :, part_at(part, half)] = blocks[2 * slot + part][depth : depth + extra, :].astype(F32)
    shard = rows.shape[0] // slots
    per, outer = inner_vectors.shape[1] // slots, outer_vectors.shape[1] // slots
    for owner in range(slots):
        rows[owner * shard : (owner + 1) * shard, :] = held[owner, 0:shard, :]
        for row in range(4):
            inner_vectors[row : row + 1, owner * per : (owner + 1) * per] = held[
                owner, shard : shard + 1, row * per : (row + 1) * per
            ]
        for row in range(2):
            outer_vectors[row : row + 1, owner * outer : (owner + 1) * outer] = held[
                owner, shard : shard + 1, 4 * per + row * outer : 4 * per + (row + 1) * outer
            ]
    widen(rows, wide)


def widen_kernel(weight, wide, rows):
    rows[...] = weight[...].astype(F32)
    widen(rows, wide)


def widen(weight, wide):
    taps, blocks = wide.shape[:2]
    inner = weight.shape[0] // taps
    row = lax.broadcasted_iota(jnp.int32, (BLOCK, BLOCK), 0) // inner
    column = lax.broadcasted_iota(jnp.int32, (BLOCK, BLOCK), 1) // inner
    own = row == column
    for tap in range(taps):
        for block in range(blocks):
            piece = weight[tap * inner : (tap + 1) * inner, block * BLOCK : (block + 1) * BLOCK]
            tall = jnp.concatenate([piece] * (BLOCK // inner), axis=0)
            wide[tap, block] = jnp.where(own, tall, 0.0).astype(BF16)


def fill_pads(pads, image, line, values):
    rows = pl.ds(pl.multiple_of((line + 1) * LINE, LINE), LINE)
    pads[0, image, rows, :] = pltpu.roll(values, 1, 0).astype(BF16)
    pads[1, image, rows, :] = values.astype(BF16)
    pads[2, image, rows, :] = pltpu.roll(values, LINE - 1, 0).astype(BF16)


def clear_pads(pads):
    images, rows, columns = pads.shape[1:]
    zeros = jnp.zeros((3, images, LINE, columns), BF16)
    pads[:, :, 0:LINE, :] = zeros
    pads[:, :, rows - LINE : rows, :] = zeros


def convolve(pads, wide, image, block, rows, turned=False):
    columns = slice(block * BLOCK, (block + 1) * BLOCK)
    value = None
    for tap in range(TAPS):
        top, left = divmod(TAPS - 1 - tap if turned else tap, 3)
        piece = pads[left, image, top * LINE : top * LINE + rows, columns]
        term = dot(piece, wide[tap, block], NT if turned else NN)
        value = term if value is None else value + term
    return value


def group_kernel(side, mask, total, vectors, red, wide, pads, grouped, stats):
    images, padded, width = pads.shape[1:]
    rows = side * LINE
    mean, inverse = moments(total, total[2:3, :])
    scale, bias = inverse * vectors[0:1, :], vectors[1:2, :]
    clear_pads(pads)
    inside = line_mask(width, side)

    def body(step, carry):
        normal = (red[line_at(step), :] - mean) * scale + bias
        fill_pads(pads, step // side, step % side, jnp.where(inside, normal * sigmoid(normal), 0.0))
        return carry

    lax.fori_loop(0, images * side, body, 0)
    for block in range(width // BLOCK):
        columns = slice(block * BLOCK, (block + 1) * BLOCK)
        sums = [0.0, 0.0]
        for image in range(images):
            at = slice(image * rows, (image + 1) * rows)
            value = convolve(pads, wide, image, block, rows)
            grouped[at, columns] = value
            masked = value * mask[at, :]
            sums = [sums[0] + column_sums(masked), sums[1] + column_sums(masked * value)]
        stats[0:1, columns] = sums[0]
        stats[1:2, columns] = sums[1]


def expand_kernel(side, mask, total, first, vectors, grouped, mine, other, act, expanded, stats):
    rows, width = grouped.shape
    mean, inverse = moments(total, first[2:3, :])
    scale, bias = inverse * vectors[2:3, :], vectors[3:4, :]
    inside = line_mask(width, side)

    def body(step, carry):
        at = line_at(step)
        normal = (grouped[at, :] - mean) * scale + bias
        act[at, :] = jnp.where(inside, normal * sigmoid(normal), 0.0).astype(BF16)
        return carry

    lax.fori_loop(0, rows // LINE, body, 0)
    half = mine.shape[1]
    for part, weight in enumerate((mine, other)):
        for at in range(0, half, BLOCK):
            value = dot(act[...], weight[:, at : at + BLOCK])
            columns = part_at(part, half, at, BLOCK)
            expanded[:, columns] = value
            masked = value * mask[...]
            stats[0:1, columns] = column_sums(masked)
            stats[1:2, columns] = column_sums(masked * value)


def output_kernel(side, valid, total, first, vectors, expanded, x, cotangent, output, grad, stats):
    rows, channels = expanded.shape
    mean, inverse = moments(total, first[2:3, 0:1])
    gains, bias = vectors[0:1, :], vectors[1:2, :]
    zero = jnp.zeros((8, channels), F32)

    def body(step, carry):
        image, line = step // side, step % side
        at = line_at(step)
        keep = valid[image].astype(F32)
        normed = (expanded[at, :] - mean) * inverse
        summed = normed * gains + bias + x[at, :].astype(F32)
        sigma = sigmoid(summed)
        output[image, line] = (summed * sigma * keep).astype(BF16)[0:side]
        here = cotangent[at, :].astype(F32) * keep * (sigma * (1.0 + summed * (1.0 - sigma)))
        grad[at, :] = here
        return carry[0] + fold(here), carry[1] + fold(here * normed)

    one, two = lax.fori_loop(0, rows // LINE, body, (zero, zero))
    stats[0:1, :] = column_sums(one)
    stats[1:2, :] = column_sums(two)


def back_expand_kernel(
    mask, total, sums, first, vectors, total_two, vectors_two, grad, expanded, grouped, mine, other, flat, dz, stats
):
    rows, width = grouped.shape
    pixels = first[2:3, 0:1]
    mean, inverse = moments(total, pixels)
    scale = inverse * vectors[0:1, :]
    shifted, scaled = sums[0:1, :] / pixels, sums[1:2, :] / pixels

    def body(step, carry):
        at = line_at(step)
        normed = (expanded[at, :] - mean) * inverse
        flat[at, :] = (scale * (grad[at, :] - mask[at, :] * (shifted + normed * scaled))).astype(BF16)
        return carry

    lax.fori_loop(0, rows // LINE, body, 0)
    half = mine.shape[1]
    for at in range(0, width, BLOCK):
        value = None
        for part, weight in enumerate((mine, other)):
            term = dot(flat[:, part_at(part, half)], weight[at : at + BLOCK, :], NT)
            value = term if value is None else value + term
        dz[:, at : at + BLOCK] = value
    mean_two, inverse_two = moments(total_two, first[2:3, :])
    gains, bias = vectors_two[2:3, :], vectors_two[3:4, :]
    zero = jnp.zeros((8, width), F32)

    def tail(step, carry):
        at = line_at(step)
        normed = (grouped[at, :] - mean_two) * inverse_two
        here = dz[at, :] * dsilu(normed * gains + bias)
        dz[at, :] = here
        return carry[0] + fold(here), carry[1] + fold(here * normed)

    one, two = lax.fori_loop(0, rows // LINE, tail, (zero, zero))
    stats[0:1, :] = column_sums(one)
    stats[1:2, :] = column_sums(two)


def weight_expand_kernel(act, flat, send, keep):
    half = send.shape[1]
    turned = act[...].T
    for part, out in ((1, send), (0, keep)):
        for at in range(0, half, BLOCK):
            out[:, at : at + BLOCK] = dot(turned, flat[:, part_at(part, half, at, BLOCK)]).astype(BF16)


def back_group_kernel(
    side, mask, total, sums, first, vectors, dz, grouped, red, wide, flat, dz_one, stats, pads
):
    images, padded, width = pads.shape[1:]
    rows = side * LINE
    pixels = first[2:3, :]
    mean, inverse = moments(total, pixels)
    scale = inverse * vectors[2:3, :]
    shifted, scaled = sums[0:1, :] / pixels, sums[1:2, :] / pixels
    clear_pads(pads)

    def body(step, carry):
        at = line_at(step)
        normed = (grouped[at, :] - mean) * inverse
        value = scale * (dz[at, :] - mask[at, :] * (shifted + normed * scaled))
        flat[at, :] = value.astype(BF16)
        fill_pads(pads, step // side, step % side, value)
        return carry

    lax.fori_loop(0, images * side, body, 0)
    for block in range(width // BLOCK):
        columns = slice(block * BLOCK, (block + 1) * BLOCK)
        for image in range(images):
            dz_one[image * rows : (image + 1) * rows, columns] = convolve(pads, wide, image, block, rows, True)
    mean_one, inverse_one = moments(first, pixels)
    gains, bias = vectors[0:1, :], vectors[1:2, :]
    inside = line_mask(width, side)
    zero = jnp.zeros((8, width), F32)

    def tail(step, carry):
        at = line_at(step)
        normed = (red[at, :] - mean_one) * inverse_one
        here = jnp.where(inside, dz_one[at, :] * dsilu(normed * gains + bias), 0.0)
        dz_one[at, :] = here
        return carry[0] + fold(here), carry[1] + fold(here * normed)

    one, two = lax.fori_loop(0, images * side, tail, (zero, zero))
    stats[0:1, :] = column_sums(one)
    stats[1:2, :] = column_sums(two)


def weight_group_kernel(side, pads, flat, out, rows_held):
    images, padded, width = pads.shape[1:]
    rows = side * LINE
    inner = width // GROUPS
    row = lax.broadcasted_iota(jnp.int32, (BLOCK, BLOCK), 0) // inner
    column = lax.broadcasted_iota(jnp.int32, (BLOCK, BLOCK), 1) // inner
    own = row == column
    lanes = 128 // inner
    pick_row = lax.broadcasted_iota(jnp.int32, (BLOCK, 128), 0) % inner
    pick_lane = lax.broadcasted_iota(jnp.int32, (BLOCK, 128), 1)
    picks = [
        jnp.where(pick_lane == pick_row + inner * lane, 1.0, 0.0).astype(BF16) for lane in range(lanes)
    ]
    for block in range(width // BLOCK):
        columns = slice(block * BLOCK, (block + 1) * BLOCK)
        turned = [flat[image * rows : (image + 1) * rows, columns].T for image in range(images)]
        for begin in range(0, TAPS, lanes):
            packed = None
            taps = range(begin, min(begin + lanes, TAPS))
            for tap in taps:
                top, left = divmod(tap, 3)
                value = None
                for image in range(images):
                    term = dot(turned[image], pads[left, image, top * LINE : top * LINE + rows, columns])
                    value = term if value is None else value + term
                term = dot(jnp.where(own, value, 0.0).astype(BF16), picks[tap - begin])
                packed = term if packed is None else packed + term
            length = len(taps) * inner
            rows_held[begin * inner : begin * inner + length, columns] = packed.T[0:length]
    owners, extra = out.shape[:2]
    shard = TAPS * inner // owners
    for owner in range(owners):
        out[owner] = jnp.concatenate(
            [rows_held[owner * shard : (owner + 1) * shard, :], jnp.zeros((extra - shard, width), F32)], axis=0
        ).astype(BF16)


def back_reduce_kernel(blocks, small, mask, first, sums, vectors, dz, red, turned, group, flat, send):
    rows, width = red.shape
    pixels = first[2:3, :]
    mean, inverse = moments(first, pixels)
    scale = inverse * vectors[0:1, :]
    shifted, scaled = sums[0:1, :] / pixels, sums[1:2, :] / pixels

    def body(step, carry):
        at = line_at(step)
        normed = (red[at, :] - mean) * inverse
        flat[at, :] = (scale * (dz[at, :] - mask[at, :] * (shifted + normed * scaled))).astype(BF16)
        return carry

    lax.fori_loop(0, rows // LINE, body, 0)
    tall, half = send.shape[1:]
    depth = tall - group.shape[1]
    columns = part_at(1, half)
    for block in range(blocks):
        owner = block_owner(block) if small else block
        send[block, 0:depth, :] = dot(turned[rows_of(owner, depth), :], flat[:, columns]).astype(BF16)
        send[block, depth:tall, :] = group[owner, :, columns]


def block_sum_kernel(small, places, turned, group, flat, near, *refs):
    arrived, outs = refs[: len(refs) - len(places)], refs[len(refs) - len(places) :]
    tall, half = near.shape[1:]
    depth = tall - group.shape[1]
    columns = part_at(0, half)
    for out, (block, chosen) in zip(outs, places):
        owner = block_owner(block) if small else block
        value = dot(turned[rows_of(owner, depth), :], flat[:, columns]) + near[block, 0:depth, :].astype(F32)
        more = group[owner, :, columns].astype(F32) + near[block, depth:tall, :].astype(F32)
        for other in chosen:
            value = value + arrived[other][0:depth, :].astype(F32)
            more = more + arrived[other][depth:tall, :].astype(F32)
        out[0:depth, :] = value.astype(BF16)
        out[depth:tall, :] = more.astype(BF16)


def expand_sum_kernel(places, keep, near, *refs):
    arrived, outs = refs[: len(refs) - len(places)], refs[len(refs) - len(places) :]
    depth = outs[0].shape[0]
    for out, (block, chosen) in zip(outs, places):
        rows = rows_of(block_owner(block), depth)
        value = keep[rows, :].astype(F32) + near[rows, :].astype(F32)
        for other in chosen:
            value = value + arrived[other][...].astype(F32)
        out[...] = value.astype(BF16)


def add_kernel(a, b, out):
    out[...] = (a[...].astype(F32) + b[...].astype(F32)).astype(out.dtype)


def join_kernel(mine, other, *outs):
    half = mine.shape[1]
    at = 0
    for out in outs:
        rows = out.shape[0]
        for part, values in enumerate((mine, other)):
            out[:, part_at(part, half)] = values[at : at + rows, :]
        at += -(-rows // 16) * 16


def pin_kernel(values, out):
    pass


def own_kernel(*refs):
    number = len(refs) // 3
    position = lax.axis_index("fsdp")
    for at, total in enumerate(refs[:number]):
        for row, out in ((1, refs[number + 2 * at]), (0, refs[number + 2 * at + 1])):
            length = out.shape[1]
            out[...] = total[row : row + 1, pl.ds(pl.multiple_of(position * length, 128), length)]


def grad_input_kernel(slots, depth, side, flat, grad, *refs):
    weights, (out, held) = refs[: 2 * slots], refs[2 * slots :]
    half = weights[0].shape[1]
    for slot in range(slots):
        columns = pl.ds(pl.multiple_of(block_owner(slot) * depth, 128), depth) if slots > 1 else slice(None)
        value = grad[:, columns]
        for part in range(2):
            value = value + dot(flat[:, part_at(part, half)], weights[2 * slot + part][0:depth, :], NT)
        held[:, columns] = value

    def body(step, carry):
        out[step // side, step % side] = held[line_at(step), :].astype(BF16)[0:side]
        return carry

    lax.fori_loop(0, flat.shape[0] // LINE, body, 0)


def pinned(values):
    anywhere = pl.BlockSpec(memory_space=pl.ANY)
    values = values.transpose(1, 2, 0, 3)
    values = pl.pallas_call(
        pin_kernel, out_shape=shape(values.shape, values.dtype), in_specs=[anywhere], out_specs=anywhere,
        input_output_aliases={0: 0}, compiler_params=pltpu.CompilerParams(vmem_limit_bytes=1 << 20), name="pin",
    )(values)
    return values.transpose(2, 0, 1, 3)


def swap_core(values):
    return lax.ppermute(values, "core", SWAP)


def swap_x(values):
    if lax.axis_size("x") == 2:
        return lax.ppermute(values, "x", SWAP)
    return (lax.psum(values.astype(F32), "x") - values.astype(F32)).astype(values.dtype)


def sum_chips(values, flips):
    got = [lax.ppermute(values, CHIPS, [(at, at ^ flip) for at in range(16)]) for flip in flips]
    for other in got:
        values = values + other
    return values


def along(values, way):
    pairs = [(f * 2 + x, (f + 2 * way * (1 - 2 * x)) % 8 * 2 + x) for f in range(8) for x in range(2)]
    return lax.ppermute(values, CHIPS, pairs)


def across(values):
    return lax.ppermute(values, "fsdp", [(f, f ^ 1) for f in range(8)])


def gather_blocks(own, early, late):
    first = along(own, 1)
    other = across(own)
    first, other, *early = together(first, other, *early)
    passed, second, first_other = swap_x(first), along(first, 1), across(first)
    second, passed, first_other, *late = together(second, passed, first_other, *late)
    passed_other, second_other = swap_x(first_other), across(second)
    return [own, first, passed, second, other, first_other, passed_other, second_other], early, late


def halves(values, core):
    half = values.shape[1] // 2
    return lax.dynamic_slice_in_dim(values, core * half, half, 1)


def per_device(
    images,
    valid,
    cotangent,
    w_reduce,
    gain_one,
    shift_one,
    w_group,
    gain_two,
    shift_two,
    w_expand,
    gain_three,
    shift_three,
):
    count, side, _, channels = images.shape
    width = w_reduce.shape[1]
    inner = width // GROUPS
    size = lax.axis_size("fsdp")
    small = size == 8 and lax.axis_size("x") == 2
    position, core = lax.axis_index("fsdp"), lax.axis_index("core")
    rows = count * side * LINE
    per, outer, shard, depth = gain_one.shape[0], gain_three.shape[0], w_group.shape[0], w_reduce.shape[0]
    extra = -(-(shard + 1) // 16) * 16
    half = width // 2

    def start_sum(values):
        return values + swap_core(values) if small else lax.psum(values, ("fsdp", "x", "core"))

    def plane_sum(values):
        return sum_chips(values, (1, 2, 3)) if small else values

    def line_sum(values):
        return sum_chips(values, (4, 8, 12)) if small else values

    def everywhere(values):
        return line_sum(plane_sum(start_sum(values)))

    def padded(values):
        return jnp.pad(values, ((0, 0), (0, 0), (0, LINE - side), (0, 0))).reshape(rows, channels)

    x, cot = padded(images), padded(cotangent)

    vectors, at = jnp.zeros((width,), BF16), 0
    for vector in (gain_one, shift_one, gain_two, shift_two, gain_three, shift_three):
        vectors = vectors + jnp.pad(vector, (at, width - at - vector.size))
        at += vector.size
    own, mask = call(
        functools.partial(pack_kernel, side),
        [shape((depth + extra, half), BF16), shape((rows, 1), F32)],
        [valid, w_reduce, w_group, vectors.reshape(1, width)], scalars=1, name="pack",
    )
    wide_shape = shape((TAPS, width // BLOCK, BLOCK, BLOCK), BF16)
    expand_half = halves(w_expand, core)
    if small:
        weights = []
        blocks, (x, expand_half), (turned,) = gather_blocks(own, (x, expand_half), (x.T,))
        for block in blocks:
            weights += [block, swap_core(block)]
        slots, slot_depth = size, depth
    else:
        whole = lax.all_gather(own, "fsdp", axis=0, tiled=False)
        block = whole[:, :depth].reshape(channels, half)
        weights = [block, swap_core(block)]
        slots, slot_depth, turned = 1, channels, x.T
    expand_mine = lax.all_gather(expand_half, "fsdp", axis=0, tiled=True)

    red, part = call(
        functools.partial(reduce_kernel, slots, slot_depth, side),
        [shape((rows, width), F32), shape((3, width), F32)],
        [valid, mask, x] + weights, scalars=1, name="reduce", flops=2 * rows * width * channels,
    )
    if small:
        wide, inner_vectors, outer_vectors = call(
            functools.partial(spread_kernel, slots, depth),
            [wide_shape, shape((4, width), F32), shape((2, channels), F32)],
            weights,
            scratch=[pltpu.VMEM((size, extra, width), F32), pltpu.VMEM((size * shard, width), F32)],
            name="spread", flops=1 << 28,
        )
    else:
        mine = whole[:, depth:]
        other = swap_core(mine)
        packed = jnp.concatenate([jnp.where(core == 0, mine, other), jnp.where(core == 0, other, mine)], axis=2)
        (wide,) = call(
            widen_kernel, [wide_shape], [packed[:, :shard].reshape(size * shard, width)],
            scratch=[pltpu.VMEM((size * shard, width), F32)], name="widen",
        )
        line = packed[:, shard].astype(F32)
        inner_vectors = line[:, : 4 * per].reshape(size, 4, per).transpose(1, 0, 2).reshape(4, width)
        outer_vectors = line[:, 4 * per : 4 * per + 2 * outer].reshape(size, 2, outer)
        outer_vectors = outer_vectors.transpose(1, 0, 2).reshape(2, channels)
    middle = plane_sum(start_sum(part))
    middle, wide, inner_vectors, outer_vectors = together(middle, wide, inner_vectors, outer_vectors)
    first = line_sum(middle)
    pad_shape = (3, count, (side + 2) * LINE, width)
    pads, grouped, part = call(
        functools.partial(group_kernel, side),
        [shape(pad_shape, BF16), shape((rows, width), F32), shape((2, width), F32)],
        [mask, first, inner_vectors, red, wide],
        name="group", flops=2 * TAPS * rows * width * BLOCK,
    )
    middle = plane_sum(start_sum(part))
    expand_other = swap_core(after(expand_mine, middle))
    total_two = line_sum(middle)
    act_two, expanded, part = call(
        functools.partial(expand_kernel, side),
        [shape((rows, width), BF16), shape((rows, channels), F32), shape((2, channels), F32)],
        [mask, total_two, first, inner_vectors, grouped, expand_mine, expand_other],
        name="expand", flops=2 * rows * width * channels,
    )
    total_three = everywhere(part)
    output, grad_summed, part = call(
        functools.partial(output_kernel, side),
        [shape(images.shape, BF16), shape((rows, channels), F32), shape((2, channels), F32)],
        [valid, total_three, first, outer_vectors, expanded, x, cot], scalars=1, name="output",
    )

    sums_three = everywhere(part)
    flat_three, dz_two, part = call(
        back_expand_kernel,
        [shape((rows, channels), BF16), shape((rows, width), F32), shape((2, width), F32)],
        [mask, total_three, sums_three, first, outer_vectors, total_two, inner_vectors, grad_summed, expanded, grouped,
         expand_mine, expand_other],
        name="back_expand", flops=2 * rows * width * channels,
    )
    middle = start_sum(part)
    act_two = after(act_two, middle)
    sums_two = line_sum(plane_sum(middle))
    send, keep = call(
        weight_expand_kernel,
        [shape((width, channels // 2), BF16)] * 2,
        [act_two, flat_three], name="weight_expand", flops=2 * rows * width * channels,
    )
    near_expand = swap_core(send)

    def expand_sums(places, arrived=()):
        return call(
            functools.partial(expand_sum_kernel, places),
            [shape((w_expand.shape[0], channels // 2), BF16)] * len(places),
            [keep, near_expand] + list(arrived), name="expand_sum",
        )

    if small:
        passed_other, second_other = expand_sums(((6, ()), (7, ())))
        sums_two, passed_other, second_other = together(sums_two, passed_other, second_other)
        got_expand = [swap_x(passed_other), across(second_other)]
    else:
        (chip,) = call(add_kernel, [shape(keep.shape, BF16)], [keep, near_expand], name="add")
        own_expand = lax.psum_scatter(chip, "fsdp", scatter_dimension=0, tiled=True)

    flat_two, dz_one, part = call(
        functools.partial(back_group_kernel, side),
        [shape((rows, width), BF16), shape((rows, width), F32), shape((2, width), F32)],
        [mask, total_two, sums_two, first, inner_vectors, dz_two, grouped, red, wide],
        scratch=[pltpu.VMEM(pad_shape, BF16)], name="back_group", flops=2 * TAPS * rows * width * BLOCK,
    )
    if small:
        first_other, passed, second = expand_sums(((5, (0,)), (2, ()), (3, (1,))), got_expand)
        part, first_other, passed, second = together(part, first_other, passed, second)
        got_expand = [swap_x(passed), along(second, -1), across(first_other)]
    sums_one = everywhere(part)
    if small:
        first_own, other = expand_sums(((1, (0, 1, 2)), (4, ())), got_expand)
        sums_one, first_own, other = together(sums_one, first_own, other)
        got_expand = [along(first_own, -1), across(other)]
    (group_term,) = call(
        functools.partial(weight_group_kernel, side),
        [shape((size, extra, width), BF16)],
        [pads, flat_two], scratch=[pltpu.VMEM((TAPS * inner, width), F32)], name="weight_group", flops=2 * TAPS * rows * width * BLOCK,
    )
    tall = depth + extra
    flat_one, send = call(
        functools.partial(back_reduce_kernel, size, small),
        [shape((rows, width), BF16), shape((size, tall, half), BF16)],
        [mask, first, sums_one, inner_vectors, dz_one, red, turned, group_term],
        name="back_reduce", flops=rows * width * channels,
    )
    near = swap_core(send)

    def sums(places, arrived=()):
        return call(
            functools.partial(block_sum_kernel, small, places),
            [shape((tall, half), BF16)] * len(places),
            [turned, group_term, flat_one, near] + list(arrived),
            name="block_sum", flops=2 * rows * depth * half * len(places),
        )

    def back_input(flat):
        (out,) = call(
            functools.partial(grad_input_kernel, slots, slot_depth, side),
            [shape(images.shape, BF16)],
            [flat, grad_summed] + weights,
            scratch=[pltpu.VMEM((rows, channels), F32)], name="grad_input", flops=2 * rows * width * channels,
        )
        return out

    def own_shards(*totals):
        if not small:
            cut = []
            for total, length in zip(totals, (per, per, outer)):
                cut += [lax.dynamic_slice_in_dim(total[row], position * length, length, 0) for row in (1, 0)]
            return cut
        lengths = (per, per, per, per, outer, outer)
        return [out.reshape(-1) for out in call(own_kernel, [shape((1, n), F32) for n in lengths], totals, name="own")]

    if small:
        passed_other, second_other = sums(((6, ()), (7, ())))
        got_x, got_y = swap_x(passed_other), across(second_other)
        grad_input = back_input(after(flat_one, second_other))
        (own_expand,) = expand_sums(((0, (0, 1)),), got_expand)
        got_x, grad_input, own_expand = together(got_x, grad_input, own_expand)
        first_other, passed, second = sums(((5, (0,)), (2, ()), (3, (1,))), (got_x, got_y))
        got = [swap_x(passed), along(second, -1), across(first_other)]
        output = pinned(after(output, second))
        got[0], output = together(got[0], output)
        first_own, other = sums(((1, (0, 1, 2)), (4, ())), got)
        got = [along(first_own, -1), across(other)]
        shards = own_shards(after(sums_one, first_own), sums_two, sums_three)
        grad_input = pinned(after(grad_input, first_own))
        got[0], grad_input, *shards = together(got[0], grad_input, *shards)
        (own_reduce,) = sums(((0, (0, 1)),), got)
    else:
        grad_input = back_input(flat_one)
        shards = own_shards(sums_one, sums_two, sums_three)
        whole = jnp.stack(sums(tuple((at, ()) for at in range(size)))).reshape(size * tall, half)
        own_reduce = lax.psum_scatter(whole, "fsdp", scatter_dimension=0, tiled=True)
    (own_expand,) = call(add_kernel, [shape(own_expand.shape, F32)], [own_expand, swap_x(own_expand)], name="add")
    (grad_w_expand,) = call(join_kernel, [shape(w_expand.shape, F32)], [own_expand, swap_core(own_expand)], name="join")
    (own_reduce,) = call(add_kernel, [shape(own_reduce.shape, F32)], [own_reduce, swap_x(own_reduce)], name="add")
    grad_w_reduce, grad_w_group = call(
        join_kernel,
        [shape(w_reduce.shape, F32), shape(w_group.shape, F32)],
        [own_reduce, swap_core(own_reduce)], name="join",
    )
    return (output, grad_input, grad_w_reduce, grad_w_group, grad_w_expand) + tuple(shards)


def solution(mesh):
    fsdp, dp = mesh.shape["fsdp"], mesh.shape["dp"]
    split = Mesh(mesh.devices.reshape(fsdp, dp // 2, 2), ("fsdp", "x", "core"))
    images, rows, vector = P(("fsdp", "x", "core"), None, None, None), P("fsdp", None), P("fsdp")
    return jax.shard_map(
        per_device,
        mesh=split,
        in_specs=(
            images, P(("fsdp", "x", "core")), images,
            rows, vector, vector, rows, vector, vector, rows, vector, vector,
        ),
        out_specs=(images, images, rows, rows, rows) + (vector,) * 6,
        check_vma=False,
    )
```

```python
import functools

import jax
import jax.numpy as jnp
from jax import lax
from jax.experimental import pallas as pl
from jax.experimental.pallas import tpu as pltpu
from jax.sharding import Mesh
from jax.sharding import PartitionSpec as P

GROUPS = 32
TAPS = 9
LINE = 16
CHUNK = 512
UNROLL = 7
LANES = 128
BLOCK = 256
epsilon = 1e-05
BF16, F32 = jnp.bfloat16, jnp.float32
SWAP = [(0, 1), (1, 0)]
NN, NT = ((1,), (0,)), ((1,), (1,))
CHIPS = ("fsdp", "x")


def silu_half(half):
    return half + half * jnp.tanh(half)


def dsilu_twice(half):
    turned = jnp.tanh(half)
    upper = 1.0 + turned
    return upper * (1.0 + half * (1.0 - turned)), upper


def dot(a, b, contract=NN):
    return lax.dot_general(a, b, (contract, ((), ())), preferred_element_type=F32)


def after(values, *others):
    return lax.optimization_barrier((values,) + others)[0]


def together(*values):
    return lax.optimization_barrier(values)


def shape(dims, dtype):
    return jax.ShapeDtypeStruct(dims, dtype)


def call(kernel, outs, args, scalars=0, scratch=(), vmem=8, name=None, flops=0, anywhere=False, aliases=()):
    vm = pl.BlockSpec(memory_space=pltpu.VMEM)
    given = pl.BlockSpec(memory_space=pl.ANY) if anywhere else vm
    sm = pl.BlockSpec(memory_space=pltpu.SMEM)
    return pl.pallas_call(
        kernel,
        out_shape=outs,
        in_specs=[sm] * scalars + [given] * (len(args) - scalars),
        out_specs=[vm] * len(outs),
        scratch_shapes=list(scratch),
        compiler_params=pltpu.CompilerParams(vmem_limit_bytes=vmem << 20),
        cost_estimate=pl.CostEstimate(flops=flops, bytes_accessed=1 << 20, transcendentals=0),
        input_output_aliases=dict(aliases),
        name=name,
    )(*args)


def moments(total, pixels):
    mean = total[0:1, :] / pixels
    inverse = lax.rsqrt(total[1:2, :] / pixels - mean * mean + epsilon)
    return mean, inverse


def chunks(columns):
    return [slice(at, min(at + CHUNK, columns)) for at in range(0, columns, CHUNK)]


def line_mask(columns, side):
    return lax.broadcasted_iota(jnp.int32, (LINE, columns), 0) < side


def each_line(lines, body):
    lax.fori_loop(0, lines, lambda step, none: body(step) or none, 0, unroll=UNROLL)


def each_line_summed(lines, width, body):
    zero = jnp.zeros((8, width), F32)

    def step_sums(step, carry):
        one, two = body(step)
        return carry[0] + fold(one), carry[1] + fold(two)

    one, two = lax.fori_loop(0, lines, step_sums, (zero, zero), unroll=UNROLL)
    return column_sums(one), column_sums(two)


def across_lanes(mask, columns):
    return jnp.concatenate([mask] * (columns // LANES), axis=1)


def column_sums(values):
    return jnp.sum(values, axis=0, keepdims=True)


def line_at(step):
    return pl.ds(pl.multiple_of(step * LINE, LINE), LINE)


def fold(values):
    return values[0:8] + values[8:16]


def part_at(part, half, at=0, length=None):
    core = lax.axis_index("core")
    side = core if part == 0 else 1 - core
    length = half if length is None else length
    return pl.ds(pl.multiple_of(side * half + at, 128), length)


def block_owner(slot):
    position = lax.axis_index("fsdp")
    way = 1 - 2 * lax.axis_index("x")
    step = (0, -way, way, 2)[slot % 4]
    owner = lax.rem(position + 2 * step + 8, 8)
    return owner if slot < 4 else owner + 1 - 2 * lax.rem(owner, 2)


def rows_of(owner, depth):
    return pl.ds(pl.multiple_of(owner * depth, 16), depth)


def pack_kernel(side, valid, weight, group, vectors, out, mask, held, row, sems):
    depth, half = weight.shape[0], out.shape[1]
    shard, extra = group.shape[0], out.shape[0] - weight.shape[0]
    columns = part_at(0, half)
    copies = [
        pltpu.make_async_copy(group, held, sems.at[0]),
        pltpu.make_async_copy(vectors, row, sems.at[1]),
        pltpu.make_async_copy(weight.at[:, columns], out.at[pl.ds(0, depth)], sems.at[2]),
    ]
    for copy in copies:
        copy.start()
    images = valid.shape[0]
    rows = mask.shape[0] // images
    inside = lax.broadcasted_iota(jnp.int32, (rows, LANES), 0) % LINE < side
    for image in range(images):
        mask[image * rows : (image + 1) * rows, :] = jnp.where(inside, valid[image].astype(F32), 0.0)
    copies[0].wait()
    copies[1].wait()
    below = [held[:, columns].astype(F32), row[:, columns].astype(F32)]
    if extra > shard + 1:
        below.append(jnp.zeros((extra - shard - 1, half), F32))
    out[depth : depth + extra, :] = jnp.concatenate(below, axis=0).astype(BF16)
    copies[2].wait()


def reduce_kernel(part, slots, depth, side, valid, mask, x, *refs):
    weights, (red, stats) = refs[:slots], refs[-2:]
    half = weights[0].shape[1]
    for at in range(0, half, BLOCK):
        total = None
        for slot in range(slots):
            if slots == 1:
                piece = x[...]
            else:
                piece = x[:, pl.ds(pl.multiple_of(block_owner(slot) * depth, 128), depth)]
            term = dot(piece, weights[slot][0:depth, at : at + BLOCK])
            total = term if total is None else total + term
        columns = part_at(part, half, at, BLOCK)
        red[:, columns] = total
        masked = total * across_lanes(mask[...], BLOCK)
        stats[0:1, columns] = column_sums(masked)
        stats[1:2, columns] = column_sums(masked * total)
    pixels = valid[0].astype(F32)
    for image in range(1, valid.shape[0]):
        pixels = pixels + valid[image].astype(F32)
    columns = part_at(part, half)
    stats[2:3, columns] = jnp.full((1, half), 1.0, F32) * (pixels * (side * side))


def spread_kernel(slots, depth, *refs):
    blocks, (wide, wide_turned, inner_vectors, outer_vectors, held, rows) = refs[: 2 * slots], refs[2 * slots :]
    extra, half = held.shape[1], held.shape[2] // 2
    for slot in range(slots):
        for part in range(2):
            held[block_owner(slot), :, part_at(part, half)] = blocks[2 * slot + part][depth : depth + extra, :].astype(F32)
    shard = rows.shape[0] // slots
    per, outer = inner_vectors.shape[1] // slots, outer_vectors.shape[1] // slots
    for owner in range(slots):
        rows[owner * shard : (owner + 1) * shard, :] = held[owner, 0:shard, :]
        for row in range(4):
            inner_vectors[row : row + 1, owner * per : (owner + 1) * per] = held[
                owner, shard : shard + 1, row * per : (row + 1) * per
            ]
        for row in range(2):
            outer_vectors[row : row + 1, owner * outer : (owner + 1) * outer] = held[
                owner, shard : shard + 1, 4 * per + row * outer : 4 * per + (row + 1) * outer
            ]
    widen(rows, wide, wide_turned)


def widen_kernel(weight, wide, wide_turned, rows):
    rows[...] = weight[...].astype(F32)
    widen(rows, wide, wide_turned)


def widen(weight, wide, wide_turned):
    taps, blocks = wide.shape[:2]
    inner = weight.shape[0] // taps
    row = lax.broadcasted_iota(jnp.int32, (BLOCK, BLOCK), 0) // inner
    column = lax.broadcasted_iota(jnp.int32, (BLOCK, BLOCK), 1) // inner
    own = row == column
    for tap in range(taps):
        for block in range(blocks):
            piece = weight[tap * inner : (tap + 1) * inner, block * BLOCK : (block + 1) * BLOCK]
            tall = jnp.concatenate([piece] * (BLOCK // inner), axis=0)
            dense = jnp.where(own, tall, 0.0)
            wide[tap, block] = dense.astype(BF16)
            wide_turned[tap, block] = dense.T.astype(BF16)


def fill_pads(pads, columns, image, line, values):
    rows = pl.ds(pl.multiple_of((line + 1) * LINE, LINE), LINE)
    pads[0, image, rows, columns] = pltpu.roll(values, 1, 0).astype(BF16)
    pads[1, image, rows, columns] = values.astype(BF16)
    pads[2, image, rows, columns] = pltpu.roll(values, LINE - 1, 0).astype(BF16)


def clear_pads(pads):
    images, rows, columns = pads.shape[1:]
    zeros = jnp.zeros((3, images, LINE, columns), BF16)
    pads[:, :, 0:LINE, :] = zeros
    pads[:, :, rows - LINE : rows, :] = zeros


def convolve(pads, wide, image, block, rows, turned=False):
    columns = slice(block * BLOCK, (block + 1) * BLOCK)
    value = None
    for tap in range(TAPS):
        top, left = divmod(TAPS - 1 - tap if turned else tap, 3)
        piece = pads[left, image, top * LINE : top * LINE + rows, columns]
        term = dot(piece, wide[tap, block])
        value = term if value is None else value + term
    return value


def group_kernel(side, mask, total, vectors, red, wide, pads, grouped, stats):
    images, padded, width = pads.shape[1:]
    rows = side * LINE
    mean, inverse = moments(total, total[2:3, :])
    scale, bias = 0.5 * inverse * vectors[0:1, :], 0.5 * vectors[1:2, :]
    clear_pads(pads)
    for part in chunks(width):
        inside = line_mask(part.stop - part.start, side)

        def body(step):
            half = (red[line_at(step), part] - mean[:, part]) * scale[:, part] + bias[:, part]
            fill_pads(pads, part, step // side, step % side, jnp.where(inside, silu_half(half), 0.0))

        each_line(images * side, body)
    for block in range(width // BLOCK):
        columns = slice(block * BLOCK, (block + 1) * BLOCK)
        sums = [0.0, 0.0]
        for image in range(images):
            at = slice(image * rows, (image + 1) * rows)
            value = convolve(pads, wide, image, block, rows)
            grouped[at, columns] = value
            masked = value * across_lanes(mask[at, :], BLOCK)
            sums = [sums[0] + column_sums(masked), sums[1] + column_sums(masked * value)]
        stats[0:1, columns] = sums[0]
        stats[1:2, columns] = sums[1]


def pair_slots(slots):
    return [(0,)] if slots == 1 else [(slot, slot + slots // 2) for slot in range(slots // 2)]


def pair_rows(weights, pair, part, columns=slice(None)):
    return jnp.concatenate([weights[2 * slot + part][:, columns] for slot in pair], axis=0)


def expand_kernel(slots, side, mask, total, first, vectors, grouped, *refs):
    weights, (act, expanded, stats, held) = refs[: 2 * slots], refs[2 * slots :]
    rows, width = grouped.shape
    mean, inverse = moments(total, first[2:3, :])
    scale, bias = 0.5 * inverse * vectors[2:3, :], 0.5 * vectors[3:4, :]
    for part in chunks(width):
        inside = line_mask(part.stop - part.start, side)

        def body(step):
            at = line_at(step)
            half = (grouped[at, part] - mean[:, part]) * scale[:, part] + bias[:, part]
            held[at, part] = jnp.where(inside, silu_half(half), 0.0).astype(BF16)

        each_line(rows // LINE, body)
    depth, half = weights[0].shape
    pairs = pair_slots(slots)
    for at, slot in enumerate(slot for pair in pairs for slot in pair):
        columns = pl.ds(pl.multiple_of(block_owner(slot) * depth, 128), depth) if slots > 1 else slice(None)
        act[:, at * depth : (at + 1) * depth] = held[:, columns]
    tall = depth * len(pairs[0])
    for part in range(2):
        for at in range(0, half, BLOCK):
            value = None
            for index, pair in enumerate(pairs):
                weight = pair_rows(weights, pair, part, slice(at, at + BLOCK))
                term = dot(act[:, index * tall : (index + 1) * tall], weight)
                value = term if value is None else value + term
            columns = part_at(part, half, at, BLOCK)
            expanded[:, columns] = value
            masked = value * across_lanes(mask[...], BLOCK)
            stats[0:1, columns] = column_sums(masked)
            stats[1:2, columns] = column_sums(masked * value)


def output_kernel(side, valid, total, first, vectors, expanded, x, cotangent, output, grad, stats):
    rows, channels = expanded.shape
    mean, inverse = moments(total, first[2:3, 0:1])
    scale, bias = inverse * vectors[0:1, :], vectors[1:2, :]
    for part in chunks(channels):

        def body(step):
            image, line = step // side, step % side
            at = line_at(step)
            keep = 0.5 * valid[image].astype(F32)
            centered = expanded[at, part] - mean[:, part]
            half = (centered * scale[:, part] + (bias[:, part] + x[at, part].astype(F32))) * keep
            slope, upper = dsilu_twice(half)
            output[image, line, :, part] = (half * upper).astype(BF16)[0:side]
            here = cotangent[at, part].astype(F32) * keep * slope
            grad[at, part] = here
            return here, here * centered

        one, two = each_line_summed(rows // LINE, part.stop - part.start, body)
        stats[0:1, part] = one
        stats[1:2, part] = two * inverse[:, part]


def back_expand_kernel(
    slots, mask, total, sums, first, vectors, total_two, vectors_two, grad, expanded, grouped, *refs
):
    weights, (flat, dz, stats) = refs[: 2 * slots], refs[2 * slots :]
    rows, width = grouped.shape
    pixels = first[2:3, 0:1]
    mean, inverse = moments(total, pixels)
    scale = inverse * vectors[0:1, :]
    shifted, scaled = scale * sums[0:1, :] / pixels, scale * inverse * sums[1:2, :] / pixels
    for part in chunks(expanded.shape[1]):

        def body(step):
            at = line_at(step)
            common = shifted[:, part] + (expanded[at, part] - mean[:, part]) * scaled[:, part]
            flat[at, part] = (scale[:, part] * grad[at, part] - across_lanes(mask[at, :], part.stop - part.start) * common).astype(BF16)

        each_line(rows // LINE, body)
    depth, half = weights[0].shape
    for pair in pair_slots(slots):
        for at in range(0, depth * len(pair), BLOCK):
            value = None
            for part in range(2):
                weight = pair_rows(weights, pair, part) if slots > 1 else weights[part][at : at + BLOCK, :]
                term = dot(flat[:, part_at(part, half)], weight, NT)
                value = term if value is None else value + term
            if slots == 1:
                dz[:, at : at + BLOCK] = value
            else:
                for index, slot in enumerate(pair):
                    columns = pl.ds(pl.multiple_of(block_owner(slot) * depth, 128), depth)
                    dz[:, columns] = value[:, index * depth : (index + 1) * depth]
    mean_two, inverse_two = moments(total_two, first[2:3, :])
    before_norm(dz, grouped, mean_two, inverse_two, vectors_two[2:3, :], vectors_two[3:4, :], stats)


def before_norm(dz, hidden, mean, inverse, gain, shift, stats, side=None):
    scale, bias = 0.5 * inverse * gain, 0.5 * shift
    rows, width = hidden.shape
    for part in chunks(width):
        inside = None if side is None else line_mask(part.stop - part.start, side)

        def body(step):
            at = line_at(step)
            centered = hidden[at, part] - mean[:, part]
            slope, _ = dsilu_twice(centered * scale[:, part] + bias[:, part])
            here = dz[at, part] * slope
            if side is not None:
                here = jnp.where(inside, here, 0.0)
            dz[at, part] = here
            return here, here * centered

        one, two = each_line_summed(rows // LINE, part.stop - part.start, body)
        stats[0:1, part] = 0.5 * one
        stats[1:2, part] = 0.5 * inverse[:, part] * two


def weight_expand_kernel(act, flat, send, keep):
    half = send.shape[1]
    turned = act[...].T
    for part, out in ((1, send), (0, keep)):
        for at in range(0, half, BLOCK):
            out[:, at : at + BLOCK] = dot(turned, flat[:, part_at(part, half, at, BLOCK)]).astype(BF16)


def back_group_kernel(
    side, mask, total, sums, first, vectors, dz, grouped, red, wide, flat, dz_one, stats, pads
):
    images, padded, width = pads.shape[1:]
    rows = side * LINE
    pixels = first[2:3, :]
    mean, inverse = moments(total, pixels)
    scale = inverse * vectors[2:3, :]
    shifted, scaled = scale * sums[0:1, :] / pixels, scale * inverse * sums[1:2, :] / pixels
    scale = 0.5 * scale
    clear_pads(pads)
    for part in chunks(width):

        def body(step):
            at = line_at(step)
            common = shifted[:, part] + (grouped[at, part] - mean[:, part]) * scaled[:, part]
            value = scale[:, part] * dz[at, part] - across_lanes(mask[at, :], part.stop - part.start) * common
            flat[at, part] = value.astype(BF16)
            fill_pads(pads, part, step // side, step % side, value)

        each_line(images * side, body)
    for block in range(width // BLOCK):
        columns = slice(block * BLOCK, (block + 1) * BLOCK)
        for image in range(images):
            dz_one[image * rows : (image + 1) * rows, columns] = convolve(pads, wide, image, block, rows, True)
    mean_one, inverse_one = moments(first, pixels)
    before_norm(dz_one, red, mean_one, inverse_one, vectors[0:1, :], vectors[1:2, :], stats, side)


def weight_group_kernel(side, pads, flat, out, held):
    images, padded, width = pads.shape[1:]
    rows = side * LINE
    inner = width // GROUPS
    row = lax.broadcasted_iota(jnp.int32, (LANES, LANES), 0) // inner
    column = lax.broadcasted_iota(jnp.int32, (LANES, LANES), 1) // inner
    own = row == column
    for at in range(0, width, LANES):
        columns = slice(at, at + LANES)
        moved = []
        for tap in range(TAPS):
            top, left = divmod(tap, 3)
            pieces = [pads[left, image, top * LINE : top * LINE + rows, columns] for image in range(images)]
            moved.append(jnp.concatenate(pieces, axis=0))
        product = dot(flat[:, columns].T, jnp.concatenate(moved, axis=1))
        for tap in range(TAPS):
            kept = jnp.where(own, product[:, tap * LANES : (tap + 1) * LANES].T, 0.0)
            value = kept[0:inner]
            for begin in range(inner, LANES, inner):
                value = value + kept[begin : begin + inner]
            held[tap * inner : (tap + 1) * inner, columns] = value
    owners, extra = out.shape[:2]
    shard = TAPS * inner // owners
    zeros = jnp.zeros((extra - shard, width), F32)
    for owner in range(owners):
        rows_here = held[owner * shard : (owner + 1) * shard, :]
        out[owner] = jnp.concatenate([rows_here, zeros], axis=0).astype(BF16)


def back_reduce_kernel(
    small, blocks, mask, first, sums, vectors, dz, red, turned, group, flat, send
):
    rows, width = red.shape
    pixels = first[2:3, :]
    mean, inverse = moments(first, pixels)
    scale = inverse * vectors[0:1, :]
    shifted, scaled = scale * sums[0:1, :] / pixels, scale * inverse * sums[1:2, :] / pixels
    scale = 0.5 * scale
    for part in chunks(width):

        def body(step):
            at = line_at(step)
            common = shifted[:, part] + (red[at, part] - mean[:, part]) * scaled[:, part]
            flat[at, part] = (scale[:, part] * dz[at, part] - across_lanes(mask[at, :], part.stop - part.start) * common).astype(BF16)

        each_line(rows // LINE, body)
    send_kernel(small, blocks, turned, group, flat, send)


def send_kernel(small, blocks, turned, group, flat, send):
    tall, half = send.shape[1:]
    depth = tall - group.shape[1]
    columns = part_at(1, half)
    for at, block in enumerate(blocks):
        owner = block_owner(block) if small else block
        send[at, 0:depth, :] = dot(turned[rows_of(owner, depth), :], flat[:, columns]).astype(BF16)
        send[at, depth:tall, :] = group[owner, :, columns]


def block_sum_kernel(small, places, turned, group, flat, near, *refs):
    arrived, outs = refs[: len(refs) - len(places)], refs[len(refs) - len(places) :]
    tall, half = near.shape[1:]
    depth = tall - group.shape[1]
    columns = part_at(0, half)
    for out, (block, at, chosen) in zip(outs, places):
        owner = block_owner(block) if small else block
        value = dot(turned[rows_of(owner, depth), :], flat[:, columns]) + near[at, 0:depth, :].astype(F32)
        more = group[owner, :, columns].astype(F32) + near[at, depth:tall, :].astype(F32)
        for other in chosen:
            value = value + arrived[other][0:depth, :].astype(F32)
            more = more + arrived[other][depth:tall, :].astype(F32)
        out[0:depth, :] = value.astype(BF16)
        out[depth:tall, :] = more.astype(BF16)


def expand_sum_kernel(places, keep, near, *refs):
    arrived, outs = refs[: len(refs) - len(places)], refs[len(refs) - len(places) :]
    depth = outs[0].shape[0]
    for out, (block, chosen) in zip(outs, places):
        at = block % 4 * 2 + block // 4
        rows = slice(at * depth, (at + 1) * depth)
        value = keep[rows, :].astype(F32) + near[rows, :].astype(F32)
        for other in chosen:
            value = value + arrived[other][...].astype(F32)
        out[...] = value.astype(BF16)


def add_kernel(a, b, out):
    out[...] = (a[...].astype(F32) + b[...].astype(F32)).astype(out.dtype)


def join_kernel(mine, mine_x, other, other_x, *outs):
    half = mine.shape[1]
    at = 0
    for out in outs:
        rows = out.shape[0]
        for part, terms in enumerate(((mine, mine_x), (other, other_x))):
            values = [term[at : at + -(-rows // 16) * 16, :].astype(F32) for term in terms]
            out[:, part_at(part, half)] = (values[0] + values[1])[0:rows]
        at += -(-rows // 16) * 16


def turn_kernel(values, out):
    out[...] = values[...].T


def pin_kernel(values, out):
    pass


def own_kernel(*refs):
    number = len(refs) // 3
    position = lax.axis_index("fsdp")
    for at, total in enumerate(refs[:number]):
        for row, out in ((1, refs[number + 2 * at]), (0, refs[number + 2 * at + 1])):
            length = out.shape[1]
            out[...] = total[row : row + 1, pl.ds(pl.multiple_of(position * length, 128), length)]


def grad_input_kernel(slots, depth, side, flat, grad, *refs):
    weights, (out, held) = refs[: 2 * slots], refs[2 * slots :]
    half = weights[0].shape[1]
    for slot in range(slots):
        columns = pl.ds(pl.multiple_of(block_owner(slot) * depth, 128), depth) if slots > 1 else slice(None)
        value = grad[:, columns]
        for part in range(2):
            value = value + dot(flat[:, part_at(part, half)], weights[2 * slot + part][0:depth, :], NT)
        held[:, columns] = value

    def body(step, carry):
        out[step // side, step % side] = held[line_at(step), :].astype(BF16)[0:side]
        return carry

    lax.fori_loop(0, flat.shape[0] // LINE, body, 0)


def pinned(values):
    anywhere = pl.BlockSpec(memory_space=pl.ANY)
    values = values.transpose(1, 2, 0, 3)
    values = pl.pallas_call(
        pin_kernel, out_shape=shape(values.shape, values.dtype), in_specs=[anywhere], out_specs=anywhere,
        input_output_aliases={0: 0}, compiler_params=pltpu.CompilerParams(vmem_limit_bytes=1 << 20), name="pin",
    )(values)
    return values.transpose(2, 0, 1, 3)


def swap_core(values):
    return lax.ppermute(values, "core", SWAP)


def swap_x(values):
    if lax.axis_size("x") == 2:
        return lax.ppermute(values, "x", SWAP)
    return (lax.psum(values.astype(F32), "x") - values.astype(F32)).astype(values.dtype)


def sum_chips(values, flips):
    got = [lax.ppermute(values, CHIPS, [(at, at ^ flip) for at in range(16)]) for flip in flips]
    for other in got:
        values = values + other
    return values


def along(values, way):
    pairs = [(f * 2 + x, (f + 2 * way * (1 - 2 * x)) % 8 * 2 + x) for f in range(8) for x in range(2)]
    return lax.ppermute(values, CHIPS, pairs)


def across(values):
    return lax.ppermute(values, "fsdp", [(f, f ^ 1) for f in range(8)])


def gather_blocks(own, early, late, beside):
    first = along(own, 1)
    other = across(own)
    first, other, *early = together(first, other, *early)
    passed, second, first_other = swap_x(first), along(first, 1), across(first)
    second, passed, first_other, *late = together(second, passed, first_other, *late)
    passed_other, second_other, beside = swap_x(first_other), across(second), along(beside(early), 1)
    blocks = [own, first, passed, second, other, first_other, passed_other, second_other]
    *blocks, beside = together(*blocks, beside)
    return blocks, early, late, beside


def halves(values, core):
    half = values.shape[1] // 2
    return lax.dynamic_slice_in_dim(values, core * half, half, 1)


def per_device(
    images,
    valid,
    cotangent,
    w_reduce,
    gain_one,
    shift_one,
    w_group,
    gain_two,
    shift_two,
    w_expand,
    gain_three,
    shift_three,
):
    count, side, _, channels = images.shape
    width = w_reduce.shape[1]
    inner = width // GROUPS
    size = lax.axis_size("fsdp")
    small = size == 8 and lax.axis_size("x") == 2
    position, core = lax.axis_index("fsdp"), lax.axis_index("core")
    rows = count * side * LINE
    per, outer, shard, depth = gain_one.shape[0], gain_three.shape[0], w_group.shape[0], w_reduce.shape[0]
    extra = -(-(shard + 1) // 16) * 16
    half = width // 2

    def start_sum(values):
        return values + swap_core(values) if small else lax.psum(values, ("fsdp", "x", "core"))

    def plane_sum(values):
        return sum_chips(values, (1, 2, 3)) if small else values

    def line_sum(values):
        return sum_chips(values, (4, 8, 12)) if small else values

    def everywhere(values):
        return line_sum(plane_sum(start_sum(values)))


    def padded(values):
        return jnp.pad(values, ((0, 0), (0, 0), (0, LINE - side), (0, 0))).reshape(rows, channels)

    x, cot = padded(images), padded(cotangent)

    vectors, at = jnp.zeros((width,), BF16), 0
    for vector in (gain_one, shift_one, gain_two, shift_two, gain_three, shift_three):
        vectors = vectors + jnp.pad(vector, (at, width - at - vector.size))
        at += vector.size
    own, mask = call(
        functools.partial(pack_kernel, side),
        [shape((depth + extra, half), BF16), shape((rows, LANES), F32)],
        [valid, w_reduce, w_group, vectors.reshape(1, width)], scalars=1, anywhere=True, vmem=60, name="pack",
        scratch=[pltpu.VMEM((shard, width), BF16), pltpu.VMEM((1, width), BF16), pltpu.SemaphoreType.DMA((3,))],
    )
    wide_shape = shape((TAPS, width // BLOCK, BLOCK, BLOCK), BF16)
    expand_own = halves(w_expand, core)
    if small:
        (turned,) = call(turn_kernel, [shape((channels, rows), BF16)], [x], name="turn")
        blocks, (x, expand_own), (turned,), expand_first = gather_blocks(
            own, (x, expand_own), (turned,), lambda early: early[1]
        )
        moving = [across(expand_first), swap_x(expand_first)]
        slots, slot_depth = size, depth
    else:
        whole = lax.all_gather(own, "fsdp", axis=0, tiled=False)
        block = whole[:, :depth].reshape(channels, half)
        blocks = [block]
        slots, slot_depth, turned = 1, channels, x.T
        expand_mine = lax.all_gather(expand_own, "fsdp", axis=0, tiled=True)
        expand_weights = [expand_mine, swap_core(expand_mine)]

    far = [swap_core(block) for block in blocks]
    weights = [half for pair in zip(blocks, far) for half in pair]

    def reduce_part(part, weights, *before):
        return call(
            functools.partial(reduce_kernel, part, slots, slot_depth, side),
            [shape((rows, width), F32), shape((3, width), F32)],
            [valid, mask, x, *weights, *before], scalars=1, name="reduce", flops=rows * width * channels,
            aliases=((3 + slots, 0), (4 + slots, 1)) if before else (),
        )

    red, part = reduce_part(1, far, *reduce_part(0, blocks))
    if small:
        wide, wide_turned, inner_vectors, outer_vectors = call(
            functools.partial(spread_kernel, slots, depth),
            [wide_shape, wide_shape, shape((4, width), F32), shape((2, channels), F32)],
            weights,
            scratch=[pltpu.VMEM((size, extra, width), F32), pltpu.VMEM((size * shard, width), F32)],
            name="spread", flops=1 << 28,
        )
    else:
        mine = whole[:, depth:]
        other = swap_core(mine)
        packed = jnp.concatenate([jnp.where(core == 0, mine, other), jnp.where(core == 0, other, mine)], axis=2)
        wide, wide_turned = call(
            widen_kernel, [wide_shape, wide_shape], [packed[:, :shard].reshape(size * shard, width)],
            scratch=[pltpu.VMEM((size * shard, width), F32)], name="widen",
        )
        line = packed[:, shard].astype(F32)
        inner_vectors = line[:, : 4 * per].reshape(size, 4, per).transpose(1, 0, 2).reshape(4, width)
        outer_vectors = line[:, 4 * per : 4 * per + 2 * outer].reshape(size, 2, outer)
        outer_vectors = outer_vectors.transpose(1, 0, 2).reshape(2, channels)
    middle = line_sum(start_sum(part))
    middle, wide, wide_turned, inner_vectors, outer_vectors = together(
        middle, wide, wide_turned, inner_vectors, outer_vectors
    )
    if small:
        middle, first_other, passed, expand_first = together(middle, *moving, expand_first)
        second = along(expand_first, 1)
    first = plane_sum(middle)
    if small:
        first, first_other, expand_own = together(first, first_other, expand_own)
        moving = [swap_x(first_other), across(expand_own)]
    pad_shape = (3, count, (side + 2) * LINE, width)
    pads, grouped, part = call(
        functools.partial(group_kernel, side),
        [shape(pad_shape, BF16), shape((rows, width), F32), shape((2, width), F32)],
        [mask, first, inner_vectors, red, wide],
        name="group", flops=2 * TAPS * rows * width * BLOCK,
    )
    if small:
        part, second = together(part, second)
        second_other = across(second)
    middle = line_sum(start_sum(part))
    if small:
        middle, passed_other, other, second_other = together(middle, *moving, second_other)
        expand_weights = []
        for block in (expand_own, expand_first, passed, second, other, first_other, passed_other, second_other):
            expand_weights += [block, swap_core(block)]
    total_two = plane_sum(middle)
    act_two, expanded, part = call(
        functools.partial(expand_kernel, slots, side),
        [shape((rows, width), BF16), shape((rows, channels), F32), shape((2, channels), F32)],
        [mask, total_two, first, inner_vectors, grouped] + expand_weights,
        scratch=[pltpu.VMEM((rows, width), BF16)], name="expand", flops=2 * rows * width * channels,
    )
    total_three = everywhere(part)
    output, grad_summed, part = call(
        functools.partial(output_kernel, side),
        [shape(images.shape, BF16), shape((rows, channels), F32), shape((2, channels), F32)],
        [valid, total_three, first, outer_vectors, expanded, x, cot], scalars=1, name="output",
    )

    sums_three = everywhere(part)
    flat_three, dz_two, part = call(
        functools.partial(back_expand_kernel, slots),
        [shape((rows, channels), BF16), shape((rows, width), F32), shape((2, width), F32)],
        [mask, total_three, sums_three, first, outer_vectors, total_two, inner_vectors, grad_summed, expanded, grouped]
        + expand_weights,
        name="back_expand", flops=2 * rows * width * channels,
    )
    middle = start_sum(part)
    act_two = after(act_two, middle)
    send, keep = call(
        weight_expand_kernel,
        [shape((width, channels // 2), BF16)] * 2,
        [act_two, flat_three], name="weight_expand", flops=2 * rows * width * channels,
    )
    near_expand = swap_core(send)
    middle = plane_sum(middle)

    def expand_sums(places, arrived=()):
        return call(
            functools.partial(expand_sum_kernel, places),
            [shape((w_expand.shape[0], channels // 2), BF16)] * len(places),
            [keep, near_expand] + list(arrived), name="expand_sum",
        )

    if small:
        middle, *moving = together(middle, *expand_sums(((6, ()), (7, ()))))
        moving = [swap_x(moving[0]), across(moving[1])]
        sums_two, *moving = together(line_sum(middle), *moving)
        sums_two, expand_first_other, expand_passed, expand_second, expand_other = together(
            sums_two, *expand_sums(((5, (0,)), (2, ()), (3, (1,)), (4, ())), moving)
        )
        expand_second = along(expand_second, -1)
    else:
        sums_two = line_sum(middle)
        (chip,) = call(add_kernel, [shape(keep.shape, BF16)], [keep, near_expand], name="add")
        own_expand = lax.psum_scatter(chip, "fsdp", scatter_dimension=0, tiled=True)
    flat_two, dz_one, part = call(
        functools.partial(back_group_kernel, side),
        [shape((rows, width), BF16), shape((rows, width), F32), shape((2, width), F32)],
        [mask, total_two, sums_two, first, inner_vectors, dz_two, grouped, red, wide_turned],
        scratch=[pltpu.VMEM(pad_shape, BF16)], name="back_group", flops=2 * TAPS * rows * width * BLOCK,
    )

    middle = start_sum(part)
    flat_two = after(flat_two, middle)
    (group_term,) = call(
        functools.partial(weight_group_kernel, side),
        [shape((size, extra, width), BF16)],
        [pads, flat_two], scratch=[pltpu.VMEM((TAPS * inner, width), F32)], name="weight_group",
        flops=2 * TAPS * rows * width * BLOCK,
    )
    middle, group_term = together(plane_sum(middle), group_term)
    if small:
        middle, expand_second, expand_first_other, expand_passed, expand_other = together(
            middle, expand_second, expand_first_other, expand_passed, expand_other
        )
        moving = [swap_x(expand_passed), expand_second, across(expand_first_other), across(expand_other)]
    sums_one = line_sum(middle)
    tall = depth + extra
    early = (6, 7) if small else tuple(range(size))
    flat_one, send = call(
        functools.partial(back_reduce_kernel, small, early),
        [shape((rows, width), BF16), shape((len(early), tall, half), BF16)],
        [mask, first, sums_one, inner_vectors, dz_one, red, turned, group_term],
        name="back_reduce", flops=2 * rows * depth * half * len(early),
    )
    near = swap_core(send)

    def sums(places, near, arrived=()):
        return call(
            functools.partial(block_sum_kernel, small, places),
            [shape((tall, half), BF16)] * len(places),
            [turned, group_term, flat_one, near] + list(arrived),
            name="block_sum", flops=2 * rows * depth * half * len(places),
        )

    def back_input(flat):
        (out,) = call(
            functools.partial(grad_input_kernel, slots, slot_depth, side),
            [shape(images.shape, BF16)],
            [flat, grad_summed] + weights,
            scratch=[pltpu.VMEM((rows, channels), F32)], name="grad_input", flops=2 * rows * width * channels,
        )
        return out

    def own_shards(*totals):
        if not small:
            cut = []
            for total, length in zip(totals, (per, per, outer)):
                cut += [lax.dynamic_slice_in_dim(total[row], position * length, length, 0) for row in (1, 0)]
            return cut
        lengths = (per, per, per, per, outer, outer)
        return [out.reshape(-1) for out in call(own_kernel, [shape((1, n), F32) for n in lengths], totals, name="own")]

    def join(own, far, outs):
        return call(
            join_kernel, [shape(out.shape, F32) for out in outs], [own, far, swap_core(own), swap_core(far)], name="join"
        )

    if small:
        late = (0, 1, 2, 3, 4, 5)
        (send,) = call(
            functools.partial(send_kernel, small, late),
            [shape((len(late), tall, half), BF16)],
            [turned, group_term, flat_one], name="send", flops=2 * rows * depth * half * len(late),
        )
        near_late = swap_core(send)
        passed_other, second_other = sums(((6, 0, ()), (7, 1, ())), near)
        second_other, *expand_moving = together(second_other, *moving)
        (expand_first_own,) = expand_sums(((1, (0, 1, 2)),), expand_moving[:3])
        moving = [swap_x(passed_other), across(second_other)]
        expand_first_own = along(expand_first_own, -1)
        grad_input = back_input(after(flat_one, second_other))
        moving[0], grad_input, expand_first_own = together(moving[0], grad_input, expand_first_own)
        (own_expand,) = expand_sums(((0, (0, 1)),), [expand_first_own, expand_moving[3]])
        first_other, passed, second = sums(((5, 5, (0,)), (2, 2, ()), (3, 3, (1,))), near_late, moving)
        moving = [swap_x(passed), along(second, -1), across(first_other)]
        output = pinned(after(output, second))
        moving[0], output = together(moving[0], output)
        first_own, other = sums(((1, 1, (0, 1, 2)), (4, 4, ())), near_late, moving)
        moving = [along(first_own, -1), across(other)]
        shards = own_shards(after(sums_one, first_own), sums_two, sums_three)
        grad_input, own_expand = pinned(after(grad_input, first_own)), after(own_expand, first_own)
        far_expand = swap_x(own_expand)
        moving[0], grad_input, far_expand, *shards = together(moving[0], grad_input, far_expand, *shards)
        (own_reduce,) = sums(((0, 0, (0, 1)),), near_late, moving)
        own_expand, far_expand = after(own_expand, own_reduce), after(far_expand, own_reduce)
        (grad_w_expand,) = join(own_expand, far_expand, [w_expand])
    else:
        grad_input = back_input(flat_one)
        shards = own_shards(sums_one, sums_two, sums_three)
        whole = jnp.stack(sums(tuple((at, at, ()) for at in range(size)), near)).reshape(size * tall, half)
        own_reduce = lax.psum_scatter(whole, "fsdp", scatter_dimension=0, tiled=True)
        (grad_w_expand,) = join(own_expand, swap_x(own_expand), [w_expand])
    grad_w_reduce, grad_w_group = join(own_reduce, swap_x(own_reduce), [w_reduce, w_group])
    return (output, grad_input, grad_w_reduce, grad_w_group, grad_w_expand) + tuple(shards)


def solution(mesh):
    fsdp, dp = mesh.shape["fsdp"], mesh.shape["dp"]
    split = Mesh(mesh.devices.reshape(fsdp, dp // 2, 2), ("fsdp", "x", "core"))
    images, rows, vector = P(("fsdp", "x", "core"), None, None, None), P("fsdp", None), P("fsdp")
    return jax.shard_map(
        per_device,
        mesh=split,
        in_specs=(
            images, P(("fsdp", "x", "core")), images,
            rows, vector, vector, rows, vector, vector, rows, vector, vector,
        ),
        out_specs=(images, images, rows, rows, rows) + (vector,) * 6,
        check_vma=False,
    )
```

```python
import functools

import jax
import jax.numpy as jnp
from jax import lax
from jax.experimental import pallas as pl
from jax.experimental.pallas import tpu as pltpu
from jax.sharding import Mesh
from jax.sharding import PartitionSpec as P

GROUPS = 32
TAPS = 9
LINE = 16
CHUNK = 512
UNROLL = 7
LANES = 128
BLOCK = 256
epsilon = 1e-05
BF16, F32 = jnp.bfloat16, jnp.float32
SWAP = [(0, 1), (1, 0)]
NN, NT = ((1,), (0,)), ((1,), (1,))
CHIPS = ("fsdp", "x")


def silu_half(half):
    return half + half * jnp.tanh(half)


def dsilu_twice(half):
    turned = jnp.tanh(half)
    upper = 1.0 + turned
    return upper * (1.0 + half * (1.0 - turned)), upper


def dot(a, b, contract=NN):
    return lax.dot_general(a, b, (contract, ((), ())), preferred_element_type=F32)


def after(values, *others):
    return lax.optimization_barrier((values,) + others)[0]


def together(*values):
    return lax.optimization_barrier(values)


def shape(dims, dtype):
    return jax.ShapeDtypeStruct(dims, dtype)


def call(kernel, outs, args, scalars=0, scratch=(), vmem=8, name=None, flops=0, anywhere=False, aliases=()):
    vm = pl.BlockSpec(memory_space=pltpu.VMEM)
    given = pl.BlockSpec(memory_space=pl.ANY) if anywhere else vm
    sm = pl.BlockSpec(memory_space=pltpu.SMEM)
    return pl.pallas_call(
        kernel,
        out_shape=outs,
        in_specs=[sm] * scalars + [given] * (len(args) - scalars),
        out_specs=[vm] * len(outs),
        scratch_shapes=list(scratch),
        compiler_params=pltpu.CompilerParams(vmem_limit_bytes=vmem << 20),
        cost_estimate=pl.CostEstimate(flops=flops, bytes_accessed=1 << 20, transcendentals=0),
        input_output_aliases=dict(aliases),
        name=name,
    )(*args)


def moments(total, pixels):
    mean = total[0:1, :] / pixels
    inverse = lax.rsqrt(total[1:2, :] / pixels - mean * mean + epsilon)
    return mean, inverse


def chunks(columns):
    return [slice(at, min(at + CHUNK, columns)) for at in range(0, columns, CHUNK)]


def line_mask(columns, side):
    return lax.broadcasted_iota(jnp.int32, (LINE, columns), 0) < side


def each_line(lines, body):
    lax.fori_loop(0, lines, lambda step, none: body(step) or none, 0, unroll=UNROLL)


def each_line_summed(lines, width, body):
    zero = jnp.zeros((8, width), F32)

    def step_sums(step, carry):
        one, two = body(step)
        return carry[0] + fold(one), carry[1] + fold(two)

    one, two = lax.fori_loop(0, lines, step_sums, (zero, zero), unroll=UNROLL)
    return column_sums(one), column_sums(two)


def across_lanes(mask, columns):
    return jnp.concatenate([mask] * (columns // LANES), axis=1)


def column_sums(values):
    return jnp.sum(values, axis=0, keepdims=True)


def line_at(step):
    return pl.ds(pl.multiple_of(step * LINE, LINE), LINE)


def fold(values):
    return values[0:8] + values[8:16]


def part_at(part, half, at=0, length=None):
    core = lax.axis_index("core")
    side = core if part == 0 else 1 - core
    length = half if length is None else length
    return pl.ds(pl.multiple_of(side * half + at, 128), length)


def block_owner(slot):
    position = lax.axis_index("fsdp")
    way = 1 - 2 * lax.axis_index("x")
    step = (0, -way, way, 2)[slot % 4]
    owner = lax.rem(position + 2 * step + 8, 8)
    return owner if slot < 4 else owner + 1 - 2 * lax.rem(owner, 2)


def rows_of(owner, depth):
    return pl.ds(pl.multiple_of(owner * depth, 16), depth)


def pack_kernel(side, valid, weight, group, vectors, out, mask, held, row, sems):
    depth, half = weight.shape[0], out.shape[1]
    shard, extra = group.shape[0], out.shape[0] - weight.shape[0]
    columns = part_at(0, half)
    copies = [
        pltpu.make_async_copy(group, held, sems.at[0]),
        pltpu.make_async_copy(vectors, row, sems.at[1]),
        pltpu.make_async_copy(weight.at[:, columns], out.at[pl.ds(0, depth)], sems.at[2]),
    ]
    for copy in copies:
        copy.start()
    images = valid.shape[0]
    rows = mask.shape[0] // images
    inside = lax.broadcasted_iota(jnp.int32, (rows, LANES), 0) % LINE < side
    for image in range(images):
        mask[image * rows : (image + 1) * rows, :] = jnp.where(inside, valid[image].astype(F32), 0.0)
    copies[0].wait()
    copies[1].wait()
    below = [held[:, columns].astype(F32), row[:, columns].astype(F32)]
    if extra > shard + 1:
        below.append(jnp.zeros((extra - shard - 1, half), F32))
    out[depth : depth + extra, :] = jnp.concatenate(below, axis=0).astype(BF16)
    copies[2].wait()


def reduce_kernel(part, slots, depth, side, valid, mask, x, *refs):
    weights, (red, stats) = refs[:slots], refs[-2:]
    half = weights[0].shape[1]
    for at in range(0, half, BLOCK):
        total = None
        for slot in range(slots):
            if slots == 1:
                piece = x[...]
            else:
                piece = x[:, pl.ds(pl.multiple_of(block_owner(slot) * depth, 128), depth)]
            term = dot(piece, weights[slot][0:depth, at : at + BLOCK])
            total = term if total is None else total + term
        columns = part_at(part, half, at, BLOCK)
        red[:, columns] = total
        masked = total * across_lanes(mask[...], BLOCK)
        stats[0:1, columns] = column_sums(masked)
        stats[1:2, columns] = column_sums(masked * total)
    pixels = valid[0].astype(F32)
    for image in range(1, valid.shape[0]):
        pixels = pixels + valid[image].astype(F32)
    columns = part_at(part, half)
    stats[2:3, columns] = jnp.full((1, half), 1.0, F32) * (pixels * (side * side))


def spread_kernel(slots, depth, *refs):
    blocks, (wide, wide_turned, inner_vectors, outer_vectors, held, rows) = refs[: 2 * slots], refs[2 * slots :]
    extra, half = held.shape[1], held.shape[2] // 2
    for slot in range(slots):
        for part in range(2):
            held[block_owner(slot), :, part_at(part, half)] = blocks[2 * slot + part][depth : depth + extra, :].astype(F32)
    shard = rows.shape[0] // slots
    per, outer = inner_vectors.shape[1] // slots, outer_vectors.shape[1] // slots
    for owner in range(slots):
        rows[owner * shard : (owner + 1) * shard, :] = held[owner, 0:shard, :]
        for row in range(4):
            inner_vectors[row : row + 1, owner * per : (owner + 1) * per] = held[
                owner, shard : shard + 1, row * per : (row + 1) * per
            ]
        for row in range(2):
            outer_vectors[row : row + 1, owner * outer : (owner + 1) * outer] = held[
                owner, shard : shard + 1, 4 * per + row * outer : 4 * per + (row + 1) * outer
            ]
    widen(rows, wide, wide_turned)


def widen_kernel(weight, wide, wide_turned, rows):
    rows[...] = weight[...].astype(F32)
    widen(rows, wide, wide_turned)


def widen(weight, wide, wide_turned):
    taps, blocks = wide.shape[:2]
    inner = weight.shape[0] // taps
    row = lax.broadcasted_iota(jnp.int32, (BLOCK, BLOCK), 0) // inner
    column = lax.broadcasted_iota(jnp.int32, (BLOCK, BLOCK), 1) // inner
    own = row == column
    for tap in range(taps):
        for block in range(blocks):
            piece = weight[tap * inner : (tap + 1) * inner, block * BLOCK : (block + 1) * BLOCK]
            tall = jnp.concatenate([piece] * (BLOCK // inner), axis=0)
            dense = jnp.where(own, tall, 0.0)
            wide[tap, block] = dense.astype(BF16)
            wide_turned[tap, block] = dense.T.astype(BF16)


def fill_pads(pads, columns, image, line, values):
    rows = pl.ds(pl.multiple_of((line + 1) * LINE, LINE), LINE)
    pads[0, image, rows, columns] = pltpu.roll(values, 1, 0).astype(BF16)
    pads[1, image, rows, columns] = values.astype(BF16)
    pads[2, image, rows, columns] = pltpu.roll(values, LINE - 1, 0).astype(BF16)


def clear_pads(pads):
    images, rows, columns = pads.shape[1:]
    zeros = jnp.zeros((3, images, LINE, columns), BF16)
    pads[:, :, 0:LINE, :] = zeros
    pads[:, :, rows - LINE : rows, :] = zeros


def convolve(pads, wide, image, block, rows, turned=False):
    columns = slice(block * BLOCK, (block + 1) * BLOCK)
    value = None
    for tap in range(TAPS):
        top, left = divmod(TAPS - 1 - tap if turned else tap, 3)
        piece = pads[left, image, top * LINE : top * LINE + rows, columns]
        term = dot(piece, wide[tap, block])
        value = term if value is None else value + term
    return value


def group_kernel(side, mask, total, vectors, red, wide, pads, grouped, stats):
    images, padded, width = pads.shape[1:]
    rows = side * LINE
    mean, inverse = moments(total, total[2:3, :])
    scale, bias = 0.5 * inverse * vectors[0:1, :], 0.5 * vectors[1:2, :]
    clear_pads(pads)
    for part in chunks(width):
        inside = line_mask(part.stop - part.start, side)

        def body(step):
            half = (red[line_at(step), part] - mean[:, part]) * scale[:, part] + bias[:, part]
            fill_pads(pads, part, step // side, step % side, jnp.where(inside, silu_half(half), 0.0))

        each_line(images * side, body)
    for block in range(width // BLOCK):
        columns = slice(block * BLOCK, (block + 1) * BLOCK)
        sums = [0.0, 0.0]
        for image in range(images):
            at = slice(image * rows, (image + 1) * rows)
            value = convolve(pads, wide, image, block, rows)
            grouped[at, columns] = value
            masked = value * across_lanes(mask[at, :], BLOCK)
            sums = [sums[0] + column_sums(masked), sums[1] + column_sums(masked * value)]
        stats[0:1, columns] = sums[0]
        stats[1:2, columns] = sums[1]


def pair_slots(slots):
    return [(0,)] if slots == 1 else [(slot, slot + slots // 2) for slot in range(slots // 2)]


def pair_rows(weights, pair, part, columns=slice(None)):
    return jnp.concatenate([weights[2 * slot + part][:, columns] for slot in pair], axis=0)


def expand_kernel(slots, side, mask, total, first, vectors, grouped, *refs):
    weights, (act, expanded, stats, held) = refs[: 2 * slots], refs[2 * slots :]
    rows, width = grouped.shape
    mean, inverse = moments(total, first[2:3, :])
    scale, bias = 0.5 * inverse * vectors[2:3, :], 0.5 * vectors[3:4, :]
    for part in chunks(width):
        inside = line_mask(part.stop - part.start, side)

        def body(step):
            at = line_at(step)
            half = (grouped[at, part] - mean[:, part]) * scale[:, part] + bias[:, part]
            held[at, part] = jnp.where(inside, silu_half(half), 0.0).astype(BF16)

        each_line(rows // LINE, body)
    depth, half = weights[0].shape
    pairs = pair_slots(slots)
    for at, slot in enumerate(slot for pair in pairs for slot in pair):
        columns = pl.ds(pl.multiple_of(block_owner(slot) * depth, 128), depth) if slots > 1 else slice(None)
        act[:, at * depth : (at + 1) * depth] = held[:, columns]
    tall = depth * len(pairs[0])
    for part in range(2):
        for at in range(0, half, BLOCK):
            value = None
            for index, pair in enumerate(pairs):
                weight = pair_rows(weights, pair, part, slice(at, at + BLOCK))
                term = dot(act[:, index * tall : (index + 1) * tall], weight)
                value = term if value is None else value + term
            columns = part_at(part, half, at, BLOCK)
            expanded[:, columns] = value
            masked = value * across_lanes(mask[...], BLOCK)
            stats[0:1, columns] = column_sums(masked)
            stats[1:2, columns] = column_sums(masked * value)


def output_kernel(side, valid, total, first, vectors, expanded, x, cotangent, output, grad, stats):
    rows, channels = expanded.shape
    mean, inverse = moments(total, first[2:3, 0:1])
    scale, bias = inverse * vectors[0:1, :], vectors[1:2, :]
    for part in chunks(channels):

        def body(step):
            image, line = step // side, step % side
            at = line_at(step)
            keep = 0.5 * valid[image].astype(F32)
            centered = expanded[at, part] - mean[:, part]
            half = (centered * scale[:, part] + (bias[:, part] + x[at, part].astype(F32))) * keep
            slope, upper = dsilu_twice(half)
            output[image, line, :, part] = (half * upper).astype(BF16)[0:side]
            here = cotangent[at, part].astype(F32) * keep * slope
            grad[at, part] = here
            return here, here * centered

        one, two = each_line_summed(rows // LINE, part.stop - part.start, body)
        stats[0:1, part] = one
        stats[1:2, part] = two * inverse[:, part]


def back_expand_kernel(
    slots, mask, total, sums, first, vectors, total_two, vectors_two, grad, expanded, grouped, *refs
):
    weights, (flat, dz, stats) = refs[: 2 * slots], refs[2 * slots :]
    rows, width = grouped.shape
    pixels = first[2:3, 0:1]
    mean, inverse = moments(total, pixels)
    scale = inverse * vectors[0:1, :]
    shifted, scaled = scale * sums[0:1, :] / pixels, scale * inverse * sums[1:2, :] / pixels
    for part in chunks(expanded.shape[1]):

        def body(step):
            at = line_at(step)
            common = shifted[:, part] + (expanded[at, part] - mean[:, part]) * scaled[:, part]
            flat[at, part] = (scale[:, part] * grad[at, part] - across_lanes(mask[at, :], part.stop - part.start) * common).astype(BF16)

        each_line(rows // LINE, body)
    depth, half = weights[0].shape
    for pair in pair_slots(slots):
        for at in range(0, depth * len(pair), BLOCK):
            value = None
            for part in range(2):
                weight = pair_rows(weights, pair, part) if slots > 1 else weights[part][at : at + BLOCK, :]
                term = dot(flat[:, part_at(part, half)], weight, NT)
                value = term if value is None else value + term
            if slots == 1:
                dz[:, at : at + BLOCK] = value
            else:
                for index, slot in enumerate(pair):
                    columns = pl.ds(pl.multiple_of(block_owner(slot) * depth, 128), depth)
                    dz[:, columns] = value[:, index * depth : (index + 1) * depth]
    mean_two, inverse_two = moments(total_two, first[2:3, :])
    before_norm(dz, grouped, mean_two, inverse_two, vectors_two[2:3, :], vectors_two[3:4, :], stats)


def before_norm(dz, hidden, mean, inverse, gain, shift, stats, side=None):
    scale, bias = 0.5 * inverse * gain, 0.5 * shift
    rows, width = hidden.shape
    for part in chunks(width):
        inside = None if side is None else line_mask(part.stop - part.start, side)

        def body(step):
            at = line_at(step)
            centered = hidden[at, part] - mean[:, part]
            slope, _ = dsilu_twice(centered * scale[:, part] + bias[:, part])
            here = dz[at, part] * slope
            if side is not None:
                here = jnp.where(inside, here, 0.0)
            dz[at, part] = here
            return here, here * centered

        one, two = each_line_summed(rows // LINE, part.stop - part.start, body)
        stats[0:1, part] = 0.5 * one
        stats[1:2, part] = 0.5 * inverse[:, part] * two


def weight_expand_kernel(act, flat, send, keep):
    half = send.shape[1]
    turned = act[...].T
    for part, out in ((1, send), (0, keep)):
        for at in range(0, half, BLOCK):
            out[:, at : at + BLOCK] = dot(turned, flat[:, part_at(part, half, at, BLOCK)]).astype(BF16)


def back_group_kernel(
    side, mask, total, sums, first, vectors, dz, grouped, red, wide, flat, dz_one, stats, pads
):
    images, padded, width = pads.shape[1:]
    rows = side * LINE
    pixels = first[2:3, :]
    mean, inverse = moments(total, pixels)
    scale = inverse * vectors[2:3, :]
    shifted, scaled = scale * sums[0:1, :] / pixels, scale * inverse * sums[1:2, :] / pixels
    scale = 0.5 * scale
    clear_pads(pads)
    for part in chunks(width):

        def body(step):
            at = line_at(step)
            common = shifted[:, part] + (grouped[at, part] - mean[:, part]) * scaled[:, part]
            value = scale[:, part] * dz[at, part] - across_lanes(mask[at, :], part.stop - part.start) * common
            flat[at, part] = value.astype(BF16)
            fill_pads(pads, part, step // side, step % side, value)

        each_line(images * side, body)
    for block in range(width // BLOCK):
        columns = slice(block * BLOCK, (block + 1) * BLOCK)
        for image in range(images):
            dz_one[image * rows : (image + 1) * rows, columns] = convolve(pads, wide, image, block, rows, True)
    mean_one, inverse_one = moments(first, pixels)
    before_norm(dz_one, red, mean_one, inverse_one, vectors[0:1, :], vectors[1:2, :], stats, side)


def weight_group_kernel(side, pads, flat, out, held):
    images, padded, width = pads.shape[1:]
    rows = side * LINE
    inner = width // GROUPS
    row = lax.broadcasted_iota(jnp.int32, (LANES, LANES), 0) // inner
    column = lax.broadcasted_iota(jnp.int32, (LANES, LANES), 1) // inner
    own = row == column
    for at in range(0, width, LANES):
        columns = slice(at, at + LANES)
        moved = []
        for tap in range(TAPS):
            top, left = divmod(tap, 3)
            pieces = [pads[left, image, top * LINE : top * LINE + rows, columns] for image in range(images)]
            moved.append(jnp.concatenate(pieces, axis=0))
        product = dot(flat[:, columns].T, jnp.concatenate(moved, axis=1))
        for tap in range(TAPS):
            kept = jnp.where(own, product[:, tap * LANES : (tap + 1) * LANES].T, 0.0)
            value = kept[0:inner]
            for begin in range(inner, LANES, inner):
                value = value + kept[begin : begin + inner]
            held[tap * inner : (tap + 1) * inner, columns] = value
    owners, extra = out.shape[:2]
    shard = TAPS * inner // owners
    zeros = jnp.zeros((extra - shard, width), F32)
    for owner in range(owners):
        rows_here = held[owner * shard : (owner + 1) * shard, :]
        out[owner] = jnp.concatenate([rows_here, zeros], axis=0).astype(BF16)


def back_reduce_kernel(
    small, blocks, mask, first, sums, vectors, dz, red, turned, group, flat, send
):
    rows, width = red.shape
    pixels = first[2:3, :]
    mean, inverse = moments(first, pixels)
    scale = inverse * vectors[0:1, :]
    shifted, scaled = scale * sums[0:1, :] / pixels, scale * inverse * sums[1:2, :] / pixels
    scale = 0.5 * scale
    for part in chunks(width):

        def body(step):
            at = line_at(step)
            common = shifted[:, part] + (red[at, part] - mean[:, part]) * scaled[:, part]
            flat[at, part] = (scale[:, part] * dz[at, part] - across_lanes(mask[at, :], part.stop - part.start) * common).astype(BF16)

        each_line(rows // LINE, body)
    send_kernel(small, blocks, turned, group, flat, send)


def send_kernel(small, blocks, turned, group, flat, send):
    tall, half = send.shape[1:]
    depth = tall - group.shape[1]
    columns = part_at(1, half)
    for at, block in enumerate(blocks):
        owner = block_owner(block) if small else block
        send[at, 0:depth, :] = dot(turned[rows_of(owner, depth), :], flat[:, columns]).astype(BF16)
        send[at, depth:tall, :] = group[owner, :, columns]


def block_sum_kernel(small, places, turned, group, flat, near, *refs):
    arrived, outs = refs[: len(refs) - len(places)], refs[len(refs) - len(places) :]
    tall, half = near.shape[1:]
    depth = tall - group.shape[1]
    columns = part_at(0, half)
    for out, (block, at, chosen) in zip(outs, places):
        owner = block_owner(block) if small else block
        value = dot(turned[rows_of(owner, depth), :], flat[:, columns]) + near[at, 0:depth, :].astype(F32)
        more = group[owner, :, columns].astype(F32) + near[at, depth:tall, :].astype(F32)
        for other in chosen:
            value = value + arrived[other][0:depth, :].astype(F32)
            more = more + arrived[other][depth:tall, :].astype(F32)
        out[0:depth, :] = value.astype(BF16)
        out[depth:tall, :] = more.astype(BF16)


def expand_sum_kernel(places, keep, near, *refs):
    arrived, outs = refs[: len(refs) - len(places)], refs[len(refs) - len(places) :]
    depth = outs[0].shape[0]
    for out, (block, chosen) in zip(outs, places):
        at = block % 4 * 2 + block // 4
        rows = slice(at * depth, (at + 1) * depth)
        value = keep[rows, :].astype(F32) + near[rows, :].astype(F32)
        for other in chosen:
            value = value + arrived[other][...].astype(F32)
        out[...] = value.astype(BF16)


def add_kernel(a, b, out):
    out[...] = (a[...].astype(F32) + b[...].astype(F32)).astype(out.dtype)


def join_kernel(mine, mine_x, other, other_x, *outs):
    half = mine.shape[1]
    at = 0
    for out in outs:
        rows = out.shape[0]
        for part, terms in enumerate(((mine, mine_x), (other, other_x))):
            values = [term[at : at + -(-rows // 16) * 16, :].astype(F32) for term in terms]
            out[:, part_at(part, half)] = (values[0] + values[1])[0:rows]
        at += -(-rows // 16) * 16


def turn_kernel(values, out):
    out[...] = values[...].T


def pin_kernel(values, out):
    pass


def own_kernel(*refs):
    number = len(refs) // 3
    position = lax.axis_index("fsdp")
    for at, total in enumerate(refs[:number]):
        for row, out in ((1, refs[number + 2 * at]), (0, refs[number + 2 * at + 1])):
            length = out.shape[1]
            out[...] = total[row : row + 1, pl.ds(pl.multiple_of(position * length, 128), length)]


def grad_input_kernel(slots, depth, side, flat, grad, *refs):
    weights, (out, held) = refs[: 2 * slots], refs[2 * slots :]
    half = weights[0].shape[1]
    for slot in range(slots):
        columns = pl.ds(pl.multiple_of(block_owner(slot) * depth, 128), depth) if slots > 1 else slice(None)
        value = grad[:, columns]
        for part in range(2):
            value = value + dot(flat[:, part_at(part, half)], weights[2 * slot + part][0:depth, :], NT)
        held[:, columns] = value

    def body(step, carry):
        out[step // side, step % side] = held[line_at(step), :].astype(BF16)[0:side]
        return carry

    lax.fori_loop(0, flat.shape[0] // LINE, body, 0)


def pinned(values):
    anywhere = pl.BlockSpec(memory_space=pl.ANY)
    values = values.transpose(1, 2, 0, 3)
    values = pl.pallas_call(
        pin_kernel, out_shape=shape(values.shape, values.dtype), in_specs=[anywhere], out_specs=anywhere,
        input_output_aliases={0: 0}, compiler_params=pltpu.CompilerParams(vmem_limit_bytes=1 << 20), name="pin",
    )(values)
    return values.transpose(2, 0, 1, 3)


def swap_core(values):
    return lax.ppermute(values, "core", SWAP)


def swap_x(values):
    if lax.axis_size("x") == 2:
        return lax.ppermute(values, "x", SWAP)
    return (lax.psum(values.astype(F32), "x") - values.astype(F32)).astype(values.dtype)


def sum_chips(values, flips):
    got = [lax.ppermute(values, CHIPS, [(at, at ^ flip) for at in range(16)]) for flip in flips]
    for other in got:
        values = values + other
    return values


def along(values, way):
    pairs = [(f * 2 + x, (f + 2 * way * (1 - 2 * x)) % 8 * 2 + x) for f in range(8) for x in range(2)]
    return lax.ppermute(values, CHIPS, pairs)


def across(values):
    return lax.ppermute(values, "fsdp", [(f, f ^ 1) for f in range(8)])


def gather_blocks(own, early, late, beside):
    first = along(own, 1)
    other = across(own)
    first, other, *early = together(first, other, *early)
    passed, second, first_other = swap_x(first), along(first, 1), across(first)
    second, passed, first_other, *late = together(second, passed, first_other, *late)
    passed_other, second_other, beside = swap_x(first_other), across(second), along(beside(early), 1)
    blocks = [own, first, passed, second, other, first_other, passed_other, second_other]
    *blocks, beside = together(*blocks, beside)
    return blocks, early, late, beside


def halves(values, core):
    half = values.shape[1] // 2
    return lax.dynamic_slice_in_dim(values, core * half, half, 1)


def per_device(
    images,
    valid,
    cotangent,
    w_reduce,
    gain_one,
    shift_one,
    w_group,
    gain_two,
    shift_two,
    w_expand,
    gain_three,
    shift_three,
):
    count, side, _, channels = images.shape
    width = w_reduce.shape[1]
    inner = width // GROUPS
    size = lax.axis_size("fsdp")
    small = size == 8 and lax.axis_size("x") == 2
    position, core = lax.axis_index("fsdp"), lax.axis_index("core")
    rows = count * side * LINE
    per, outer, shard, depth = gain_one.shape[0], gain_three.shape[0], w_group.shape[0], w_reduce.shape[0]
    extra = -(-(shard + 1) // 16) * 16
    half = width // 2

    def start_sum(values):
        return values + swap_core(values) if small else lax.psum(values, ("fsdp", "x", "core"))

    def plane_sum(values):
        return sum_chips(values, (1, 2, 3)) if small else values

    def line_sum(values):
        return sum_chips(values, (4, 8, 12)) if small else values

    def everywhere(values):
        return line_sum(plane_sum(start_sum(values)))


    def padded(values):
        return jnp.pad(values, ((0, 0), (0, 0), (0, LINE - side), (0, 0))).reshape(rows, channels)

    x, cot = padded(images), padded(cotangent)

    vectors, at = jnp.zeros((width,), BF16), 0
    for vector in (gain_one, shift_one, gain_two, shift_two, gain_three, shift_three):
        vectors = vectors + jnp.pad(vector, (at, width - at - vector.size))
        at += vector.size
    own, mask = call(
        functools.partial(pack_kernel, side),
        [shape((depth + extra, half), BF16), shape((rows, LANES), F32)],
        [valid, w_reduce, w_group, vectors.reshape(1, width)], scalars=1, anywhere=True, vmem=60, name="pack",
        scratch=[pltpu.VMEM((shard, width), BF16), pltpu.VMEM((1, width), BF16), pltpu.SemaphoreType.DMA((3,))],
    )
    wide_shape = shape((TAPS, width // BLOCK, BLOCK, BLOCK), BF16)
    expand_own = halves(w_expand, core)
    if small:
        (turned,) = call(turn_kernel, [shape((channels, rows), BF16)], [x], name="turn")
        blocks, (x, expand_own), (turned,), expand_first = gather_blocks(
            own, (x, expand_own), (turned,), lambda early: early[1]
        )
        second, other = along(expand_first, 1), across(expand_own)
        slots, slot_depth = size, depth
    else:
        whole = lax.all_gather(own, "fsdp", axis=0, tiled=False)
        block = whole[:, :depth].reshape(channels, half)
        blocks = [block]
        slots, slot_depth, turned = 1, channels, x.T
        expand_mine = lax.all_gather(expand_own, "fsdp", axis=0, tiled=True)
        expand_weights = [expand_mine, swap_core(expand_mine)]

    far = [swap_core(block) for block in blocks]
    weights = [half for pair in zip(blocks, far) for half in pair]

    def reduce_part(part, weights, *before):
        return call(
            functools.partial(reduce_kernel, part, slots, slot_depth, side),
            [shape((rows, width), F32), shape((3, width), F32)],
            [valid, mask, x, *weights, *before], scalars=1, name="reduce", flops=rows * width * channels,
            aliases=((3 + slots, 0), (4 + slots, 1)) if before else (),
        )

    red, part = reduce_part(1, far, *reduce_part(0, blocks))
    if small:
        wide, wide_turned, inner_vectors, outer_vectors = call(
            functools.partial(spread_kernel, slots, depth),
            [wide_shape, wide_shape, shape((4, width), F32), shape((2, channels), F32)],
            weights,
            scratch=[pltpu.VMEM((size, extra, width), F32), pltpu.VMEM((size * shard, width), F32)],
            name="spread", flops=1 << 28,
        )
    else:
        mine = whole[:, depth:]
        other = swap_core(mine)
        packed = jnp.concatenate([jnp.where(core == 0, mine, other), jnp.where(core == 0, other, mine)], axis=2)
        wide, wide_turned = call(
            widen_kernel, [wide_shape, wide_shape], [packed[:, :shard].reshape(size * shard, width)],
            scratch=[pltpu.VMEM((size * shard, width), F32)], name="widen",
        )
        line = packed[:, shard].astype(F32)
        inner_vectors = line[:, : 4 * per].reshape(size, 4, per).transpose(1, 0, 2).reshape(4, width)
        outer_vectors = line[:, 4 * per : 4 * per + 2 * outer].reshape(size, 2, outer)
        outer_vectors = outer_vectors.transpose(1, 0, 2).reshape(2, channels)
    middle = start_sum(part)
    if small:
        middle, other = together(middle, other)
    middle, wide, wide_turned, inner_vectors, outer_vectors = together(
        plane_sum(middle), wide, wide_turned, inner_vectors, outer_vectors
    )
    if small:
        middle, second, expand_first = together(middle, second, expand_first)
        first_other, passed = across(expand_first), swap_x(expand_first)
    first = line_sum(middle)
    if small:
        first, first_other, second = together(first, first_other, second)
        second_other, passed_other = across(second), swap_x(first_other)
    pad_shape = (3, count, (side + 2) * LINE, width)
    pads, grouped, part = call(
        functools.partial(group_kernel, side),
        [shape(pad_shape, BF16), shape((rows, width), F32), shape((2, width), F32)],
        [mask, first, inner_vectors, red, wide],
        name="group", flops=2 * TAPS * rows * width * BLOCK,
    )
    if small:
        part, passed = together(part, passed)
    middle = line_sum(start_sum(part))
    if small:
        middle, passed_other, second_other = together(middle, passed_other, second_other)
        expand_weights = []
        for block in (expand_own, expand_first, passed, second, other, first_other, passed_other, second_other):
            expand_weights += [block, swap_core(block)]
    total_two = plane_sum(middle)
    act_two, expanded, part = call(
        functools.partial(expand_kernel, slots, side),
        [shape((rows, width), BF16), shape((rows, channels), F32), shape((2, channels), F32)],
        [mask, total_two, first, inner_vectors, grouped] + expand_weights,
        scratch=[pltpu.VMEM((rows, width), BF16)], name="expand", flops=2 * rows * width * channels,
    )
    total_three = everywhere(part)
    output, grad_summed, part = call(
        functools.partial(output_kernel, side),
        [shape(images.shape, BF16), shape((rows, channels), F32), shape((2, channels), F32)],
        [valid, total_three, first, outer_vectors, expanded, x, cot], scalars=1, name="output",
    )

    sums_three = everywhere(part)
    flat_three, dz_two, part = call(
        functools.partial(back_expand_kernel, slots),
        [shape((rows, channels), BF16), shape((rows, width), F32), shape((2, width), F32)],
        [mask, total_three, sums_three, first, outer_vectors, total_two, inner_vectors, grad_summed, expanded, grouped]
        + expand_weights,
        name="back_expand", flops=2 * rows * width * channels,
    )
    middle = start_sum(part)
    act_two = after(act_two, middle)
    send, keep = call(
        weight_expand_kernel,
        [shape((width, channels // 2), BF16)] * 2,
        [act_two, flat_three], name="weight_expand", flops=2 * rows * width * channels,
    )
    near_expand = swap_core(send)
    middle = plane_sum(middle)

    def expand_sums(places, arrived=()):
        return call(
            functools.partial(expand_sum_kernel, places),
            [shape((w_expand.shape[0], channels // 2), BF16)] * len(places),
            [keep, near_expand] + list(arrived), name="expand_sum",
        )

    if small:
        middle, *moving = together(middle, *expand_sums(((6, ()), (7, ()))))
        moving = [swap_x(moving[0]), across(moving[1])]
        sums_two, *moving = together(line_sum(middle), *moving)
        sums_two, expand_first_other, expand_passed, expand_second, expand_other = together(
            sums_two, *expand_sums(((5, (0,)), (2, ()), (3, (1,)), (4, ())), moving)
        )
        expand_second, expand_other = along(expand_second, -1), across(expand_other)
    else:
        sums_two = line_sum(middle)
        (chip,) = call(add_kernel, [shape(keep.shape, BF16)], [keep, near_expand], name="add")
        own_expand = lax.psum_scatter(chip, "fsdp", scatter_dimension=0, tiled=True)
    flat_two, dz_one, part = call(
        functools.partial(back_group_kernel, side),
        [shape((rows, width), BF16), shape((rows, width), F32), shape((2, width), F32)],
        [mask, total_two, sums_two, first, inner_vectors, dz_two, grouped, red, wide_turned],
        scratch=[pltpu.VMEM(pad_shape, BF16)], name="back_group", flops=2 * TAPS * rows * width * BLOCK,
    )

    middle = start_sum(part)
    flat_two = after(flat_two, middle)
    (group_term,) = call(
        functools.partial(weight_group_kernel, side),
        [shape((size, extra, width), BF16)],
        [pads, flat_two], scratch=[pltpu.VMEM((TAPS * inner, width), F32)], name="weight_group",
        flops=2 * TAPS * rows * width * BLOCK,
    )
    middle, group_term = together(plane_sum(middle), group_term)
    if small:
        middle, expand_second, expand_first_other, expand_passed, expand_other = together(
            middle, expand_second, expand_first_other, expand_passed, expand_other
        )
        moving = [swap_x(expand_passed), across(expand_first_other)]
    sums_one = line_sum(middle)
    if small:
        sums_one, *moving = together(sums_one, *moving)
        (expand_first_own,) = expand_sums(((1, (0, 1, 2)),), moving + [expand_second])
    tall = depth + extra
    early = (6, 7) if small else tuple(range(size))
    flat_one, send = call(
        functools.partial(back_reduce_kernel, small, early),
        [shape((rows, width), BF16), shape((len(early), tall, half), BF16)],
        [mask, first, sums_one, inner_vectors, dz_one, red, turned, group_term],
        name="back_reduce", flops=2 * rows * depth * half * len(early),
    )
    near = swap_core(send)

    def sums(places, near, arrived=()):
        return call(
            functools.partial(block_sum_kernel, small, places),
            [shape((tall, half), BF16)] * len(places),
            [turned, group_term, flat_one, near] + list(arrived),
            name="block_sum", flops=2 * rows * depth * half * len(places),
        )

    def back_input(flat):
        (out,) = call(
            functools.partial(grad_input_kernel, slots, slot_depth, side),
            [shape(images.shape, BF16)],
            [flat, grad_summed] + weights,
            scratch=[pltpu.VMEM((rows, channels), F32)], name="grad_input", flops=2 * rows * width * channels,
        )
        return out

    def own_shards(*totals):
        if not small:
            cut = []
            for total, length in zip(totals, (per, per, outer)):
                cut += [lax.dynamic_slice_in_dim(total[row], position * length, length, 0) for row in (1, 0)]
            return cut
        lengths = (per, per, per, per, outer, outer)
        return [out.reshape(-1) for out in call(own_kernel, [shape((1, n), F32) for n in lengths], totals, name="own")]

    def join(own, far, outs):
        return call(
            join_kernel, [shape(out.shape, F32) for out in outs], [own, far, swap_core(own), swap_core(far)], name="join"
        )

    if small:
        late = (0, 1, 2, 3, 4, 5)
        (send,) = call(
            functools.partial(send_kernel, small, late),
            [shape((len(late), tall, half), BF16)],
            [turned, group_term, flat_one], name="send", flops=2 * rows * depth * half * len(late),
        )
        near_late = swap_core(send)
        passed_other, second_other = sums(((6, 0, ()), (7, 1, ())), near)
        second_other, expand_first_own = together(second_other, expand_first_own)
        moving = [swap_x(passed_other), across(second_other)]
        expand_first_own = along(expand_first_own, -1)
        grad_input = back_input(after(flat_one, second_other))
        moving[0], grad_input, expand_first_own = together(moving[0], grad_input, expand_first_own)
        (own_expand,) = expand_sums(((0, (0, 1)),), [expand_first_own, expand_other])
        first_other, passed, second = sums(((5, 5, (0,)), (2, 2, ()), (3, 3, (1,))), near_late, moving)
        moving = [swap_x(passed), along(second, -1), across(first_other)]
        output = pinned(after(output, second))
        moving[0], output = together(moving[0], output)
        first_own, other = sums(((1, 1, (0, 1, 2)), (4, 4, ())), near_late, moving)
        moving = [along(first_own, -1), across(other)]
        shards = own_shards(after(sums_one, first_own), sums_two, sums_three)
        grad_input, own_expand = pinned(after(grad_input, first_own)), after(own_expand, first_own)
        far_expand = swap_x(own_expand)
        moving[0], grad_input, far_expand, *shards = together(moving[0], grad_input, far_expand, *shards)
        (own_reduce,) = sums(((0, 0, (0, 1)),), near_late, moving)
        own_expand, far_expand = after(own_expand, own_reduce), after(far_expand, own_reduce)
        (grad_w_expand,) = join(own_expand, far_expand, [w_expand])
    else:
        grad_input = back_input(flat_one)
        shards = own_shards(sums_one, sums_two, sums_three)
        whole = jnp.stack(sums(tuple((at, at, ()) for at in range(size)), near)).reshape(size * tall, half)
        own_reduce = lax.psum_scatter(whole, "fsdp", scatter_dimension=0, tiled=True)
        (grad_w_expand,) = join(own_expand, swap_x(own_expand), [w_expand])
    grad_w_reduce, grad_w_group = join(own_reduce, swap_x(own_reduce), [w_reduce, w_group])
    return (output, grad_input, grad_w_reduce, grad_w_group, grad_w_expand) + tuple(shards)


def solution(mesh):
    fsdp, dp = mesh.shape["fsdp"], mesh.shape["dp"]
    split = Mesh(mesh.devices.reshape(fsdp, dp // 2, 2), ("fsdp", "x", "core"))
    images, rows, vector = P(("fsdp", "x", "core"), None, None, None), P("fsdp", None), P("fsdp")
    return jax.shard_map(
        per_device,
        mesh=split,
        in_specs=(
            images, P(("fsdp", "x", "core")), images,
            rows, vector, vector, rows, vector, vector, rows, vector, vector,
        ),
        out_specs=(images, images, rows, rows, rows) + (vector,) * 6,
        check_vma=False,
    )
```

```python
import functools

import jax
import jax.numpy as jnp
from jax import lax
from jax.experimental import pallas as pl
from jax.experimental.pallas import tpu as pltpu
from jax.sharding import Mesh
from jax.sharding import PartitionSpec as P

GROUPS = 32
TAPS = 9
LINE = 16
CHUNK = 512
UNROLL = 7
LANES = 128
BLOCK = 256
epsilon = 1e-05
BF16, F32 = jnp.bfloat16, jnp.float32
SWAP = [(0, 1), (1, 0)]
NN, NT = ((1,), (0,)), ((1,), (1,))
CHIPS = ("fsdp", "x")


def silu_half(half):
    return half + half * jnp.tanh(half)


def dsilu_twice(half):
    turned = jnp.tanh(half)
    upper = 1.0 + turned
    return upper * (1.0 + half * (1.0 - turned)), upper


def dot(a, b, contract=NN):
    return lax.dot_general(a, b, (contract, ((), ())), preferred_element_type=F32)


def after(values, *others):
    return lax.optimization_barrier((values,) + others)[0]


def together(*values):
    return lax.optimization_barrier(values)


def shape(dims, dtype):
    return jax.ShapeDtypeStruct(dims, dtype)


def call(kernel, outs, args, scalars=0, scratch=(), vmem=8, name=None, flops=0, anywhere=False, aliases=()):
    vm = pl.BlockSpec(memory_space=pltpu.VMEM)
    given = pl.BlockSpec(memory_space=pl.ANY) if anywhere else vm
    sm = pl.BlockSpec(memory_space=pltpu.SMEM)
    return pl.pallas_call(
        kernel,
        out_shape=outs,
        in_specs=[sm] * scalars + [given] * (len(args) - scalars),
        out_specs=[vm] * len(outs),
        scratch_shapes=list(scratch),
        compiler_params=pltpu.CompilerParams(vmem_limit_bytes=vmem << 20),
        cost_estimate=pl.CostEstimate(flops=flops, bytes_accessed=1 << 20, transcendentals=0),
        input_output_aliases=dict(aliases),
        name=name,
    )(*args)


def moments(total, pixels):
    mean = total[0:1, :] / pixels
    inverse = lax.rsqrt(total[1:2, :] / pixels - mean * mean + epsilon)
    return mean, inverse


def chunks(columns):
    return [slice(at, min(at + CHUNK, columns)) for at in range(0, columns, CHUNK)]


def line_mask(columns, side):
    return lax.broadcasted_iota(jnp.int32, (LINE, columns), 0) < side


def each_line(lines, body):
    lax.fori_loop(0, lines, lambda step, none: body(step) or none, 0, unroll=UNROLL)


def each_line_summed(lines, width, body):
    zero = jnp.zeros((8, width), F32)

    def step_sums(step, carry):
        one, two = body(step)
        return carry[0] + fold(one), carry[1] + fold(two)

    one, two = lax.fori_loop(0, lines, step_sums, (zero, zero), unroll=UNROLL)
    return column_sums(one), column_sums(two)


def across_lanes(mask, columns):
    return jnp.concatenate([mask] * (columns // LANES), axis=1)


def column_sums(values):
    return jnp.sum(values, axis=0, keepdims=True)


def line_at(step):
    return pl.ds(pl.multiple_of(step * LINE, LINE), LINE)


def fold(values):
    return values[0:8] + values[8:16]


def part_at(part, half, at=0, length=None):
    core = lax.axis_index("core")
    side = core if part == 0 else 1 - core
    length = half if length is None else length
    return pl.ds(pl.multiple_of(side * half + at, 128), length)


def block_owner(slot):
    position = lax.axis_index("fsdp")
    way = 1 - 2 * lax.axis_index("x")
    step = (0, -way, way, 2)[slot % 4]
    owner = lax.rem(position + 2 * step + 8, 8)
    return owner if slot < 4 else owner + 1 - 2 * lax.rem(owner, 2)


def rows_of(owner, depth):
    return pl.ds(pl.multiple_of(owner * depth, 16), depth)


def pack_kernel(weight, group, vectors, out, held, row, sems):
    depth, half = weight.shape[0], out.shape[1]
    shard, extra = group.shape[0], out.shape[0] - weight.shape[0]
    columns = part_at(0, half)
    copies = [
        pltpu.make_async_copy(group, held, sems.at[0]),
        pltpu.make_async_copy(vectors, row, sems.at[1]),
        pltpu.make_async_copy(weight.at[:, columns], out.at[pl.ds(0, depth)], sems.at[2]),
    ]
    for copy in copies:
        copy.start()
    copies[0].wait()
    copies[1].wait()
    below = [held[:, columns].astype(F32), row[...].astype(F32)]
    if extra > shard + 2:
        below.append(jnp.zeros((extra - shard - 2, half), F32))
    out[depth : depth + extra, :] = jnp.concatenate(below, axis=0).astype(BF16)
    copies[2].wait()


def turn_kernel(side, valid, x, x_other, turned, mask):
    rows = x.shape[0]
    turned[:, 0:rows] = x[...].T
    turned[:, rows : 2 * rows] = x_other[...].T
    images = valid.shape[0]
    rows = 2 * rows // images
    inside = lax.broadcasted_iota(jnp.int32, (rows, LANES), 0) % LINE < side
    for image in range(images):
        mask[image * rows : (image + 1) * rows, :] = jnp.where(inside, valid[image].astype(F32), 0.0)


def reduce_kernel(slots, depth, side, valid, mask, x, x_other, *refs):
    weights, (red, stats) = refs[:slots], refs[slots:]
    half, rows = red.shape[1], x.shape[0]
    for at in range(0, half, BLOCK):
        sums = [0.0, 0.0]
        for begin, pixels in ((0, x), (rows, x_other)):
            total = None
            for slot in range(slots):
                if slots == 1:
                    piece = pixels[...]
                else:
                    piece = pixels[:, pl.ds(pl.multiple_of(block_owner(slot) * depth, 128), depth)]
                term = dot(piece, weights[slot][0:depth, at : at + BLOCK])
                total = term if total is None else total + term
            red[begin : begin + rows, at : at + BLOCK] = total
            masked = total * across_lanes(mask[begin : begin + rows, :], BLOCK)
            sums = [sums[0] + column_sums(masked), sums[1] + column_sums(masked * total)]
        stats[0:1, at : at + BLOCK] = sums[0]
        stats[1:2, at : at + BLOCK] = sums[1]
    pixels = valid[0].astype(F32)
    for image in range(1, valid.shape[0]):
        pixels = pixels + valid[image].astype(F32)
    stats[2:3, :] = jnp.full((1, half), 1.0, F32) * (pixels * (side * side))


def spread_kernel(slots, depth, *refs):
    blocks, (wide, wide_turned, inner_vectors, outer_vectors, held, rows) = refs[:slots], refs[slots:]
    extra = held.shape[1]
    for slot in range(slots):
        held[block_owner(slot)] = blocks[slot][depth : depth + extra, :].astype(F32)
    shard, ours = rows.shape[0] // slots, slots // 2
    per, outer = inner_vectors.shape[1] // ours, outer_vectors.shape[1] // ours
    core = lax.axis_index("core")
    for owner in range(slots):
        rows[owner * shard : (owner + 1) * shard, :] = held[owner, 0:shard, :]
    for at in range(ours):
        owner = core * ours + at
        for row in range(4):
            inner_vectors[row : row + 1, at * per : (at + 1) * per] = held[
                owner, shard : shard + 1, row * per : (row + 1) * per
            ]
        for row in range(2):
            outer_vectors[row : row + 1, at * outer : (at + 1) * outer] = held[
                owner, shard + 1 : shard + 2, row * outer : (row + 1) * outer
            ]
    widen(rows, wide, wide_turned)


def widen_kernel(weight, wide, wide_turned, rows):
    rows[...] = weight[...].astype(F32)
    widen(rows, wide, wide_turned)


def widen(weight, wide, wide_turned):
    taps, blocks = wide.shape[:2]
    inner = weight.shape[0] // taps
    row = lax.broadcasted_iota(jnp.int32, (BLOCK, BLOCK), 0) // inner
    column = lax.broadcasted_iota(jnp.int32, (BLOCK, BLOCK), 1) // inner
    own = row == column
    for tap in range(taps):
        for block in range(blocks):
            piece = weight[tap * inner : (tap + 1) * inner, block * BLOCK : (block + 1) * BLOCK]
            tall = jnp.concatenate([piece] * (BLOCK // inner), axis=0)
            dense = jnp.where(own, tall, 0.0)
            wide[tap, block] = dense.astype(BF16)
            wide_turned[tap, block] = dense.T.astype(BF16)


def fill_pads(pads, columns, image, line, values):
    rows = pl.ds(pl.multiple_of((line + 1) * LINE, LINE), LINE)
    pads[0, image, rows, columns] = pltpu.roll(values, 1, 0).astype(BF16)
    pads[1, image, rows, columns] = values.astype(BF16)
    pads[2, image, rows, columns] = pltpu.roll(values, LINE - 1, 0).astype(BF16)


def clear_pads(pads):
    images, rows, columns = pads.shape[1:]
    zeros = jnp.zeros((3, images, LINE, columns), BF16)
    pads[:, :, 0:LINE, :] = zeros
    pads[:, :, rows - LINE : rows, :] = zeros


def convolve(pads, wide, image, block, rows, turned=False):
    columns = slice(block * BLOCK, (block + 1) * BLOCK)
    value = None
    for tap in range(TAPS):
        top, left = divmod(TAPS - 1 - tap if turned else tap, 3)
        piece = pads[left, image, top * LINE : top * LINE + rows, columns]
        term = dot(piece, wide[tap, block])
        value = term if value is None else value + term
    return value


def group_kernel(side, mask, total, vectors, red, wide, pads, grouped, stats):
    images, padded, width = pads.shape[1:]
    rows = side * LINE
    mean, inverse = moments(total, total[2:3, :])
    scale, bias = 0.5 * inverse * vectors[0:1, :], 0.5 * vectors[1:2, :]
    clear_pads(pads)
    for part in chunks(width):
        inside = line_mask(part.stop - part.start, side)

        def body(step):
            half = (red[line_at(step), part] - mean[:, part]) * scale[:, part] + bias[:, part]
            fill_pads(pads, part, step // side, step % side, jnp.where(inside, silu_half(half), 0.0))

        each_line(images * side, body)
    for block in range(width // BLOCK):
        columns = slice(block * BLOCK, (block + 1) * BLOCK)
        sums = [0.0, 0.0]
        for image in range(images):
            at = slice(image * rows, (image + 1) * rows)
            value = convolve(pads, wide, image, block, rows)
            grouped[at, columns] = value
            masked = value * across_lanes(mask[at, :], BLOCK)
            sums = [sums[0] + column_sums(masked), sums[1] + column_sums(masked * value)]
        stats[0:1, columns] = sums[0]
        stats[1:2, columns] = sums[1]


def act_kernel(side, total, first, vectors, grouped, act):
    rows, width = grouped.shape
    mean, inverse = moments(total, first[2:3, :])
    scale, bias = 0.5 * inverse * vectors[2:3, :], 0.5 * vectors[3:4, :]
    for part in chunks(width):
        inside = line_mask(part.stop - part.start, side)

        def body(step):
            at = line_at(step)
            half = (grouped[at, part] - mean[:, part]) * scale[:, part] + bias[:, part]
            act[at, part] = jnp.where(inside, silu_half(half), 0.0).astype(BF16)

        each_line(rows // LINE, body)


def assemble_kernel(*refs):
    blocks, out = refs[:-1], refs[-1]
    depth = blocks[0].shape[0]
    for slot, block in enumerate(blocks):
        out[rows_of(block_owner(slot), depth), :] = block[...]


def expand_kernel(mask, act_mine, act_far, weight, act, expanded, stats):
    rows, half = act_mine.shape
    middle = rows // 2
    act[:, part_at(0, half)] = act_mine[...]
    act[0:middle, part_at(1, half)] = act_far[middle:rows, :]
    act[middle:rows, part_at(1, half)] = act_far[0:middle, :]
    for at in range(0, weight.shape[1], BLOCK):
        sums = [0.0, 0.0]
        for begin in (0, middle):
            here = slice(begin, begin + middle)
            value = dot(act[here, :], weight[:, at : at + BLOCK])
            expanded[here, at : at + BLOCK] = value
            masked = value * across_lanes(mask[here, :], BLOCK)
            sums = [sums[0] + column_sums(masked), sums[1] + column_sums(masked * value)]
        stats[0:1, at : at + BLOCK] = sums[0]
        stats[1:2, at : at + BLOCK] = sums[1]


def output_kernel(
    side, valid, total, first, vectors, expanded, x, x_other, cotangent, cotangent_far, keep_out, send_out, grad, stats
):
    rows, channels = expanded.shape
    middle = rows // 2
    mean, inverse = moments(total, first[2:3, 0:1])
    scale, bias = inverse * vectors[0:1, :], vectors[1:2, :]
    for part in chunks(channels):
        length = part.stop - part.start
        whole = part_at(0, channels, part.start, length)
        ends = []
        for begin, pixels, incoming, columns, out in (
            (0, x, cotangent, whole, keep_out), (middle, x_other, cotangent_far, part, send_out)
        ):

            def body(step):
                at = line_at(step)
                here = pl.ds(pl.multiple_of(begin + step * LINE, LINE), LINE)
                keep = 0.5 * valid[(begin // LINE + step) // side].astype(F32)
                centered = expanded[here, part] - mean[:, part]
                half = (centered * scale[:, part] + (bias[:, part] + pixels[at, whole].astype(F32))) * keep
                slope, upper = dsilu_twice(half)
                out[at, part] = (half * upper).astype(BF16)
                value = incoming[at, columns].astype(F32) * keep * slope
                grad[here, part] = value
                return value, value * centered

            ends.append(each_line_summed(middle // LINE, length, body))
        stats[0:1, part] = ends[0][0] + ends[1][0]
        stats[1:2, part] = (ends[0][1] + ends[1][1]) * inverse[:, part]


def back_expand_kernel(mask, total, sums, first, vectors, grad, expanded, weight, flat, send):
    rows, channels = expanded.shape
    pixels = first[2:3, 0:1]
    mean, inverse = moments(total, pixels)
    scale = inverse * vectors[0:1, :]
    shifted, scaled = scale * sums[0:1, :] / pixels, scale * inverse * sums[1:2, :] / pixels
    for part in chunks(channels):

        def body(step):
            at = line_at(step)
            common = shifted[:, part] + (expanded[at, part] - mean[:, part]) * scaled[:, part]
            counted = across_lanes(mask[at, :], part.stop - part.start)
            flat[at, part] = (scale[:, part] * grad[at, part] - counted * common).astype(BF16)

        each_line(rows // LINE, body)
    back_part_kernel(1, flat, weight, send)


def back_part_kernel(part, flat, weight, out):
    half = out.shape[1]
    for at in range(0, half, BLOCK):
        rows = pl.ds(pl.multiple_of(part_at(part, half).start + at, BLOCK), BLOCK)
        out[:, at : at + BLOCK] = dot(flat[...], weight[rows, :], NT).astype(out.dtype)


def back_act_kernel(total, first, vectors, mine, far, grouped, dz, stats):
    mean, inverse = moments(total, first[2:3, :])
    lines = grouped.shape[0] // LINE

    def gradient(step, part):
        there = lax.rem(step + lines // 2, lines)
        return mine[line_at(step), part] + far[line_at(there), part].astype(F32)

    before_norm(dz, gradient, grouped, mean, inverse, vectors[2:3, :], vectors[3:4, :], stats)


def before_norm(dz, gradient, hidden, mean, inverse, gain, shift, stats, side=None):
    scale, bias = 0.5 * inverse * gain, 0.5 * shift
    rows, width = hidden.shape
    for part in chunks(width):
        inside = None if side is None else line_mask(part.stop - part.start, side)

        def body(step):
            at = line_at(step)
            centered = hidden[at, part] - mean[:, part]
            slope, _ = dsilu_twice(centered * scale[:, part] + bias[:, part])
            here = gradient(step, part) * slope
            if side is not None:
                here = jnp.where(inside, here, 0.0)
            dz[at, part] = here
            return here, here * centered

        one, two = each_line_summed(rows // LINE, part.stop - part.start, body)
        stats[0:1, part] = 0.5 * one
        stats[1:2, part] = 0.5 * inverse[:, part] * two


def weight_expand_kernel(act, flat, out):
    turned = act[...].T
    for at in range(0, out.shape[1], BLOCK):
        out[:, at : at + BLOCK] = dot(turned, flat[:, at : at + BLOCK]).astype(BF16)


def back_group_kernel(
    side, mask, total, sums, first, vectors, dz, grouped, red, wide, flat, dz_one, stats, pads
):
    images, padded, width = pads.shape[1:]
    rows = side * LINE
    pixels = first[2:3, :]
    mean, inverse = moments(total, pixels)
    scale = inverse * vectors[2:3, :]
    shifted, scaled = scale * sums[0:1, :] / pixels, scale * inverse * sums[1:2, :] / pixels
    scale = 0.5 * scale
    clear_pads(pads)
    for part in chunks(width):

        def body(step):
            at = line_at(step)
            common = shifted[:, part] + (grouped[at, part] - mean[:, part]) * scaled[:, part]
            value = scale[:, part] * dz[at, part] - across_lanes(mask[at, :], part.stop - part.start) * common
            flat[at, part] = value.astype(BF16)
            fill_pads(pads, part, step // side, step % side, value)

        each_line(images * side, body)
    for block in range(width // BLOCK):
        columns = slice(block * BLOCK, (block + 1) * BLOCK)
        for image in range(images):
            dz_one[image * rows : (image + 1) * rows, columns] = convolve(pads, wide, image, block, rows, True)
    mean_one, inverse_one = moments(first, pixels)

    def gradient(step, part):
        return dz_one[line_at(step), part]

    before_norm(dz_one, gradient, red, mean_one, inverse_one, vectors[0:1, :], vectors[1:2, :], stats, side)


def weight_group_kernel(side, inner, pads, flat, out, held):
    images, padded, width = pads.shape[1:]
    rows = side * LINE
    row = lax.broadcasted_iota(jnp.int32, (LANES, LANES), 0) // inner
    column = lax.broadcasted_iota(jnp.int32, (LANES, LANES), 1) // inner
    own = row == column
    for at in range(0, width, LANES):
        columns = slice(at, at + LANES)
        moved = []
        for tap in range(TAPS):
            top, left = divmod(tap, 3)
            pieces = [pads[left, image, top * LINE : top * LINE + rows, columns] for image in range(images)]
            moved.append(jnp.concatenate(pieces, axis=0))
        product = dot(flat[:, columns].T, jnp.concatenate(moved, axis=1))
        for tap in range(TAPS):
            kept = jnp.where(own, product[:, tap * LANES : (tap + 1) * LANES].T, 0.0)
            value = kept[0:inner]
            for begin in range(inner, LANES, inner):
                value = value + kept[begin : begin + inner]
            held[tap * inner : (tap + 1) * inner, columns] = value
    owners, extra = out.shape[:2]
    shard = TAPS * inner // owners
    zeros = jnp.zeros((extra - shard, width), F32)
    for owner in range(owners):
        rows_here = held[owner * shard : (owner + 1) * shard, :]
        out[owner] = jnp.concatenate([rows_here, zeros], axis=0).astype(BF16)


def back_reduce_kernel(small, places, mask, first, sums, vectors, dz, red, turned, group, flat, *outs):
    rows, width = red.shape
    pixels = first[2:3, :]
    mean, inverse = moments(first, pixels)
    scale = inverse * vectors[0:1, :]
    shifted, scaled = scale * sums[0:1, :] / pixels, scale * inverse * sums[1:2, :] / pixels
    scale = 0.5 * scale
    for part in chunks(width):

        def body(step):
            at = line_at(step)
            common = shifted[:, part] + (red[at, part] - mean[:, part]) * scaled[:, part]
            counted = across_lanes(mask[at, :], part.stop - part.start)
            flat[at, part] = (scale[:, part] * dz[at, part] - counted * common).astype(BF16)

        each_line(rows // LINE, body)
    block_sum_kernel(small, places, turned, group, flat, *outs)


def block_sum_kernel(small, places, turned, group, flat, *refs):
    arrived, outs = refs[: len(refs) - len(places)], refs[len(refs) - len(places) :]
    tall, half = outs[0].shape
    depth = tall - group.shape[1]
    for out, (block, chosen) in zip(outs, places):
        owner = block_owner(block) if small else block
        value = dot(turned[rows_of(owner, depth), :], flat[...])
        more = group[owner].astype(F32)
        for other in chosen:
            value = value + arrived[other][0:depth, :].astype(F32)
            more = more + arrived[other][depth:tall, :].astype(F32)
        out[0:depth, :] = value.astype(BF16)
        out[depth:tall, :] = more.astype(BF16)


def expand_sum_kernel(places, keep, *refs):
    arrived, outs = refs[: len(refs) - len(places)], refs[len(refs) - len(places) :]
    depth = outs[0].shape[0]
    for out, (block, chosen) in zip(outs, places):
        value = keep[rows_of(block_owner(block), depth), :]
        if chosen:
            value = value.astype(F32)
            for other in chosen:
                value = value + arrived[other][...].astype(F32)
        out[...] = value.astype(BF16)


def join_kernel(mine, mine_x, other, other_x, *outs):
    half = mine.shape[1]
    at = 0
    for out in outs:
        rows = out.shape[0]
        for part, terms in enumerate(((mine, mine_x), (other, other_x))):
            values = [term[at : at + -(-rows // 16) * 16, :].astype(F32) for term in terms]
            out[:, part_at(part, half)] = (values[0] + values[1])[0:rows]
        at += -(-rows // 16) * 16


def pin_kernel(values, out):
    pass


def own_kernel(sizes, near, far, *outs):
    position, core, ours = lax.axis_index("fsdp"), lax.axis_index("core"), lax.axis_size("fsdp") // 2
    side, place, at = position // ours, lax.rem(position, ours), 0
    for index, length in enumerate(sizes):
        columns = pl.ds(pl.multiple_of(at + place * length, 128), length)
        for row, out in ((1, outs[2 * index]), (0, outs[2 * index + 1])):
            out[...] = jnp.where(side == core, near[row : row + 1, columns], far[row : row + 1, columns])
        at += ours * length


def back_input_kernel(slots, depth, begin, flat, grad, *refs):
    weights, refs = refs[:slots], refs[slots:]
    half = grad.shape[1]
    out, held = refs[-2:]
    rows = slice(begin, begin + held.shape[0])
    for slot in range(slots):
        columns = pl.ds(pl.multiple_of(block_owner(slot) * depth, 128), depth) if slots > 1 else slice(None)
        held[:, columns] = dot(flat[rows, :], weights[slot][0:depth, :], NT)
    columns = part_at(0, half)
    held[:, columns] = held[:, columns] + grad[rows, :]
    if len(refs) == 2:
        out[...] = held[...].astype(BF16)
        return
    far = refs[0]
    side = out.shape[1]

    def body(step):
        at = line_at(step)
        out[step // side, step % side] = (held[at, :] + far[at, :].astype(F32)).astype(BF16)[0:side]

    each_line(held.shape[0] // LINE, body)


def far_half_kernel(values, out):
    out[...] = values[:, part_at(1, out.shape[1])]


def image_kernel(keep, far, out):
    half, side = keep.shape[1], out.shape[1]

    def body(step):
        at = line_at(step)
        for part, values in enumerate((keep, far)):
            out[step // side, step % side, :, part_at(part, half)] = values[at, :][0:side]

    each_line(keep.shape[0] // LINE, body)


def pinned(values):
    anywhere = pl.BlockSpec(memory_space=pl.ANY)
    values = values.transpose(1, 2, 0, 3)
    values = pl.pallas_call(
        pin_kernel, out_shape=shape(values.shape, values.dtype), in_specs=[anywhere], out_specs=anywhere,
        input_output_aliases={0: 0}, compiler_params=pltpu.CompilerParams(vmem_limit_bytes=1 << 20), name="pin",
    )(values)
    return values.transpose(2, 0, 1, 3)


def swap_core(values):
    return lax.ppermute(values, "core", SWAP)


def swap_x(values):
    if lax.axis_size("x") == 2:
        return lax.ppermute(values, "x", SWAP)
    return (lax.psum(values.astype(F32), "x") - values.astype(F32)).astype(values.dtype)


def sum_chips(values, flips):
    got = [lax.ppermute(values, CHIPS, [(at, at ^ flip) for at in range(16)]) for flip in flips]
    for other in got:
        values = values + other
    return values


def along(values, way):
    pairs = [(f * 2 + x, (f + 2 * way * (1 - 2 * x)) % 8 * 2 + x) for f in range(8) for x in range(2)]
    return lax.ppermute(values, CHIPS, pairs)


def across(values):
    return lax.ppermute(values, "fsdp", [(f, f ^ 1) for f in range(8)])


def halves(values, core):
    half = values.shape[1] // 2
    return lax.dynamic_slice_in_dim(values, core * half, half, 1)


def both(near, far, core):
    first, second = jnp.where(core == 0, near, far), jnp.where(core == 0, far, near)
    return jnp.concatenate([first, second], axis=-1)


def per_device(
    images,
    valid,
    cotangent,
    w_reduce,
    gain_one,
    shift_one,
    w_group,
    gain_two,
    shift_two,
    w_expand,
    gain_three,
    shift_three,
):
    count, side, _, channels = images.shape
    width = w_reduce.shape[1]
    inner = width // GROUPS
    size = lax.axis_size("fsdp")
    small = size == 8 and lax.axis_size("x") == 2
    position, core = lax.axis_index("fsdp"), lax.axis_index("core")
    rows = count * side * LINE
    per, outer, shard, depth = gain_one.shape[0], gain_three.shape[0], w_group.shape[0], w_reduce.shape[0]
    extra = -(-(shard + 2) // 16) * 16
    half, half_out = width // 2, channels // 2

    def plane_sum(values):
        return sum_chips(values, (1, 2, 3)) if small else lax.psum(values, CHIPS)

    def line_sum(values):
        return sum_chips(values, (4, 8, 12)) if small else values

    def everywhere(values):
        return line_sum(plane_sum(values))

    def padded(values):
        return jnp.pad(values, ((0, 0), (0, 0), (0, LINE - side), (0, 0))).reshape(rows, channels)

    vectors = jnp.zeros((2 * half,), BF16)
    for at, vector in (
        (0, gain_one), (per, shift_one), (2 * per, gain_two), (3 * per, shift_two),
        (half, gain_three), (half + outer, shift_three),
    ):
        vectors = vectors + jnp.pad(vector, (at, 2 * half - at - vector.size))
    (own,) = call(
        pack_kernel, [shape((depth + extra, half), BF16)], [w_reduce, w_group, vectors.reshape(2, half)],
        anywhere=True, vmem=60, name="pack",
        scratch=[pltpu.VMEM((shard, width), BF16), pltpu.VMEM((2, half), BF16), pltpu.SemaphoreType.DMA((3,))],
    )
    wide_shape = shape((TAPS, half // BLOCK, BLOCK, BLOCK), BF16)
    expand_own, x = halves(w_expand, core), padded(images)

    def turn(x, x_other, valid_other):
        valid_both = jnp.concatenate([valid, valid_other])
        turned, mask = call(
            functools.partial(turn_kernel, side),
            [shape((channels, 2 * rows), BF16), shape((2 * rows, LANES), F32)],
            [valid_both, x, x_other], scalars=1, name="turn",
        )
        return valid_both, turned, mask

    if small:
        first = along(own, 1)
        other = across(own)
        first, other, x, expand_own = together(first, other, x, expand_own)
        x_other, valid_other = swap_core(x), swap_core(valid)
        passed, second, first_other = swap_x(first), along(first, 1), across(first)
        second, passed, first_other, x_other, valid_other = together(second, passed, first_other, x_other, valid_other)
        passed_other, second_other, expand_first = swap_x(first_other), across(second), along(expand_own, 1)
        valid_both, turned, mask = turn(x, x_other, valid_other)
        weights = [own, first, passed, second, other, first_other, passed_other, second_other]
        *weights, expand_first, turned, mask = together(*weights, expand_first, turned, mask)
        second, other = along(expand_first, 1), across(expand_own)
        slots, slot_depth = size, depth
    else:
        x_other, valid_other = swap_core(x), swap_core(valid)
        valid_both, turned, mask = turn(x, x_other, valid_other)
        whole = lax.all_gather(own, "fsdp", axis=0, tiled=False)
        weights = [whole[:, :depth].reshape(channels, half)]
        slots, slot_depth = 1, channels

    pixels, across_cores = 2 * rows, 2 * count
    red, part = call(
        functools.partial(reduce_kernel, slots, slot_depth, side),
        [shape((pixels, half), F32), shape((3, half), F32)],
        [valid_both, mask, x, x_other, *weights], scalars=1, name="reduce", flops=2 * rows * width * channels,
    )
    if small:
        wide, wide_turned, inner_vectors, outer_vectors = call(
            functools.partial(spread_kernel, slots, depth),
            [wide_shape, wide_shape, shape((4, half), F32), shape((2, half_out), F32)],
            weights,
            scratch=[pltpu.VMEM((size, extra, half), F32), pltpu.VMEM((size * shard, half), F32)],
            name="spread", flops=1 << 28,
        )
        middle, wide, wide_turned, inner_vectors, outer_vectors = together(
            plane_sum(part), wide, wide_turned, inner_vectors, outer_vectors
        )
        middle, second, other, expand_first = together(middle, second, other, expand_first)
        first_other, passed = across(expand_first), swap_x(expand_first)
        first = line_sum(middle)
        first, first_other, second = together(first, first_other, second)
        second_other, passed_other = across(second), swap_x(first_other)
    else:
        packed = whole[:, depth:]
        wide, wide_turned = call(
            widen_kernel, [wide_shape, wide_shape], [packed[:, :shard].reshape(size * shard, half)],
            scratch=[pltpu.VMEM((size * shard, half), F32)], name="widen",
        )
        line = packed[:, shard, : 4 * per].astype(F32).reshape(size, 4, per).transpose(1, 0, 2).reshape(4, width)
        inner_vectors = halves(line, core)
        line = packed[:, shard + 1, : 2 * outer].astype(F32).reshape(size, 2, outer).transpose(1, 0, 2)
        outer_vectors = halves(line.reshape(2, channels), core)
        first = everywhere(part)
    pad_shape = (3, across_cores, (side + 2) * LINE, half)
    pads, grouped, part = call(
        functools.partial(group_kernel, side),
        [shape(pad_shape, BF16), shape((pixels, half), F32), shape((2, half), F32)],
        [mask, first, inner_vectors, red, wide],
        name="group", flops=2 * TAPS * rows * width * BLOCK,
    )
    if small:
        part, passed = together(part, passed)
        middle = line_sum(part)
        middle, passed_other, second_other = together(middle, passed_other, second_other)
        blocks = (expand_own, expand_first, passed, second, other, first_other, passed_other, second_other)
        total_two = plane_sum(middle)
    else:
        total_two = everywhere(part)
    (act_mine,) = call(
        functools.partial(act_kernel, side), [shape((pixels, half), BF16)], [total_two, first, inner_vectors, grouped],
        name="act",
    )
    act_far = swap_core(act_mine)
    if small:
        act_mine, *blocks = together(act_mine, *blocks)
        (weight_three,) = call(assemble_kernel, [shape((width, half_out), BF16)], blocks, name="assemble")
    else:
        weight_three = lax.all_gather(expand_own, "fsdp", axis=0, tiled=True)
    act_two, expanded, part = call(
        expand_kernel,
        [shape((pixels, width), BF16), shape((pixels, half_out), F32), shape((2, half_out), F32)],
        [mask, act_mine, act_far, weight_three],
        name="expand", flops=2 * rows * width * channels,
    )
    cot = padded(after(cotangent, grouped))
    cot_far = swap_core(call(far_half_kernel, [shape((rows, half_out), BF16)], [cot], name="far_half")[0])
    middle, cot, cot_far = together(plane_sum(part), cot, cot_far)
    total_three = line_sum(middle)
    keep_out, send_out, grad_summed, part = call(
        functools.partial(output_kernel, side),
        [shape((rows, half_out), BF16), shape((rows, half_out), BF16), shape((pixels, half_out), F32),
         shape((2, half_out), F32)],
        [valid_both, total_three, first, outer_vectors, expanded, x, x_other, cot, cot_far], scalars=1, name="output",
    )

    sums_three = everywhere(part)
    flat_three, send = call(
        back_expand_kernel,
        [shape((pixels, half_out), BF16), shape((pixels, half), BF16)],
        [mask, total_three, sums_three, first, outer_vectors, grad_summed, expanded, weight_three],
        name="back_expand", flops=rows * width * channels,
    )
    far = swap_core(send)
    (mine,) = call(
        functools.partial(back_part_kernel, 0), [shape((pixels, half), F32)], [flat_three, weight_three],
        name="back_part", flops=rows * width * channels,
    )
    dz_two, part = call(
        back_act_kernel,
        [shape((pixels, half), F32), shape((2, half), F32)],
        [total_two, first, inner_vectors, mine, far, grouped], name="back_act",
    )
    (expand_term,) = call(
        weight_expand_kernel, [shape((width, half_out), BF16)], [after(act_two, part), flat_three],
        name="weight_expand", flops=2 * rows * width * channels,
    )
    far_out = swap_core(after(send_out, part))
    middle = plane_sum(part)

    def expand_sums(places, arrived=()):
        return call(
            functools.partial(expand_sum_kernel, places),
            [shape((w_expand.shape[0], half_out), BF16)] * len(places),
            [expand_term] + list(arrived), name="expand_sum",
        )

    if small:
        middle, *moving = together(middle, *expand_sums(((6, ()), (7, ()))))
        moving = [swap_x(moving[0]), across(moving[1])]
        sums_two, *moving = together(line_sum(middle), *moving)
        sums_two, expand_first_other, expand_passed, expand_second, expand_other = together(
            sums_two, *expand_sums(((5, (0,)), (2, ()), (3, (1,)), (4, ())), moving)
        )
        expand_second, expand_other = along(expand_second, -1), across(expand_other)
    else:
        sums_two = line_sum(middle)
        own_expand = lax.psum_scatter(expand_term, "fsdp", scatter_dimension=0, tiled=True)
    flat_two, dz_one, part = call(
        functools.partial(back_group_kernel, side),
        [shape((pixels, half), BF16), shape((pixels, half), F32), shape((2, half), F32)],
        [mask, total_two, sums_two, first, inner_vectors, dz_two, grouped, red, wide_turned],
        scratch=[pltpu.VMEM(pad_shape, BF16)], name="back_group", flops=2 * TAPS * rows * width * BLOCK,
    )
    (group_term,) = call(
        functools.partial(weight_group_kernel, side, inner),
        [shape((size, extra, half), BF16)],
        [pads, after(flat_two, part)], scratch=[pltpu.VMEM((TAPS * inner, half), F32)], name="weight_group",
        flops=2 * TAPS * rows * width * BLOCK,
    )
    middle, group_term = together(plane_sum(part), group_term)
    if small:
        middle, expand_second, expand_first_other, expand_passed, expand_other = together(
            middle, expand_second, expand_first_other, expand_passed, expand_other
        )
        moving = [swap_x(expand_passed), across(expand_first_other)]
    sums_one = line_sum(middle)
    if small:
        sums_one, *moving = together(sums_one, *moving)
        (expand_first_own,) = expand_sums(((1, (0, 1, 2)),), moving + [expand_second])
    tall = depth + extra
    places = ((6, ()), (7, ())) if small else tuple((at, ()) for at in range(size))
    flat_one, *moving = call(
        functools.partial(back_reduce_kernel, small, places),
        [shape((pixels, half), BF16)] + [shape((tall, half), BF16)] * len(places),
        [mask, first, sums_one, inner_vectors, dz_one, red, turned, group_term],
        name="back_reduce", flops=2 * rows * depth * width * len(places),
    )

    def sums(places, arrived):
        return call(
            functools.partial(block_sum_kernel, small, places),
            [shape((tall, half), BF16)] * len(places),
            [turned, group_term, flat_one] + list(arrived),
            name="block_sum", flops=2 * rows * depth * width * len(places),
        )

    def back_input(begin, flat, *far):
        out = shape(images.shape, BF16) if far else shape((rows, channels), BF16)
        return call(
            functools.partial(back_input_kernel, slots, slot_depth, begin),
            [out], [flat, grad_summed, *weights, *far],
            scratch=[pltpu.VMEM((rows, channels), F32)], name="back_input", flops=rows * width * channels,
        )[0]

    def own_shards(totals):
        near = jnp.concatenate(totals, axis=1)
        far = swap_core(near)
        lengths = (per, per, outer)
        if small:
            outs = call(
                functools.partial(own_kernel, lengths), [shape((1, n), F32) for n in lengths for _ in range(2)], [near, far],
                name="own",
            )
            return [out.reshape(-1) for out in outs]
        cut, at = [], 0
        for total, length in zip(totals, lengths):
            whole = both(total, far[:, at : at + total.shape[1]], core)
            at += total.shape[1]
            cut += [lax.dynamic_slice_in_dim(whole[row], position * length, length, 0) for row in (1, 0)]
        return cut

    def image_of(far_out):
        return call(image_kernel, [shape(images.shape, BF16)], [keep_out, far_out], name="image")[0]

    def join(own, far, outs):
        return call(
            join_kernel, [shape(out.shape, F32) for out in outs], [own, far, swap_core(own), swap_core(far)], name="join"
        )

    if small:
        flat_here = after(flat_one, *moving)
        moving[1], expand_first_own = together(moving[1], expand_first_own)
        moving = [swap_x(moving[0]), across(moving[1])]
        expand_first_own = along(expand_first_own, -1)
        far_input = swap_core(back_input(rows, flat_here))
        moving[0], far_input, expand_first_own = together(moving[0], far_input, expand_first_own)
        (own_expand,) = expand_sums(((0, (0, 1)),), [expand_first_own, expand_other])
        first_other, passed, second = sums(((5, (0,)), (2, ()), (3, (1,))), moving)
        moving = [swap_x(passed), along(second, -1), across(first_other)]
        far_out, second = together(far_out, second)
        grad_input, output = back_input(0, after(flat_one, second), far_input), pinned(image_of(far_out))
        moving[0], grad_input, output = together(moving[0], grad_input, output)
        first_own, other = sums(((1, (0, 1, 2)), (4, ())), moving)
        moving = [along(first_own, -1), across(other)]
        shards = own_shards([after(sums_one, first_own), sums_two, sums_three])
        grad_input, own_expand = pinned(after(grad_input, first_own)), after(own_expand, first_own)
        far_expand = swap_x(own_expand)
        moving[0], grad_input, far_expand, *shards = together(moving[0], grad_input, far_expand, *shards)
        (own_reduce,) = sums(((0, (0, 1)),), moving)
        own_expand, far_expand = after(own_expand, own_reduce), after(far_expand, own_reduce)
        (grad_w_expand,) = join(own_expand, far_expand, [w_expand])
        far_reduce, grad_w_expand = together(swap_x(own_reduce), grad_w_expand)
    else:
        grad_input, output = back_input(0, flat_one, swap_core(back_input(rows, flat_one))), image_of(far_out)
        shards = own_shards([sums_one, sums_two, sums_three])
        whole = jnp.stack(moving).reshape(size * tall, half)
        own_reduce = lax.psum_scatter(whole, "fsdp", scatter_dimension=0, tiled=True)
        (grad_w_expand,) = join(own_expand, swap_x(own_expand), [w_expand])
        far_reduce = swap_x(own_reduce)
    grad_w_reduce, grad_w_group = join(own_reduce, far_reduce, [w_reduce, w_group])
    return (output, grad_input, grad_w_reduce, grad_w_group, grad_w_expand) + tuple(shards)


def solution(mesh):
    fsdp, dp = mesh.shape["fsdp"], mesh.shape["dp"]
    split = Mesh(mesh.devices.reshape(fsdp, dp // 2, 2), ("fsdp", "x", "core"))
    images, rows, vector = P(("fsdp", "x", "core"), None, None, None), P("fsdp", None), P("fsdp")
    return jax.shard_map(
        per_device,
        mesh=split,
        in_specs=(
            images, P(("fsdp", "x", "core")), images,
            rows, vector, vector, rows, vector, vector, rows, vector, vector,
        ),
        out_specs=(images, images, rows, rows, rows) + (vector,) * 6,
        check_vma=False,
    )
```

```python
import functools

import jax
import jax.numpy as jnp
from jax import lax
from jax.experimental import pallas as pl
from jax.experimental.pallas import tpu as pltpu
from jax.sharding import Mesh
from jax.sharding import PartitionSpec as P

GROUPS = 32
TAPS = 9
LINE = 16
CHUNK = 512
UNROLL = 7
LANES = 128
BLOCK = 256
epsilon = 1e-05
BF16, F32 = jnp.bfloat16, jnp.float32
SWAP = [(0, 1), (1, 0)]
NN, NT = ((1,), (0,)), ((1,), (1,))
CHIPS = ("fsdp", "x")


def silu_half(half):
    return half + half * jnp.tanh(half)


def dsilu_twice(half):
    turned = jnp.tanh(half)
    upper = 1.0 + turned
    return upper * (1.0 + half * (1.0 - turned)), upper


def dot(a, b, contract=NN):
    return lax.dot_general(a, b, (contract, ((), ())), preferred_element_type=F32)


def after(values, *others):
    return lax.optimization_barrier((values,) + others)[0]


def together(*values):
    return lax.optimization_barrier(values)


def shape(dims, dtype):
    return jax.ShapeDtypeStruct(dims, dtype)


def call(kernel, outs, args, scalars=0, scratch=(), vmem=8, name=None, flops=0, anywhere=False, aliases=()):
    vm = pl.BlockSpec(memory_space=pltpu.VMEM)
    given = pl.BlockSpec(memory_space=pl.ANY) if anywhere else vm
    sm = pl.BlockSpec(memory_space=pltpu.SMEM)
    return pl.pallas_call(
        kernel,
        out_shape=outs,
        in_specs=[sm] * scalars + [given] * (len(args) - scalars),
        out_specs=[vm] * len(outs),
        scratch_shapes=list(scratch),
        compiler_params=pltpu.CompilerParams(vmem_limit_bytes=vmem << 20),
        cost_estimate=pl.CostEstimate(flops=0, bytes_accessed=0, transcendentals=0),
        input_output_aliases=dict(aliases),
        name=name,
    )(*args)


def moments(total, pixels):
    mean = total[0:1, :] / pixels
    inverse = lax.rsqrt(total[1:2, :] / pixels - mean * mean + epsilon)
    return mean, inverse


def chunks(columns):
    return [slice(at, min(at + CHUNK, columns)) for at in range(0, columns, CHUNK)]


def line_mask(columns, side):
    return lax.broadcasted_iota(jnp.int32, (LINE, columns), 0) < side


def each_line(lines, body):
    lax.fori_loop(0, lines, lambda step, none: body(step) or none, 0, unroll=UNROLL)


def each_line_summed(lines, width, body):
    zero = jnp.zeros((8, width), F32)

    def step_sums(step, carry):
        one, two = body(step)
        return carry[0] + fold(one), carry[1] + fold(two)

    one, two = lax.fori_loop(0, lines, step_sums, (zero, zero), unroll=UNROLL)
    return column_sums(one), column_sums(two)


def across_lanes(mask, columns):
    return jnp.concatenate([mask] * (columns // LANES), axis=1)


def column_sums(values):
    return jnp.sum(values, axis=0, keepdims=True)


def line_at(step):
    return pl.ds(pl.multiple_of(step * LINE, LINE), LINE)


def fold(values):
    return values[0:8] + values[8:16]


def part_at(part, half, at=0, length=None):
    core = lax.axis_index("core")
    side = core if part == 0 else 1 - core
    length = half if length is None else length
    return pl.ds(pl.multiple_of(side * half + at, 128), length)


def block_owner(slot):
    position = lax.axis_index("fsdp")
    way = 1 - 2 * lax.axis_index("x")
    step = (0, -way, way, 2)[slot % 4]
    owner = lax.rem(position + 2 * step + 8, 8)
    return owner if slot < 4 else owner + 1 - 2 * lax.rem(owner, 2)


def rows_of(owner, depth):
    return pl.ds(pl.multiple_of(owner * depth, 16), depth)


def pack_kernel(weight, group, *refs):
    vectors, (out, held, *rows, sems) = refs[:6], refs[6:]
    depth, half = weight.shape[0], out.shape[1]
    shard, extra = group.shape[0], out.shape[0] - weight.shape[0]
    columns = part_at(0, half)
    copies = [pltpu.make_async_copy(group, held, sems.at[0])]
    copies += [pltpu.make_async_copy(vector, row, sems.at[2 + at]) for at, (vector, row) in enumerate(zip(vectors, rows))]
    copies.append(pltpu.make_async_copy(weight.at[:, columns], out.at[pl.ds(0, depth)], sems.at[1]))
    for copy in copies:
        copy.start()
    for copy in copies[:-1]:
        copy.wait()
    below = [held[:, columns].astype(F32)]
    for begin, end in ((0, 4), (4, 6)):
        line = [row[...].astype(F32).reshape(1, row.shape[0]) for row in rows[begin:end]]
        missing = half - sum(piece.shape[1] for piece in line)
        below.append(jnp.concatenate(line + ([jnp.zeros((1, missing), F32)] if missing else []), axis=1))
    if extra > shard + 2:
        below.append(jnp.zeros((extra - shard - 2, half), F32))
    out[depth : depth + extra, :] = jnp.concatenate(below, axis=0).astype(BF16)
    copies[-1].wait()


def turn_kernel(side, valid, x, x_other, turned, mask):
    rows = x.shape[0]
    turned[:, 0:rows] = x[...].T
    turned[:, rows : 2 * rows] = x_other[...].T
    images = valid.shape[0]
    rows = 2 * rows // images
    inside = lax.broadcasted_iota(jnp.int32, (rows, LANES), 0) % LINE < side
    for image in range(images):
        mask[image * rows : (image + 1) * rows, :] = jnp.where(inside, valid[image].astype(F32), 0.0)


def reduce_kernel(slots, depth, side, valid, mask, x, x_other, *refs):
    weights, (red, stats) = refs[:slots], refs[slots:]
    half, rows = red.shape[1], x.shape[0]
    for at in range(0, half, BLOCK):
        sums = [0.0, 0.0]
        for begin, pixels in ((0, x), (rows, x_other)):
            total = None
            for slot in range(slots):
                if slots == 1:
                    piece = pixels[...]
                else:
                    piece = pixels[:, pl.ds(pl.multiple_of(block_owner(slot) * depth, 128), depth)]
                term = dot(piece, weights[slot][0:depth, at : at + BLOCK])
                total = term if total is None else total + term
            red[begin : begin + rows, at : at + BLOCK] = total
            masked = total * across_lanes(mask[begin : begin + rows, :], BLOCK)
            sums = [sums[0] + column_sums(masked), sums[1] + column_sums(masked * total)]
        stats[0:1, at : at + BLOCK] = sums[0]
        stats[1:2, at : at + BLOCK] = sums[1]
    pixels = valid[0].astype(F32)
    for image in range(1, valid.shape[0]):
        pixels = pixels + valid[image].astype(F32)
    stats[2:3, :] = jnp.full((1, half), 1.0, F32) * (pixels * (side * side))


def spread_kernel(slots, depth, *refs):
    blocks, (wide, wide_turned, inner_vectors, outer_vectors, held, rows) = refs[:slots], refs[slots:]
    extra = held.shape[1]
    for slot in range(slots):
        held[block_owner(slot)] = blocks[slot][depth : depth + extra, :].astype(F32)
    shard, ours = rows.shape[0] // slots, slots // 2
    per, outer = inner_vectors.shape[1] // ours, outer_vectors.shape[1] // ours
    core = lax.axis_index("core")
    for owner in range(slots):
        rows[owner * shard : (owner + 1) * shard, :] = held[owner, 0:shard, :]
    for at in range(ours):
        owner = core * ours + at
        for row in range(4):
            inner_vectors[row : row + 1, at * per : (at + 1) * per] = held[
                owner, shard : shard + 1, row * per : (row + 1) * per
            ]
        for row in range(2):
            outer_vectors[row : row + 1, at * outer : (at + 1) * outer] = held[
                owner, shard + 1 : shard + 2, row * outer : (row + 1) * outer
            ]
    widen(rows, wide, wide_turned)


def widen_kernel(weight, wide, wide_turned, rows):
    rows[...] = weight[...].astype(F32)
    widen(rows, wide, wide_turned)


def widen(weight, wide, wide_turned):
    taps, blocks = wide.shape[:2]
    inner = weight.shape[0] // taps
    row = lax.broadcasted_iota(jnp.int32, (BLOCK, BLOCK), 0) // inner
    column = lax.broadcasted_iota(jnp.int32, (BLOCK, BLOCK), 1) // inner
    own = row == column
    for tap in range(taps):
        for block in range(blocks):
            piece = weight[tap * inner : (tap + 1) * inner, block * BLOCK : (block + 1) * BLOCK]
            tall = jnp.concatenate([piece] * (BLOCK // inner), axis=0)
            dense = jnp.where(own, tall, 0.0)
            wide[tap, block] = dense.astype(BF16)
            wide_turned[tap, block] = dense.T.astype(BF16)


def fill_pads(pads, columns, image, line, values):
    rows = pl.ds(pl.multiple_of((line + 1) * LINE, LINE), LINE)
    pads[0, image, rows, columns] = pltpu.roll(values, 1, 0).astype(BF16)
    pads[1, image, rows, columns] = values.astype(BF16)
    pads[2, image, rows, columns] = pltpu.roll(values, LINE - 1, 0).astype(BF16)


def clear_pads(pads):
    images, rows, columns = pads.shape[1:]
    zeros = jnp.zeros((3, images, LINE, columns), BF16)
    pads[:, :, 0:LINE, :] = zeros
    pads[:, :, rows - LINE : rows, :] = zeros


def convolve(pads, wide, image, block, rows, turned=False):
    columns = slice(block * BLOCK, (block + 1) * BLOCK)
    value = None
    for tap in range(TAPS):
        top, left = divmod(TAPS - 1 - tap if turned else tap, 3)
        piece = pads[left, image, top * LINE : top * LINE + rows, columns]
        term = dot(piece, wide[tap, block])
        value = term if value is None else value + term
    return value


def group_kernel(side, mask, total, vectors, red, wide, pads, grouped, stats):
    images, padded, width = pads.shape[1:]
    rows = side * LINE
    mean, inverse = moments(total, total[2:3, :])
    scale, bias = 0.5 * inverse * vectors[0:1, :], 0.5 * vectors[1:2, :]
    clear_pads(pads)
    for part in chunks(width):
        inside = line_mask(part.stop - part.start, side)

        def body(step):
            half = (red[line_at(step), part] - mean[:, part]) * scale[:, part] + bias[:, part]
            fill_pads(pads, part, step // side, step % side, jnp.where(inside, silu_half(half), 0.0))

        each_line(images * side, body)
    for block in range(width // BLOCK):
        columns = slice(block * BLOCK, (block + 1) * BLOCK)
        sums = [0.0, 0.0]
        for image in range(images):
            at = slice(image * rows, (image + 1) * rows)
            value = convolve(pads, wide, image, block, rows)
            grouped[at, columns] = value
            masked = value * across_lanes(mask[at, :], BLOCK)
            sums = [sums[0] + column_sums(masked), sums[1] + column_sums(masked * value)]
        stats[0:1, columns] = sums[0]
        stats[1:2, columns] = sums[1]


def act_kernel(side, total, first, vectors, grouped, act):
    rows, width = grouped.shape
    mean, inverse = moments(total, first[2:3, :])
    scale, bias = 0.5 * inverse * vectors[2:3, :], 0.5 * vectors[3:4, :]
    for part in chunks(width):
        inside = line_mask(part.stop - part.start, side)

        def body(step):
            at = line_at(step)
            half = (grouped[at, part] - mean[:, part]) * scale[:, part] + bias[:, part]
            act[at, part] = jnp.where(inside, silu_half(half), 0.0).astype(BF16)

        each_line(rows // LINE, body)


def assemble_kernel(*refs):
    blocks, out = refs[:-1], refs[-1]
    depth = blocks[0].shape[0]
    for slot, block in enumerate(blocks):
        out[rows_of(block_owner(slot), depth), :] = block[...]


def expand_kernel(mask, act_mine, act_far, weight, act, expanded, stats):
    rows, half = act_mine.shape
    middle = rows // 2
    act[:, part_at(0, half)] = act_mine[...]
    act[0:middle, part_at(1, half)] = act_far[middle:rows, :]
    act[middle:rows, part_at(1, half)] = act_far[0:middle, :]
    for at in range(0, weight.shape[1], BLOCK):
        sums = [0.0, 0.0]
        for begin in (0, middle):
            here = slice(begin, begin + middle)
            value = dot(act[here, :], weight[:, at : at + BLOCK])
            expanded[here, at : at + BLOCK] = value
            masked = value * across_lanes(mask[here, :], BLOCK)
            sums = [sums[0] + column_sums(masked), sums[1] + column_sums(masked * value)]
        stats[0:1, at : at + BLOCK] = sums[0]
        stats[1:2, at : at + BLOCK] = sums[1]


def output_kernel(
    side, valid, total, first, vectors, expanded, x, x_other, cotangent, cotangent_far, keep_out, send_out, grad, stats
):
    rows, channels = expanded.shape
    middle = rows // 2
    mean, inverse = moments(total, first[2:3, 0:1])
    scale, bias = inverse * vectors[0:1, :], vectors[1:2, :]
    for part in chunks(channels):
        length = part.stop - part.start
        whole = part_at(0, channels, part.start, length)
        ends = []
        for begin, pixels, incoming, columns, out in (
            (0, x, cotangent, whole, keep_out), (middle, x_other, cotangent_far, part, send_out)
        ):

            def body(step):
                at = line_at(step)
                here = pl.ds(pl.multiple_of(begin + step * LINE, LINE), LINE)
                keep = 0.5 * valid[(begin // LINE + step) // side].astype(F32)
                centered = expanded[here, part] - mean[:, part]
                half = (centered * scale[:, part] + (bias[:, part] + pixels[at, whole].astype(F32))) * keep
                slope, upper = dsilu_twice(half)
                out[at, part] = (half * upper).astype(BF16)
                value = incoming[at, columns].astype(F32) * keep * slope
                grad[here, part] = value
                return value, value * centered

            ends.append(each_line_summed(middle // LINE, length, body))
        stats[0:1, part] = ends[0][0] + ends[1][0]
        stats[1:2, part] = (ends[0][1] + ends[1][1]) * inverse[:, part]


def back_expand_kernel(mask, total, sums, first, vectors, grad, expanded, weight, flat, send):
    rows, channels = expanded.shape
    pixels = first[2:3, 0:1]
    mean, inverse = moments(total, pixels)
    scale = inverse * vectors[0:1, :]
    shifted, scaled = scale * sums[0:1, :] / pixels, scale * inverse * sums[1:2, :] / pixels
    for part in chunks(channels):

        def body(step):
            at = line_at(step)
            common = shifted[:, part] + (expanded[at, part] - mean[:, part]) * scaled[:, part]
            counted = across_lanes(mask[at, :], part.stop - part.start)
            flat[at, part] = (scale[:, part] * grad[at, part] - counted * common).astype(BF16)

        each_line(rows // LINE, body)
    back_part_kernel(1, flat, weight, send)


def back_part_kernel(part, flat, weight, out):
    half = out.shape[1]
    for at in range(0, half, BLOCK):
        rows = pl.ds(pl.multiple_of(part_at(part, half).start + at, BLOCK), BLOCK)
        out[:, at : at + BLOCK] = dot(flat[...], weight[rows, :], NT).astype(out.dtype)


def back_act_kernel(total, first, vectors, mine, far, grouped, dz, stats):
    mean, inverse = moments(total, first[2:3, :])
    lines = grouped.shape[0] // LINE

    def gradient(step, part):
        there = lax.rem(step + lines // 2, lines)
        return mine[line_at(step), part] + far[line_at(there), part].astype(F32)

    before_norm(dz, gradient, grouped, mean, inverse, vectors[2:3, :], vectors[3:4, :], stats)


def before_norm(dz, gradient, hidden, mean, inverse, gain, shift, stats, side=None):
    scale, bias = 0.5 * inverse * gain, 0.5 * shift
    rows, width = hidden.shape
    for part in chunks(width):
        inside = None if side is None else line_mask(part.stop - part.start, side)

        def body(step):
            at = line_at(step)
            centered = hidden[at, part] - mean[:, part]
            slope, _ = dsilu_twice(centered * scale[:, part] + bias[:, part])
            here = gradient(step, part) * slope
            if side is not None:
                here = jnp.where(inside, here, 0.0)
            dz[at, part] = here
            return here, here * centered

        one, two = each_line_summed(rows // LINE, part.stop - part.start, body)
        stats[0:1, part] = 0.5 * one
        stats[1:2, part] = 0.5 * inverse[:, part] * two


def weight_expand_kernel(act, flat, out):
    turned = act[...].T
    for at in range(0, out.shape[1], BLOCK):
        out[:, at : at + BLOCK] = dot(turned, flat[:, at : at + BLOCK]).astype(BF16)


def back_group_kernel(
    side, mask, total, sums, first, vectors, dz, grouped, red, wide, flat, dz_one, stats, pads
):
    images, padded, width = pads.shape[1:]
    rows = side * LINE
    pixels = first[2:3, :]
    mean, inverse = moments(total, pixels)
    scale = inverse * vectors[2:3, :]
    shifted, scaled = scale * sums[0:1, :] / pixels, scale * inverse * sums[1:2, :] / pixels
    scale = 0.5 * scale
    clear_pads(pads)
    for part in chunks(width):

        def body(step):
            at = line_at(step)
            common = shifted[:, part] + (grouped[at, part] - mean[:, part]) * scaled[:, part]
            value = scale[:, part] * dz[at, part] - across_lanes(mask[at, :], part.stop - part.start) * common
            flat[at, part] = value.astype(BF16)
            fill_pads(pads, part, step // side, step % side, value)

        each_line(images * side, body)
    for block in range(width // BLOCK):
        columns = slice(block * BLOCK, (block + 1) * BLOCK)
        for image in range(images):
            dz_one[image * rows : (image + 1) * rows, columns] = convolve(pads, wide, image, block, rows, True)
    mean_one, inverse_one = moments(first, pixels)

    def gradient(step, part):
        return dz_one[line_at(step), part]

    before_norm(dz_one, gradient, red, mean_one, inverse_one, vectors[0:1, :], vectors[1:2, :], stats, side)


def weight_group_kernel(side, inner, pads, flat, out, held):
    images, padded, width = pads.shape[1:]
    rows = side * LINE
    row = lax.broadcasted_iota(jnp.int32, (LANES, LANES), 0) // inner
    column = lax.broadcasted_iota(jnp.int32, (LANES, LANES), 1) // inner
    own = row == column
    for at in range(0, width, LANES):
        columns = slice(at, at + LANES)
        moved = []
        for tap in range(TAPS):
            top, left = divmod(tap, 3)
            pieces = [pads[left, image, top * LINE : top * LINE + rows, columns] for image in range(images)]
            moved.append(jnp.concatenate(pieces, axis=0))
        product = dot(flat[:, columns].T, jnp.concatenate(moved, axis=1))
        for tap in range(TAPS):
            kept = jnp.where(own, product[:, tap * LANES : (tap + 1) * LANES].T, 0.0)
            value = kept[0:inner]
            for begin in range(inner, LANES, inner):
                value = value + kept[begin : begin + inner]
            held[tap * inner : (tap + 1) * inner, columns] = value
    owners, extra = out.shape[:2]
    shard = TAPS * inner // owners
    zeros = jnp.zeros((extra - shard, width), F32)
    for owner in range(owners):
        rows_here = held[owner * shard : (owner + 1) * shard, :]
        out[owner] = jnp.concatenate([rows_here, zeros], axis=0).astype(BF16)


def back_reduce_kernel(small, places, mask, first, sums, vectors, dz, red, turned, group, flat, *outs):
    rows, width = red.shape
    pixels = first[2:3, :]
    mean, inverse = moments(first, pixels)
    scale = inverse * vectors[0:1, :]
    shifted, scaled = scale * sums[0:1, :] / pixels, scale * inverse * sums[1:2, :] / pixels
    scale = 0.5 * scale
    for part in chunks(width):

        def body(step):
            at = line_at(step)
            common = shifted[:, part] + (red[at, part] - mean[:, part]) * scaled[:, part]
            counted = across_lanes(mask[at, :], part.stop - part.start)
            flat[at, part] = (scale[:, part] * dz[at, part] - counted * common).astype(BF16)

        each_line(rows // LINE, body)
    block_sum_kernel(small, places, turned, group, flat, *outs)


def block_sum_kernel(small, places, turned, group, flat, *refs):
    arrived, outs = refs[: len(refs) - len(places)], refs[len(refs) - len(places) :]
    tall, half = outs[0].shape
    depth = tall - group.shape[1]
    for out, (block, chosen) in zip(outs, places):
        owner = block_owner(block) if small else block
        value = dot(turned[rows_of(owner, depth), :], flat[...])
        more = group[owner].astype(F32)
        for other in chosen:
            value = value + arrived[other][0:depth, :].astype(F32)
            more = more + arrived[other][depth:tall, :].astype(F32)
        out[0:depth, :] = value.astype(BF16)
        out[depth:tall, :] = more.astype(BF16)


def expand_sum_kernel(places, keep, *refs):
    arrived, outs = refs[: len(refs) - len(places)], refs[len(refs) - len(places) :]
    depth = outs[0].shape[0]
    for out, (block, chosen) in zip(outs, places):
        value = keep[rows_of(block_owner(block), depth), :]
        if chosen:
            value = value.astype(F32)
            for other in chosen:
                value = value + arrived[other][...].astype(F32)
        out[...] = value.astype(BF16)


def join_kernel(mine, mine_x, other, other_x, *outs):
    half = mine.shape[1]
    at = 0
    for out in outs:
        rows = out.shape[0]
        for part, terms in enumerate(((mine, mine_x), (other, other_x))):
            values = [term[at : at + -(-rows // 16) * 16, :].astype(F32) for term in terms]
            out[:, part_at(part, half)] = (values[0] + values[1])[0:rows]
        at += -(-rows // 16) * 16


def pin_kernel(values, out):
    pass


def own_kernel(sizes, near, far, *outs):
    position, core, ours = lax.axis_index("fsdp"), lax.axis_index("core"), lax.axis_size("fsdp") // 2
    side, place, at = position // ours, lax.rem(position, ours), 0
    for index, length in enumerate(sizes):
        columns = pl.ds(pl.multiple_of(at + place * length, 128), length)
        for row, out in ((1, outs[2 * index]), (0, outs[2 * index + 1])):
            out[...] = jnp.where(side == core, near[row : row + 1, columns], far[row : row + 1, columns])
        at += ours * length


def back_input_kernel(slots, depth, begin, flat, grad, *refs):
    weights, refs = refs[:slots], refs[slots:]
    half = grad.shape[1]
    out, held = refs[-2:]
    rows = slice(begin, begin + held.shape[0])
    for slot in range(slots):
        columns = pl.ds(pl.multiple_of(block_owner(slot) * depth, 128), depth) if slots > 1 else slice(None)
        held[:, columns] = dot(flat[rows, :], weights[slot][0:depth, :], NT)
    columns = part_at(0, half)
    held[:, columns] = held[:, columns] + grad[rows, :]
    if len(refs) == 2:
        out[...] = held[...].astype(BF16)
        return
    far = refs[0]
    side = out.shape[1]

    def body(step):
        at = line_at(step)
        out[step // side, step % side] = (held[at, :] + far[at, :].astype(F32)).astype(BF16)[0:side]

    each_line(held.shape[0] // LINE, body)


def far_half_kernel(values, out):
    out[...] = values[:, part_at(1, out.shape[1])]


def image_kernel(keep, far, out):
    half, side = keep.shape[1], out.shape[1]

    def body(step):
        at = line_at(step)
        for part, values in enumerate((keep, far)):
            out[step // side, step % side, :, part_at(part, half)] = values[at, :][0:side]

    each_line(keep.shape[0] // LINE, body)


def pinned(values):
    anywhere = pl.BlockSpec(memory_space=pl.ANY)
    values = values.transpose(1, 2, 0, 3)
    values = pl.pallas_call(
        pin_kernel, out_shape=shape(values.shape, values.dtype), in_specs=[anywhere], out_specs=anywhere,
        input_output_aliases={0: 0}, compiler_params=pltpu.CompilerParams(vmem_limit_bytes=1 << 20), name="pin",
    )(values)
    return values.transpose(2, 0, 1, 3)


def swap_core(values):
    return lax.ppermute(values, "core", SWAP)


def swap_x(values):
    if lax.axis_size("x") == 2:
        return lax.ppermute(values, "x", SWAP)
    return (lax.psum(values.astype(F32), "x") - values.astype(F32)).astype(values.dtype)


def sum_chips(values, flips):
    got = [lax.ppermute(values, CHIPS, [(at, at ^ flip) for at in range(16)]) for flip in flips]
    got = together(*got)
    for other in got:
        values = values + other
    return values


def along(values, way):
    pairs = [(f * 2 + x, (f + 2 * way * (1 - 2 * x)) % 8 * 2 + x) for f in range(8) for x in range(2)]
    return lax.ppermute(values, CHIPS, pairs)


def across(values):
    return lax.ppermute(values, "fsdp", [(f, f ^ 1) for f in range(8)])


def halves(values, core):
    half = values.shape[1] // 2
    return lax.dynamic_slice_in_dim(values, core * half, half, 1)


def both(near, far, core):
    first, second = jnp.where(core == 0, near, far), jnp.where(core == 0, far, near)
    return jnp.concatenate([first, second], axis=-1)


def per_device(
    images,
    valid,
    cotangent,
    w_reduce,
    gain_one,
    shift_one,
    w_group,
    gain_two,
    shift_two,
    w_expand,
    gain_three,
    shift_three,
):
    count, side, _, channels = images.shape
    width = w_reduce.shape[1]
    inner = width // GROUPS
    size = lax.axis_size("fsdp")
    small = size == 8 and lax.axis_size("x") == 2
    position, core = lax.axis_index("fsdp"), lax.axis_index("core")
    rows = count * side * LINE
    per, outer, shard, depth = gain_one.shape[0], gain_three.shape[0], w_group.shape[0], w_reduce.shape[0]
    extra = -(-(shard + 2) // 16) * 16
    half, half_out = width // 2, channels // 2

    def plane_sum(values):
        return sum_chips(values, (1, 2, 3)) if small else lax.psum(values, CHIPS)

    def line_sum(values):
        return sum_chips(values, (4, 8, 12)) if small else values

    def everywhere(values):
        return line_sum(plane_sum(values))

    def padded(values):
        return jnp.pad(values, ((0, 0), (0, 0), (0, LINE - side), (0, 0))).reshape(rows, channels)

    vectors = (gain_one, shift_one, gain_two, shift_two, gain_three, shift_three)
    (own,) = call(
        pack_kernel, [shape((depth + extra, half), BF16)], [w_reduce, w_group, *vectors],
        anywhere=True, vmem=60, name="pack",
        scratch=[pltpu.VMEM((shard, width), BF16)] + [pltpu.VMEM(vector.shape, BF16) for vector in vectors]
        + [pltpu.SemaphoreType.DMA((8,))],
    )
    wide_shape = shape((TAPS, half // BLOCK, BLOCK, BLOCK), BF16)
    expand_own, x = halves(w_expand, core), padded(images)

    def turn(x, x_other, valid_other):
        valid_both = jnp.concatenate([valid, valid_other])
        turned, mask = call(
            functools.partial(turn_kernel, side),
            [shape((channels, 2 * rows), BF16), shape((2 * rows, LANES), F32)],
            [valid_both, x, x_other], scalars=1, name="turn",
        )
        return valid_both, turned, mask

    if small:
        first = along(own, 1)
        other = across(own)
        x_other, valid_other = padded(swap_core(images)), swap_core(valid)
        first, other, x, x_other, expand_own = together(first, other, x, x_other, expand_own)
        passed, second, first_other = swap_x(first), along(first, 1), across(first)
        second, passed, first_other, valid_other = together(second, passed, first_other, valid_other)
        passed_other, second_other, expand_first = swap_x(first_other), across(second), along(expand_own, 1)
        valid_both, turned, mask = turn(x, x_other, valid_other)
        weights = [own, first, passed, second, other, first_other, passed_other, second_other]
        *weights, turned, mask = together(*weights, turned, mask)
        second, other = along(expand_first, 1), across(expand_own)
        slots, slot_depth = size, depth
    else:
        x_other, valid_other = swap_core(x), swap_core(valid)
        valid_both, turned, mask = turn(x, x_other, valid_other)
        whole = lax.all_gather(own, "fsdp", axis=0, tiled=False)
        weights = [whole[:, :depth].reshape(channels, half)]
        slots, slot_depth = 1, channels

    pixels, across_cores = 2 * rows, 2 * count
    red, part = call(
        functools.partial(reduce_kernel, slots, slot_depth, side),
        [shape((pixels, half), F32), shape((3, half), F32)],
        [valid_both, mask, x, x_other, *weights], scalars=1, name="reduce", flops=2 * rows * width * channels,
    )
    if small:
        wide, wide_turned, inner_vectors, outer_vectors = call(
            functools.partial(spread_kernel, slots, depth),
            [wide_shape, wide_shape, shape((4, half), F32), shape((2, half_out), F32)],
            weights,
            scratch=[pltpu.VMEM((size, extra, half), F32), pltpu.VMEM((size * shard, half), F32)],
            name="spread", flops=1 << 28,
        )
        middle, wide, wide_turned, inner_vectors, outer_vectors = together(
            plane_sum(part), wide, wide_turned, inner_vectors, outer_vectors
        )
        middle, second, other, expand_first = together(middle, second, other, expand_first)
        first_other, passed = across(expand_first), swap_x(expand_first)
        first = line_sum(middle)
        first, first_other, second = together(first, first_other, second)
        second_other, passed_other = across(second), swap_x(first_other)
    else:
        packed = whole[:, depth:]
        wide, wide_turned = call(
            widen_kernel, [wide_shape, wide_shape], [packed[:, :shard].reshape(size * shard, half)],
            scratch=[pltpu.VMEM((size * shard, half), F32)], name="widen",
        )
        line = packed[:, shard, : 4 * per].astype(F32).reshape(size, 4, per).transpose(1, 0, 2).reshape(4, width)
        inner_vectors = halves(line, core)
        line = packed[:, shard + 1, : 2 * outer].astype(F32).reshape(size, 2, outer).transpose(1, 0, 2)
        outer_vectors = halves(line.reshape(2, channels), core)
        first = everywhere(part)
    pad_shape = (3, across_cores, (side + 2) * LINE, half)
    pads, grouped, part = call(
        functools.partial(group_kernel, side),
        [shape(pad_shape, BF16), shape((pixels, half), F32), shape((2, half), F32)],
        [mask, first, inner_vectors, red, wide],
        name="group", flops=2 * TAPS * rows * width * BLOCK,
    )
    if small:
        part, passed = together(part, passed)
        middle = line_sum(part)
        middle, passed_other, second_other = together(middle, passed_other, second_other)
        blocks = (expand_own, expand_first, passed, second, other, first_other, passed_other, second_other)
        total_two = plane_sum(middle)
    else:
        total_two = everywhere(part)
    (act_mine,) = call(
        functools.partial(act_kernel, side), [shape((pixels, half), BF16)], [total_two, first, inner_vectors, grouped],
        name="act",
    )
    act_far = swap_core(act_mine)
    if small:
        act_mine, *blocks = together(act_mine, *blocks)
        (weight_three,) = call(assemble_kernel, [shape((width, half_out), BF16)], blocks, name="assemble")
    else:
        weight_three = lax.all_gather(expand_own, "fsdp", axis=0, tiled=True)
    act_two, expanded, part = call(
        expand_kernel,
        [shape((pixels, width), BF16), shape((pixels, half_out), F32), shape((2, half_out), F32)],
        [mask, act_mine, act_far, weight_three],
        name="expand", flops=2 * rows * width * channels,
    )
    cot = padded(after(cotangent, grouped))
    cot_far = swap_core(call(far_half_kernel, [shape((rows, half_out), BF16)], [cot], name="far_half")[0])
    middle, cot, cot_far = together(plane_sum(part), cot, cot_far)
    total_three = line_sum(middle)
    keep_out, send_out, grad_summed, part = call(
        functools.partial(output_kernel, side),
        [shape((rows, half_out), BF16), shape((rows, half_out), BF16), shape((pixels, half_out), F32),
         shape((2, half_out), F32)],
        [valid_both, total_three, first, outer_vectors, expanded, x, x_other, cot, cot_far], scalars=1, name="output",
    )

    sums_three = everywhere(part)
    flat_three, send = call(
        back_expand_kernel,
        [shape((pixels, half_out), BF16), shape((pixels, half), BF16)],
        [mask, total_three, sums_three, first, outer_vectors, grad_summed, expanded, weight_three],
        name="back_expand", flops=rows * width * channels,
    )
    far = swap_core(send)
    (mine,) = call(
        functools.partial(back_part_kernel, 0), [shape((pixels, half), F32)], [flat_three, weight_three],
        name="back_part", flops=rows * width * channels,
    )
    dz_two, part = call(
        back_act_kernel,
        [shape((pixels, half), F32), shape((2, half), F32)],
        [total_two, first, inner_vectors, mine, far, grouped], name="back_act",
    )
    (expand_term,) = call(
        weight_expand_kernel, [shape((width, half_out), BF16)], [after(act_two, part), flat_three],
        name="weight_expand", flops=2 * rows * width * channels,
    )
    far_out = swap_core(after(send_out, part))
    middle = plane_sum(part)

    def expand_sums(places, arrived=()):
        return call(
            functools.partial(expand_sum_kernel, places),
            [shape((w_expand.shape[0], half_out), BF16)] * len(places),
            [expand_term] + list(arrived), name="expand_sum",
        )

    if small:
        middle, *moving = together(middle, *expand_sums(((6, ()), (7, ()))))
        moving = [swap_x(moving[0]), across(moving[1])]
        sums_two, *moving = together(line_sum(middle), *moving)
        sums_two, expand_first_other, expand_passed, expand_second, expand_other = together(
            sums_two, *expand_sums(((5, (0,)), (2, ()), (3, (1,)), (4, ())), moving)
        )
        expand_second, expand_other = along(expand_second, -1), across(expand_other)
    else:
        sums_two = line_sum(middle)
        own_expand = lax.psum_scatter(expand_term, "fsdp", scatter_dimension=0, tiled=True)
    flat_two, dz_one, part = call(
        functools.partial(back_group_kernel, side),
        [shape((pixels, half), BF16), shape((pixels, half), F32), shape((2, half), F32)],
        [mask, total_two, sums_two, first, inner_vectors, dz_two, grouped, red, wide_turned],
        scratch=[pltpu.VMEM(pad_shape, BF16)], name="back_group", flops=2 * TAPS * rows * width * BLOCK,
    )
    (group_term,) = call(
        functools.partial(weight_group_kernel, side, inner),
        [shape((size, extra, half), BF16)],
        [pads, after(flat_two, part)], scratch=[pltpu.VMEM((TAPS * inner, half), F32)], name="weight_group",
        flops=2 * TAPS * rows * width * BLOCK,
    )
    middle, group_term = together(plane_sum(part), group_term)
    if small:
        middle, expand_second, expand_first_other, expand_passed, expand_other = together(
            middle, expand_second, expand_first_other, expand_passed, expand_other
        )
        moving = [swap_x(expand_passed), across(expand_first_other)]
    sums_one = line_sum(middle)
    if small:
        sums_one, *moving = together(sums_one, *moving)
        (expand_first_own,) = expand_sums(((1, (0, 1, 2)),), moving + [expand_second])
    tall = depth + extra
    places = ((6, ()), (7, ())) if small else tuple((at, ()) for at in range(size))
    flat_one, *moving = call(
        functools.partial(back_reduce_kernel, small, places),
        [shape((pixels, half), BF16)] + [shape((tall, half), BF16)] * len(places),
        [mask, first, sums_one, inner_vectors, dz_one, red, turned, group_term],
        name="back_reduce", flops=2 * rows * depth * width * len(places),
    )

    def sums(places, arrived):
        return call(
            functools.partial(block_sum_kernel, small, places),
            [shape((tall, half), BF16)] * len(places),
            [turned, group_term, flat_one] + list(arrived),
            name="block_sum", flops=2 * rows * depth * width * len(places),
        )

    def back_input(begin, flat, *far):
        out = shape(images.shape, BF16) if far else shape((rows, channels), BF16)
        return call(
            functools.partial(back_input_kernel, slots, slot_depth, begin),
            [out], [flat, grad_summed, *weights, *far],
            scratch=[pltpu.VMEM((rows, channels), F32)], name="back_input", flops=rows * width * channels,
        )[0]

    def own_shards(totals):
        near = jnp.concatenate(totals, axis=1)
        far = swap_core(near)
        lengths = (per, per, outer)
        if small:
            outs = call(
                functools.partial(own_kernel, lengths), [shape((1, n), F32) for n in lengths for _ in range(2)], [near, far],
                name="own",
            )
            return [out.reshape(-1) for out in outs]
        cut, at = [], 0
        for total, length in zip(totals, lengths):
            whole = both(total, far[:, at : at + total.shape[1]], core)
            at += total.shape[1]
            cut += [lax.dynamic_slice_in_dim(whole[row], position * length, length, 0) for row in (1, 0)]
        return cut

    def image_of(far_out):
        return call(image_kernel, [shape(images.shape, BF16)], [keep_out, far_out], name="image")[0]

    def join(own, far, outs):
        return call(
            join_kernel, [shape(out.shape, F32) for out in outs], [own, far, swap_core(own), swap_core(far)], name="join"
        )

    if small:
        moving[1], expand_first_own = together(moving[1], expand_first_own)
        moving = [swap_x(moving[0]), across(moving[1])]
        expand_first_own = along(expand_first_own, -1)
        shards = own_shards([sums_one, sums_two, sums_three])
        moving[0], expand_first_own, *shards = together(moving[0], expand_first_own, *shards)
        (own_expand,) = expand_sums(((0, (0, 1)),), [expand_first_own, expand_other])
        first_other, passed, second = sums(((5, (0,)), (2, ()), (3, (1,))), moving)
        moving = [swap_x(passed), along(second, -1), across(first_other)]
        far_input = swap_core(after(back_input(rows, flat_one), second))
        output = pinned(image_of(after(far_out, second)))
        moving[0], output = together(moving[0], output)
        first_own, other = sums(((1, (0, 1, 2)), (4, ())), moving)
        moving = [along(first_own, -1), across(other)]
        grad_input, own_expand = pinned(back_input(0, after(flat_one, first_own), far_input)), after(own_expand, first_own)
        far_expand = swap_x(own_expand)
        moving[0], grad_input, far_expand = together(moving[0], grad_input, far_expand)
        (own_reduce,) = sums(((0, (0, 1)),), moving)
        own_expand, far_expand = after(own_expand, own_reduce), after(far_expand, own_reduce)
        (grad_w_expand,) = join(own_expand, far_expand, [w_expand])
        far_reduce, grad_w_expand = together(swap_x(own_reduce), grad_w_expand)
    else:
        grad_input, output = back_input(0, flat_one, swap_core(back_input(rows, flat_one))), image_of(far_out)
        shards = own_shards([sums_one, sums_two, sums_three])
        whole = jnp.stack(moving).reshape(size * tall, half)
        own_reduce = lax.psum_scatter(whole, "fsdp", scatter_dimension=0, tiled=True)
        (grad_w_expand,) = join(own_expand, swap_x(own_expand), [w_expand])
        far_reduce = swap_x(own_reduce)
    grad_w_reduce, grad_w_group = join(own_reduce, far_reduce, [w_reduce, w_group])
    return (output, grad_input, grad_w_reduce, grad_w_group, grad_w_expand) + tuple(shards)


def solution(mesh):
    fsdp, dp = mesh.shape["fsdp"], mesh.shape["dp"]
    split = Mesh(mesh.devices.reshape(fsdp, dp // 2, 2), ("fsdp", "x", "core"))
    images, rows, vector = P(("fsdp", "x", "core"), None, None, None), P("fsdp", None), P("fsdp")
    return jax.shard_map(
        per_device,
        mesh=split,
        in_specs=(
            images, P(("fsdp", "x", "core")), images,
            rows, vector, vector, rows, vector, vector, rows, vector, vector,
        ),
        out_specs=(images, images, rows, rows, rows) + (vector,) * 6,
        check_vma=False,
    )
```

```python
import functools

import jax
import jax.numpy as jnp
from jax import lax
from jax.experimental import pallas as pl
from jax.experimental.pallas import tpu as pltpu
from jax.sharding import Mesh
from jax.sharding import PartitionSpec as P

GROUPS = 32
TAPS = 9
LINE = 16
CHUNK = 512
UNROLL = 7
LANES = 128
BLOCK = 256
epsilon = 1e-05
BF16, F32 = jnp.bfloat16, jnp.float32
SWAP = [(0, 1), (1, 0)]
NN, NT = ((1,), (0,)), ((1,), (1,))
CHIPS = ("fsdp", "x")


def silu_half(half):
    return half + half * jnp.tanh(half)


def dsilu_twice(half):
    turned = jnp.tanh(half)
    upper = 1.0 + turned
    return upper * (1.0 + half * (1.0 - turned)), upper


def dot(a, b, contract=NN):
    return lax.dot_general(a, b, (contract, ((), ())), preferred_element_type=F32)


def after(values, *others):
    return lax.optimization_barrier((values,) + others)[0]


def together(*values):
    return lax.optimization_barrier(values)


def shape(dims, dtype):
    return jax.ShapeDtypeStruct(dims, dtype)


def call(kernel, outs, args, scalars=0, scratch=(), vmem=8, name=None, flops=0, anywhere=False, aliases=()):
    vm = pl.BlockSpec(memory_space=pltpu.VMEM)
    given = pl.BlockSpec(memory_space=pl.ANY) if anywhere else vm
    sm = pl.BlockSpec(memory_space=pltpu.SMEM)
    return pl.pallas_call(
        kernel,
        out_shape=outs,
        in_specs=[sm] * scalars + [given] * (len(args) - scalars),
        out_specs=[vm] * len(outs),
        scratch_shapes=list(scratch),
        compiler_params=pltpu.CompilerParams(vmem_limit_bytes=vmem << 20),
        cost_estimate=pl.CostEstimate(flops=0, bytes_accessed=0, transcendentals=0),
        input_output_aliases=dict(aliases),
        name=name,
    )(*args)


def moments(total, pixels):
    mean = total[0:1, :] / pixels
    inverse = lax.rsqrt(total[1:2, :] / pixels - mean * mean + epsilon)
    return mean, inverse


def chunks(columns):
    return [slice(at, min(at + CHUNK, columns)) for at in range(0, columns, CHUNK)]


def line_mask(columns, side):
    return lax.broadcasted_iota(jnp.int32, (LINE, columns), 0) < side


def each_line(lines, body):
    lax.fori_loop(0, lines, lambda step, none: body(step) or none, 0, unroll=UNROLL)


def each_line_summed(lines, width, body):
    zero = jnp.zeros((8, width), F32)

    def step_sums(step, carry):
        one, two = body(step)
        return carry[0] + fold(one), carry[1] + fold(two)

    one, two = lax.fori_loop(0, lines, step_sums, (zero, zero), unroll=UNROLL)
    return column_sums(one), column_sums(two)


def across_lanes(mask, columns):
    return jnp.concatenate([mask] * (columns // LANES), axis=1)


def column_sums(values):
    return jnp.sum(values, axis=0, keepdims=True)


def line_at(step):
    return pl.ds(pl.multiple_of(step * LINE, LINE), LINE)


def fold(values):
    return values[0:8] + values[8:16]


def part_at(part, half, at=0, length=None):
    core = lax.axis_index("core")
    side = core if part == 0 else 1 - core
    length = half if length is None else length
    return pl.ds(pl.multiple_of(side * half + at, 128), length)


def block_owner(slot):
    position = lax.axis_index("fsdp")
    way = 1 - 2 * lax.axis_index("x")
    step = (0, -way, way, 2)[slot % 4]
    owner = lax.rem(position + 2 * step + 8, 8)
    return owner if slot < 4 else owner + 1 - 2 * lax.rem(owner, 2)


def rows_of(owner, depth):
    return pl.ds(pl.multiple_of(owner * depth, 16), depth)


def pack_kernel(weight, group, *refs):
    vectors, (out, held, *rows, sems) = refs[:6], refs[6:]
    depth, half = weight.shape[0], out.shape[1]
    shard, extra = group.shape[0], out.shape[0] - weight.shape[0]
    columns = part_at(0, half)
    copies = [pltpu.make_async_copy(group, held, sems.at[0])]
    copies += [pltpu.make_async_copy(vector, row, sems.at[2 + at]) for at, (vector, row) in enumerate(zip(vectors, rows))]
    copies.append(pltpu.make_async_copy(weight.at[:, columns], out.at[pl.ds(0, depth)], sems.at[1]))
    for copy in copies:
        copy.start()
    for copy in copies[:-1]:
        copy.wait()
    below = [held[:, columns].astype(F32)]
    for begin, end in ((0, 4), (4, 6)):
        line = [row[...].astype(F32).reshape(1, row.shape[0]) for row in rows[begin:end]]
        missing = half - sum(piece.shape[1] for piece in line)
        below.append(jnp.concatenate(line + ([jnp.zeros((1, missing), F32)] if missing else []), axis=1))
    if extra > shard + 2:
        below.append(jnp.zeros((extra - shard - 2, half), F32))
    out[depth : depth + extra, :] = jnp.concatenate(below, axis=0).astype(BF16)
    copies[-1].wait()


def turn_kernel(side, valid, x, x_other, turned, mask):
    rows = x.shape[0]
    turned[:, 0:rows] = x[...].T
    turned[:, rows : 2 * rows] = x_other[...].T
    images = valid.shape[0]
    rows = 2 * rows // images
    inside = lax.broadcasted_iota(jnp.int32, (rows, LANES), 0) % LINE < side
    for image in range(images):
        mask[image * rows : (image + 1) * rows, :] = jnp.where(inside, valid[image].astype(F32), 0.0)


def reduce_kernel(slots, depth, side, valid, mask, x, x_other, *refs):
    weights, (red, stats) = refs[:slots], refs[slots:]
    half, rows = red.shape[1], x.shape[0]
    for at in range(0, half, BLOCK):
        sums = [0.0, 0.0]
        for begin, pixels in ((0, x), (rows, x_other)):
            total = None
            for slot in range(slots):
                if slots == 1:
                    piece = pixels[...]
                else:
                    piece = pixels[:, pl.ds(pl.multiple_of(block_owner(slot) * depth, 128), depth)]
                term = dot(piece, weights[slot][0:depth, at : at + BLOCK])
                total = term if total is None else total + term
            red[begin : begin + rows, at : at + BLOCK] = total
            masked = total * across_lanes(mask[begin : begin + rows, :], BLOCK)
            sums = [sums[0] + column_sums(masked), sums[1] + column_sums(masked * total)]
        stats[0:1, at : at + BLOCK] = sums[0]
        stats[1:2, at : at + BLOCK] = sums[1]
    pixels = valid[0].astype(F32)
    for image in range(1, valid.shape[0]):
        pixels = pixels + valid[image].astype(F32)
    stats[2:3, :] = jnp.full((1, half), 1.0, F32) * (pixels * (side * side))


def spread_kernel(slots, depth, *refs):
    blocks, (wide, wide_turned, inner_vectors, outer_vectors, held, rows) = refs[:slots], refs[slots:]
    extra = held.shape[1]
    for slot in range(slots):
        held[block_owner(slot)] = blocks[slot][depth : depth + extra, :].astype(F32)
    shard, ours = rows.shape[0] // slots, slots // 2
    per, outer = inner_vectors.shape[1] // ours, outer_vectors.shape[1] // ours
    core = lax.axis_index("core")
    for owner in range(slots):
        rows[owner * shard : (owner + 1) * shard, :] = held[owner, 0:shard, :]
    for at in range(ours):
        owner = core * ours + at
        for row in range(4):
            inner_vectors[row : row + 1, at * per : (at + 1) * per] = held[
                owner, shard : shard + 1, row * per : (row + 1) * per
            ]
        for row in range(2):
            outer_vectors[row : row + 1, at * outer : (at + 1) * outer] = held[
                owner, shard + 1 : shard + 2, row * outer : (row + 1) * outer
            ]
    widen(rows, wide, wide_turned)


def widen_kernel(weight, wide, wide_turned, rows):
    rows[...] = weight[...].astype(F32)
    widen(rows, wide, wide_turned)


def widen(weight, wide, wide_turned):
    taps, blocks = wide.shape[:2]
    inner = weight.shape[0] // taps
    row = lax.broadcasted_iota(jnp.int32, (BLOCK, BLOCK), 0) // inner
    column = lax.broadcasted_iota(jnp.int32, (BLOCK, BLOCK), 1) // inner
    own = row == column
    for tap in range(taps):
        for block in range(blocks):
            piece = weight[tap * inner : (tap + 1) * inner, block * BLOCK : (block + 1) * BLOCK]
            tall = jnp.concatenate([piece] * (BLOCK // inner), axis=0)
            dense = jnp.where(own, tall, 0.0)
            wide[tap, block] = dense.astype(BF16)
            wide_turned[tap, block] = dense.T.astype(BF16)


def fill_pads(pads, columns, image, line, values):
    rows = pl.ds(pl.multiple_of((line + 1) * LINE, LINE), LINE)
    pads[0, image, rows, columns] = pltpu.roll(values, 1, 0).astype(BF16)
    pads[1, image, rows, columns] = values.astype(BF16)
    pads[2, image, rows, columns] = pltpu.roll(values, LINE - 1, 0).astype(BF16)


def clear_pads(pads):
    images, rows, columns = pads.shape[1:]
    zeros = jnp.zeros((3, images, LINE, columns), BF16)
    pads[:, :, 0:LINE, :] = zeros
    pads[:, :, rows - LINE : rows, :] = zeros


def convolve(pads, wide, image, block, rows, turned=False):
    columns = slice(block * BLOCK, (block + 1) * BLOCK)
    value = None
    for tap in range(TAPS):
        top, left = divmod(TAPS - 1 - tap if turned else tap, 3)
        piece = pads[left, image, top * LINE : top * LINE + rows, columns]
        term = dot(piece, wide[tap, block])
        value = term if value is None else value + term
    return value


def group_kernel(side, mask, total, vectors, red, wide, pads, grouped, stats):
    images, padded, width = pads.shape[1:]
    rows = side * LINE
    mean, inverse = moments(total, total[2:3, :])
    scale, bias = 0.5 * inverse * vectors[0:1, :], 0.5 * vectors[1:2, :]
    clear_pads(pads)
    for part in chunks(width):
        inside = line_mask(part.stop - part.start, side)

        def body(step):
            half = (red[line_at(step), part] - mean[:, part]) * scale[:, part] + bias[:, part]
            fill_pads(pads, part, step // side, step % side, jnp.where(inside, silu_half(half), 0.0))

        each_line(images * side, body)
    for block in range(width // BLOCK):
        columns = slice(block * BLOCK, (block + 1) * BLOCK)
        sums = [0.0, 0.0]
        for image in range(images):
            at = slice(image * rows, (image + 1) * rows)
            value = convolve(pads, wide, image, block, rows)
            grouped[at, columns] = value
            masked = value * across_lanes(mask[at, :], BLOCK)
            sums = [sums[0] + column_sums(masked), sums[1] + column_sums(masked * value)]
        stats[0:1, columns] = sums[0]
        stats[1:2, columns] = sums[1]


def act_kernel(side, total, first, vectors, grouped, act):
    rows, width = grouped.shape
    mean, inverse = moments(total, first[2:3, :])
    scale, bias = 0.5 * inverse * vectors[2:3, :], 0.5 * vectors[3:4, :]
    for part in chunks(width):
        inside = line_mask(part.stop - part.start, side)

        def body(step):
            at = line_at(step)
            half = (grouped[at, part] - mean[:, part]) * scale[:, part] + bias[:, part]
            act[at, part] = jnp.where(inside, silu_half(half), 0.0).astype(BF16)

        each_line(rows // LINE, body)


def assemble_kernel(*refs):
    blocks, out = refs[:-1], refs[-1]
    depth = blocks[0].shape[0]
    for slot, block in enumerate(blocks):
        out[rows_of(block_owner(slot), depth), :] = block[...]


def expand_kernel(mask, act_mine, act_far, weight, act, expanded, stats):
    rows, half = act_mine.shape
    middle = rows // 2
    act[:, part_at(0, half)] = act_mine[...]
    act[0:middle, part_at(1, half)] = act_far[middle:rows, :]
    act[middle:rows, part_at(1, half)] = act_far[0:middle, :]
    for at in range(0, weight.shape[1], BLOCK):
        sums = [0.0, 0.0]
        for begin in (0, middle):
            here = slice(begin, begin + middle)
            value = dot(act[here, :], weight[:, at : at + BLOCK])
            expanded[here, at : at + BLOCK] = value
            masked = value * across_lanes(mask[here, :], BLOCK)
            sums = [sums[0] + column_sums(masked), sums[1] + column_sums(masked * value)]
        stats[0:1, at : at + BLOCK] = sums[0]
        stats[1:2, at : at + BLOCK] = sums[1]


def output_kernel(
    side, valid, total, first, vectors, expanded, x, x_other, cotangent, cotangent_far, keep_out, send_out, grad, stats
):
    rows, channels = expanded.shape
    middle = rows // 2
    mean, inverse = moments(total, first[2:3, 0:1])
    scale, bias = inverse * vectors[0:1, :], vectors[1:2, :]
    for part in chunks(channels):
        length = part.stop - part.start
        whole = part_at(0, channels, part.start, length)
        ends = []
        for begin, pixels, incoming, columns, out in (
            (0, x, cotangent, whole, keep_out), (middle, x_other, cotangent_far, part, send_out)
        ):

            def body(step):
                at = line_at(step)
                here = pl.ds(pl.multiple_of(begin + step * LINE, LINE), LINE)
                keep = 0.5 * valid[(begin // LINE + step) // side].astype(F32)
                centered = expanded[here, part] - mean[:, part]
                half = (centered * scale[:, part] + (bias[:, part] + pixels[at, whole].astype(F32))) * keep
                slope, upper = dsilu_twice(half)
                out[at, part] = (half * upper).astype(BF16)
                value = incoming[at, columns].astype(F32) * keep * slope
                grad[here, part] = value
                return value, value * centered

            ends.append(each_line_summed(middle // LINE, length, body))
        stats[0:1, part] = ends[0][0] + ends[1][0]
        stats[1:2, part] = (ends[0][1] + ends[1][1]) * inverse[:, part]


def back_expand_kernel(mask, total, sums, first, vectors, grad, expanded, weight, flat, send):
    rows, channels = expanded.shape
    pixels = first[2:3, 0:1]
    mean, inverse = moments(total, pixels)
    scale = inverse * vectors[0:1, :]
    shifted, scaled = scale * sums[0:1, :] / pixels, scale * inverse * sums[1:2, :] / pixels
    for part in chunks(channels):

        def body(step):
            at = line_at(step)
            common = shifted[:, part] + (expanded[at, part] - mean[:, part]) * scaled[:, part]
            counted = across_lanes(mask[at, :], part.stop - part.start)
            flat[at, part] = (scale[:, part] * grad[at, part] - counted * common).astype(BF16)

        each_line(rows // LINE, body)
    back_part_kernel(1, flat, weight, send)


def back_part_kernel(part, flat, weight, out):
    half = out.shape[1]
    for at in range(0, half, BLOCK):
        rows = pl.ds(pl.multiple_of(part_at(part, half).start + at, BLOCK), BLOCK)
        out[:, at : at + BLOCK] = dot(flat[...], weight[rows, :], NT).astype(out.dtype)


def back_act_kernel(total, first, vectors, mine, far, grouped, dz, stats):
    mean, inverse = moments(total, first[2:3, :])
    lines = grouped.shape[0] // LINE

    def gradient(step, part):
        there = lax.rem(step + lines // 2, lines)
        return mine[line_at(step), part] + far[line_at(there), part].astype(F32)

    before_norm(dz, gradient, grouped, mean, inverse, vectors[2:3, :], vectors[3:4, :], stats)


def before_norm(dz, gradient, hidden, mean, inverse, gain, shift, stats, side=None):
    scale, bias = 0.5 * inverse * gain, 0.5 * shift
    rows, width = hidden.shape
    for part in chunks(width):
        inside = None if side is None else line_mask(part.stop - part.start, side)

        def body(step):
            at = line_at(step)
            centered = hidden[at, part] - mean[:, part]
            slope, _ = dsilu_twice(centered * scale[:, part] + bias[:, part])
            here = gradient(step, part) * slope
            if side is not None:
                here = jnp.where(inside, here, 0.0)
            dz[at, part] = here
            return here, here * centered

        one, two = each_line_summed(rows // LINE, part.stop - part.start, body)
        stats[0:1, part] = 0.5 * one
        stats[1:2, part] = 0.5 * inverse[:, part] * two


def weight_expand_kernel(act, flat, out):
    turned = act[...].T
    for at in range(0, out.shape[1], BLOCK):
        out[:, at : at + BLOCK] = dot(turned, flat[:, at : at + BLOCK]).astype(BF16)


def back_group_kernel(
    side, mask, total, sums, first, vectors, dz, grouped, red, wide, flat, dz_one, stats, pads
):
    images, padded, width = pads.shape[1:]
    rows = side * LINE
    pixels = first[2:3, :]
    mean, inverse = moments(total, pixels)
    scale = inverse * vectors[2:3, :]
    shifted, scaled = scale * sums[0:1, :] / pixels, scale * inverse * sums[1:2, :] / pixels
    scale = 0.5 * scale
    clear_pads(pads)
    for part in chunks(width):

        def body(step):
            at = line_at(step)
            common = shifted[:, part] + (grouped[at, part] - mean[:, part]) * scaled[:, part]
            value = scale[:, part] * dz[at, part] - across_lanes(mask[at, :], part.stop - part.start) * common
            flat[at, part] = value.astype(BF16)
            fill_pads(pads, part, step // side, step % side, value)

        each_line(images * side, body)
    for block in range(width // BLOCK):
        columns = slice(block * BLOCK, (block + 1) * BLOCK)
        for image in range(images):
            dz_one[image * rows : (image + 1) * rows, columns] = convolve(pads, wide, image, block, rows, True)
    mean_one, inverse_one = moments(first, pixels)

    def gradient(step, part):
        return dz_one[line_at(step), part]

    before_norm(dz_one, gradient, red, mean_one, inverse_one, vectors[0:1, :], vectors[1:2, :], stats, side)


def weight_group_kernel(side, inner, pads, flat, out, held):
    images, padded, width = pads.shape[1:]
    rows = side * LINE
    row = lax.broadcasted_iota(jnp.int32, (LANES, LANES), 0) // inner
    column = lax.broadcasted_iota(jnp.int32, (LANES, LANES), 1) // inner
    own = row == column
    for at in range(0, width, LANES):
        columns = slice(at, at + LANES)
        moved = []
        for tap in range(TAPS):
            top, left = divmod(tap, 3)
            pieces = [pads[left, image, top * LINE : top * LINE + rows, columns] for image in range(images)]
            moved.append(jnp.concatenate(pieces, axis=0))
        product = dot(flat[:, columns].T, jnp.concatenate(moved, axis=1))
        for tap in range(TAPS):
            kept = jnp.where(own, product[:, tap * LANES : (tap + 1) * LANES].T, 0.0)
            value = kept[0:inner]
            for begin in range(inner, LANES, inner):
                value = value + kept[begin : begin + inner]
            held[tap * inner : (tap + 1) * inner, columns] = value
    owners, extra = out.shape[:2]
    shard = TAPS * inner // owners
    zeros = jnp.zeros((extra - shard, width), F32)
    for owner in range(owners):
        rows_here = held[owner * shard : (owner + 1) * shard, :]
        out[owner] = jnp.concatenate([rows_here, zeros], axis=0).astype(BF16)


def back_reduce_kernel(small, places, mask, first, sums, vectors, dz, red, turned, group, flat, *outs):
    rows, width = red.shape
    pixels = first[2:3, :]
    mean, inverse = moments(first, pixels)
    scale = inverse * vectors[0:1, :]
    shifted, scaled = scale * sums[0:1, :] / pixels, scale * inverse * sums[1:2, :] / pixels
    scale = 0.5 * scale
    for part in chunks(width):

        def body(step):
            at = line_at(step)
            common = shifted[:, part] + (red[at, part] - mean[:, part]) * scaled[:, part]
            counted = across_lanes(mask[at, :], part.stop - part.start)
            flat[at, part] = (scale[:, part] * dz[at, part] - counted * common).astype(BF16)

        each_line(rows // LINE, body)
    block_sum_kernel(small, places, turned, group, flat, *outs)


def block_sum_kernel(small, places, turned, group, flat, *refs):
    arrived, outs = refs[: len(refs) - len(places)], refs[len(refs) - len(places) :]
    tall, half = outs[0].shape
    depth = tall - group.shape[1]
    for out, (block, chosen) in zip(outs, places):
        owner = block_owner(block) if small else block
        value = dot(turned[rows_of(owner, depth), :], flat[...])
        more = group[owner].astype(F32)
        for other in chosen:
            value = value + arrived[other][0:depth, :].astype(F32)
            more = more + arrived[other][depth:tall, :].astype(F32)
        out[0:depth, :] = value.astype(BF16)
        out[depth:tall, :] = more.astype(BF16)


def expand_sum_kernel(places, depth, keep, *refs):
    arrived, outs = refs[: len(refs) - len(places)], refs[len(refs) - len(places) :]
    for out, blocks in zip(outs, places):
        for at, (block, chosen) in enumerate(blocks):
            value = keep[rows_of(block_owner(block), depth), :]
            if chosen:
                value = value.astype(F32)
                for other, begin in chosen:
                    value = value + arrived[other][begin * depth : (begin + 1) * depth, :].astype(F32)
            out[at * depth : (at + 1) * depth, :] = value.astype(BF16)


def join_kernel(mine, mine_x, other, other_x, *outs):
    half = mine.shape[1]
    at = 0
    for out in outs:
        rows = out.shape[0]
        for part, terms in enumerate(((mine, mine_x), (other, other_x))):
            values = [term[at : at + -(-rows // 16) * 16, :].astype(F32) for term in terms]
            out[:, part_at(part, half)] = (values[0] + values[1])[0:rows]
        at += -(-rows // 16) * 16


def pin_kernel(values, out):
    pass


def own_kernel(sizes, near, far, *outs):
    position, core, ours = lax.axis_index("fsdp"), lax.axis_index("core"), lax.axis_size("fsdp") // 2
    side, place, at = position // ours, lax.rem(position, ours), 0
    for index, length in enumerate(sizes):
        columns = pl.ds(pl.multiple_of(at + place * length, 128), length)
        for row, out in ((1, outs[2 * index]), (0, outs[2 * index + 1])):
            out[...] = jnp.where(side == core, near[row : row + 1, columns], far[row : row + 1, columns])
        at += ours * length


def back_input_kernel(slots, depth, begin, flat, grad, *refs):
    weights, refs = refs[:slots], refs[slots:]
    half = grad.shape[1]
    out, held = refs[-2:]
    rows = slice(begin, begin + held.shape[0])
    for slot in range(slots):
        columns = pl.ds(pl.multiple_of(block_owner(slot) * depth, 128), depth) if slots > 1 else slice(None)
        held[:, columns] = dot(flat[rows, :], weights[slot][0:depth, :], NT)
    columns = part_at(0, half)
    held[:, columns] = held[:, columns] + grad[rows, :]
    if len(refs) == 2:
        out[...] = held[...].astype(BF16)
        return
    far = refs[0]
    side = out.shape[1]

    def body(step):
        at = line_at(step)
        out[step // side, step % side] = (held[at, :] + far[at, :].astype(F32)).astype(BF16)[0:side]

    each_line(held.shape[0] // LINE, body)


def far_half_kernel(values, out):
    out[...] = values[:, part_at(1, out.shape[1])]


def image_kernel(keep, far, out):
    half, side = keep.shape[1], out.shape[1]

    def body(step):
        at = line_at(step)
        for part, values in enumerate((keep, far)):
            out[step // side, step % side, :, part_at(part, half)] = values[at, :][0:side]

    each_line(keep.shape[0] // LINE, body)


def pinned(values):
    anywhere = pl.BlockSpec(memory_space=pl.ANY)
    values = values.transpose(1, 2, 0, 3)
    values = pl.pallas_call(
        pin_kernel, out_shape=shape(values.shape, values.dtype), in_specs=[anywhere], out_specs=anywhere,
        input_output_aliases={0: 0}, compiler_params=pltpu.CompilerParams(vmem_limit_bytes=1 << 20), name="pin",
    )(values)
    return values.transpose(2, 0, 1, 3)


def swap_core(values):
    return lax.ppermute(values, "core", SWAP)


def swap_x(values):
    if lax.axis_size("x") == 2:
        return lax.ppermute(values, "x", SWAP)
    return (lax.psum(values.astype(F32), "x") - values.astype(F32)).astype(values.dtype)


def sum_chips(values, flips):
    got = []
    for flip in (*flips, 0):
        pairs = [(2 * at + core, 2 * (at ^ flip) + 1 - core) for at in range(16) for core in range(2)]
        got.append(lax.ppermute(values, (*CHIPS, "core"), pairs))
    got = together(*got)
    total = got[0]
    for other in got[1:]:
        total = total + other
    return total


def along(values, way):
    pairs = [(f * 2 + x, (f + 2 * way * (1 - 2 * x)) % 8 * 2 + x) for f in range(8) for x in range(2)]
    return lax.ppermute(values, CHIPS, pairs)


def across(values):
    return lax.ppermute(values, "fsdp", [(f, f ^ 1) for f in range(8)])


def halves(values, core):
    half = values.shape[1] // 2
    return lax.dynamic_slice_in_dim(values, core * half, half, 1)


def both(near, far, core):
    first, second = jnp.where(core == 0, near, far), jnp.where(core == 0, far, near)
    return jnp.concatenate([first, second], axis=-1)


def per_device(
    images,
    valid,
    cotangent,
    w_reduce,
    gain_one,
    shift_one,
    w_group,
    gain_two,
    shift_two,
    w_expand,
    gain_three,
    shift_three,
):
    count, side, _, channels = images.shape
    width = w_reduce.shape[1]
    inner = width // GROUPS
    size = lax.axis_size("fsdp")
    small = size == 8 and lax.axis_size("x") == 2
    position, core = lax.axis_index("fsdp"), lax.axis_index("core")
    rows = count * side * LINE
    per, outer, shard, depth = gain_one.shape[0], gain_three.shape[0], w_group.shape[0], w_reduce.shape[0]
    extra = -(-(shard + 2) // 16) * 16
    half, half_out = width // 2, channels // 2

    def plane_sum(values):
        return sum_chips(values, (1, 2, 3)) if small else lax.psum(values, CHIPS)

    def line_sum(values):
        return sum_chips(values, (4, 8, 12)) if small else values

    def everywhere(values):
        return line_sum(plane_sum(values))

    def padded(values):
        return jnp.pad(values, ((0, 0), (0, 0), (0, LINE - side), (0, 0))).reshape(rows, channels)

    vectors = (gain_one, shift_one, gain_two, shift_two, gain_three, shift_three)
    (own,) = call(
        pack_kernel, [shape((depth + extra, half), BF16)], [w_reduce, w_group, *vectors],
        anywhere=True, vmem=60, name="pack",
        scratch=[pltpu.VMEM((shard, width), BF16)] + [pltpu.VMEM(vector.shape, BF16) for vector in vectors]
        + [pltpu.SemaphoreType.DMA((8,))],
    )
    wide_shape = shape((TAPS, half // BLOCK, BLOCK, BLOCK), BF16)
    expand_own, x = halves(w_expand, core), padded(images)

    def turn(x, x_other, valid_other):
        valid_both = jnp.concatenate([valid, valid_other])
        turned, mask = call(
            functools.partial(turn_kernel, side),
            [shape((channels, 2 * rows), BF16), shape((2 * rows, LANES), F32)],
            [valid_both, x, x_other], scalars=1, name="turn",
        )
        return valid_both, turned, mask

    if small:
        first = along(own, 1)
        other = across(own)
        x_other, valid_other = padded(swap_core(images)), swap_core(valid)
        first, other, x, x_other, expand_own = together(first, other, x, x_other, expand_own)
        passed, second, first_other = swap_x(first), along(first, 1), across(first)
        second, passed, first_other, valid_other = together(second, passed, first_other, valid_other)
        passed_other, second_other, expand_first = swap_x(first_other), across(second), along(expand_own, 1)
        valid_both, turned, mask = turn(x, x_other, valid_other)
        weights = [own, first, passed, second, other, first_other, passed_other, second_other]
        *weights, turned, mask = together(*weights, turned, mask)
        second, other = along(expand_first, 1), across(expand_own)
        slots, slot_depth = size, depth
    else:
        x_other, valid_other = swap_core(x), swap_core(valid)
        valid_both, turned, mask = turn(x, x_other, valid_other)
        whole = lax.all_gather(own, "fsdp", axis=0, tiled=False)
        weights = [whole[:, :depth].reshape(channels, half)]
        slots, slot_depth = 1, channels

    pixels, across_cores = 2 * rows, 2 * count
    red, part = call(
        functools.partial(reduce_kernel, slots, slot_depth, side),
        [shape((pixels, half), F32), shape((3, half), F32)],
        [valid_both, mask, x, x_other, *weights], scalars=1, name="reduce", flops=2 * rows * width * channels,
    )
    if small:
        wide, wide_turned, inner_vectors, outer_vectors = call(
            functools.partial(spread_kernel, slots, depth),
            [wide_shape, wide_shape, shape((4, half), F32), shape((2, half_out), F32)],
            weights,
            scratch=[pltpu.VMEM((size, extra, half), F32), pltpu.VMEM((size * shard, half), F32)],
            name="spread", flops=1 << 28,
        )
        middle, wide, wide_turned, inner_vectors, outer_vectors = together(
            plane_sum(part), wide, wide_turned, inner_vectors, outer_vectors
        )
        middle, second, other, expand_first = together(middle, second, other, expand_first)
        first_other, passed = across(expand_first), swap_x(expand_first)
        first = line_sum(middle)
        first, first_other, second = together(first, first_other, second)
        second_other, passed_other = across(second), swap_x(first_other)
    else:
        packed = whole[:, depth:]
        wide, wide_turned = call(
            widen_kernel, [wide_shape, wide_shape], [packed[:, :shard].reshape(size * shard, half)],
            scratch=[pltpu.VMEM((size * shard, half), F32)], name="widen",
        )
        line = packed[:, shard, : 4 * per].astype(F32).reshape(size, 4, per).transpose(1, 0, 2).reshape(4, width)
        inner_vectors = halves(line, core)
        line = packed[:, shard + 1, : 2 * outer].astype(F32).reshape(size, 2, outer).transpose(1, 0, 2)
        outer_vectors = halves(line.reshape(2, channels), core)
        first = everywhere(part)
    pad_shape = (3, across_cores, (side + 2) * LINE, half)
    pads, grouped, part = call(
        functools.partial(group_kernel, side),
        [shape(pad_shape, BF16), shape((pixels, half), F32), shape((2, half), F32)],
        [mask, first, inner_vectors, red, wide],
        name="group", flops=2 * TAPS * rows * width * BLOCK,
    )
    if small:
        part, passed = together(part, passed)
        middle = line_sum(part)
        middle, passed_other, second_other = together(middle, passed_other, second_other)
        blocks = (expand_own, expand_first, passed, second, other, first_other, passed_other, second_other)
        total_two = plane_sum(middle)
    else:
        total_two = everywhere(part)
    (act_mine,) = call(
        functools.partial(act_kernel, side), [shape((pixels, half), BF16)], [total_two, first, inner_vectors, grouped],
        name="act",
    )
    act_far = swap_core(act_mine)
    if small:
        act_mine, *blocks = together(act_mine, *blocks)
        (weight_three,) = call(assemble_kernel, [shape((width, half_out), BF16)], blocks, name="assemble")
    else:
        weight_three = lax.all_gather(expand_own, "fsdp", axis=0, tiled=True)
    act_two, expanded, part = call(
        expand_kernel,
        [shape((pixels, width), BF16), shape((pixels, half_out), F32), shape((2, half_out), F32)],
        [mask, act_mine, act_far, weight_three],
        name="expand", flops=2 * rows * width * channels,
    )
    cot = padded(after(cotangent, grouped))
    cot_far = swap_core(call(far_half_kernel, [shape((rows, half_out), BF16)], [cot], name="far_half")[0])
    middle, cot, cot_far = together(plane_sum(part), cot, cot_far)
    total_three = line_sum(middle)
    keep_out, send_out, grad_summed, part = call(
        functools.partial(output_kernel, side),
        [shape((rows, half_out), BF16), shape((rows, half_out), BF16), shape((pixels, half_out), F32),
         shape((2, half_out), F32)],
        [valid_both, total_three, first, outer_vectors, expanded, x, x_other, cot, cot_far], scalars=1, name="output",
    )

    sums_three = everywhere(part)
    flat_three, send = call(
        back_expand_kernel,
        [shape((pixels, half_out), BF16), shape((pixels, half), BF16)],
        [mask, total_three, sums_three, first, outer_vectors, grad_summed, expanded, weight_three],
        name="back_expand", flops=rows * width * channels,
    )
    far = swap_core(send)
    (mine,) = call(
        functools.partial(back_part_kernel, 0), [shape((pixels, half), F32)], [flat_three, weight_three],
        name="back_part", flops=rows * width * channels,
    )
    dz_two, part = call(
        back_act_kernel,
        [shape((pixels, half), F32), shape((2, half), F32)],
        [total_two, first, inner_vectors, mine, far, grouped], name="back_act",
    )
    (expand_term,) = call(
        weight_expand_kernel, [shape((width, half_out), BF16)], [after(act_two, part), flat_three],
        name="weight_expand", flops=2 * rows * width * channels,
    )
    far_out = swap_core(after(send_out, part))
    middle = plane_sum(part)

    def expand_sums(places, arrived=()):
        return call(
            functools.partial(expand_sum_kernel, places, w_expand.shape[0]),
            [shape((w_expand.shape[0] * len(blocks), half_out), BF16) for blocks in places],
            [expand_term] + list(arrived), name="expand_sum",
        )

    if small:
        middle, *moving = together(middle, *expand_sums((((6, ()), (2, ())), ((7, ()), (4, ())))))
        moving = [swap_x(moving[0]), across(moving[1])]
        sums_two = line_sum(middle)
    else:
        sums_two = line_sum(middle)
        own_expand = lax.psum_scatter(expand_term, "fsdp", scatter_dimension=0, tiled=True)
    flat_two, dz_one, part = call(
        functools.partial(back_group_kernel, side),
        [shape((pixels, half), BF16), shape((pixels, half), F32), shape((2, half), F32)],
        [mask, total_two, sums_two, first, inner_vectors, dz_two, grouped, red, wide_turned],
        scratch=[pltpu.VMEM(pad_shape, BF16)], name="back_group", flops=2 * TAPS * rows * width * BLOCK,
    )
    (group_term,) = call(
        functools.partial(weight_group_kernel, side, inner),
        [shape((size, extra, half), BF16)],
        [pads, after(flat_two, part)], scratch=[pltpu.VMEM((TAPS * inner, half), F32)], name="weight_group",
        flops=2 * TAPS * rows * width * BLOCK,
    )
    middle, group_term = together(plane_sum(part), group_term)
    if small:
        middle, *moving = together(middle, *moving)
        middle, expand_first_other, expand_second = together(middle, *expand_sums((((5, ((0, 0),)),), ((3, ((1, 0),)),)), moving))
        expand_first_other, expand_second = across(expand_first_other), along(expand_second, -1)
    sums_one = line_sum(middle)
    if small:
        sums_one, expand_first_other, expand_second = together(sums_one, expand_first_other, expand_second)
        expand_passed, expand_other = moving
        (expand_first_own,) = expand_sums((((1, ((0, 1), (1, 0), (2, 0))),),), (expand_passed, expand_first_other, expand_second))
    tall = depth + extra
    places = ((6, ()), (7, ())) if small else tuple((at, ()) for at in range(size))
    flat_one, *moving = call(
        functools.partial(back_reduce_kernel, small, places),
        [shape((pixels, half), BF16)] + [shape((tall, half), BF16)] * len(places),
        [mask, first, sums_one, inner_vectors, dz_one, red, turned, group_term],
        name="back_reduce", flops=2 * rows * depth * width * len(places),
    )

    def sums(places, arrived):
        return call(
            functools.partial(block_sum_kernel, small, places),
            [shape((tall, half), BF16)] * len(places),
            [turned, group_term, flat_one] + list(arrived),
            name="block_sum", flops=2 * rows * depth * width * len(places),
        )

    def back_input(begin, flat, *far):
        out = shape(images.shape, BF16) if far else shape((rows, channels), BF16)
        return call(
            functools.partial(back_input_kernel, slots, slot_depth, begin),
            [out], [flat, grad_summed, *weights, *far],
            scratch=[pltpu.VMEM((rows, channels), F32)], name="back_input", flops=rows * width * channels,
        )[0]

    def own_shards(totals):
        near = jnp.concatenate(totals, axis=1)
        far = swap_core(near)
        lengths = (per, per, outer)
        if small:
            outs = call(
                functools.partial(own_kernel, lengths), [shape((1, n), F32) for n in lengths for _ in range(2)], [near, far],
                name="own",
            )
            return [out.reshape(-1) for out in outs]
        cut, at = [], 0
        for total, length in zip(totals, lengths):
            whole = both(total, far[:, at : at + total.shape[1]], core)
            at += total.shape[1]
            cut += [lax.dynamic_slice_in_dim(whole[row], position * length, length, 0) for row in (1, 0)]
        return cut

    def image_of(far_out):
        return call(image_kernel, [shape(images.shape, BF16)], [keep_out, far_out], name="image")[0]

    def join(own, far, outs):
        return call(
            join_kernel, [shape(out.shape, F32) for out in outs], [own, far, swap_core(own), swap_core(far)], name="join"
        )

    if small:
        moving[1], expand_first_own = together(moving[1], expand_first_own)
        moving = [swap_x(moving[0]), across(moving[1])]
        expand_first_own = along(expand_first_own, -1)
        shards = own_shards([sums_one, sums_two, sums_three])
        moving[0], expand_first_own, *shards = together(moving[0], expand_first_own, *shards)
        (own_expand,) = expand_sums((((0, ((0, 0), (1, 1))),),), [expand_first_own, expand_other])
        first_other, passed, second = sums(((5, (0,)), (2, ()), (3, (1,))), moving)
        moving = [swap_x(passed), along(second, -1), across(first_other)]
        far_input = swap_core(after(back_input(rows, flat_one), second))
        output = pinned(image_of(after(far_out, second)))
        moving[0], output = together(moving[0], output)
        first_own, other = sums(((1, (0, 1, 2)), (4, ())), moving)
        moving = [along(first_own, -1), across(other)]
        grad_input, own_expand = pinned(back_input(0, after(flat_one, first_own), far_input)), after(own_expand, first_own)
        far_expand = swap_x(own_expand)
        moving[0], grad_input, far_expand = together(moving[0], grad_input, far_expand)
        (own_reduce,) = sums(((0, (0, 1)),), moving)
        own_expand, far_expand = after(own_expand, own_reduce), after(far_expand, own_reduce)
        (grad_w_expand,) = join(own_expand, far_expand, [w_expand])
        far_reduce, grad_w_expand = together(swap_x(own_reduce), grad_w_expand)
    else:
        grad_input, output = back_input(0, flat_one, swap_core(back_input(rows, flat_one))), image_of(far_out)
        shards = own_shards([sums_one, sums_two, sums_three])
        whole = jnp.stack(moving).reshape(size * tall, half)
        own_reduce = lax.psum_scatter(whole, "fsdp", scatter_dimension=0, tiled=True)
        (grad_w_expand,) = join(own_expand, swap_x(own_expand), [w_expand])
        far_reduce = swap_x(own_reduce)
    grad_w_reduce, grad_w_group = join(own_reduce, far_reduce, [w_reduce, w_group])
    return (output, grad_input, grad_w_reduce, grad_w_group, grad_w_expand) + tuple(shards)


def solution(mesh):
    fsdp, dp = mesh.shape["fsdp"], mesh.shape["dp"]
    split = Mesh(mesh.devices.reshape(fsdp, dp // 2, 2), ("fsdp", "x", "core"))
    images, rows, vector = P(("fsdp", "x", "core"), None, None, None), P("fsdp", None), P("fsdp")
    return jax.shard_map(
        per_device,
        mesh=split,
        in_specs=(
            images, P(("fsdp", "x", "core")), images,
            rows, vector, vector, rows, vector, vector, rows, vector, vector,
        ),
        out_specs=(images, images, rows, rows, rows) + (vector,) * 6,
        check_vma=False,
    )
```

```python
import functools

import jax
import jax.numpy as jnp
from jax import lax
from jax.experimental import pallas as pl
from jax.experimental.pallas import tpu as pltpu
from jax.sharding import Mesh
from jax.sharding import PartitionSpec as P

GROUPS = 32
TAPS = 9
LINE = 16
CHUNK = 512
UNROLL = 7
LANES = 128
BLOCK = 256
epsilon = 1e-05
BF16, F32 = jnp.bfloat16, jnp.float32
SWAP = [(0, 1), (1, 0)]
NN, NT = ((1,), (0,)), ((1,), (1,))
CHIPS = ("fsdp", "x")


def silu_half(half):
    return half + half * jnp.tanh(half)


def dsilu_twice(half):
    turned = jnp.tanh(half)
    upper = 1.0 + turned
    return upper * (1.0 + half * (1.0 - turned)), upper


def dot(a, b, contract=NN):
    return lax.dot_general(a, b, (contract, ((), ())), preferred_element_type=F32)


def after(values, *others):
    return lax.optimization_barrier((values,) + others)[0]


def together(*values):
    return lax.optimization_barrier(values)


def shape(dims, dtype):
    return jax.ShapeDtypeStruct(dims, dtype)


def call(kernel, outs, args, scalars=0, scratch=(), vmem=8, name=None, flops=0, anywhere=False, aliases=()):
    vm = pl.BlockSpec(memory_space=pltpu.VMEM)
    given = pl.BlockSpec(memory_space=pl.ANY) if anywhere else vm
    sm = pl.BlockSpec(memory_space=pltpu.SMEM)
    return pl.pallas_call(
        kernel,
        out_shape=outs,
        in_specs=[sm] * scalars + [given] * (len(args) - scalars),
        out_specs=[vm] * len(outs),
        scratch_shapes=list(scratch),
        compiler_params=pltpu.CompilerParams(vmem_limit_bytes=vmem << 20),
        cost_estimate=pl.CostEstimate(flops=0, bytes_accessed=0, transcendentals=0),
        input_output_aliases=dict(aliases),
        name=name,
    )(*args)


def moments(total, pixels):
    mean = total[0:1, :] / pixels
    inverse = lax.rsqrt(total[1:2, :] / pixels - mean * mean + epsilon)
    return mean, inverse


def chunks(columns):
    return [slice(at, min(at + CHUNK, columns)) for at in range(0, columns, CHUNK)]


def line_mask(columns, side):
    return lax.broadcasted_iota(jnp.int32, (LINE, columns), 0) < side


def each_line(lines, body):
    lax.fori_loop(0, lines, lambda step, none: body(step) or none, 0, unroll=UNROLL)


def each_line_summed(lines, width, body):
    zero = jnp.zeros((8, width), F32)

    def step_sums(step, carry):
        one, two = body(step)
        return carry[0] + fold(one), carry[1] + fold(two)

    one, two = lax.fori_loop(0, lines, step_sums, (zero, zero), unroll=UNROLL)
    return column_sums(one), column_sums(two)


def across_lanes(mask, columns):
    return jnp.concatenate([mask] * (columns // LANES), axis=1)


def column_sums(values):
    return jnp.sum(values, axis=0, keepdims=True)


def line_at(step):
    return pl.ds(pl.multiple_of(step * LINE, LINE), LINE)


def fold(values):
    return values[0:8] + values[8:16]


def part_at(part, half, at=0, length=None):
    core = lax.axis_index("core")
    side = core if part == 0 else 1 - core
    length = half if length is None else length
    return pl.ds(pl.multiple_of(side * half + at, 128), length)


def block_owner(slot):
    position = lax.axis_index("fsdp")
    way = 1 - 2 * lax.axis_index("x")
    step = (0, -way, way, 2)[slot % 4]
    owner = lax.rem(position + 2 * step + 8, 8)
    return owner if slot < 4 else owner + 1 - 2 * lax.rem(owner, 2)


def rows_of(owner, depth):
    return pl.ds(pl.multiple_of(owner * depth, 16), depth)


def pack_kernel(weight, group, *refs):
    vectors, (out, held, *rows, sems) = refs[:6], refs[6:]
    depth, half = weight.shape[0], out.shape[1]
    shard, extra = group.shape[0], out.shape[0] - weight.shape[0]
    columns = part_at(0, half)
    copies = [pltpu.make_async_copy(group, held, sems.at[0])]
    copies += [pltpu.make_async_copy(vector, row, sems.at[2 + at]) for at, (vector, row) in enumerate(zip(vectors, rows))]
    copies.append(pltpu.make_async_copy(weight.at[:, columns], out.at[pl.ds(0, depth)], sems.at[1]))
    for copy in copies:
        copy.start()
    for copy in copies[:-1]:
        copy.wait()
    below = [held[:, columns].astype(F32)]
    for begin, end in ((0, 4), (4, 6)):
        line = [row[...].astype(F32).reshape(1, row.shape[0]) for row in rows[begin:end]]
        missing = half - sum(piece.shape[1] for piece in line)
        below.append(jnp.concatenate(line + ([jnp.zeros((1, missing), F32)] if missing else []), axis=1))
    if extra > shard + 2:
        below.append(jnp.zeros((extra - shard - 2, half), F32))
    out[depth : depth + extra, :] = jnp.concatenate(below, axis=0).astype(BF16)
    copies[-1].wait()


def turn_kernel(side, valid, x, x_other, turned, mask):
    rows = x.shape[0]
    turned[:, 0:rows] = x[...].T
    turned[:, rows : 2 * rows] = x_other[...].T
    images = valid.shape[0]
    rows = 2 * rows // images
    inside = lax.broadcasted_iota(jnp.int32, (rows, LANES), 0) % LINE < side
    for image in range(images):
        mask[image * rows : (image + 1) * rows, :] = jnp.where(inside, valid[image].astype(F32), 0.0)


def reduce_kernel(slots, depth, side, last, valid, mask, x, x_other, *refs):
    weights, refs = refs[: len(slots)], refs[len(slots) :]
    before, red = (None, refs[0]) if len(refs) == 1 + last else refs[:2]
    half, rows = red.shape[1], x.shape[0]
    for at in range(0, half, BLOCK):
        sums = [0.0, 0.0]
        for begin, pixels in ((0, x), (rows, x_other)):
            here = (slice(begin, begin + rows), slice(at, at + BLOCK))
            total = None if before is None else before[here]
            for slot, weight in zip(slots, weights):
                if slot is None:
                    piece = pixels[...]
                else:
                    piece = pixels[:, pl.ds(pl.multiple_of(block_owner(slot) * depth, 128), depth)]
                term = dot(piece, weight[0:depth, at : at + BLOCK])
                total = term if total is None else total + term
            red[here] = total
            if last:
                masked = total * across_lanes(mask[begin : begin + rows, :], BLOCK)
                sums = [sums[0] + column_sums(masked), sums[1] + column_sums(masked * total)]
        if last:
            refs[-1][0:1, at : at + BLOCK] = sums[0]
            refs[-1][1:2, at : at + BLOCK] = sums[1]
    if last:
        pixels = valid[0].astype(F32)
        for image in range(1, valid.shape[0]):
            pixels = pixels + valid[image].astype(F32)
        refs[-1][2:3, :] = jnp.full((1, half), 1.0, F32) * (pixels * (side * side))


def spread_kernel(slots, depth, *refs):
    blocks, (wide, wide_turned, inner_vectors, outer_vectors, held, rows) = refs[:slots], refs[slots:]
    extra = held.shape[1]
    for slot in range(slots):
        held[block_owner(slot)] = blocks[slot][depth : depth + extra, :].astype(F32)
    shard, ours = rows.shape[0] // slots, slots // 2
    per, outer = inner_vectors.shape[1] // ours, outer_vectors.shape[1] // ours
    core = lax.axis_index("core")
    for owner in range(slots):
        rows[owner * shard : (owner + 1) * shard, :] = held[owner, 0:shard, :]
    for at in range(ours):
        owner = core * ours + at
        for row in range(4):
            inner_vectors[row : row + 1, at * per : (at + 1) * per] = held[
                owner, shard : shard + 1, row * per : (row + 1) * per
            ]
        for row in range(2):
            outer_vectors[row : row + 1, at * outer : (at + 1) * outer] = held[
                owner, shard + 1 : shard + 2, row * outer : (row + 1) * outer
            ]
    widen(rows, wide, wide_turned)


def widen_kernel(weight, wide, wide_turned, rows):
    rows[...] = weight[...].astype(F32)
    widen(rows, wide, wide_turned)


def widen(weight, wide, wide_turned):
    taps, blocks = wide.shape[:2]
    inner = weight.shape[0] // taps
    row = lax.broadcasted_iota(jnp.int32, (BLOCK, BLOCK), 0) // inner
    column = lax.broadcasted_iota(jnp.int32, (BLOCK, BLOCK), 1) // inner
    own = row == column
    for tap in range(taps):
        for block in range(blocks):
            piece = weight[tap * inner : (tap + 1) * inner, block * BLOCK : (block + 1) * BLOCK]
            tall = jnp.concatenate([piece] * (BLOCK // inner), axis=0)
            dense = jnp.where(own, tall, 0.0)
            wide[tap, block] = dense.astype(BF16)
            wide_turned[tap, block] = dense.T.astype(BF16)


def fill_pads(pads, columns, image, line, values):
    rows = pl.ds(pl.multiple_of((line + 1) * LINE, LINE), LINE)
    pads[0, image, rows, columns] = pltpu.roll(values, 1, 0).astype(BF16)
    pads[1, image, rows, columns] = values.astype(BF16)
    pads[2, image, rows, columns] = pltpu.roll(values, LINE - 1, 0).astype(BF16)


def clear_pads(pads):
    images, rows, columns = pads.shape[1:]
    zeros = jnp.zeros((3, images, LINE, columns), BF16)
    pads[:, :, 0:LINE, :] = zeros
    pads[:, :, rows - LINE : rows, :] = zeros


def convolve(pads, wide, image, block, rows, turned=False):
    columns = slice(block * BLOCK, (block + 1) * BLOCK)
    value = None
    for tap in range(TAPS):
        top, left = divmod(TAPS - 1 - tap if turned else tap, 3)
        piece = pads[left, image, top * LINE : top * LINE + rows, columns]
        term = dot(piece, wide[tap, block])
        value = term if value is None else value + term
    return value


def group_kernel(side, mask, total, vectors, red, wide, pads, grouped, stats):
    images, padded, width = pads.shape[1:]
    rows = side * LINE
    mean, inverse = moments(total, total[2:3, :])
    scale, bias = 0.5 * inverse * vectors[0:1, :], 0.5 * vectors[1:2, :]
    clear_pads(pads)
    for part in chunks(width):
        inside = line_mask(part.stop - part.start, side)

        def body(step):
            half = (red[line_at(step), part] - mean[:, part]) * scale[:, part] + bias[:, part]
            fill_pads(pads, part, step // side, step % side, jnp.where(inside, silu_half(half), 0.0))

        each_line(images * side, body)
    for block in range(width // BLOCK):
        columns = slice(block * BLOCK, (block + 1) * BLOCK)
        sums = [0.0, 0.0]
        for image in range(images):
            at = slice(image * rows, (image + 1) * rows)
            value = convolve(pads, wide, image, block, rows)
            grouped[at, columns] = value
            masked = value * across_lanes(mask[at, :], BLOCK)
            sums = [sums[0] + column_sums(masked), sums[1] + column_sums(masked * value)]
        stats[0:1, columns] = sums[0]
        stats[1:2, columns] = sums[1]


def act_kernel(side, total, first, vectors, grouped, act):
    rows, width = grouped.shape
    mean, inverse = moments(total, first[2:3, :])
    scale, bias = 0.5 * inverse * vectors[2:3, :], 0.5 * vectors[3:4, :]
    for part in chunks(width):
        inside = line_mask(part.stop - part.start, side)

        def body(step):
            at = line_at(step)
            half = (grouped[at, part] - mean[:, part]) * scale[:, part] + bias[:, part]
            act[at, part] = jnp.where(inside, silu_half(half), 0.0).astype(BF16)

        each_line(rows // LINE, body)


def assemble_kernel(*refs):
    blocks, out = refs[:-1], refs[-1]
    depth = blocks[0].shape[0]
    for slot, block in enumerate(blocks):
        out[rows_of(block_owner(slot), depth), :] = block[...]


def expand_kernel(mask, act_mine, act_far, weight, act, expanded, stats):
    rows, half = act_mine.shape
    middle = rows // 2
    act[:, part_at(0, half)] = act_mine[...]
    act[0:middle, part_at(1, half)] = act_far[middle:rows, :]
    act[middle:rows, part_at(1, half)] = act_far[0:middle, :]
    for at in range(0, weight.shape[1], BLOCK):
        sums = [0.0, 0.0]
        for begin in (0, middle):
            here = slice(begin, begin + middle)
            value = dot(act[here, :], weight[:, at : at + BLOCK])
            expanded[here, at : at + BLOCK] = value
            masked = value * across_lanes(mask[here, :], BLOCK)
            sums = [sums[0] + column_sums(masked), sums[1] + column_sums(masked * value)]
        stats[0:1, at : at + BLOCK] = sums[0]
        stats[1:2, at : at + BLOCK] = sums[1]


def output_kernel(
    side, valid, total, first, vectors, expanded, x, x_other, cotangent, cotangent_far, keep_out, send_out, grad, stats
):
    rows, channels = expanded.shape
    middle = rows // 2
    mean, inverse = moments(total, first[2:3, 0:1])
    scale, bias = inverse * vectors[0:1, :], vectors[1:2, :]
    for part in chunks(channels):
        length = part.stop - part.start
        whole = part_at(0, channels, part.start, length)
        ends = []
        for begin, pixels, incoming, columns, out in (
            (0, x, cotangent, whole, keep_out), (middle, x_other, cotangent_far, part, send_out)
        ):

            def body(step):
                at = line_at(step)
                here = pl.ds(pl.multiple_of(begin + step * LINE, LINE), LINE)
                keep = 0.5 * valid[(begin // LINE + step) // side].astype(F32)
                centered = expanded[here, part] - mean[:, part]
                half = (centered * scale[:, part] + (bias[:, part] + pixels[at, whole].astype(F32))) * keep
                slope, upper = dsilu_twice(half)
                out[at, part] = (half * upper).astype(BF16)
                value = incoming[at, columns].astype(F32) * keep * slope
                grad[here, part] = value
                return value, value * centered

            ends.append(each_line_summed(middle // LINE, length, body))
        stats[0:1, part] = ends[0][0] + ends[1][0]
        stats[1:2, part] = (ends[0][1] + ends[1][1]) * inverse[:, part]


def back_expand_kernel(mask, total, sums, first, vectors, grad, expanded, weight, flat, send):
    rows, channels = expanded.shape
    pixels = first[2:3, 0:1]
    mean, inverse = moments(total, pixels)
    scale = inverse * vectors[0:1, :]
    shifted, scaled = scale * sums[0:1, :] / pixels, scale * inverse * sums[1:2, :] / pixels
    for part in chunks(channels):

        def body(step):
            at = line_at(step)
            common = shifted[:, part] + (expanded[at, part] - mean[:, part]) * scaled[:, part]
            counted = across_lanes(mask[at, :], part.stop - part.start)
            flat[at, part] = (scale[:, part] * grad[at, part] - counted * common).astype(BF16)

        each_line(rows // LINE, body)
    back_part_kernel(1, flat, weight, send)


def back_part_kernel(part, flat, weight, out):
    half = out.shape[1]
    for at in range(0, half, BLOCK):
        rows = pl.ds(pl.multiple_of(part_at(part, half).start + at, BLOCK), BLOCK)
        out[:, at : at + BLOCK] = dot(flat[...], weight[rows, :], NT).astype(out.dtype)


def back_act_kernel(total, first, vectors, mine, far, grouped, dz, stats):
    mean, inverse = moments(total, first[2:3, :])
    lines = grouped.shape[0] // LINE

    def gradient(step, part):
        there = lax.rem(step + lines // 2, lines)
        return mine[line_at(step), part] + far[line_at(there), part].astype(F32)

    before_norm(dz, gradient, grouped, mean, inverse, vectors[2:3, :], vectors[3:4, :], stats)


def before_norm(dz, gradient, hidden, mean, inverse, gain, shift, stats, side=None):
    scale, bias = 0.5 * inverse * gain, 0.5 * shift
    rows, width = hidden.shape
    for part in chunks(width):
        inside = None if side is None else line_mask(part.stop - part.start, side)

        def body(step):
            at = line_at(step)
            centered = hidden[at, part] - mean[:, part]
            slope, _ = dsilu_twice(centered * scale[:, part] + bias[:, part])
            here = gradient(step, part) * slope
            if side is not None:
                here = jnp.where(inside, here, 0.0)
            dz[at, part] = here
            return here, here * centered

        one, two = each_line_summed(rows // LINE, part.stop - part.start, body)
        stats[0:1, part] = 0.5 * one
        stats[1:2, part] = 0.5 * inverse[:, part] * two


def weight_expand_kernel(act, flat, out):
    turned = act[...].T
    for at in range(0, out.shape[1], BLOCK):
        out[:, at : at + BLOCK] = dot(turned, flat[:, at : at + BLOCK]).astype(BF16)


def back_group_kernel(
    side, mask, total, sums, first, vectors, dz, grouped, red, wide, flat, dz_one, stats, pads
):
    images, padded, width = pads.shape[1:]
    rows = side * LINE
    pixels = first[2:3, :]
    mean, inverse = moments(total, pixels)
    scale = inverse * vectors[2:3, :]
    shifted, scaled = scale * sums[0:1, :] / pixels, scale * inverse * sums[1:2, :] / pixels
    scale = 0.5 * scale
    clear_pads(pads)
    for part in chunks(width):

        def body(step):
            at = line_at(step)
            common = shifted[:, part] + (grouped[at, part] - mean[:, part]) * scaled[:, part]
            value = scale[:, part] * dz[at, part] - across_lanes(mask[at, :], part.stop - part.start) * common
            flat[at, part] = value.astype(BF16)
            fill_pads(pads, part, step // side, step % side, value)

        each_line(images * side, body)
    for block in range(width // BLOCK):
        columns = slice(block * BLOCK, (block + 1) * BLOCK)
        for image in range(images):
            dz_one[image * rows : (image + 1) * rows, columns] = convolve(pads, wide, image, block, rows, True)
    mean_one, inverse_one = moments(first, pixels)

    def gradient(step, part):
        return dz_one[line_at(step), part]

    before_norm(dz_one, gradient, red, mean_one, inverse_one, vectors[0:1, :], vectors[1:2, :], stats, side)


def weight_group_kernel(side, inner, pads, flat, out, held):
    images, padded, width = pads.shape[1:]
    rows = side * LINE
    row = lax.broadcasted_iota(jnp.int32, (LANES, LANES), 0) // inner
    column = lax.broadcasted_iota(jnp.int32, (LANES, LANES), 1) // inner
    own = row == column
    for at in range(0, width, LANES):
        columns = slice(at, at + LANES)
        moved = []
        for tap in range(TAPS):
            top, left = divmod(tap, 3)
            pieces = [pads[left, image, top * LINE : top * LINE + rows, columns] for image in range(images)]
            moved.append(jnp.concatenate(pieces, axis=0))
        product = dot(flat[:, columns].T, jnp.concatenate(moved, axis=1))
        for tap in range(TAPS):
            kept = jnp.where(own, product[:, tap * LANES : (tap + 1) * LANES].T, 0.0)
            value = kept[0:inner]
            for begin in range(inner, LANES, inner):
                value = value + kept[begin : begin + inner]
            held[tap * inner : (tap + 1) * inner, columns] = value
    owners, extra = out.shape[:2]
    shard = TAPS * inner // owners
    zeros = jnp.zeros((extra - shard, width), F32)
    for owner in range(owners):
        rows_here = held[owner * shard : (owner + 1) * shard, :]
        out[owner] = jnp.concatenate([rows_here, zeros], axis=0).astype(BF16)


def back_reduce_kernel(small, places, mask, first, sums, vectors, dz, red, turned, group, flat, *outs):
    rows, width = red.shape
    pixels = first[2:3, :]
    mean, inverse = moments(first, pixels)
    scale = inverse * vectors[0:1, :]
    shifted, scaled = scale * sums[0:1, :] / pixels, scale * inverse * sums[1:2, :] / pixels
    scale = 0.5 * scale
    for part in chunks(width):

        def body(step):
            at = line_at(step)
            common = shifted[:, part] + (red[at, part] - mean[:, part]) * scaled[:, part]
            counted = across_lanes(mask[at, :], part.stop - part.start)
            flat[at, part] = (scale[:, part] * dz[at, part] - counted * common).astype(BF16)

        each_line(rows // LINE, body)
    block_sum_kernel(small, places, turned, group, flat, *outs)


def block_sum_kernel(small, places, turned, group, flat, *outs):
    tall, half = outs[0].shape
    depth = tall - group.shape[1]
    for out, block in zip(outs, places):
        owner = block_owner(block) if small else block
        out[0:depth, :] = dot(turned[rows_of(owner, depth), :], flat[...]).astype(out.dtype)
        out[depth:tall, :] = group[owner].astype(out.dtype)


def arrived_kernel(numbers, *refs):
    terms, arrived, outs = refs[: len(numbers)], refs[len(numbers) : -len(numbers)], refs[-len(numbers) :]
    at = 0
    for out, term, number in zip(outs, terms, numbers):
        value = term[...]
        for other in arrived[at : at + number]:
            value = value + other[...].astype(F32)
        out[...] = value.astype(BF16)
        at += number


def expand_sum_kernel(places, depth, keep, *refs):
    arrived, outs = refs[: len(refs) - len(places)], refs[len(refs) - len(places) :]
    for out, blocks in zip(outs, places):
        for at, (block, chosen) in enumerate(blocks):
            value = keep[rows_of(block_owner(block), depth), :]
            if chosen:
                value = value.astype(F32)
                for other, begin in chosen:
                    value = value + arrived[other][begin * depth : (begin + 1) * depth, :].astype(F32)
            out[at * depth : (at + 1) * depth, :] = value.astype(BF16)


def join_kernel(mine, mine_x, other, other_x, *outs):
    half = mine.shape[1]
    at = 0
    for out in outs:
        rows = out.shape[0]
        for part, terms in enumerate(((mine, mine_x), (other, other_x))):
            values = [term[at : at + -(-rows // 16) * 16, :].astype(F32) for term in terms]
            out[:, part_at(part, half)] = (values[0] + values[1])[0:rows]
        at += -(-rows // 16) * 16


def pin_kernel(values, out):
    pass


def own_kernel(sizes, near, far, *outs):
    position, core, ours = lax.axis_index("fsdp"), lax.axis_index("core"), lax.axis_size("fsdp") // 2
    side, place, at = position // ours, lax.rem(position, ours), 0
    for index, length in enumerate(sizes):
        columns = pl.ds(pl.multiple_of(at + place * length, 128), length)
        for row, out in ((1, outs[2 * index]), (0, outs[2 * index + 1])):
            out[...] = jnp.where(side == core, near[row : row + 1, columns], far[row : row + 1, columns])
        at += ours * length


def back_input_kernel(slots, depth, begin, flat, grad, *refs):
    weights, refs = refs[:slots], refs[slots:]
    half = grad.shape[1]
    out, held = refs[-2:]
    rows = slice(begin, begin + held.shape[0])
    for slot in range(slots):
        columns = pl.ds(pl.multiple_of(block_owner(slot) * depth, 128), depth) if slots > 1 else slice(None)
        held[:, columns] = dot(flat[rows, :], weights[slot][0:depth, :], NT)
    columns = part_at(0, half)
    held[:, columns] = held[:, columns] + grad[rows, :]
    if len(refs) == 2:
        out[...] = held[...].astype(BF16)
        return
    far = refs[0]
    side = out.shape[1]

    def body(step):
        at = line_at(step)
        out[step // side, step % side] = (held[at, :] + far[at, :].astype(F32)).astype(BF16)[0:side]

    each_line(held.shape[0] // LINE, body)


def far_half_kernel(values, out):
    out[...] = values[:, part_at(1, out.shape[1])]


def image_kernel(keep, far, out):
    half, side = keep.shape[1], out.shape[1]

    def body(step):
        at = line_at(step)
        for part, values in enumerate((keep, far)):
            out[step // side, step % side, :, part_at(part, half)] = values[at, :][0:side]

    each_line(keep.shape[0] // LINE, body)


def pinned(values):
    anywhere = pl.BlockSpec(memory_space=pl.ANY)
    values = values.transpose(1, 2, 0, 3)
    values = pl.pallas_call(
        pin_kernel, out_shape=shape(values.shape, values.dtype), in_specs=[anywhere], out_specs=anywhere,
        input_output_aliases={0: 0}, compiler_params=pltpu.CompilerParams(vmem_limit_bytes=1 << 20), name="pin",
    )(values)
    return values.transpose(2, 0, 1, 3)


def swap_core(values):
    return lax.ppermute(values, "core", SWAP)


def swap_x(values):
    if lax.axis_size("x") == 2:
        return lax.ppermute(values, "x", SWAP)
    return (lax.psum(values.astype(F32), "x") - values.astype(F32)).astype(values.dtype)


def sum_chips(values, flips):
    got = []
    for flip in (*flips, 0):
        pairs = [(2 * at + core, 2 * (at ^ flip) + 1 - core) for at in range(16) for core in range(2)]
        got.append(lax.ppermute(values, (*CHIPS, "core"), pairs))
    got = together(*got)
    total = got[0]
    for other in got[1:]:
        total = total + other
    return total


def along(values, way):
    pairs = [(f * 2 + x, (f + 2 * way * (1 - 2 * x)) % 8 * 2 + x) for f in range(8) for x in range(2)]
    return lax.ppermute(values, CHIPS, pairs)


def across(values):
    return lax.ppermute(values, "fsdp", [(f, f ^ 1) for f in range(8)])


def halves(values, core):
    half = values.shape[1] // 2
    return lax.dynamic_slice_in_dim(values, core * half, half, 1)


def both(near, far, core):
    first, second = jnp.where(core == 0, near, far), jnp.where(core == 0, far, near)
    return jnp.concatenate([first, second], axis=-1)


def per_device(
    images,
    valid,
    cotangent,
    w_reduce,
    gain_one,
    shift_one,
    w_group,
    gain_two,
    shift_two,
    w_expand,
    gain_three,
    shift_three,
):
    count, side, _, channels = images.shape
    width = w_reduce.shape[1]
    inner = width // GROUPS
    size = lax.axis_size("fsdp")
    small = size == 8 and lax.axis_size("x") == 2
    position, core = lax.axis_index("fsdp"), lax.axis_index("core")
    rows = count * side * LINE
    per, outer, shard, depth = gain_one.shape[0], gain_three.shape[0], w_group.shape[0], w_reduce.shape[0]
    extra = -(-(shard + 2) // 16) * 16
    half, half_out = width // 2, channels // 2

    def plane_sum(values):
        return sum_chips(values, (1, 2, 3)) if small else lax.psum(values, CHIPS)

    def line_sum(values):
        return sum_chips(values, (4, 12, 8)) if small else values

    def everywhere(values):
        return line_sum(plane_sum(values))

    def padded(values):
        return jnp.pad(values, ((0, 0), (0, 0), (0, LINE - side), (0, 0))).reshape(rows, channels)

    vectors = (gain_one, shift_one, gain_two, shift_two, gain_three, shift_three)
    (own,) = call(
        pack_kernel, [shape((depth + extra, half), BF16)], [w_reduce, w_group, *vectors],
        anywhere=True, vmem=60, name="pack",
        scratch=[pltpu.VMEM((shard, width), BF16)] + [pltpu.VMEM(vector.shape, BF16) for vector in vectors]
        + [pltpu.SemaphoreType.DMA((8,))],
    )
    wide_shape = shape((TAPS, half // BLOCK, BLOCK, BLOCK), BF16)
    expand_own, x = halves(w_expand, core), padded(images)

    def turn(x, x_other, valid_other):
        valid_both = jnp.concatenate([valid, valid_other])
        turned, mask = call(
            functools.partial(turn_kernel, side),
            [shape((channels, 2 * rows), BF16), shape((2 * rows, LANES), F32)],
            [valid_both, x, x_other], scalars=1, name="turn",
        )
        return valid_both, turned, mask

    pixels, across_cores = 2 * rows, 2 * count

    def reduce_part(slots, last, depth, weights, *before):
        return call(
            functools.partial(reduce_kernel, slots, depth, side, last),
            [shape((pixels, half), F32), shape((3, half), F32)][: 1 + last],
            [valid_both, mask, x, x_other, *weights, *before], scalars=1, name="reduce", flops=2 * rows * width * channels,
        )

    if small:
        other = across(own)
        first = along(own, 1)
        x_other, valid_other = padded(swap_core(images)), swap_core(valid)
        first, other, x, x_other, expand_own = together(first, other, x, x_other, expand_own)
        passed, second, first_other = swap_x(first), along(first, 1), across(first)
        second, passed, first_other, valid_other = together(second, passed, first_other, valid_other)
        passed_other, second_other, expand_first = swap_x(first_other), across(second), along(expand_own, 1)
        valid_both, turned, mask = turn(x, x_other, valid_other)
        weights = [own, first, passed, second, other, first_other, passed_other, second_other]
        (before,) = reduce_part((0, 1, 2, 3, 4, 5), False, depth, weights[:6])
        turned, mask, before, *weights[6:] = together(turned, mask, before, *weights[6:])
        second, other = along(expand_first, 1), across(expand_own)
        slots, slot_depth = size, depth
    else:
        x_other, valid_other = swap_core(x), swap_core(valid)
        valid_both, turned, mask = turn(x, x_other, valid_other)
        whole = lax.all_gather(own, "fsdp", axis=0, tiled=False)
        weights = [whole[:, :depth].reshape(channels, half)]
        slots, slot_depth = 1, channels


    if small:
        red, part = reduce_part((6, 7), True, depth, weights[6:], before)
    else:
        red, part = reduce_part((None,), True, channels, weights)
    if small:
        wide, wide_turned, inner_vectors, outer_vectors = call(
            functools.partial(spread_kernel, slots, depth),
            [wide_shape, wide_shape, shape((4, half), F32), shape((2, half_out), F32)],
            weights,
            scratch=[pltpu.VMEM((size, extra, half), F32), pltpu.VMEM((size * shard, half), F32)],
            name="spread", flops=1 << 28,
        )
        middle, wide, wide_turned, inner_vectors, outer_vectors = together(
            plane_sum(part), wide, wide_turned, inner_vectors, outer_vectors
        )
        middle, second, other, expand_first = together(middle, second, other, expand_first)
        first_other, passed = across(expand_first), swap_x(expand_first)
        first = line_sum(middle)
        first, second = together(first, second)
        second_other, passed_other = across(second), swap_x(first_other)
    else:
        packed = whole[:, depth:]
        wide, wide_turned = call(
            widen_kernel, [wide_shape, wide_shape], [packed[:, :shard].reshape(size * shard, half)],
            scratch=[pltpu.VMEM((size * shard, half), F32)], name="widen",
        )
        line = packed[:, shard, : 4 * per].astype(F32).reshape(size, 4, per).transpose(1, 0, 2).reshape(4, width)
        inner_vectors = halves(line, core)
        line = packed[:, shard + 1, : 2 * outer].astype(F32).reshape(size, 2, outer).transpose(1, 0, 2)
        outer_vectors = halves(line.reshape(2, channels), core)
        first = everywhere(part)
    pad_shape = (3, across_cores, (side + 2) * LINE, half)
    pads, grouped, part = call(
        functools.partial(group_kernel, side),
        [shape(pad_shape, BF16), shape((pixels, half), F32), shape((2, half), F32)],
        [mask, first, inner_vectors, red, wide],
        name="group", flops=2 * TAPS * rows * width * BLOCK,
    )
    if small:
        part, passed = together(part, passed)
        middle = line_sum(part)
        middle, passed_other, second_other = together(middle, passed_other, second_other)
        blocks = (expand_own, expand_first, passed, second, other, first_other, passed_other, second_other)
        total_two = plane_sum(middle)
    else:
        total_two = everywhere(part)
    (act_mine,) = call(
        functools.partial(act_kernel, side), [shape((pixels, half), BF16)], [total_two, first, inner_vectors, grouped],
        name="act",
    )
    act_far = swap_core(act_mine)
    if small:
        act_mine, *blocks = together(act_mine, *blocks)
        (weight_three,) = call(assemble_kernel, [shape((width, half_out), BF16)], blocks, name="assemble")
    else:
        weight_three = lax.all_gather(expand_own, "fsdp", axis=0, tiled=True)
    act_two, expanded, part = call(
        expand_kernel,
        [shape((pixels, width), BF16), shape((pixels, half_out), F32), shape((2, half_out), F32)],
        [mask, act_mine, act_far, weight_three],
        name="expand", flops=2 * rows * width * channels,
    )
    cot = padded(after(cotangent, grouped))
    cot_far = swap_core(call(far_half_kernel, [shape((rows, half_out), BF16)], [cot], name="far_half")[0])
    middle, cot, cot_far = together(plane_sum(part), cot, cot_far)
    total_three = line_sum(middle)
    keep_out, send_out, grad_summed, part = call(
        functools.partial(output_kernel, side),
        [shape((rows, half_out), BF16), shape((rows, half_out), BF16), shape((pixels, half_out), F32),
         shape((2, half_out), F32)],
        [valid_both, total_three, first, outer_vectors, expanded, x, x_other, cot, cot_far], scalars=1, name="output",
    )

    sums_three = everywhere(part)
    flat_three, send = call(
        back_expand_kernel,
        [shape((pixels, half_out), BF16), shape((pixels, half), BF16)],
        [mask, total_three, sums_three, first, outer_vectors, grad_summed, expanded, weight_three],
        name="back_expand", flops=rows * width * channels,
    )
    far = swap_core(send)
    (mine,) = call(
        functools.partial(back_part_kernel, 0), [shape((pixels, half), F32)], [flat_three, weight_three],
        name="back_part", flops=rows * width * channels,
    )
    dz_two, part = call(
        back_act_kernel,
        [shape((pixels, half), F32), shape((2, half), F32)],
        [total_two, first, inner_vectors, mine, far, grouped], name="back_act",
    )
    (expand_term,) = call(
        weight_expand_kernel, [shape((width, half_out), BF16)], [after(act_two, part), flat_three],
        name="weight_expand", flops=2 * rows * width * channels,
    )
    far_out = swap_core(after(send_out, part))
    middle = plane_sum(part)

    def expand_sums(places, arrived=()):
        return call(
            functools.partial(expand_sum_kernel, places, w_expand.shape[0]),
            [shape((w_expand.shape[0] * len(blocks), half_out), BF16) for blocks in places],
            [expand_term] + list(arrived), name="expand_sum",
        )

    if small:
        middle, *moving = together(middle, *expand_sums((((6, ()), (2, ())), ((7, ()), (4, ())))))
        moving = [swap_x(moving[0]), across(moving[1])]
        sums_two = line_sum(middle)
    else:
        sums_two = line_sum(middle)
        own_expand = lax.psum_scatter(expand_term, "fsdp", scatter_dimension=0, tiled=True)
    flat_two, dz_one, part = call(
        functools.partial(back_group_kernel, side),
        [shape((pixels, half), BF16), shape((pixels, half), F32), shape((2, half), F32)],
        [mask, total_two, sums_two, first, inner_vectors, dz_two, grouped, red, wide_turned],
        scratch=[pltpu.VMEM(pad_shape, BF16)], name="back_group", flops=2 * TAPS * rows * width * BLOCK,
    )
    (group_term,) = call(
        functools.partial(weight_group_kernel, side, inner),
        [shape((size, extra, half), BF16)],
        [pads, after(flat_two, part)], scratch=[pltpu.VMEM((TAPS * inner, half), F32)], name="weight_group",
        flops=2 * TAPS * rows * width * BLOCK,
    )
    middle, group_term = together(plane_sum(part), group_term)
    if small:
        middle, *moving = together(middle, *moving)
        middle, expand_first_other, expand_second = together(middle, *expand_sums((((5, ((0, 0),)),), ((3, ((1, 0),)),)), moving))
        expand_first_other, expand_second = across(expand_first_other), along(expand_second, -1)
    sums_one = line_sum(middle)
    if small:
        sums_one, expand_first_other, expand_second = together(sums_one, expand_first_other, expand_second)
        expand_passed, expand_other = moving
        (expand_first_own,) = expand_sums((((1, ((0, 1), (1, 0), (2, 0))),),), (expand_passed, expand_first_other, expand_second))
    tall = depth + extra
    places = (6, 7) if small else tuple(range(size))
    flat_one, *moving = call(
        functools.partial(back_reduce_kernel, small, places),
        [shape((pixels, half), BF16)] + [shape((tall, half), BF16)] * len(places),
        [mask, first, sums_one, inner_vectors, dz_one, red, turned, group_term],
        name="back_reduce", flops=2 * rows * depth * width * len(places),
    )

    def terms_of(places):
        return call(
            functools.partial(block_sum_kernel, small, places),
            [shape((tall, half), F32)] * len(places),
            [turned, group_term, flat_one],
            name="block_sum", flops=2 * rows * depth * width * len(places),
        )

    def sums(terms, *arrived):
        numbers = tuple(len(some) for some in arrived)
        return call(
            functools.partial(arrived_kernel, numbers), [shape((tall, half), BF16)] * len(terms),
            [*terms, *(value for some in arrived for value in some)], name="arrived",
        )

    def back_input(begin, flat, *far):
        out = shape(images.shape, BF16) if far else shape((rows, channels), BF16)
        return call(
            functools.partial(back_input_kernel, slots, slot_depth, begin),
            [out], [flat, grad_summed, *weights, *far],
            scratch=[pltpu.VMEM((rows, channels), F32)], name="back_input", flops=rows * width * channels,
        )[0]

    def own_shards(totals):
        near = jnp.concatenate(totals, axis=1)
        far = swap_core(near)
        lengths = (per, per, outer)
        if small:
            outs = call(
                functools.partial(own_kernel, lengths), [shape((1, n), F32) for n in lengths for _ in range(2)], [near, far],
                name="own",
            )
            return [out.reshape(-1) for out in outs]
        cut, at = [], 0
        for total, length in zip(totals, lengths):
            whole = both(total, far[:, at : at + total.shape[1]], core)
            at += total.shape[1]
            cut += [lax.dynamic_slice_in_dim(whole[row], position * length, length, 0) for row in (1, 0)]
        return cut

    def image_of(far_out):
        return call(image_kernel, [shape(images.shape, BF16)], [keep_out, far_out], name="image")[0]

    def join(own, far, outs):
        return call(
            join_kernel, [shape(out.shape, F32) for out in outs], [own, far, swap_core(own), swap_core(far)], name="join"
        )

    if small:
        moving[1], expand_first_own = together(moving[1], expand_first_own)
        moving = [swap_x(moving[0]), across(moving[1])]
        expand_first_own = along(expand_first_own, -1)
        terms = terms_of((5, 2, 3, 1, 4, 0))
        shards = own_shards([sums_one, sums_two, sums_three])
        moving[0], expand_first_own, *shards = together(moving[0], expand_first_own, *shards)
        (own_expand,) = expand_sums((((0, ((0, 0), (1, 1))),),), [expand_first_own, expand_other])
        first_other, passed, second = sums(terms[0:3], moving[0:1], (), moving[1:2])
        moving = [swap_x(passed), along(second, -1), across(first_other)]
        far_input = swap_core(after(back_input(rows, flat_one), second))
        output = pinned(image_of(after(far_out, second)))
        moving[0], output = together(moving[0], output)
        first_own, other = sums(terms[3:5], moving, ())
        moving = [along(first_own, -1), across(other)]
        grad_input, own_expand = pinned(back_input(0, after(flat_one, first_own), far_input)), after(own_expand, first_own)
        far_expand = swap_x(own_expand)
        moving[0], grad_input, far_expand = together(moving[0], grad_input, far_expand)
        (own_reduce,) = sums(terms[5:6], moving)
        own_expand, far_expand = after(own_expand, own_reduce), after(far_expand, own_reduce)
        (grad_w_expand,) = join(own_expand, far_expand, [w_expand])
        far_reduce, grad_w_expand = together(swap_x(own_reduce), grad_w_expand)
    else:
        grad_input, output = back_input(0, flat_one, swap_core(back_input(rows, flat_one))), image_of(far_out)
        shards = own_shards([sums_one, sums_two, sums_three])
        whole = jnp.stack(moving).reshape(size * tall, half)
        own_reduce = lax.psum_scatter(whole, "fsdp", scatter_dimension=0, tiled=True)
        (grad_w_expand,) = join(own_expand, swap_x(own_expand), [w_expand])
        far_reduce = swap_x(own_reduce)
    grad_w_reduce, grad_w_group = join(own_reduce, far_reduce, [w_reduce, w_group])
    return (output, grad_input, grad_w_reduce, grad_w_group, grad_w_expand) + tuple(shards)


def solution(mesh):
    fsdp, dp = mesh.shape["fsdp"], mesh.shape["dp"]
    split = Mesh(mesh.devices.reshape(fsdp, dp // 2, 2), ("fsdp", "x", "core"))
    images, rows, vector = P(("fsdp", "x", "core"), None, None, None), P("fsdp", None), P("fsdp")
    return jax.shard_map(
        per_device,
        mesh=split,
        in_specs=(
            images, P(("fsdp", "x", "core")), images,
            rows, vector, vector, rows, vector, vector, rows, vector, vector,
        ),
        out_specs=(images, images, rows, rows, rows) + (vector,) * 6,
        check_vma=False,
    )
```

```python
import functools

import jax
import jax.numpy as jnp
from jax import lax
from jax.experimental import pallas as pl
from jax.experimental.pallas import tpu as pltpu
from jax.sharding import Mesh
from jax.sharding import PartitionSpec as P

GROUPS = 32
TAPS = 9
LINE = 16
CHUNK = 512
UNROLL = 7
LANES = 128
BLOCK = 256
epsilon = 1e-05
BF16, F32 = jnp.bfloat16, jnp.float32
SWAP = [(0, 1), (1, 0)]
NN, NT = ((1,), (0,)), ((1,), (1,))
CHIPS = ("fsdp", "x")


def silu_half(half):
    return half + half * jnp.tanh(half)


def dsilu_twice(half):
    turned = jnp.tanh(half)
    upper = 1.0 + turned
    return upper * (1.0 + half * (1.0 - turned)), upper


def dot(a, b, contract=NN):
    return lax.dot_general(a, b, (contract, ((), ())), preferred_element_type=F32)


def after(values, *others):
    return lax.optimization_barrier((values,) + others)[0]


def together(*values):
    return lax.optimization_barrier(values)


def shape(dims, dtype):
    return jax.ShapeDtypeStruct(dims, dtype)


def call(kernel, outs, args, scalars=0, scratch=(), vmem=8, name=None, flops=0, anywhere=False, aliases=()):
    vm = pl.BlockSpec(memory_space=pltpu.VMEM)
    given = pl.BlockSpec(memory_space=pl.ANY) if anywhere else vm
    sm = pl.BlockSpec(memory_space=pltpu.SMEM)
    return pl.pallas_call(
        kernel,
        out_shape=outs,
        in_specs=[sm] * scalars + [given] * (len(args) - scalars),
        out_specs=[vm] * len(outs),
        scratch_shapes=list(scratch),
        compiler_params=pltpu.CompilerParams(vmem_limit_bytes=vmem << 20),
        cost_estimate=pl.CostEstimate(flops=0, bytes_accessed=0, transcendentals=0),
        input_output_aliases=dict(aliases),
        name=name,
    )(*args)


def moments(total, pixels):
    mean = total[0:1, :] / pixels
    inverse = lax.rsqrt(total[1:2, :] / pixels - mean * mean + epsilon)
    return mean, inverse


def chunks(columns):
    return [slice(at, min(at + CHUNK, columns)) for at in range(0, columns, CHUNK)]


def line_mask(columns, side):
    return lax.broadcasted_iota(jnp.int32, (LINE, columns), 0) < side


def each_line(lines, body):
    lax.fori_loop(0, lines, lambda step, none: body(step) or none, 0, unroll=UNROLL)


def each_line_summed(lines, width, body):
    zero = jnp.zeros((8, width), F32)

    def step_sums(step, carry):
        one, two = body(step)
        return carry[0] + fold(one), carry[1] + fold(two)

    one, two = lax.fori_loop(0, lines, step_sums, (zero, zero), unroll=UNROLL)
    return column_sums(one), column_sums(two)


def across_lanes(mask, columns):
    return jnp.concatenate([mask] * (columns // LANES), axis=1)


def column_sums(values):
    return jnp.sum(values, axis=0, keepdims=True)


def line_at(step):
    return pl.ds(pl.multiple_of(step * LINE, LINE), LINE)


def fold(values):
    return values[0:8] + values[8:16]


def part_at(part, half, at=0, length=None):
    core = lax.axis_index("core")
    side = core if part == 0 else 1 - core
    length = half if length is None else length
    return pl.ds(pl.multiple_of(side * half + at, 128), length)


def block_owner(slot):
    position = lax.axis_index("fsdp")
    way = 1 - 2 * lax.axis_index("x")
    step = (0, -way, way, 2)[slot % 4]
    owner = lax.rem(position + 2 * step + 8, 8)
    return owner if slot < 4 else owner + 1 - 2 * lax.rem(owner, 2)


def rows_of(owner, depth):
    return pl.ds(pl.multiple_of(owner * depth, 16), depth)


def pack_kernel(weight, group, *refs):
    vectors, (out, held, *rows, sems) = refs[:6], refs[6:]
    depth, half = weight.shape[0], out.shape[1]
    shard, extra = group.shape[0], out.shape[0] - weight.shape[0]
    columns = part_at(0, half)
    copies = [pltpu.make_async_copy(group, held, sems.at[0])]
    copies += [pltpu.make_async_copy(vector, row, sems.at[2 + at]) for at, (vector, row) in enumerate(zip(vectors, rows))]
    copies.append(pltpu.make_async_copy(weight.at[:, columns], out.at[pl.ds(0, depth)], sems.at[1]))
    for copy in copies:
        copy.start()
    for copy in copies[:-1]:
        copy.wait()
    below = [held[:, columns].astype(F32)]
    for begin, end in ((0, 4), (4, 6)):
        line = [row[...].astype(F32).reshape(1, row.shape[0]) for row in rows[begin:end]]
        missing = half - sum(piece.shape[1] for piece in line)
        below.append(jnp.concatenate(line + ([jnp.zeros((1, missing), F32)] if missing else []), axis=1))
    if extra > shard + 2:
        below.append(jnp.zeros((extra - shard - 2, half), F32))
    out[depth : depth + extra, :] = jnp.concatenate(below, axis=0).astype(BF16)
    copies[-1].wait()


def mask_kernel(side, valid, mask):
    images = valid.shape[0]
    rows = mask.shape[0] // images
    inside = lax.broadcasted_iota(jnp.int32, (rows, LANES), 0) % LINE < side
    for image in range(images):
        mask[image * rows : (image + 1) * rows, :] = jnp.where(inside, valid[image].astype(F32), 0.0)


def turn_kernel(x, x_other, turned):
    rows = x.shape[0]
    turned[:, 0:rows] = x[...].T
    turned[:, rows : 2 * rows] = x_other[...].T


def reduce_kernel(slots, depth, side, last, valid, mask, x, x_other, *refs):
    weights, refs = refs[: len(slots)], refs[len(slots) :]
    before, red = (None, refs[0]) if len(refs) == 1 + last else refs[:2]
    half, rows = red.shape[1], x.shape[0]
    for at in range(0, half, BLOCK):
        sums = [0.0, 0.0]
        for begin, pixels in ((0, x), (rows, x_other)):
            here = (slice(begin, begin + rows), slice(at, at + BLOCK))
            total = None if before is None else before[here]
            for slot, weight in zip(slots, weights):
                if slot is None:
                    piece = pixels[...]
                else:
                    piece = pixels[:, pl.ds(pl.multiple_of(block_owner(slot) * depth, 128), depth)]
                term = dot(piece, weight[0:depth, at : at + BLOCK])
                total = term if total is None else total + term
            red[here] = total
            if last:
                masked = total * across_lanes(mask[begin : begin + rows, :], BLOCK)
                sums = [sums[0] + column_sums(masked), sums[1] + column_sums(masked * total)]
        if last:
            refs[-1][0:1, at : at + BLOCK] = sums[0]
            refs[-1][1:2, at : at + BLOCK] = sums[1]
    if last:
        pixels = valid[0].astype(F32)
        for image in range(1, valid.shape[0]):
            pixels = pixels + valid[image].astype(F32)
        refs[-1][2:3, :] = jnp.full((1, half), 1.0, F32) * (pixels * (side * side))


def spread_kernel(slots, depth, *refs):
    blocks, (wide, wide_turned, inner_vectors, outer_vectors, held, rows) = refs[:slots], refs[slots:]
    extra = held.shape[1]
    for slot in range(slots):
        held[block_owner(slot)] = blocks[slot][depth : depth + extra, :].astype(F32)
    shard, ours = rows.shape[0] // slots, slots // 2
    per, outer = inner_vectors.shape[1] // ours, outer_vectors.shape[1] // ours
    core = lax.axis_index("core")
    for owner in range(slots):
        rows[owner * shard : (owner + 1) * shard, :] = held[owner, 0:shard, :]
    for at in range(ours):
        owner = core * ours + at
        for row in range(4):
            inner_vectors[row : row + 1, at * per : (at + 1) * per] = held[
                owner, shard : shard + 1, row * per : (row + 1) * per
            ]
        for row in range(2):
            outer_vectors[row : row + 1, at * outer : (at + 1) * outer] = held[
                owner, shard + 1 : shard + 2, row * outer : (row + 1) * outer
            ]
    widen(rows, wide, wide_turned)


def widen_kernel(weight, wide, wide_turned, rows):
    rows[...] = weight[...].astype(F32)
    widen(rows, wide, wide_turned)


def widen(weight, wide, wide_turned):
    taps, blocks = wide.shape[:2]
    inner = weight.shape[0] // taps
    row = lax.broadcasted_iota(jnp.int32, (BLOCK, BLOCK), 0) // inner
    column = lax.broadcasted_iota(jnp.int32, (BLOCK, BLOCK), 1) // inner
    own = row == column
    for tap in range(taps):
        for block in range(blocks):
            piece = weight[tap * inner : (tap + 1) * inner, block * BLOCK : (block + 1) * BLOCK]
            tall = jnp.concatenate([piece] * (BLOCK // inner), axis=0)
            dense = jnp.where(own, tall, 0.0)
            wide[tap, block] = dense.astype(BF16)
            wide_turned[tap, block] = dense.T.astype(BF16)


def fill_pads(pads, columns, image, line, values):
    rows = pl.ds(pl.multiple_of((line + 1) * LINE, LINE), LINE)
    pads[0, image, rows, columns] = pltpu.roll(values, 1, 0).astype(BF16)
    pads[1, image, rows, columns] = values.astype(BF16)
    pads[2, image, rows, columns] = pltpu.roll(values, LINE - 1, 0).astype(BF16)


def clear_pads(pads):
    images, rows, columns = pads.shape[1:]
    zeros = jnp.zeros((3, images, LINE, columns), BF16)
    pads[:, :, 0:LINE, :] = zeros
    pads[:, :, rows - LINE : rows, :] = zeros


def convolve(pads, wide, image, block, rows, turned=False):
    columns = slice(block * BLOCK, (block + 1) * BLOCK)
    value = None
    for tap in range(TAPS):
        top, left = divmod(TAPS - 1 - tap if turned else tap, 3)
        piece = pads[left, image, top * LINE : top * LINE + rows, columns]
        term = dot(piece, wide[tap, block])
        value = term if value is None else value + term
    return value


def group_kernel(side, mask, total, vectors, red, wide, pads, grouped, stats):
    images, padded, width = pads.shape[1:]
    rows = side * LINE
    mean, inverse = moments(total, total[2:3, :])
    scale, bias = 0.5 * inverse * vectors[0:1, :], 0.5 * vectors[1:2, :]
    clear_pads(pads)
    for part in chunks(width):
        inside = line_mask(part.stop - part.start, side)

        def body(step):
            half = (red[line_at(step), part] - mean[:, part]) * scale[:, part] + bias[:, part]
            fill_pads(pads, part, step // side, step % side, jnp.where(inside, silu_half(half), 0.0))

        each_line(images * side, body)
    for block in range(width // BLOCK):
        columns = slice(block * BLOCK, (block + 1) * BLOCK)
        sums = [0.0, 0.0]
        for image in range(images):
            at = slice(image * rows, (image + 1) * rows)
            value = convolve(pads, wide, image, block, rows)
            grouped[at, columns] = value
            masked = value * across_lanes(mask[at, :], BLOCK)
            sums = [sums[0] + column_sums(masked), sums[1] + column_sums(masked * value)]
        stats[0:1, columns] = sums[0]
        stats[1:2, columns] = sums[1]


def act_kernel(side, total, first, vectors, grouped, act):
    rows, width = grouped.shape
    mean, inverse = moments(total, first[2:3, :])
    scale, bias = 0.5 * inverse * vectors[2:3, :], 0.5 * vectors[3:4, :]
    for part in chunks(width):
        inside = line_mask(part.stop - part.start, side)

        def body(step):
            at = line_at(step)
            half = (grouped[at, part] - mean[:, part]) * scale[:, part] + bias[:, part]
            act[at, part] = jnp.where(inside, silu_half(half), 0.0).astype(BF16)

        each_line(rows // LINE, body)


def assemble_kernel(*refs):
    blocks, out = refs[:-1], refs[-1]
    depth = blocks[0].shape[0]
    for slot, block in enumerate(blocks):
        out[rows_of(block_owner(slot), depth), :] = block[...]


def expand_kernel(mask, act_mine, act_far, weight, act, expanded, stats):
    rows, half = act_mine.shape
    middle = rows // 2
    act[:, part_at(0, half)] = act_mine[...]
    act[0:middle, part_at(1, half)] = act_far[middle:rows, :]
    act[middle:rows, part_at(1, half)] = act_far[0:middle, :]
    for at in range(0, weight.shape[1], BLOCK):
        sums = [0.0, 0.0]
        for begin in (0, middle):
            here = slice(begin, begin + middle)
            value = dot(act[here, :], weight[:, at : at + BLOCK])
            expanded[here, at : at + BLOCK] = value
            masked = value * across_lanes(mask[here, :], BLOCK)
            sums = [sums[0] + column_sums(masked), sums[1] + column_sums(masked * value)]
        stats[0:1, at : at + BLOCK] = sums[0]
        stats[1:2, at : at + BLOCK] = sums[1]


def output_kernel(
    side, valid, total, first, vectors, expanded, x, x_other, cotangent, cotangent_far, keep_out, send_out, grad, stats
):
    rows, channels = expanded.shape
    middle = rows // 2
    mean, inverse = moments(total, first[2:3, 0:1])
    scale, bias = inverse * vectors[0:1, :], vectors[1:2, :]
    for part in chunks(channels):
        length = part.stop - part.start
        whole = part_at(0, channels, part.start, length)
        ends = []
        for begin, pixels, incoming, columns, out in (
            (0, x, cotangent, whole, keep_out), (middle, x_other, cotangent_far, part, send_out)
        ):

            def body(step):
                at = line_at(step)
                here = pl.ds(pl.multiple_of(begin + step * LINE, LINE), LINE)
                keep = 0.5 * valid[(begin // LINE + step) // side].astype(F32)
                centered = expanded[here, part] - mean[:, part]
                half = (centered * scale[:, part] + (bias[:, part] + pixels[at, whole].astype(F32))) * keep
                slope, upper = dsilu_twice(half)
                out[at, part] = (half * upper).astype(BF16)
                value = incoming[at, columns].astype(F32) * keep * slope
                grad[here, part] = value
                return value, value * centered

            ends.append(each_line_summed(middle // LINE, length, body))
        stats[0:1, part] = ends[0][0] + ends[1][0]
        stats[1:2, part] = (ends[0][1] + ends[1][1]) * inverse[:, part]


def back_expand_kernel(mask, total, sums, first, vectors, grad, expanded, weight, flat, send):
    rows, channels = expanded.shape
    pixels = first[2:3, 0:1]
    mean, inverse = moments(total, pixels)
    scale = inverse * vectors[0:1, :]
    shifted, scaled = scale * sums[0:1, :] / pixels, scale * inverse * sums[1:2, :] / pixels
    for part in chunks(channels):

        def body(step):
            at = line_at(step)
            common = shifted[:, part] + (expanded[at, part] - mean[:, part]) * scaled[:, part]
            counted = across_lanes(mask[at, :], part.stop - part.start)
            flat[at, part] = (scale[:, part] * grad[at, part] - counted * common).astype(BF16)

        each_line(rows // LINE, body)
    back_part_kernel(1, flat, weight, send)


def back_part_kernel(part, flat, weight, out):
    half = out.shape[1]
    for at in range(0, half, BLOCK):
        rows = pl.ds(pl.multiple_of(part_at(part, half).start + at, BLOCK), BLOCK)
        out[:, at : at + BLOCK] = dot(flat[...], weight[rows, :], NT).astype(out.dtype)


def back_act_kernel(total, first, vectors, mine, far, grouped, dz, stats):
    mean, inverse = moments(total, first[2:3, :])
    lines = grouped.shape[0] // LINE

    def gradient(step, part):
        there = lax.rem(step + lines // 2, lines)
        return mine[line_at(step), part] + far[line_at(there), part].astype(F32)

    before_norm(dz, gradient, grouped, mean, inverse, vectors[2:3, :], vectors[3:4, :], stats)


def before_norm(dz, gradient, hidden, mean, inverse, gain, shift, stats, side=None):
    scale, bias = 0.5 * inverse * gain, 0.5 * shift
    rows, width = hidden.shape
    for part in chunks(width):
        inside = None if side is None else line_mask(part.stop - part.start, side)

        def body(step):
            at = line_at(step)
            centered = hidden[at, part] - mean[:, part]
            slope, _ = dsilu_twice(centered * scale[:, part] + bias[:, part])
            here = gradient(step, part) * slope
            if side is not None:
                here = jnp.where(inside, here, 0.0)
            dz[at, part] = here
            return here, here * centered

        one, two = each_line_summed(rows // LINE, part.stop - part.start, body)
        stats[0:1, part] = 0.5 * one
        stats[1:2, part] = 0.5 * inverse[:, part] * two


def weight_expand_kernel(act, flat, out):
    turned = act[...].T
    for at in range(0, out.shape[1], BLOCK):
        out[:, at : at + BLOCK] = dot(turned, flat[:, at : at + BLOCK]).astype(BF16)


def back_group_kernel(
    side, mask, total, sums, first, vectors, dz, grouped, red, wide, flat, dz_one, stats, pads
):
    images, padded, width = pads.shape[1:]
    rows = side * LINE
    pixels = first[2:3, :]
    mean, inverse = moments(total, pixels)
    scale = inverse * vectors[2:3, :]
    shifted, scaled = scale * sums[0:1, :] / pixels, scale * inverse * sums[1:2, :] / pixels
    scale = 0.5 * scale
    clear_pads(pads)
    for part in chunks(width):

        def body(step):
            at = line_at(step)
            common = shifted[:, part] + (grouped[at, part] - mean[:, part]) * scaled[:, part]
            value = scale[:, part] * dz[at, part] - across_lanes(mask[at, :], part.stop - part.start) * common
            flat[at, part] = value.astype(BF16)
            fill_pads(pads, part, step // side, step % side, value)

        each_line(images * side, body)
    for block in range(width // BLOCK):
        columns = slice(block * BLOCK, (block + 1) * BLOCK)
        for image in range(images):
            dz_one[image * rows : (image + 1) * rows, columns] = convolve(pads, wide, image, block, rows, True)
    mean_one, inverse_one = moments(first, pixels)

    def gradient(step, part):
        return dz_one[line_at(step), part]

    before_norm(dz_one, gradient, red, mean_one, inverse_one, vectors[0:1, :], vectors[1:2, :], stats, side)


def weight_group_kernel(side, inner, pads, flat, out, held):
    images, padded, width = pads.shape[1:]
    rows = side * LINE
    row = lax.broadcasted_iota(jnp.int32, (LANES, LANES), 0) // inner
    column = lax.broadcasted_iota(jnp.int32, (LANES, LANES), 1) // inner
    own = row == column
    for at in range(0, width, LANES):
        columns = slice(at, at + LANES)
        moved = []
        for tap in range(TAPS):
            top, left = divmod(tap, 3)
            pieces = [pads[left, image, top * LINE : top * LINE + rows, columns] for image in range(images)]
            moved.append(jnp.concatenate(pieces, axis=0))
        product = dot(flat[:, columns].T, jnp.concatenate(moved, axis=1))
        for tap in range(TAPS):
            kept = jnp.where(own, product[:, tap * LANES : (tap + 1) * LANES].T, 0.0)
            value = kept[0:inner]
            for begin in range(inner, LANES, inner):
                value = value + kept[begin : begin + inner]
            held[tap * inner : (tap + 1) * inner, columns] = value
    owners, extra = out.shape[:2]
    shard = TAPS * inner // owners
    zeros = jnp.zeros((extra - shard, width), F32)
    for owner in range(owners):
        rows_here = held[owner * shard : (owner + 1) * shard, :]
        out[owner] = jnp.concatenate([rows_here, zeros], axis=0).astype(BF16)


def back_reduce_kernel(small, places, mask, first, sums, vectors, dz, red, turned, group, flat, *outs):
    rows, width = red.shape
    pixels = first[2:3, :]
    mean, inverse = moments(first, pixels)
    scale = inverse * vectors[0:1, :]
    shifted, scaled = scale * sums[0:1, :] / pixels, scale * inverse * sums[1:2, :] / pixels
    scale = 0.5 * scale
    for part in chunks(width):

        def body(step):
            at = line_at(step)
            common = shifted[:, part] + (red[at, part] - mean[:, part]) * scaled[:, part]
            counted = across_lanes(mask[at, :], part.stop - part.start)
            flat[at, part] = (scale[:, part] * dz[at, part] - counted * common).astype(BF16)

        each_line(rows // LINE, body)
    block_sum_kernel(small, places, turned, group, flat, *outs)


def block_sum_kernel(small, places, turned, group, flat, *outs):
    tall, half = outs[0].shape
    depth = tall - group.shape[1]
    for out, block in zip(outs, places):
        owner = block_owner(block) if small else block
        out[0:depth, :] = dot(turned[rows_of(owner, depth), :], flat[...]).astype(out.dtype)
        out[depth:tall, :] = group[owner].astype(out.dtype)


def arrived_kernel(numbers, *refs):
    terms, arrived, outs = refs[: len(numbers)], refs[len(numbers) : -len(numbers)], refs[-len(numbers) :]
    at = 0
    for out, term, number in zip(outs, terms, numbers):
        value = term[...]
        for other in arrived[at : at + number]:
            value = value + other[...].astype(F32)
        out[...] = value.astype(BF16)
        at += number


def expand_sum_kernel(places, depth, keep, *refs):
    arrived, outs = refs[: len(refs) - len(places)], refs[len(refs) - len(places) :]
    for out, blocks in zip(outs, places):
        for at, (block, chosen) in enumerate(blocks):
            value = keep[rows_of(block_owner(block), depth), :]
            if chosen:
                value = value.astype(F32)
                for other, begin in chosen:
                    value = value + arrived[other][begin * depth : (begin + 1) * depth, :].astype(F32)
            out[at * depth : (at + 1) * depth, :] = value.astype(BF16)


def join_kernel(mine, mine_x, other, other_x, *outs):
    half = mine.shape[1]
    at = 0
    for out in outs:
        rows = out.shape[0]
        for part, terms in enumerate(((mine, mine_x), (other, other_x))):
            values = [term[at : at + -(-rows // 16) * 16, :].astype(F32) for term in terms]
            out[:, part_at(part, half)] = (values[0] + values[1])[0:rows]
        at += -(-rows // 16) * 16


def pin_kernel(values, out):
    pass


def own_kernel(sizes, near, far, *outs):
    position, core, ours = lax.axis_index("fsdp"), lax.axis_index("core"), lax.axis_size("fsdp") // 2
    side, place, at = position // ours, lax.rem(position, ours), 0
    for index, length in enumerate(sizes):
        columns = pl.ds(pl.multiple_of(at + place * length, 128), length)
        for row, out in ((1, outs[2 * index]), (0, outs[2 * index + 1])):
            out[...] = jnp.where(side == core, near[row : row + 1, columns], far[row : row + 1, columns])
        at += ours * length


def back_input_kernel(slots, depth, begin, flat, grad, *refs):
    weights, refs = refs[:slots], refs[slots:]
    half = grad.shape[1]
    out, held = refs[-2:]
    rows = slice(begin, begin + held.shape[0])
    for slot in range(slots):
        columns = pl.ds(pl.multiple_of(block_owner(slot) * depth, 128), depth) if slots > 1 else slice(None)
        held[:, columns] = dot(flat[rows, :], weights[slot][0:depth, :], NT)
    columns = part_at(0, half)
    held[:, columns] = held[:, columns] + grad[rows, :]
    if len(refs) == 2:
        out[...] = held[...].astype(BF16)
        return
    far = refs[0]
    side = out.shape[1]

    def body(step):
        at = line_at(step)
        out[step // side, step % side] = (held[at, :] + far[at, :].astype(F32)).astype(BF16)[0:side]

    each_line(held.shape[0] // LINE, body)


def far_half_kernel(values, out):
    out[...] = values[:, part_at(1, out.shape[1])]


def image_kernel(keep, far, out):
    half, side = keep.shape[1], out.shape[1]

    def body(step):
        at = line_at(step)
        for part, values in enumerate((keep, far)):
            out[step // side, step % side, :, part_at(part, half)] = values[at, :][0:side]

    each_line(keep.shape[0] // LINE, body)


def pinned(values):
    anywhere = pl.BlockSpec(memory_space=pl.ANY)
    values = values.transpose(1, 2, 0, 3)
    values = pl.pallas_call(
        pin_kernel, out_shape=shape(values.shape, values.dtype), in_specs=[anywhere], out_specs=anywhere,
        input_output_aliases={0: 0}, compiler_params=pltpu.CompilerParams(vmem_limit_bytes=1 << 20), name="pin",
    )(values)
    return values.transpose(2, 0, 1, 3)


def swap_core(values):
    return lax.ppermute(values, "core", SWAP)


def swap_x(values):
    if lax.axis_size("x") == 2:
        return lax.ppermute(values, "x", SWAP)
    return (lax.psum(values.astype(F32), "x") - values.astype(F32)).astype(values.dtype)


def sum_chips(values, flips):
    got = []
    for flip in (*flips, 0):
        pairs = [(2 * at + core, 2 * (at ^ flip) + 1 - core) for at in range(16) for core in range(2)]
        got.append(lax.ppermute(values, (*CHIPS, "core"), pairs))
    got = together(*got)
    total = got[0]
    for other in got[1:]:
        total = total + other
    return total


def along(values, way):
    pairs = [(f * 2 + x, (f + 2 * way * (1 - 2 * x)) % 8 * 2 + x) for f in range(8) for x in range(2)]
    return lax.ppermute(values, CHIPS, pairs)


def across(values):
    return lax.ppermute(values, "fsdp", [(f, f ^ 1) for f in range(8)])


def halves(values, core):
    half = values.shape[1] // 2
    return lax.dynamic_slice_in_dim(values, core * half, half, 1)


def both(near, far, core):
    first, second = jnp.where(core == 0, near, far), jnp.where(core == 0, far, near)
    return jnp.concatenate([first, second], axis=-1)


def per_device(
    images,
    valid,
    cotangent,
    w_reduce,
    gain_one,
    shift_one,
    w_group,
    gain_two,
    shift_two,
    w_expand,
    gain_three,
    shift_three,
):
    count, side, _, channels = images.shape
    width = w_reduce.shape[1]
    inner = width // GROUPS
    size = lax.axis_size("fsdp")
    small = size == 8 and lax.axis_size("x") == 2
    position, core = lax.axis_index("fsdp"), lax.axis_index("core")
    rows = count * side * LINE
    per, outer, shard, depth = gain_one.shape[0], gain_three.shape[0], w_group.shape[0], w_reduce.shape[0]
    extra = -(-(shard + 2) // 16) * 16
    half, half_out = width // 2, channels // 2

    def plane_sum(values):
        return sum_chips(values, (1, 2, 3)) if small else lax.psum(values, CHIPS)

    def line_sum(values):
        return sum_chips(values, (4, 12, 8)) if small else values

    def everywhere(values):
        return line_sum(plane_sum(values))

    def padded(values):
        return jnp.pad(values, ((0, 0), (0, 0), (0, LINE - side), (0, 0))).reshape(rows, channels)

    vectors = (gain_one, shift_one, gain_two, shift_two, gain_three, shift_three)
    (own,) = call(
        pack_kernel, [shape((depth + extra, half), BF16)], [w_reduce, w_group, *vectors],
        anywhere=True, vmem=60, name="pack",
        scratch=[pltpu.VMEM((shard, width), BF16)] + [pltpu.VMEM(vector.shape, BF16) for vector in vectors]
        + [pltpu.SemaphoreType.DMA((8,))],
    )
    wide_shape = shape((TAPS, half // BLOCK, BLOCK, BLOCK), BF16)
    expand_own, x = halves(w_expand, core), padded(images)

    def mask_of(valid_other):
        valid_both = jnp.concatenate([valid, valid_other])
        (mask,) = call(
            functools.partial(mask_kernel, side), [shape((2 * rows, LANES), F32)], [valid_both], scalars=1, name="mask"
        )
        return valid_both, mask

    pixels, across_cores = 2 * rows, 2 * count

    def reduce_part(slots, last, depth, weights, *before):
        return call(
            functools.partial(reduce_kernel, slots, depth, side, last),
            [shape((pixels, half), F32), shape((3, half), F32)][: 1 + last],
            [valid_both, mask, x, x_other, *weights, *before], scalars=1, name="reduce", flops=2 * rows * width * channels,
        )

    if small:
        other = across(own)
        first = along(own, 1)
        x_other, valid_other = padded(swap_core(images)), swap_core(valid)
        first, other, x, x_other, expand_own = together(first, other, x, x_other, expand_own)
        passed, second, first_other = swap_x(first), along(first, 1), across(first)
        second, passed, first_other, valid_other = together(second, passed, first_other, valid_other)
        passed_other, second_other, expand_first = swap_x(first_other), across(second), along(expand_own, 1)
        valid_both, mask = mask_of(valid_other)
        weights = [own, first, passed, second, other, first_other, passed_other, second_other]
        (before,) = reduce_part((0, 1, 2, 3, 4, 5), False, depth, weights[:6])
        mask, before, *weights[6:] = together(mask, before, *weights[6:])
        second, other = along(expand_first, 1), across(expand_own)
        slots, slot_depth = size, depth
    else:
        x_other, valid_other = swap_core(x), swap_core(valid)
        valid_both, mask = mask_of(valid_other)
        whole = lax.all_gather(own, "fsdp", axis=0, tiled=False)
        weights = [whole[:, :depth].reshape(channels, half)]
        slots, slot_depth = 1, channels


    if small:
        red, part = reduce_part((6, 7), True, depth, weights[6:], before)
    else:
        red, part = reduce_part((None,), True, channels, weights)
    if small:
        wide, wide_turned, inner_vectors, outer_vectors = call(
            functools.partial(spread_kernel, slots, depth),
            [wide_shape, wide_shape, shape((4, half), F32), shape((2, half_out), F32)],
            weights,
            scratch=[pltpu.VMEM((size, extra, half), F32), pltpu.VMEM((size * shard, half), F32)],
            name="spread", flops=1 << 28,
        )
        middle, wide, wide_turned, inner_vectors, outer_vectors = together(
            plane_sum(part), wide, wide_turned, inner_vectors, outer_vectors
        )
        middle, second, other, expand_first = together(middle, second, other, expand_first)
        first_other, passed = across(expand_first), swap_x(expand_first)
        first = line_sum(middle)
        first, second = together(first, second)
        second_other, passed_other = across(second), swap_x(first_other)
    else:
        packed = whole[:, depth:]
        wide, wide_turned = call(
            widen_kernel, [wide_shape, wide_shape], [packed[:, :shard].reshape(size * shard, half)],
            scratch=[pltpu.VMEM((size * shard, half), F32)], name="widen",
        )
        line = packed[:, shard, : 4 * per].astype(F32).reshape(size, 4, per).transpose(1, 0, 2).reshape(4, width)
        inner_vectors = halves(line, core)
        line = packed[:, shard + 1, : 2 * outer].astype(F32).reshape(size, 2, outer).transpose(1, 0, 2)
        outer_vectors = halves(line.reshape(2, channels), core)
        first = everywhere(part)
    pad_shape = (3, across_cores, (side + 2) * LINE, half)
    pads, grouped, part = call(
        functools.partial(group_kernel, side),
        [shape(pad_shape, BF16), shape((pixels, half), F32), shape((2, half), F32)],
        [mask, first, inner_vectors, red, wide],
        name="group", flops=2 * TAPS * rows * width * BLOCK,
    )
    if small:
        part, passed = together(part, passed)
        middle = line_sum(part)
        middle, passed_other, second_other = together(middle, passed_other, second_other)
        blocks = (expand_own, expand_first, passed, second, other, first_other, passed_other, second_other)
        total_two = plane_sum(middle)
    else:
        total_two = everywhere(part)
    (act_mine,) = call(
        functools.partial(act_kernel, side), [shape((pixels, half), BF16)], [total_two, first, inner_vectors, grouped],
        name="act",
    )
    act_far = swap_core(act_mine)
    if small:
        act_mine, *blocks = together(act_mine, *blocks)
        (weight_three,) = call(assemble_kernel, [shape((width, half_out), BF16)], blocks, name="assemble")
    else:
        weight_three = lax.all_gather(expand_own, "fsdp", axis=0, tiled=True)
    act_two, expanded, part = call(
        expand_kernel,
        [shape((pixels, width), BF16), shape((pixels, half_out), F32), shape((2, half_out), F32)],
        [mask, act_mine, act_far, weight_three],
        name="expand", flops=2 * rows * width * channels,
    )
    cot = padded(after(cotangent, grouped))
    cot_far = swap_core(call(far_half_kernel, [shape((rows, half_out), BF16)], [cot], name="far_half")[0])
    middle, cot, cot_far = together(plane_sum(part), cot, cot_far)
    total_three = line_sum(middle)
    keep_out, send_out, grad_summed, part = call(
        functools.partial(output_kernel, side),
        [shape((rows, half_out), BF16), shape((rows, half_out), BF16), shape((pixels, half_out), F32),
         shape((2, half_out), F32)],
        [valid_both, total_three, first, outer_vectors, expanded, x, x_other, cot, cot_far], scalars=1, name="output",
    )

    (turned,) = call(turn_kernel, [shape((channels, pixels), BF16)], [x, after(x_other, part)], name="turn")
    middle, turned = together(plane_sum(part), turned)
    sums_three = line_sum(middle)
    flat_three, send = call(
        back_expand_kernel,
        [shape((pixels, half_out), BF16), shape((pixels, half), BF16)],
        [mask, total_three, sums_three, first, outer_vectors, grad_summed, expanded, weight_three],
        name="back_expand", flops=rows * width * channels,
    )
    far = swap_core(send)
    (mine,) = call(
        functools.partial(back_part_kernel, 0), [shape((pixels, half), F32)], [flat_three, weight_three],
        name="back_part", flops=rows * width * channels,
    )
    dz_two, part = call(
        back_act_kernel,
        [shape((pixels, half), F32), shape((2, half), F32)],
        [total_two, first, inner_vectors, mine, far, grouped], name="back_act",
    )
    (expand_term,) = call(
        weight_expand_kernel, [shape((width, half_out), BF16)], [after(act_two, part), flat_three],
        name="weight_expand", flops=2 * rows * width * channels,
    )
    far_out = swap_core(after(send_out, part))
    middle = plane_sum(part)

    def expand_sums(places, arrived=()):
        return call(
            functools.partial(expand_sum_kernel, places, w_expand.shape[0]),
            [shape((w_expand.shape[0] * len(blocks), half_out), BF16) for blocks in places],
            [expand_term] + list(arrived), name="expand_sum",
        )

    if small:
        middle, *moving = together(middle, *expand_sums((((6, ()), (2, ())), ((7, ()), (4, ())))))
        moving = [swap_x(moving[0]), across(moving[1])]
        sums_two = line_sum(middle)
    else:
        sums_two = line_sum(middle)
        own_expand = lax.psum_scatter(expand_term, "fsdp", scatter_dimension=0, tiled=True)
    flat_two, dz_one, part = call(
        functools.partial(back_group_kernel, side),
        [shape((pixels, half), BF16), shape((pixels, half), F32), shape((2, half), F32)],
        [mask, total_two, sums_two, first, inner_vectors, dz_two, grouped, red, wide_turned],
        scratch=[pltpu.VMEM(pad_shape, BF16)], name="back_group", flops=2 * TAPS * rows * width * BLOCK,
    )
    (group_term,) = call(
        functools.partial(weight_group_kernel, side, inner),
        [shape((size, extra, half), BF16)],
        [pads, after(flat_two, part)], scratch=[pltpu.VMEM((TAPS * inner, half), F32)], name="weight_group",
        flops=2 * TAPS * rows * width * BLOCK,
    )
    middle, group_term = together(plane_sum(part), group_term)
    if small:
        middle, *moving = together(middle, *moving)
        middle, expand_first_other, expand_second = together(middle, *expand_sums((((5, ((0, 0),)),), ((3, ((1, 0),)),)), moving))
        expand_first_other, expand_second = across(expand_first_other), along(expand_second, -1)
    sums_one = line_sum(middle)
    if small:
        sums_one, expand_first_other, expand_second = together(sums_one, expand_first_other, expand_second)
        expand_passed, expand_other = moving
        (expand_first_own,) = expand_sums((((1, ((0, 1), (1, 0), (2, 0))),),), (expand_passed, expand_first_other, expand_second))
    tall = depth + extra
    places = (6, 7) if small else tuple(range(size))
    flat_one, *moving = call(
        functools.partial(back_reduce_kernel, small, places),
        [shape((pixels, half), BF16)] + [shape((tall, half), BF16)] * len(places),
        [mask, first, sums_one, inner_vectors, dz_one, red, turned, group_term],
        name="back_reduce", flops=2 * rows * depth * width * len(places),
    )

    def terms_of(places):
        return call(
            functools.partial(block_sum_kernel, small, places),
            [shape((tall, half), F32)] * len(places),
            [turned, group_term, flat_one],
            name="block_sum", flops=2 * rows * depth * width * len(places),
        )

    def sums(terms, *arrived):
        numbers = tuple(len(some) for some in arrived)
        return call(
            functools.partial(arrived_kernel, numbers), [shape((tall, half), BF16)] * len(terms),
            [*terms, *(value for some in arrived for value in some)], name="arrived",
        )

    def back_input(begin, flat, *far):
        out = shape(images.shape, BF16) if far else shape((rows, channels), BF16)
        return call(
            functools.partial(back_input_kernel, slots, slot_depth, begin),
            [out], [flat, grad_summed, *weights, *far],
            scratch=[pltpu.VMEM((rows, channels), F32)], name="back_input", flops=rows * width * channels,
        )[0]

    def own_shards(totals):
        near = jnp.concatenate(totals, axis=1)
        far = swap_core(near)
        lengths = (per, per, outer)
        if small:
            outs = call(
                functools.partial(own_kernel, lengths), [shape((1, n), F32) for n in lengths for _ in range(2)], [near, far],
                name="own",
            )
            return [out.reshape(-1) for out in outs]
        cut, at = [], 0
        for total, length in zip(totals, lengths):
            whole = both(total, far[:, at : at + total.shape[1]], core)
            at += total.shape[1]
            cut += [lax.dynamic_slice_in_dim(whole[row], position * length, length, 0) for row in (1, 0)]
        return cut

    def image_of(far_out):
        return call(image_kernel, [shape(images.shape, BF16)], [keep_out, far_out], name="image")[0]

    def join(own, far, outs):
        return call(
            join_kernel, [shape(out.shape, F32) for out in outs], [own, far, swap_core(own), swap_core(far)], name="join"
        )

    if small:
        moving[1], expand_first_own = together(moving[1], expand_first_own)
        moving = [swap_x(moving[0]), across(moving[1])]
        expand_first_own = along(expand_first_own, -1)
        terms = terms_of((5, 2, 3, 1, 4, 0))
        shards = own_shards([sums_one, sums_two, sums_three])
        moving[0], expand_first_own, *shards = together(moving[0], expand_first_own, *shards)
        (own_expand,) = expand_sums((((0, ((0, 0), (1, 1))),),), [expand_first_own, expand_other])
        first_other, passed, second = sums(terms[0:3], moving[0:1], (), moving[1:2])
        moving = [swap_x(passed), along(second, -1), across(first_other)]
        far_input = swap_core(after(back_input(rows, flat_one), second))
        output = pinned(image_of(after(far_out, second)))
        moving[0], output = together(moving[0], output)
        first_own, other = sums(terms[3:5], moving, ())
        moving = [along(first_own, -1), across(other)]
        grad_input, own_expand = pinned(back_input(0, after(flat_one, first_own), far_input)), after(own_expand, first_own)
        far_expand = swap_x(own_expand)
        moving[0], grad_input, far_expand = together(moving[0], grad_input, far_expand)
        (own_reduce,) = sums(terms[5:6], moving)
        own_expand, far_expand = after(own_expand, own_reduce), after(far_expand, own_reduce)
        (grad_w_expand,) = join(own_expand, far_expand, [w_expand])
        far_reduce, grad_w_expand = together(swap_x(own_reduce), grad_w_expand)
    else:
        grad_input, output = back_input(0, flat_one, swap_core(back_input(rows, flat_one))), image_of(far_out)
        shards = own_shards([sums_one, sums_two, sums_three])
        whole = jnp.stack(moving).reshape(size * tall, half)
        own_reduce = lax.psum_scatter(whole, "fsdp", scatter_dimension=0, tiled=True)
        (grad_w_expand,) = join(own_expand, swap_x(own_expand), [w_expand])
        far_reduce = swap_x(own_reduce)
    grad_w_reduce, grad_w_group = join(own_reduce, far_reduce, [w_reduce, w_group])
    return (output, grad_input, grad_w_reduce, grad_w_group, grad_w_expand) + tuple(shards)


def solution(mesh):
    fsdp, dp = mesh.shape["fsdp"], mesh.shape["dp"]
    split = Mesh(mesh.devices.reshape(fsdp, dp // 2, 2), ("fsdp", "x", "core"))
    images, rows, vector = P(("fsdp", "x", "core"), None, None, None), P("fsdp", None), P("fsdp")
    return jax.shard_map(
        per_device,
        mesh=split,
        in_specs=(
            images, P(("fsdp", "x", "core")), images,
            rows, vector, vector, rows, vector, vector, rows, vector, vector,
        ),
        out_specs=(images, images, rows, rows, rows) + (vector,) * 6,
        check_vma=False,
    )
```

```python
import functools

import jax
import jax.numpy as jnp
from jax import lax
from jax.experimental import pallas as pl
from jax.experimental.pallas import tpu as pltpu
from jax.sharding import Mesh
from jax.sharding import PartitionSpec as P

GROUPS = 32
TAPS = 9
LINE = 16
CHUNK = 512
UNROLL = 7
LANES = 128
BLOCK = 256
epsilon = 1e-05
BF16, F32 = jnp.bfloat16, jnp.float32
SWAP = [(0, 1), (1, 0)]
NN, NT = ((1,), (0,)), ((1,), (1,))
CHIPS = ("fsdp", "x")


def silu_half(half):
    return half + half * jnp.tanh(half)


def dsilu_twice(half):
    turned = jnp.tanh(half)
    upper = 1.0 + turned
    return upper * (1.0 + half * (1.0 - turned)), upper


def dot(a, b, contract=NN):
    return lax.dot_general(a, b, (contract, ((), ())), preferred_element_type=F32)


def after(values, *others):
    return lax.optimization_barrier((values,) + others)[0]


def together(*values):
    return lax.optimization_barrier(values)


def shape(dims, dtype):
    return jax.ShapeDtypeStruct(dims, dtype)


def call(kernel, outs, args, scalars=0, scratch=(), vmem=8, name=None, flops=0, anywhere=False, aliases=()):
    vm = pl.BlockSpec(memory_space=pltpu.VMEM)
    given = pl.BlockSpec(memory_space=pl.ANY) if anywhere else vm
    sm = pl.BlockSpec(memory_space=pltpu.SMEM)
    return pl.pallas_call(
        kernel,
        out_shape=outs,
        in_specs=[sm] * scalars + [given] * (len(args) - scalars),
        out_specs=[vm] * len(outs),
        scratch_shapes=list(scratch),
        compiler_params=pltpu.CompilerParams(vmem_limit_bytes=vmem << 20),
        cost_estimate=pl.CostEstimate(flops=0, bytes_accessed=0, transcendentals=0),
        input_output_aliases=dict(aliases),
        name=name,
    )(*args)


def moments(total, pixels):
    mean = total[0:1, :] / pixels
    inverse = lax.rsqrt(total[1:2, :] / pixels - mean * mean + epsilon)
    return mean, inverse


def chunks(columns):
    return [slice(at, min(at + CHUNK, columns)) for at in range(0, columns, CHUNK)]


def line_mask(columns, side):
    return lax.broadcasted_iota(jnp.int32, (LINE, columns), 0) < side


def each_line(lines, body):
    lax.fori_loop(0, lines, lambda step, none: body(step) or none, 0, unroll=UNROLL)


def each_line_summed(lines, width, body):
    zero = jnp.zeros((8, width), F32)

    def step_sums(step, carry):
        one, two = body(step)
        return carry[0] + fold(one), carry[1] + fold(two)

    one, two = lax.fori_loop(0, lines, step_sums, (zero, zero), unroll=UNROLL)
    return column_sums(one), column_sums(two)


def across_lanes(mask, columns):
    return jnp.concatenate([mask] * (columns // LANES), axis=1)


def column_sums(values):
    return jnp.sum(values, axis=0, keepdims=True)


def line_at(step):
    return pl.ds(pl.multiple_of(step * LINE, LINE), LINE)


def fold(values):
    return values[0:8] + values[8:16]


def part_at(part, half, at=0, length=None):
    core = lax.axis_index("core")
    side = core if part == 0 else 1 - core
    length = half if length is None else length
    return pl.ds(pl.multiple_of(side * half + at, 128), length)


def block_owner(slot):
    position = lax.axis_index("fsdp")
    way = 1 - 2 * lax.axis_index("x")
    step = (0, -way, way, 2)[slot % 4]
    owner = lax.rem(position + 2 * step + 8, 8)
    return owner if slot < 4 else owner + 1 - 2 * lax.rem(owner, 2)


def rows_of(owner, depth):
    return pl.ds(pl.multiple_of(owner * depth, 16), depth)


def pack_kernel(weight, group, *refs):
    vectors, (out, held, *rows, sems) = refs[:6], refs[6:]
    depth, half = weight.shape[0], out.shape[1]
    shard, extra = group.shape[0], out.shape[0] - weight.shape[0]
    columns = part_at(0, half)
    copies = [pltpu.make_async_copy(group, held, sems.at[0])]
    copies += [pltpu.make_async_copy(vector, row, sems.at[2 + at]) for at, (vector, row) in enumerate(zip(vectors, rows))]
    copies.append(pltpu.make_async_copy(weight.at[:, columns], out.at[pl.ds(0, depth)], sems.at[1]))
    for copy in copies:
        copy.start()
    for copy in copies[:-1]:
        copy.wait()
    below = [held[:, columns].astype(F32)]
    for begin, end in ((0, 4), (4, 6)):
        line = [row[...].astype(F32).reshape(1, row.shape[0]) for row in rows[begin:end]]
        missing = half - sum(piece.shape[1] for piece in line)
        below.append(jnp.concatenate(line + ([jnp.zeros((1, missing), F32)] if missing else []), axis=1))
    if extra > shard + 2:
        below.append(jnp.zeros((extra - shard - 2, half), F32))
    out[depth : depth + extra, :] = jnp.concatenate(below, axis=0).astype(BF16)
    copies[-1].wait()


def mask_kernel(side, valid, mask):
    images = valid.shape[0]
    rows = mask.shape[0] // images
    inside = lax.broadcasted_iota(jnp.int32, (rows, LANES), 0) % LINE < side
    for image in range(images):
        mask[image * rows : (image + 1) * rows, :] = jnp.where(inside, valid[image].astype(F32), 0.0)


def turn_kernel(x, x_other, turned):
    rows = x.shape[0]
    turned[:, 0:rows] = x[...].T
    turned[:, rows : 2 * rows] = x_other[...].T


def reduce_kernel(slots, depth, side, last, valid, mask, x, x_other, *refs):
    weights, refs = refs[: len(slots)], refs[len(slots) :]
    before, red = (None, refs[0]) if len(refs) == 1 + last else refs[:2]
    half, rows = red.shape[1], x.shape[0]
    for at in range(0, half, BLOCK):
        sums = [0.0, 0.0]
        for begin, pixels in ((0, x), (rows, x_other)):
            here = (slice(begin, begin + rows), slice(at, at + BLOCK))
            total = None if before is None else before[here]
            for slot, weight in zip(slots, weights):
                if slot is None:
                    piece = pixels[...]
                else:
                    piece = pixels[:, pl.ds(pl.multiple_of(block_owner(slot) * depth, 128), depth)]
                term = dot(piece, weight[0:depth, at : at + BLOCK])
                total = term if total is None else total + term
            red[here] = total
            if last:
                masked = total * across_lanes(mask[begin : begin + rows, :], BLOCK)
                sums = [sums[0] + column_sums(masked), sums[1] + column_sums(masked * total)]
        if last:
            refs[-1][0:1, at : at + BLOCK] = sums[0]
            refs[-1][1:2, at : at + BLOCK] = sums[1]
    if last:
        pixels = valid[0].astype(F32)
        for image in range(1, valid.shape[0]):
            pixels = pixels + valid[image].astype(F32)
        refs[-1][2:3, :] = jnp.full((1, half), 1.0, F32) * (pixels * (side * side))


def spread_kernel(slots, depth, *refs):
    blocks, (wide, wide_turned, inner_vectors, outer_vectors, held, rows) = refs[:slots], refs[slots:]
    extra = held.shape[1]
    for slot in range(slots):
        held[block_owner(slot)] = blocks[slot][depth : depth + extra, :].astype(F32)
    shard, ours = rows.shape[0] // slots, slots // 2
    per, outer = inner_vectors.shape[1] // ours, outer_vectors.shape[1] // ours
    core = lax.axis_index("core")
    for owner in range(slots):
        rows[owner * shard : (owner + 1) * shard, :] = held[owner, 0:shard, :]
    for at in range(ours):
        owner = core * ours + at
        for row in range(4):
            inner_vectors[row : row + 1, at * per : (at + 1) * per] = held[
                owner, shard : shard + 1, row * per : (row + 1) * per
            ]
        for row in range(2):
            outer_vectors[row : row + 1, at * outer : (at + 1) * outer] = held[
                owner, shard + 1 : shard + 2, row * outer : (row + 1) * outer
            ]
    widen(rows, wide, wide_turned)


def widen_kernel(weight, wide, wide_turned, rows):
    rows[...] = weight[...].astype(F32)
    widen(rows, wide, wide_turned)


def widen(weight, wide, wide_turned):
    taps, blocks = wide.shape[:2]
    inner = weight.shape[0] // taps
    row = lax.broadcasted_iota(jnp.int32, (BLOCK, BLOCK), 0) // inner
    column = lax.broadcasted_iota(jnp.int32, (BLOCK, BLOCK), 1) // inner
    own = row == column
    for tap in range(taps):
        for block in range(blocks):
            piece = weight[tap * inner : (tap + 1) * inner, block * BLOCK : (block + 1) * BLOCK]
            tall = jnp.concatenate([piece] * (BLOCK // inner), axis=0)
            dense = jnp.where(own, tall, 0.0)
            wide[tap, block] = dense.astype(BF16)
            wide_turned[tap, block] = dense.T.astype(BF16)


def fill_pads(pads, columns, image, line, values):
    rows = pl.ds(pl.multiple_of((line + 1) * LINE, LINE), LINE)
    pads[0, image, rows, columns] = pltpu.roll(values, 1, 0).astype(BF16)
    pads[1, image, rows, columns] = values.astype(BF16)
    pads[2, image, rows, columns] = pltpu.roll(values, LINE - 1, 0).astype(BF16)


def clear_pads(pads):
    images, rows, columns = pads.shape[1:]
    zeros = jnp.zeros((3, images, LINE, columns), BF16)
    pads[:, :, 0:LINE, :] = zeros
    pads[:, :, rows - LINE : rows, :] = zeros


def convolve(pads, wide, image, block, rows, turned=False):
    columns = slice(block * BLOCK, (block + 1) * BLOCK)
    value = None
    for tap in range(TAPS):
        top, left = divmod(TAPS - 1 - tap if turned else tap, 3)
        piece = pads[left, image, top * LINE : top * LINE + rows, columns]
        term = dot(piece, wide[tap, block])
        value = term if value is None else value + term
    return value


def group_kernel(side, mask, total, vectors, red, wide, pads, grouped, stats):
    images, padded, width = pads.shape[1:]
    rows = side * LINE
    mean, inverse = moments(total, total[2:3, :])
    scale, bias = 0.5 * inverse * vectors[0:1, :], 0.5 * vectors[1:2, :]
    clear_pads(pads)
    for part in chunks(width):
        inside = line_mask(part.stop - part.start, side)

        def body(step):
            half = (red[line_at(step), part] - mean[:, part]) * scale[:, part] + bias[:, part]
            fill_pads(pads, part, step // side, step % side, jnp.where(inside, silu_half(half), 0.0))

        each_line(images * side, body)
    for block in range(width // BLOCK):
        columns = slice(block * BLOCK, (block + 1) * BLOCK)
        sums = [0.0, 0.0]
        for image in range(images):
            at = slice(image * rows, (image + 1) * rows)
            value = convolve(pads, wide, image, block, rows)
            grouped[at, columns] = value
            masked = value * across_lanes(mask[at, :], BLOCK)
            sums = [sums[0] + column_sums(masked), sums[1] + column_sums(masked * value)]
        stats[0:1, columns] = sums[0]
        stats[1:2, columns] = sums[1]


def act_kernel(side, total, first, vectors, grouped, act):
    rows, width = grouped.shape
    mean, inverse = moments(total, first[2:3, :])
    scale, bias = 0.5 * inverse * vectors[2:3, :], 0.5 * vectors[3:4, :]
    for part in chunks(width):
        inside = line_mask(part.stop - part.start, side)

        def body(step):
            at = line_at(step)
            half = (grouped[at, part] - mean[:, part]) * scale[:, part] + bias[:, part]
            act[at, part] = jnp.where(inside, silu_half(half), 0.0).astype(BF16)

        each_line(rows // LINE, body)


def assemble_kernel(*refs):
    blocks, out = refs[:-1], refs[-1]
    depth = blocks[0].shape[0]
    for slot, block in enumerate(blocks):
        out[rows_of(block_owner(slot), depth), :] = block[...]


def expand_kernel(mask, act_mine, act_far, weight, act, expanded, stats):
    rows, half = act_mine.shape
    middle = rows // 2
    act[:, part_at(0, half)] = act_mine[...]
    act[0:middle, part_at(1, half)] = act_far[middle:rows, :]
    act[middle:rows, part_at(1, half)] = act_far[0:middle, :]
    for at in range(0, weight.shape[1], BLOCK):
        sums = [0.0, 0.0]
        for begin in (0, middle):
            here = slice(begin, begin + middle)
            value = dot(act[here, :], weight[:, at : at + BLOCK])
            expanded[here, at : at + BLOCK] = value
            masked = value * across_lanes(mask[here, :], BLOCK)
            sums = [sums[0] + column_sums(masked), sums[1] + column_sums(masked * value)]
        stats[0:1, at : at + BLOCK] = sums[0]
        stats[1:2, at : at + BLOCK] = sums[1]


def output_kernel(
    side, valid, total, first, vectors, expanded, x, x_other, cotangent, cotangent_far, keep_out, send_out, grad, stats
):
    rows, channels = expanded.shape
    middle = rows // 2
    mean, inverse = moments(total, first[2:3, 0:1])
    scale, bias = inverse * vectors[0:1, :], vectors[1:2, :]
    for part in chunks(channels):
        length = part.stop - part.start
        whole = part_at(0, channels, part.start, length)
        ends = []
        for begin, pixels, incoming, columns, out in (
            (0, x, cotangent, whole, keep_out), (middle, x_other, cotangent_far, part, send_out)
        ):

            def body(step):
                at = line_at(step)
                here = pl.ds(pl.multiple_of(begin + step * LINE, LINE), LINE)
                keep = 0.5 * valid[(begin // LINE + step) // side].astype(F32)
                centered = expanded[here, part] - mean[:, part]
                half = (centered * scale[:, part] + (bias[:, part] + pixels[at, whole].astype(F32))) * keep
                slope, upper = dsilu_twice(half)
                out[at, part] = (half * upper).astype(BF16)
                value = incoming[at, columns].astype(F32) * keep * slope
                grad[here, part] = value
                return value, value * centered

            ends.append(each_line_summed(middle // LINE, length, body))
        stats[0:1, part] = ends[0][0] + ends[1][0]
        stats[1:2, part] = (ends[0][1] + ends[1][1]) * inverse[:, part]


def back_expand_kernel(mask, total, sums, first, vectors, grad, expanded, weight, flat, send):
    rows, channels = expanded.shape
    pixels = first[2:3, 0:1]
    mean, inverse = moments(total, pixels)
    scale = inverse * vectors[0:1, :]
    shifted, scaled = scale * sums[0:1, :] / pixels, scale * inverse * sums[1:2, :] / pixels
    for part in chunks(channels):

        def body(step):
            at = line_at(step)
            common = shifted[:, part] + (expanded[at, part] - mean[:, part]) * scaled[:, part]
            counted = across_lanes(mask[at, :], part.stop - part.start)
            flat[at, part] = (scale[:, part] * grad[at, part] - counted * common).astype(BF16)

        each_line(rows // LINE, body)
    back_part_kernel(1, flat, weight, send)


def back_part_kernel(part, flat, weight, out):
    half = out.shape[1]
    for at in range(0, half, BLOCK):
        rows = pl.ds(pl.multiple_of(part_at(part, half).start + at, BLOCK), BLOCK)
        out[:, at : at + BLOCK] = dot(flat[...], weight[rows, :], NT).astype(out.dtype)


def back_act_kernel(total, first, vectors, mine, far, grouped, dz, stats):
    mean, inverse = moments(total, first[2:3, :])
    lines = grouped.shape[0] // LINE

    def gradient(step, part):
        there = lax.rem(step + lines // 2, lines)
        return mine[line_at(step), part] + far[line_at(there), part].astype(F32)

    before_norm(dz, gradient, grouped, mean, inverse, vectors[2:3, :], vectors[3:4, :], stats)


def before_norm(dz, gradient, hidden, mean, inverse, gain, shift, stats, side=None):
    scale, bias = 0.5 * inverse * gain, 0.5 * shift
    rows, width = hidden.shape
    for part in chunks(width):
        inside = None if side is None else line_mask(part.stop - part.start, side)

        def body(step):
            at = line_at(step)
            centered = hidden[at, part] - mean[:, part]
            slope, _ = dsilu_twice(centered * scale[:, part] + bias[:, part])
            here = gradient(step, part) * slope
            if side is not None:
                here = jnp.where(inside, here, 0.0)
            dz[at, part] = here
            return here, here * centered

        one, two = each_line_summed(rows // LINE, part.stop - part.start, body)
        stats[0:1, part] = 0.5 * one
        stats[1:2, part] = 0.5 * inverse[:, part] * two


def weight_expand_kernel(act, flat, out):
    turned = act[...].T
    for at in range(0, out.shape[1], BLOCK):
        out[:, at : at + BLOCK] = dot(turned, flat[:, at : at + BLOCK]).astype(BF16)


def back_group_kernel(
    side, mask, total, sums, first, vectors, dz, grouped, red, wide, flat, dz_one, stats, pads
):
    images, padded, width = pads.shape[1:]
    rows = side * LINE
    pixels = first[2:3, :]
    mean, inverse = moments(total, pixels)
    scale = inverse * vectors[2:3, :]
    shifted, scaled = scale * sums[0:1, :] / pixels, scale * inverse * sums[1:2, :] / pixels
    scale = 0.5 * scale
    clear_pads(pads)
    for part in chunks(width):

        def body(step):
            at = line_at(step)
            common = shifted[:, part] + (grouped[at, part] - mean[:, part]) * scaled[:, part]
            value = scale[:, part] * dz[at, part] - across_lanes(mask[at, :], part.stop - part.start) * common
            flat[at, part] = value.astype(BF16)
            fill_pads(pads, part, step // side, step % side, value)

        each_line(images * side, body)
    for block in range(width // BLOCK):
        columns = slice(block * BLOCK, (block + 1) * BLOCK)
        for image in range(images):
            dz_one[image * rows : (image + 1) * rows, columns] = convolve(pads, wide, image, block, rows, True)
    mean_one, inverse_one = moments(first, pixels)

    def gradient(step, part):
        return dz_one[line_at(step), part]

    before_norm(dz_one, gradient, red, mean_one, inverse_one, vectors[0:1, :], vectors[1:2, :], stats, side)


def weight_group_kernel(side, inner, pads, flat, out, held):
    images, padded, width = pads.shape[1:]
    rows = side * LINE
    row = lax.broadcasted_iota(jnp.int32, (LANES, LANES), 0) // inner
    column = lax.broadcasted_iota(jnp.int32, (LANES, LANES), 1) // inner
    own = row == column
    for at in range(0, width, LANES):
        columns = slice(at, at + LANES)
        moved = []
        for tap in range(TAPS):
            top, left = divmod(tap, 3)
            pieces = [pads[left, image, top * LINE : top * LINE + rows, columns] for image in range(images)]
            moved.append(jnp.concatenate(pieces, axis=0))
        product = dot(flat[:, columns].T, jnp.concatenate(moved, axis=1))
        for tap in range(TAPS):
            kept = jnp.where(own, product[:, tap * LANES : (tap + 1) * LANES].T, 0.0)
            value = kept[0:inner]
            for begin in range(inner, LANES, inner):
                value = value + kept[begin : begin + inner]
            held[tap * inner : (tap + 1) * inner, columns] = value
    owners, extra = out.shape[:2]
    shard = TAPS * inner // owners
    zeros = jnp.zeros((extra - shard, width), F32)
    for owner in range(owners):
        rows_here = held[owner * shard : (owner + 1) * shard, :]
        out[owner] = jnp.concatenate([rows_here, zeros], axis=0).astype(BF16)


def back_reduce_kernel(small, places, mask, first, sums, vectors, dz, red, turned, group, flat, *outs):
    rows, width = red.shape
    pixels = first[2:3, :]
    mean, inverse = moments(first, pixels)
    scale = inverse * vectors[0:1, :]
    shifted, scaled = scale * sums[0:1, :] / pixels, scale * inverse * sums[1:2, :] / pixels
    scale = 0.5 * scale
    for part in chunks(width):

        def body(step):
            at = line_at(step)
            common = shifted[:, part] + (red[at, part] - mean[:, part]) * scaled[:, part]
            counted = across_lanes(mask[at, :], part.stop - part.start)
            flat[at, part] = (scale[:, part] * dz[at, part] - counted * common).astype(BF16)

        each_line(rows // LINE, body)
    block_sum_kernel(small, places, turned, group, flat, *outs)


def block_sum_kernel(small, places, turned, group, flat, *outs):
    tall, half = outs[0].shape
    depth = tall - group.shape[1]
    for out, block in zip(outs, places):
        owner = block_owner(block) if small else block
        out[0:depth, :] = dot(turned[rows_of(owner, depth), :], flat[...]).astype(out.dtype)
        out[depth:tall, :] = group[owner].astype(out.dtype)


def arrived_kernel(numbers, *refs):
    terms, arrived, outs = refs[: len(numbers)], refs[len(numbers) : -len(numbers)], refs[-len(numbers) :]
    at = 0
    for out, term, number in zip(outs, terms, numbers):
        value = term[...]
        for other in arrived[at : at + number]:
            value = value + other[...].astype(F32)
        out[...] = value.astype(BF16)
        at += number


def expand_sum_kernel(places, depth, keep, *refs):
    arrived, outs = refs[: len(refs) - len(places)], refs[len(refs) - len(places) :]
    for out, blocks in zip(outs, places):
        for at, (block, chosen) in enumerate(blocks):
            value = keep[rows_of(block_owner(block), depth), :]
            if chosen:
                value = value.astype(F32)
                for other, begin in chosen:
                    value = value + arrived[other][begin * depth : (begin + 1) * depth, :].astype(F32)
            out[at * depth : (at + 1) * depth, :] = value.astype(BF16)


def join_kernel(mine, mine_x, other, other_x, *outs):
    half = mine.shape[1]
    at = 0
    for out in outs:
        rows = out.shape[0]
        for part, terms in enumerate(((mine, mine_x), (other, other_x))):
            values = [term[at : at + -(-rows // 16) * 16, :].astype(F32) for term in terms]
            out[:, part_at(part, half)] = (values[0] + values[1])[0:rows]
        at += -(-rows // 16) * 16


def pin_kernel(values, out):
    pass


def own_kernel(sizes, near, far, *outs):
    position, core, ours = lax.axis_index("fsdp"), lax.axis_index("core"), lax.axis_size("fsdp") // 2
    side, place, at = position // ours, lax.rem(position, ours), 0
    for index, length in enumerate(sizes):
        columns = pl.ds(pl.multiple_of(at + place * length, 128), length)
        for row, out in ((1, outs[2 * index]), (0, outs[2 * index + 1])):
            out[...] = jnp.where(side == core, near[row : row + 1, columns], far[row : row + 1, columns])
        at += ours * length


def back_input_kernel(slots, depth, begin, flat, grad, *refs):
    weights, refs = refs[:slots], refs[slots:]
    half = grad.shape[1]
    out, held = refs[-2:]
    rows = slice(begin, begin + held.shape[0])
    for slot in range(slots):
        columns = pl.ds(pl.multiple_of(block_owner(slot) * depth, 128), depth) if slots > 1 else slice(None)
        held[:, columns] = dot(flat[rows, :], weights[slot][0:depth, :], NT)
    columns = part_at(0, half)
    held[:, columns] = held[:, columns] + grad[rows, :]
    if len(refs) == 2:
        out[...] = held[...].astype(BF16)
        return
    far = refs[0]
    side = out.shape[1]

    def body(step):
        at = line_at(step)
        out[step // side, step % side] = (held[at, :] + far[at, :].astype(F32)).astype(BF16)[0:side]

    each_line(held.shape[0] // LINE, body)


def far_half_kernel(values, out):
    out[...] = values[:, part_at(1, out.shape[1])]


def image_kernel(keep, far, out):
    half, side = keep.shape[1], out.shape[1]

    def body(step):
        at = line_at(step)
        for part, values in enumerate((keep, far)):
            out[step // side, step % side, :, part_at(part, half)] = values[at, :][0:side]

    each_line(keep.shape[0] // LINE, body)


def pinned(values):
    anywhere = pl.BlockSpec(memory_space=pl.ANY)
    values = values.transpose(1, 2, 0, 3)
    values = pl.pallas_call(
        pin_kernel, out_shape=shape(values.shape, values.dtype), in_specs=[anywhere], out_specs=anywhere,
        input_output_aliases={0: 0}, compiler_params=pltpu.CompilerParams(vmem_limit_bytes=1 << 20), name="pin",
    )(values)
    return values.transpose(2, 0, 1, 3)


def swap_core(values):
    return lax.ppermute(values, "core", SWAP)


def swap_x(values):
    if lax.axis_size("x") == 2:
        return lax.ppermute(values, "x", SWAP)
    return (lax.psum(values.astype(F32), "x") - values.astype(F32)).astype(values.dtype)


def sum_chips(values, flips):
    got = []
    for flip in (0, *flips):
        pairs = [(2 * at + core, 2 * (at ^ flip) + 1 - core) for at in range(16) for core in range(2)]
        got.append(lax.ppermute(values, (*CHIPS, "core"), pairs))
    got = together(*got)
    total = got[0]
    for other in got[1:]:
        total = total + other
    return total


def along(values, way):
    pairs = [(f * 2 + x, (f + 2 * way * (1 - 2 * x)) % 8 * 2 + x) for f in range(8) for x in range(2)]
    return lax.ppermute(values, CHIPS, pairs)


def across(values):
    return lax.ppermute(values, "fsdp", [(f, f ^ 1) for f in range(8)])


def halves(values, core):
    half = values.shape[1] // 2
    return lax.dynamic_slice_in_dim(values, core * half, half, 1)


def both(near, far, core):
    first, second = jnp.where(core == 0, near, far), jnp.where(core == 0, far, near)
    return jnp.concatenate([first, second], axis=-1)


def per_device(
    images,
    valid,
    cotangent,
    w_reduce,
    gain_one,
    shift_one,
    w_group,
    gain_two,
    shift_two,
    w_expand,
    gain_three,
    shift_three,
):
    count, side, _, channels = images.shape
    width = w_reduce.shape[1]
    inner = width // GROUPS
    size = lax.axis_size("fsdp")
    small = size == 8 and lax.axis_size("x") == 2
    position, core = lax.axis_index("fsdp"), lax.axis_index("core")
    rows = count * side * LINE
    per, outer, shard, depth = gain_one.shape[0], gain_three.shape[0], w_group.shape[0], w_reduce.shape[0]
    extra = -(-(shard + 2) // 16) * 16
    half, half_out = width // 2, channels // 2

    def plane_sum(values):
        return sum_chips(values, (1, 2, 3)) if small else lax.psum(values, CHIPS)

    def line_sum(values):
        return sum_chips(values, (4, 12, 8)) if small else values

    def everywhere(values):
        return line_sum(plane_sum(values))

    def padded(values):
        return jnp.pad(values, ((0, 0), (0, 0), (0, LINE - side), (0, 0))).reshape(rows, channels)

    vectors = (gain_one, shift_one, gain_two, shift_two, gain_three, shift_three)
    (own,) = call(
        pack_kernel, [shape((depth + extra, half), BF16)], [w_reduce, w_group, *vectors],
        anywhere=True, vmem=60, name="pack",
        scratch=[pltpu.VMEM((shard, width), BF16)] + [pltpu.VMEM(vector.shape, BF16) for vector in vectors]
        + [pltpu.SemaphoreType.DMA((8,))],
    )
    wide_shape = shape((TAPS, half // BLOCK, BLOCK, BLOCK), BF16)
    expand_own, x = halves(w_expand, core), padded(images)

    def mask_of(valid_other):
        valid_both = jnp.concatenate([valid, valid_other])
        (mask,) = call(
            functools.partial(mask_kernel, side), [shape((2 * rows, LANES), F32)], [valid_both], scalars=1, name="mask"
        )
        return valid_both, mask

    pixels, across_cores = 2 * rows, 2 * count

    def reduce_part(slots, last, depth, weights, *before):
        return call(
            functools.partial(reduce_kernel, slots, depth, side, last),
            [shape((pixels, half), F32), shape((3, half), F32)][: 1 + last],
            [valid_both, mask, x, x_other, *weights, *before], scalars=1, name="reduce", flops=2 * rows * width * channels,
        )

    if small:
        other = across(own)
        first = along(own, 1)
        x_other, valid_other = padded(swap_core(images)), swap_core(valid)
        first, other, x, x_other, expand_own = together(first, other, x, x_other, expand_own)
        passed, second, first_other = swap_x(first), along(first, 1), across(first)
        second, passed, first_other, valid_other = together(second, passed, first_other, valid_other)
        passed_other, second_other, expand_first = swap_x(first_other), across(second), along(expand_own, 1)
        valid_both, mask = mask_of(valid_other)
        weights = [own, first, passed, second, other, first_other, passed_other, second_other]
        (before,) = reduce_part((0, 1, 2, 3, 4, 5), False, depth, weights[:6])
        mask, before, *weights[6:] = together(mask, before, *weights[6:])
        second, other = along(expand_first, 1), across(expand_own)
        slots, slot_depth = size, depth
    else:
        x_other, valid_other = swap_core(x), swap_core(valid)
        valid_both, mask = mask_of(valid_other)
        whole = lax.all_gather(own, "fsdp", axis=0, tiled=False)
        weights = [whole[:, :depth].reshape(channels, half)]
        slots, slot_depth = 1, channels


    if small:
        red, part = reduce_part((6, 7), True, depth, weights[6:], before)
    else:
        red, part = reduce_part((None,), True, channels, weights)
    if small:
        wide, wide_turned, inner_vectors, outer_vectors = call(
            functools.partial(spread_kernel, slots, depth),
            [wide_shape, wide_shape, shape((4, half), F32), shape((2, half_out), F32)],
            weights,
            scratch=[pltpu.VMEM((size, extra, half), F32), pltpu.VMEM((size * shard, half), F32)],
            name="spread", flops=1 << 28,
        )
        middle, wide, wide_turned, inner_vectors, outer_vectors = together(
            plane_sum(part), wide, wide_turned, inner_vectors, outer_vectors
        )
        middle, second, other, expand_first = together(middle, second, other, expand_first)
        first_other, passed = across(expand_first), swap_x(expand_first)
        first = line_sum(middle)
        first, second = together(first, second)
        second_other, passed_other = across(second), swap_x(first_other)
    else:
        packed = whole[:, depth:]
        wide, wide_turned = call(
            widen_kernel, [wide_shape, wide_shape], [packed[:, :shard].reshape(size * shard, half)],
            scratch=[pltpu.VMEM((size * shard, half), F32)], name="widen",
        )
        line = packed[:, shard, : 4 * per].astype(F32).reshape(size, 4, per).transpose(1, 0, 2).reshape(4, width)
        inner_vectors = halves(line, core)
        line = packed[:, shard + 1, : 2 * outer].astype(F32).reshape(size, 2, outer).transpose(1, 0, 2)
        outer_vectors = halves(line.reshape(2, channels), core)
        first = everywhere(part)
    pad_shape = (3, across_cores, (side + 2) * LINE, half)
    pads, grouped, part = call(
        functools.partial(group_kernel, side),
        [shape(pad_shape, BF16), shape((pixels, half), F32), shape((2, half), F32)],
        [mask, first, inner_vectors, red, wide],
        name="group", flops=2 * TAPS * rows * width * BLOCK,
    )
    if small:
        part, passed = together(part, passed)
        middle = line_sum(part)
        middle, passed_other, second_other = together(middle, passed_other, second_other)
        blocks = (expand_own, expand_first, passed, second, other, first_other, passed_other, second_other)
        total_two = plane_sum(middle)
    else:
        total_two = everywhere(part)
    (act_mine,) = call(
        functools.partial(act_kernel, side), [shape((pixels, half), BF16)], [total_two, first, inner_vectors, grouped],
        name="act",
    )
    act_far = swap_core(act_mine)
    if small:
        act_mine, *blocks = together(act_mine, *blocks)
        (weight_three,) = call(assemble_kernel, [shape((width, half_out), BF16)], blocks, name="assemble")
    else:
        weight_three = lax.all_gather(expand_own, "fsdp", axis=0, tiled=True)
    act_two, expanded, part = call(
        expand_kernel,
        [shape((pixels, width), BF16), shape((pixels, half_out), F32), shape((2, half_out), F32)],
        [mask, act_mine, act_far, weight_three],
        name="expand", flops=2 * rows * width * channels,
    )
    cot = padded(after(cotangent, grouped))
    cot_far = swap_core(call(far_half_kernel, [shape((rows, half_out), BF16)], [cot], name="far_half")[0])
    middle, cot, cot_far = together(plane_sum(part), cot, cot_far)
    total_three = line_sum(middle)
    keep_out, send_out, grad_summed, part = call(
        functools.partial(output_kernel, side),
        [shape((rows, half_out), BF16), shape((rows, half_out), BF16), shape((pixels, half_out), F32),
         shape((2, half_out), F32)],
        [valid_both, total_three, first, outer_vectors, expanded, x, x_other, cot, cot_far], scalars=1, name="output",
    )

    (turned,) = call(turn_kernel, [shape((channels, pixels), BF16)], [x, after(x_other, part)], name="turn")
    middle, turned = together(plane_sum(part), turned)
    sums_three = line_sum(middle)
    flat_three, send = call(
        back_expand_kernel,
        [shape((pixels, half_out), BF16), shape((pixels, half), BF16)],
        [mask, total_three, sums_three, first, outer_vectors, grad_summed, expanded, weight_three],
        name="back_expand", flops=rows * width * channels,
    )
    far = swap_core(send)
    (mine,) = call(
        functools.partial(back_part_kernel, 0), [shape((pixels, half), F32)], [flat_three, weight_three],
        name="back_part", flops=rows * width * channels,
    )
    dz_two, part = call(
        back_act_kernel,
        [shape((pixels, half), F32), shape((2, half), F32)],
        [total_two, first, inner_vectors, mine, far, grouped], name="back_act",
    )
    (expand_term,) = call(
        weight_expand_kernel, [shape((width, half_out), BF16)], [after(act_two, part), flat_three],
        name="weight_expand", flops=2 * rows * width * channels,
    )
    far_out = swap_core(after(send_out, part))
    middle = plane_sum(part)

    def expand_sums(places, arrived=()):
        return call(
            functools.partial(expand_sum_kernel, places, w_expand.shape[0]),
            [shape((w_expand.shape[0] * len(blocks), half_out), BF16) for blocks in places],
            [expand_term] + list(arrived), name="expand_sum",
        )

    if small:
        middle, *moving = together(middle, *expand_sums((((6, ()), (2, ())), ((7, ()), (4, ())))))
        moving = [swap_x(moving[0]), across(moving[1])]
        sums_two = line_sum(middle)
    else:
        sums_two = line_sum(middle)
        own_expand = lax.psum_scatter(expand_term, "fsdp", scatter_dimension=0, tiled=True)
    flat_two, dz_one, part = call(
        functools.partial(back_group_kernel, side),
        [shape((pixels, half), BF16), shape((pixels, half), F32), shape((2, half), F32)],
        [mask, total_two, sums_two, first, inner_vectors, dz_two, grouped, red, wide_turned],
        scratch=[pltpu.VMEM(pad_shape, BF16)], name="back_group", flops=2 * TAPS * rows * width * BLOCK,
    )
    (group_term,) = call(
        functools.partial(weight_group_kernel, side, inner),
        [shape((size, extra, half), BF16)],
        [pads, after(flat_two, part)], scratch=[pltpu.VMEM((TAPS * inner, half), F32)], name="weight_group",
        flops=2 * TAPS * rows * width * BLOCK,
    )
    middle, group_term = together(plane_sum(part), group_term)
    if small:
        middle, *moving = together(middle, *moving)
        middle, expand_first_other, expand_second = together(middle, *expand_sums((((5, ((0, 0),)),), ((3, ((1, 0),)),)), moving))
        expand_first_other, expand_second = across(expand_first_other), along(expand_second, -1)
    sums_one = line_sum(middle)
    if small:
        sums_one, expand_first_other, expand_second = together(sums_one, expand_first_other, expand_second)
        expand_passed, expand_other = moving
        (expand_first_own,) = expand_sums((((1, ((0, 1), (1, 0), (2, 0))),),), (expand_passed, expand_first_other, expand_second))
    tall = depth + extra
    places = (6, 7) if small else tuple(range(size))
    flat_one, *moving = call(
        functools.partial(back_reduce_kernel, small, places),
        [shape((pixels, half), BF16)] + [shape((tall, half), BF16)] * len(places),
        [mask, first, sums_one, inner_vectors, dz_one, red, turned, group_term],
        name="back_reduce", flops=2 * rows * depth * width * len(places),
    )

    def terms_of(places):
        return call(
            functools.partial(block_sum_kernel, small, places),
            [shape((tall, half), F32)] * len(places),
            [turned, group_term, flat_one],
            name="block_sum", flops=2 * rows * depth * width * len(places),
        )

    def sums(terms, *arrived):
        numbers = tuple(len(some) for some in arrived)
        return call(
            functools.partial(arrived_kernel, numbers), [shape((tall, half), BF16)] * len(terms),
            [*terms, *(value for some in arrived for value in some)], name="arrived",
        )

    def back_input(begin, flat, *far):
        out = shape(images.shape, BF16) if far else shape((rows, channels), BF16)
        return call(
            functools.partial(back_input_kernel, slots, slot_depth, begin),
            [out], [flat, grad_summed, *weights, *far],
            scratch=[pltpu.VMEM((rows, channels), F32)], name="back_input", flops=rows * width * channels,
        )[0]

    def own_shards(totals):
        near = jnp.concatenate(totals, axis=1)
        far = swap_core(near)
        lengths = (per, per, outer)
        if small:
            outs = call(
                functools.partial(own_kernel, lengths), [shape((1, n), F32) for n in lengths for _ in range(2)], [near, far],
                name="own",
            )
            return [out.reshape(-1) for out in outs]
        cut, at = [], 0
        for total, length in zip(totals, lengths):
            whole = both(total, far[:, at : at + total.shape[1]], core)
            at += total.shape[1]
            cut += [lax.dynamic_slice_in_dim(whole[row], position * length, length, 0) for row in (1, 0)]
        return cut

    def image_of(far_out):
        return call(image_kernel, [shape(images.shape, BF16)], [keep_out, far_out], name="image")[0]

    def join(own, far, outs):
        return call(
            join_kernel, [shape(out.shape, F32) for out in outs], [own, far, swap_core(own), swap_core(far)], name="join"
        )

    if small:
        moving[1], expand_first_own = together(moving[1], expand_first_own)
        moving = [swap_x(moving[0]), across(moving[1])]
        expand_first_own = along(expand_first_own, -1)
        terms = terms_of((5, 2, 3, 1, 4, 0))
        shards = own_shards([sums_one, sums_two, sums_three])
        moving[0], expand_first_own, *shards = together(moving[0], expand_first_own, *shards)
        (own_expand,) = expand_sums((((0, ((0, 0), (1, 1))),),), [expand_first_own, expand_other])
        first_other, passed, second = sums(terms[0:3], moving[0:1], (), moving[1:2])
        moving = [swap_x(passed), along(second, -1), across(first_other)]
        far_input = swap_core(after(back_input(rows, flat_one), second))
        output = pinned(image_of(after(far_out, second)))
        moving[0], output = together(moving[0], output)
        first_own, other = sums(terms[3:5], moving, ())
        moving = [along(first_own, -1), across(other)]
        grad_input, own_expand = pinned(back_input(0, after(flat_one, first_own), far_input)), after(own_expand, first_own)
        far_expand = swap_x(own_expand)
        moving[0], grad_input, far_expand = together(moving[0], grad_input, far_expand)
        (own_reduce,) = sums(terms[5:6], moving)
        own_expand, far_expand = after(own_expand, own_reduce), after(far_expand, own_reduce)
        (grad_w_expand,) = join(own_expand, far_expand, [w_expand])
        far_reduce, grad_w_expand = together(swap_x(own_reduce), grad_w_expand)
    else:
        grad_input, output = back_input(0, flat_one, swap_core(back_input(rows, flat_one))), image_of(far_out)
        shards = own_shards([sums_one, sums_two, sums_three])
        whole = jnp.stack(moving).reshape(size * tall, half)
        own_reduce = lax.psum_scatter(whole, "fsdp", scatter_dimension=0, tiled=True)
        (grad_w_expand,) = join(own_expand, swap_x(own_expand), [w_expand])
        far_reduce = swap_x(own_reduce)
    grad_w_reduce, grad_w_group = join(own_reduce, far_reduce, [w_reduce, w_group])
    return (output, grad_input, grad_w_reduce, grad_w_group, grad_w_expand) + tuple(shards)


def solution(mesh):
    fsdp, dp = mesh.shape["fsdp"], mesh.shape["dp"]
    split = Mesh(mesh.devices.reshape(fsdp, dp // 2, 2), ("fsdp", "x", "core"))
    images, rows, vector = P(("fsdp", "x", "core"), None, None, None), P("fsdp", None), P("fsdp")
    return jax.shard_map(
        per_device,
        mesh=split,
        in_specs=(
            images, P(("fsdp", "x", "core")), images,
            rows, vector, vector, rows, vector, vector, rows, vector, vector,
        ),
        out_specs=(images, images, rows, rows, rows) + (vector,) * 6,
        check_vma=False,
    )
```

```python
import functools

import jax
import jax.numpy as jnp
from jax import lax
from jax.experimental import pallas as pl
from jax.experimental.pallas import tpu as pltpu
from jax.sharding import Mesh
from jax.sharding import PartitionSpec as P

GROUPS = 32
TAPS = 9
LINE = 16
CHUNK = 512
UNROLL = 7
LANES = 128
BLOCK = 256
epsilon = 1e-05
BF16, F32 = jnp.bfloat16, jnp.float32
SWAP = [(0, 1), (1, 0)]
NN, NT = ((1,), (0,)), ((1,), (1,))
CHIPS = ("fsdp", "x")


def silu_half(half):
    return half + half * jnp.tanh(half)


def dsilu_twice(half):
    turned = jnp.tanh(half)
    upper = 1.0 + turned
    return upper * (1.0 + half * (1.0 - turned)), upper


def dot(a, b, contract=NN):
    return lax.dot_general(a, b, (contract, ((), ())), preferred_element_type=F32)


def after(values, *others):
    return lax.optimization_barrier((values,) + others)[0]


def together(*values):
    return lax.optimization_barrier(values)


def shape(dims, dtype):
    return jax.ShapeDtypeStruct(dims, dtype)


def call(kernel, outs, args, scalars=0, scratch=(), vmem=8, name=None, flops=0, anywhere=False, aliases=()):
    vm = pl.BlockSpec(memory_space=pltpu.VMEM)
    given = pl.BlockSpec(memory_space=pl.ANY) if anywhere else vm
    sm = pl.BlockSpec(memory_space=pltpu.SMEM)
    return pl.pallas_call(
        kernel,
        out_shape=outs,
        in_specs=[sm] * scalars + [given] * (len(args) - scalars),
        out_specs=[vm] * len(outs),
        scratch_shapes=list(scratch),
        compiler_params=pltpu.CompilerParams(vmem_limit_bytes=vmem << 20),
        cost_estimate=pl.CostEstimate(flops=0, bytes_accessed=0, transcendentals=0),
        input_output_aliases=dict(aliases),
        name=name,
    )(*args)


def moments(total, pixels):
    mean = total[0:1, :] / pixels
    inverse = lax.rsqrt(total[1:2, :] / pixels - mean * mean + epsilon)
    return mean, inverse


def chunks(columns):
    return [slice(at, min(at + CHUNK, columns)) for at in range(0, columns, CHUNK)]


def line_mask(columns, side):
    return lax.broadcasted_iota(jnp.int32, (LINE, columns), 0) < side


def each_line(lines, body):
    lax.fori_loop(0, lines, lambda step, none: body(step) or none, 0, unroll=UNROLL)


def each_line_summed(lines, width, body):
    zero = jnp.zeros((8, width), F32)

    def step_sums(step, carry):
        one, two = body(step)
        return carry[0] + fold(one), carry[1] + fold(two)

    one, two = lax.fori_loop(0, lines, step_sums, (zero, zero), unroll=UNROLL)
    return column_sums(one), column_sums(two)


def across_lanes(mask, columns):
    return jnp.concatenate([mask] * (columns // LANES), axis=1)


def column_sums(values):
    return jnp.sum(values, axis=0, keepdims=True)


def line_at(step):
    return pl.ds(pl.multiple_of(step * LINE, LINE), LINE)


def fold(values):
    return values[0:8] + values[8:16]


def part_at(part, half, at=0, length=None):
    core = lax.axis_index("core")
    side = core if part == 0 else 1 - core
    length = half if length is None else length
    return pl.ds(pl.multiple_of(side * half + at, 128), length)


def block_owner(slot):
    position = lax.axis_index("fsdp")
    way = 1 - 2 * lax.axis_index("x")
    step = (0, -way, way, 2)[slot % 4]
    owner = lax.rem(position + 2 * step + 8, 8)
    return owner if slot < 4 else owner + 1 - 2 * lax.rem(owner, 2)


def rows_of(owner, depth):
    return pl.ds(pl.multiple_of(owner * depth, 16), depth)


def pack_kernel(weight, group, *refs):
    vectors, (out, held, *rows, sems) = refs[:6], refs[6:]
    depth, half = weight.shape[0], out.shape[1]
    shard, extra = group.shape[0], out.shape[0] - weight.shape[0]
    columns = part_at(0, half)
    copies = [pltpu.make_async_copy(group, held, sems.at[0])]
    copies += [pltpu.make_async_copy(vector, row, sems.at[2 + at]) for at, (vector, row) in enumerate(zip(vectors, rows))]
    copies.append(pltpu.make_async_copy(weight.at[:, columns], out.at[pl.ds(0, depth)], sems.at[1]))
    for copy in copies:
        copy.start()
    for copy in copies[:-1]:
        copy.wait()
    below = [held[:, columns].astype(F32)]
    for begin, end in ((0, 4), (4, 6)):
        line = [row[...].astype(F32).reshape(1, row.shape[0]) for row in rows[begin:end]]
        missing = half - sum(piece.shape[1] for piece in line)
        below.append(jnp.concatenate(line + ([jnp.zeros((1, missing), F32)] if missing else []), axis=1))
    if extra > shard + 2:
        below.append(jnp.zeros((extra - shard - 2, half), F32))
    out[depth : depth + extra, :] = jnp.concatenate(below, axis=0).astype(BF16)
    copies[-1].wait()


def mask_kernel(side, valid, mask):
    images = valid.shape[0]
    rows = mask.shape[0] // images
    inside = lax.broadcasted_iota(jnp.int32, (rows, LANES), 0) % LINE < side
    for image in range(images):
        mask[image * rows : (image + 1) * rows, :] = jnp.where(inside, valid[image].astype(F32), 0.0)


def turn_kernel(x, x_other, turned):
    rows = x.shape[0]
    turned[:, 0:rows] = x[...].T
    turned[:, rows : 2 * rows] = x_other[...].T


def reduce_kernel(slots, depth, side, last, valid, mask, x, x_other, *refs):
    weights, refs = refs[: len(slots)], refs[len(slots) :]
    before, red = (None, refs[0]) if len(refs) == 1 + last else refs[:2]
    half, rows = red.shape[1], x.shape[0]
    for at in range(0, half, BLOCK):
        sums = [0.0, 0.0]
        for begin, pixels in ((0, x), (rows, x_other)):
            here = (slice(begin, begin + rows), slice(at, at + BLOCK))
            total = None if before is None else before[here]
            for slot, weight in zip(slots, weights):
                if slot is None:
                    piece = pixels[...]
                else:
                    piece = pixels[:, pl.ds(pl.multiple_of(block_owner(slot) * depth, 128), depth)]
                term = dot(piece, weight[0:depth, at : at + BLOCK])
                total = term if total is None else total + term
            red[here] = total
            if last:
                masked = total * across_lanes(mask[begin : begin + rows, :], BLOCK)
                sums = [sums[0] + column_sums(masked), sums[1] + column_sums(masked * total)]
        if last:
            refs[-1][0:1, at : at + BLOCK] = sums[0]
            refs[-1][1:2, at : at + BLOCK] = sums[1]
    if last:
        pixels = valid[0].astype(F32)
        for image in range(1, valid.shape[0]):
            pixels = pixels + valid[image].astype(F32)
        refs[-1][2:3, :] = jnp.full((1, half), 1.0, F32) * (pixels * (side * side))


def spread_kernel(slots, depth, *refs):
    blocks, (wide, wide_turned, inner_vectors, outer_vectors, held, rows) = refs[:slots], refs[slots:]
    extra = held.shape[1]
    for slot in range(slots):
        held[block_owner(slot)] = blocks[slot][depth : depth + extra, :].astype(F32)
    shard, ours = rows.shape[0] // slots, slots // 2
    per, outer = inner_vectors.shape[1] // ours, outer_vectors.shape[1] // ours
    core = lax.axis_index("core")
    for owner in range(slots):
        rows[owner * shard : (owner + 1) * shard, :] = held[owner, 0:shard, :]
    for at in range(ours):
        owner = core * ours + at
        for row in range(4):
            inner_vectors[row : row + 1, at * per : (at + 1) * per] = held[
                owner, shard : shard + 1, row * per : (row + 1) * per
            ]
        for row in range(2):
            outer_vectors[row : row + 1, at * outer : (at + 1) * outer] = held[
                owner, shard + 1 : shard + 2, row * outer : (row + 1) * outer
            ]
    widen(rows, wide, wide_turned)


def widen_kernel(weight, wide, wide_turned, rows):
    rows[...] = weight[...].astype(F32)
    widen(rows, wide, wide_turned)


def widen(weight, wide, wide_turned):
    taps, blocks = wide.shape[:2]
    inner = weight.shape[0] // taps
    row = lax.broadcasted_iota(jnp.int32, (BLOCK, BLOCK), 0) // inner
    column = lax.broadcasted_iota(jnp.int32, (BLOCK, BLOCK), 1) // inner
    own = row == column
    for tap in range(taps):
        for block in range(blocks):
            piece = weight[tap * inner : (tap + 1) * inner, block * BLOCK : (block + 1) * BLOCK]
            tall = jnp.concatenate([piece] * (BLOCK // inner), axis=0)
            dense = jnp.where(own, tall, 0.0)
            wide[tap, block] = dense.astype(BF16)
            wide_turned[tap, block] = dense.T.astype(BF16)


def fill_pads(pads, columns, image, line, values):
    rows = pl.ds(pl.multiple_of((line + 1) * LINE, LINE), LINE)
    pads[0, image, rows, columns] = pltpu.roll(values, 1, 0).astype(BF16)
    pads[1, image, rows, columns] = values.astype(BF16)
    pads[2, image, rows, columns] = pltpu.roll(values, LINE - 1, 0).astype(BF16)


def clear_pads(pads):
    images, rows, columns = pads.shape[1:]
    zeros = jnp.zeros((3, images, LINE, columns), BF16)
    pads[:, :, 0:LINE, :] = zeros
    pads[:, :, rows - LINE : rows, :] = zeros


def convolve(pads, wide, image, block, rows, turned=False):
    columns = slice(block * BLOCK, (block + 1) * BLOCK)
    value = None
    for tap in range(TAPS):
        top, left = divmod(TAPS - 1 - tap if turned else tap, 3)
        piece = pads[left, image, top * LINE : top * LINE + rows, columns]
        term = dot(piece, wide[tap, block])
        value = term if value is None else value + term
    return value


def group_kernel(side, mask, total, vectors, red, wide, pads, grouped, stats):
    images, padded, width = pads.shape[1:]
    rows = side * LINE
    mean, inverse = moments(total, total[2:3, :])
    scale, bias = 0.5 * inverse * vectors[0:1, :], 0.5 * vectors[1:2, :]
    clear_pads(pads)
    for part in chunks(width):
        inside = line_mask(part.stop - part.start, side)

        def body(step):
            half = (red[line_at(step), part] - mean[:, part]) * scale[:, part] + bias[:, part]
            fill_pads(pads, part, step // side, step % side, jnp.where(inside, silu_half(half), 0.0))

        each_line(images * side, body)
    for block in range(width // BLOCK):
        columns = slice(block * BLOCK, (block + 1) * BLOCK)
        sums = [0.0, 0.0]
        for image in range(images):
            at = slice(image * rows, (image + 1) * rows)
            value = convolve(pads, wide, image, block, rows)
            grouped[at, columns] = value
            masked = value * across_lanes(mask[at, :], BLOCK)
            sums = [sums[0] + column_sums(masked), sums[1] + column_sums(masked * value)]
        stats[0:1, columns] = sums[0]
        stats[1:2, columns] = sums[1]


def act_kernel(side, total, first, vectors, grouped, act):
    rows, width = grouped.shape
    mean, inverse = moments(total, first[2:3, :])
    scale, bias = 0.5 * inverse * vectors[2:3, :], 0.5 * vectors[3:4, :]
    for part in chunks(width):
        inside = line_mask(part.stop - part.start, side)

        def body(step):
            at = line_at(step)
            half = (grouped[at, part] - mean[:, part]) * scale[:, part] + bias[:, part]
            act[at, part] = jnp.where(inside, silu_half(half), 0.0).astype(BF16)

        each_line(rows // LINE, body)


def assemble_kernel(*refs):
    blocks, out = refs[:-1], refs[-1]
    depth = blocks[0].shape[0]
    for slot, block in enumerate(blocks):
        out[rows_of(block_owner(slot), depth), :] = block[...]


def expand_near_kernel(act_mine, weight, out):
    rows, half = act_mine.shape
    for at in range(0, weight.shape[1], BLOCK):
        out[:, at : at + BLOCK] = dot(act_mine[...], weight[part_at(0, half), at : at + BLOCK])


def expand_kernel(mask, act_mine, act_far, weight, near, act, expanded, stats):
    rows, half = act_mine.shape
    middle = rows // 2
    act[:, part_at(0, half)] = act_mine[...]
    act[0:middle, part_at(1, half)] = act_far[middle:rows, :]
    act[middle:rows, part_at(1, half)] = act_far[0:middle, :]
    for at in range(0, weight.shape[1], BLOCK):
        sums = [0.0, 0.0]
        for begin in (0, middle):
            here = slice(begin, begin + middle)
            value = near[here, at : at + BLOCK] + dot(act[here, part_at(1, half)], weight[part_at(1, half), at : at + BLOCK])
            expanded[here, at : at + BLOCK] = value
            masked = value * across_lanes(mask[here, :], BLOCK)
            sums = [sums[0] + column_sums(masked), sums[1] + column_sums(masked * value)]
        stats[0:1, at : at + BLOCK] = sums[0]
        stats[1:2, at : at + BLOCK] = sums[1]


def output_kernel(
    side, valid, total, first, vectors, expanded, x, x_other, cotangent, cotangent_far, keep_out, send_out, grad, stats
):
    rows, channels = expanded.shape
    middle = rows // 2
    mean, inverse = moments(total, first[2:3, 0:1])
    scale, bias = inverse * vectors[0:1, :], vectors[1:2, :]
    for part in chunks(channels):
        length = part.stop - part.start
        whole = part_at(0, channels, part.start, length)
        ends = []
        for begin, pixels, incoming, columns, out in (
            (0, x, cotangent, whole, keep_out), (middle, x_other, cotangent_far, part, send_out)
        ):

            def body(step):
                at = line_at(step)
                here = pl.ds(pl.multiple_of(begin + step * LINE, LINE), LINE)
                keep = 0.5 * valid[(begin // LINE + step) // side].astype(F32)
                centered = expanded[here, part] - mean[:, part]
                half = (centered * scale[:, part] + (bias[:, part] + pixels[at, whole].astype(F32))) * keep
                slope, upper = dsilu_twice(half)
                out[at, part] = (half * upper).astype(BF16)
                value = incoming[at, columns].astype(F32) * keep * slope
                grad[here, part] = value
                return value, value * centered

            ends.append(each_line_summed(middle // LINE, length, body))
        stats[0:1, part] = ends[0][0] + ends[1][0]
        stats[1:2, part] = (ends[0][1] + ends[1][1]) * inverse[:, part]


def back_expand_kernel(mask, total, sums, first, vectors, grad, expanded, weight, flat, send):
    rows, channels = expanded.shape
    pixels = first[2:3, 0:1]
    mean, inverse = moments(total, pixels)
    scale = inverse * vectors[0:1, :]
    shifted, scaled = scale * sums[0:1, :] / pixels, scale * inverse * sums[1:2, :] / pixels
    for part in chunks(channels):

        def body(step):
            at = line_at(step)
            common = shifted[:, part] + (expanded[at, part] - mean[:, part]) * scaled[:, part]
            counted = across_lanes(mask[at, :], part.stop - part.start)
            flat[at, part] = (scale[:, part] * grad[at, part] - counted * common).astype(BF16)

        each_line(rows // LINE, body)
    back_part_kernel(1, flat, weight, send)


def back_part_kernel(part, flat, weight, out):
    half = out.shape[1]
    for at in range(0, half, BLOCK):
        rows = pl.ds(pl.multiple_of(part_at(part, half).start + at, BLOCK), BLOCK)
        out[:, at : at + BLOCK] = dot(flat[...], weight[rows, :], NT).astype(out.dtype)


def back_act_kernel(total, first, vectors, mine, far, grouped, dz, stats):
    mean, inverse = moments(total, first[2:3, :])
    lines = grouped.shape[0] // LINE

    def gradient(step, part):
        there = lax.rem(step + lines // 2, lines)
        return mine[line_at(step), part] + far[line_at(there), part].astype(F32)

    before_norm(dz, gradient, grouped, mean, inverse, vectors[2:3, :], vectors[3:4, :], stats)


def before_norm(dz, gradient, hidden, mean, inverse, gain, shift, stats, side=None):
    scale, bias = 0.5 * inverse * gain, 0.5 * shift
    rows, width = hidden.shape
    for part in chunks(width):
        inside = None if side is None else line_mask(part.stop - part.start, side)

        def body(step):
            at = line_at(step)
            centered = hidden[at, part] - mean[:, part]
            slope, _ = dsilu_twice(centered * scale[:, part] + bias[:, part])
            here = gradient(step, part) * slope
            if side is not None:
                here = jnp.where(inside, here, 0.0)
            dz[at, part] = here
            return here, here * centered

        one, two = each_line_summed(rows // LINE, part.stop - part.start, body)
        stats[0:1, part] = 0.5 * one
        stats[1:2, part] = 0.5 * inverse[:, part] * two


def weight_expand_kernel(act, flat, out):
    turned = act[...].T
    for at in range(0, out.shape[1], BLOCK):
        out[:, at : at + BLOCK] = dot(turned, flat[:, at : at + BLOCK]).astype(BF16)


def back_group_kernel(
    side, mask, total, sums, first, vectors, dz, grouped, red, wide, flat, dz_one, stats, pads
):
    images, padded, width = pads.shape[1:]
    rows = side * LINE
    pixels = first[2:3, :]
    mean, inverse = moments(total, pixels)
    scale = inverse * vectors[2:3, :]
    shifted, scaled = scale * sums[0:1, :] / pixels, scale * inverse * sums[1:2, :] / pixels
    scale = 0.5 * scale
    clear_pads(pads)
    for part in chunks(width):

        def body(step):
            at = line_at(step)
            common = shifted[:, part] + (grouped[at, part] - mean[:, part]) * scaled[:, part]
            value = scale[:, part] * dz[at, part] - across_lanes(mask[at, :], part.stop - part.start) * common
            flat[at, part] = value.astype(BF16)
            fill_pads(pads, part, step // side, step % side, value)

        each_line(images * side, body)
    for block in range(width // BLOCK):
        columns = slice(block * BLOCK, (block + 1) * BLOCK)
        for image in range(images):
            dz_one[image * rows : (image + 1) * rows, columns] = convolve(pads, wide, image, block, rows, True)
    mean_one, inverse_one = moments(first, pixels)

    def gradient(step, part):
        return dz_one[line_at(step), part]

    before_norm(dz_one, gradient, red, mean_one, inverse_one, vectors[0:1, :], vectors[1:2, :], stats, side)


def weight_group_kernel(side, inner, pads, flat, out, held):
    images, padded, width = pads.shape[1:]
    rows = side * LINE
    row = lax.broadcasted_iota(jnp.int32, (LANES, LANES), 0) // inner
    column = lax.broadcasted_iota(jnp.int32, (LANES, LANES), 1) // inner
    own = row == column
    for at in range(0, width, LANES):
        columns = slice(at, at + LANES)
        moved = []
        for tap in range(TAPS):
            top, left = divmod(tap, 3)
            pieces = [pads[left, image, top * LINE : top * LINE + rows, columns] for image in range(images)]
            moved.append(jnp.concatenate(pieces, axis=0))
        product = dot(flat[:, columns].T, jnp.concatenate(moved, axis=1))
        for tap in range(TAPS):
            kept = jnp.where(own, product[:, tap * LANES : (tap + 1) * LANES].T, 0.0)
            value = kept[0:inner]
            for begin in range(inner, LANES, inner):
                value = value + kept[begin : begin + inner]
            held[tap * inner : (tap + 1) * inner, columns] = value
    owners, extra = out.shape[:2]
    shard = TAPS * inner // owners
    zeros = jnp.zeros((extra - shard, width), F32)
    for owner in range(owners):
        rows_here = held[owner * shard : (owner + 1) * shard, :]
        out[owner] = jnp.concatenate([rows_here, zeros], axis=0).astype(BF16)


def back_reduce_kernel(small, places, mask, first, sums, vectors, dz, red, turned, group, flat, *outs):
    rows, width = red.shape
    pixels = first[2:3, :]
    mean, inverse = moments(first, pixels)
    scale = inverse * vectors[0:1, :]
    shifted, scaled = scale * sums[0:1, :] / pixels, scale * inverse * sums[1:2, :] / pixels
    scale = 0.5 * scale
    for part in chunks(width):

        def body(step):
            at = line_at(step)
            common = shifted[:, part] + (red[at, part] - mean[:, part]) * scaled[:, part]
            counted = across_lanes(mask[at, :], part.stop - part.start)
            flat[at, part] = (scale[:, part] * dz[at, part] - counted * common).astype(BF16)

        each_line(rows // LINE, body)
    block_sum_kernel(small, places, turned, group, flat, *outs)


def block_sum_kernel(small, places, turned, group, flat, *outs):
    tall, half = outs[0].shape
    depth = tall - group.shape[1]
    for out, block in zip(outs, places):
        owner = block_owner(block) if small else block
        out[0:depth, :] = dot(turned[rows_of(owner, depth), :], flat[...]).astype(out.dtype)
        out[depth:tall, :] = group[owner].astype(out.dtype)


def arrived_kernel(numbers, *refs):
    terms, arrived, outs = refs[: len(numbers)], refs[len(numbers) : -len(numbers)], refs[-len(numbers) :]
    at = 0
    for out, term, number in zip(outs, terms, numbers):
        value = term[...]
        for other in arrived[at : at + number]:
            value = value + other[...].astype(F32)
        out[...] = value.astype(BF16)
        at += number


def expand_sum_kernel(places, depth, keep, *refs):
    arrived, outs = refs[: len(refs) - len(places)], refs[len(refs) - len(places) :]
    for out, blocks in zip(outs, places):
        for at, (block, chosen) in enumerate(blocks):
            value = keep[rows_of(block_owner(block), depth), :]
            if chosen:
                value = value.astype(F32)
                for other, begin in chosen:
                    value = value + arrived[other][begin * depth : (begin + 1) * depth, :].astype(F32)
            out[at * depth : (at + 1) * depth, :] = value.astype(BF16)


def join_kernel(mine, mine_x, other, other_x, *outs):
    half = mine.shape[1]
    at = 0
    for out in outs:
        rows = out.shape[0]
        for part, terms in enumerate(((mine, mine_x), (other, other_x))):
            values = [term[at : at + -(-rows // 16) * 16, :].astype(F32) for term in terms]
            out[:, part_at(part, half)] = (values[0] + values[1])[0:rows]
        at += -(-rows // 16) * 16


def pin_kernel(values, out):
    pass


def own_kernel(sizes, near, far, *outs):
    position, core, ours = lax.axis_index("fsdp"), lax.axis_index("core"), lax.axis_size("fsdp") // 2
    side, place, at = position // ours, lax.rem(position, ours), 0
    for index, length in enumerate(sizes):
        columns = pl.ds(pl.multiple_of(at + place * length, 128), length)
        for row, out in ((1, outs[2 * index]), (0, outs[2 * index + 1])):
            out[...] = jnp.where(side == core, near[row : row + 1, columns], far[row : row + 1, columns])
        at += ours * length


def back_input_kernel(slots, depth, begin, flat, grad, *refs):
    weights, refs = refs[:slots], refs[slots:]
    half = grad.shape[1]
    out, held = refs[-2:]
    rows = slice(begin, begin + held.shape[0])
    for slot in range(slots):
        columns = pl.ds(pl.multiple_of(block_owner(slot) * depth, 128), depth) if slots > 1 else slice(None)
        held[:, columns] = dot(flat[rows, :], weights[slot][0:depth, :], NT)
    columns = part_at(0, half)
    held[:, columns] = held[:, columns] + grad[rows, :]
    if len(refs) == 2:
        out[...] = held[...].astype(BF16)
        return
    far = refs[0]
    side = out.shape[1]

    def body(step):
        at = line_at(step)
        out[step // side, step % side] = (held[at, :] + far[at, :].astype(F32)).astype(BF16)[0:side]

    each_line(held.shape[0] // LINE, body)


def far_half_kernel(values, out):
    out[...] = values[:, part_at(1, out.shape[1])]


def image_kernel(keep, far, out):
    half, side = keep.shape[1], out.shape[1]

    def body(step):
        at = line_at(step)
        for part, values in enumerate((keep, far)):
            out[step // side, step % side, :, part_at(part, half)] = values[at, :][0:side]

    each_line(keep.shape[0] // LINE, body)


def pinned(values):
    anywhere = pl.BlockSpec(memory_space=pl.ANY)
    values = values.transpose(1, 2, 0, 3)
    values = pl.pallas_call(
        pin_kernel, out_shape=shape(values.shape, values.dtype), in_specs=[anywhere], out_specs=anywhere,
        input_output_aliases={0: 0}, compiler_params=pltpu.CompilerParams(vmem_limit_bytes=1 << 20), name="pin",
    )(values)
    return values.transpose(2, 0, 1, 3)


def swap_core(values):
    return lax.ppermute(values, "core", SWAP)


def swap_x(values):
    if lax.axis_size("x") == 2:
        return lax.ppermute(values, "x", SWAP)
    return (lax.psum(values.astype(F32), "x") - values.astype(F32)).astype(values.dtype)


def sum_chips(values, flips):
    got = []
    for flip in (0, *flips):
        pairs = [(2 * at + core, 2 * (at ^ flip) + 1 - core) for at in range(16) for core in range(2)]
        got.append(lax.ppermute(values, (*CHIPS, "core"), pairs))
    got = together(*got)
    total = got[0]
    for other in got[1:]:
        total = total + other
    return total


def along(values, way):
    pairs = [(f * 2 + x, (f + 2 * way * (1 - 2 * x)) % 8 * 2 + x) for f in range(8) for x in range(2)]
    return lax.ppermute(values, CHIPS, pairs)


def across(values):
    return lax.ppermute(values, "fsdp", [(f, f ^ 1) for f in range(8)])


def halves(values, core):
    half = values.shape[1] // 2
    return lax.dynamic_slice_in_dim(values, core * half, half, 1)


def both(near, far, core):
    first, second = jnp.where(core == 0, near, far), jnp.where(core == 0, far, near)
    return jnp.concatenate([first, second], axis=-1)


def per_device(
    images,
    valid,
    cotangent,
    w_reduce,
    gain_one,
    shift_one,
    w_group,
    gain_two,
    shift_two,
    w_expand,
    gain_three,
    shift_three,
):
    count, side, _, channels = images.shape
    width = w_reduce.shape[1]
    inner = width // GROUPS
    size = lax.axis_size("fsdp")
    small = size == 8 and lax.axis_size("x") == 2
    position, core = lax.axis_index("fsdp"), lax.axis_index("core")
    rows = count * side * LINE
    per, outer, shard, depth = gain_one.shape[0], gain_three.shape[0], w_group.shape[0], w_reduce.shape[0]
    extra = -(-(shard + 2) // 16) * 16
    half, half_out = width // 2, channels // 2

    def plane_sum(values):
        return sum_chips(values, (1, 2, 3)) if small else lax.psum(values, CHIPS)

    def line_sum(values):
        return sum_chips(values, (4, 12, 8)) if small else values

    def everywhere(values):
        return line_sum(plane_sum(values))

    def padded(values):
        return jnp.pad(values, ((0, 0), (0, 0), (0, LINE - side), (0, 0))).reshape(rows, channels)

    vectors = (gain_one, shift_one, gain_two, shift_two, gain_three, shift_three)
    (own,) = call(
        pack_kernel, [shape((depth + extra, half), BF16)], [w_reduce, w_group, *vectors],
        anywhere=True, vmem=60, name="pack",
        scratch=[pltpu.VMEM((shard, width), BF16)] + [pltpu.VMEM(vector.shape, BF16) for vector in vectors]
        + [pltpu.SemaphoreType.DMA((8,))],
    )
    wide_shape = shape((TAPS, half // BLOCK, BLOCK, BLOCK), BF16)
    expand_own, x = halves(w_expand, core), padded(images)

    def mask_of(valid_other):
        valid_both = jnp.concatenate([valid, valid_other])
        (mask,) = call(
            functools.partial(mask_kernel, side), [shape((2 * rows, LANES), F32)], [valid_both], scalars=1, name="mask"
        )
        return valid_both, mask

    pixels, across_cores = 2 * rows, 2 * count

    def reduce_part(slots, last, depth, weights, *before):
        return call(
            functools.partial(reduce_kernel, slots, depth, side, last),
            [shape((pixels, half), F32), shape((3, half), F32)][: 1 + last],
            [valid_both, mask, x, x_other, *weights, *before], scalars=1, name="reduce", flops=2 * rows * width * channels,
        )

    if small:
        other = across(own)
        first = along(own, 1)
        x_other, valid_other = padded(swap_core(images)), swap_core(valid)
        first, other, x, x_other, expand_own = together(first, other, x, x_other, expand_own)
        passed, second, first_other = swap_x(first), along(first, 1), across(first)
        second, passed, first_other, valid_other = together(second, passed, first_other, valid_other)
        passed_other, second_other, expand_first = swap_x(first_other), across(second), along(expand_own, 1)
        valid_both, mask = mask_of(valid_other)
        weights = [own, first, passed, second, other, first_other, passed_other, second_other]
        (before,) = reduce_part((0, 1, 2, 3, 4, 5), False, depth, weights[:6])
        mask, before, *weights[6:] = together(mask, before, *weights[6:])
        second, other = along(expand_first, 1), across(expand_own)
        slots, slot_depth = size, depth
    else:
        x_other, valid_other = swap_core(x), swap_core(valid)
        valid_both, mask = mask_of(valid_other)
        whole = lax.all_gather(own, "fsdp", axis=0, tiled=False)
        weights = [whole[:, :depth].reshape(channels, half)]
        slots, slot_depth = 1, channels


    if small:
        red, part = reduce_part((6, 7), True, depth, weights[6:], before)
    else:
        red, part = reduce_part((None,), True, channels, weights)
    if small:
        wide, wide_turned, inner_vectors, outer_vectors = call(
            functools.partial(spread_kernel, slots, depth),
            [wide_shape, wide_shape, shape((4, half), F32), shape((2, half_out), F32)],
            weights,
            scratch=[pltpu.VMEM((size, extra, half), F32), pltpu.VMEM((size * shard, half), F32)],
            name="spread", flops=1 << 28,
        )
        middle, wide, wide_turned, inner_vectors, outer_vectors = together(
            plane_sum(part), wide, wide_turned, inner_vectors, outer_vectors
        )
        middle, second, other, expand_first = together(middle, second, other, expand_first)
        first_other, passed = across(expand_first), swap_x(expand_first)
        first = line_sum(middle)
        first, second = together(first, second)
        second_other, passed_other = across(second), swap_x(first_other)
    else:
        packed = whole[:, depth:]
        wide, wide_turned = call(
            widen_kernel, [wide_shape, wide_shape], [packed[:, :shard].reshape(size * shard, half)],
            scratch=[pltpu.VMEM((size * shard, half), F32)], name="widen",
        )
        line = packed[:, shard, : 4 * per].astype(F32).reshape(size, 4, per).transpose(1, 0, 2).reshape(4, width)
        inner_vectors = halves(line, core)
        line = packed[:, shard + 1, : 2 * outer].astype(F32).reshape(size, 2, outer).transpose(1, 0, 2)
        outer_vectors = halves(line.reshape(2, channels), core)
        first = everywhere(part)
    pad_shape = (3, across_cores, (side + 2) * LINE, half)
    pads, grouped, part = call(
        functools.partial(group_kernel, side),
        [shape(pad_shape, BF16), shape((pixels, half), F32), shape((2, half), F32)],
        [mask, first, inner_vectors, red, wide],
        name="group", flops=2 * TAPS * rows * width * BLOCK,
    )
    if small:
        part, passed = together(part, passed)
        middle = line_sum(part)
        middle, passed_other, second_other = together(middle, passed_other, second_other)
        blocks = (expand_own, expand_first, passed, second, other, first_other, passed_other, second_other)
        total_two = plane_sum(middle)
    else:
        total_two = everywhere(part)
    (act_mine,) = call(
        functools.partial(act_kernel, side), [shape((pixels, half), BF16)], [total_two, first, inner_vectors, grouped],
        name="act",
    )
    act_far = swap_core(act_mine)
    if small:
        act_mine, *blocks = together(act_mine, *blocks)
        (weight_three,) = call(assemble_kernel, [shape((width, half_out), BF16)], blocks, name="assemble")
    else:
        weight_three = lax.all_gather(expand_own, "fsdp", axis=0, tiled=True)
    (near,) = call(
        expand_near_kernel, [shape((pixels, half_out), F32)], [act_mine, weight_three], name="expand_near",
        flops=rows * width * channels,
    )
    act_two, expanded, part = call(
        expand_kernel,
        [shape((pixels, width), BF16), shape((pixels, half_out), F32), shape((2, half_out), F32)],
        [mask, act_mine, act_far, weight_three, near],
        name="expand", flops=2 * rows * width * channels,
    )
    cot = padded(after(cotangent, grouped))
    cot_far = swap_core(call(far_half_kernel, [shape((rows, half_out), BF16)], [cot], name="far_half")[0])
    middle, cot, cot_far = together(plane_sum(part), cot, cot_far)
    total_three = line_sum(middle)
    keep_out, send_out, grad_summed, part = call(
        functools.partial(output_kernel, side),
        [shape((rows, half_out), BF16), shape((rows, half_out), BF16), shape((pixels, half_out), F32),
         shape((2, half_out), F32)],
        [valid_both, total_three, first, outer_vectors, expanded, x, x_other, cot, cot_far], scalars=1, name="output",
    )

    (turned,) = call(turn_kernel, [shape((channels, pixels), BF16)], [x, after(x_other, part)], name="turn")
    middle, turned = together(plane_sum(part), turned)
    sums_three = line_sum(middle)
    flat_three, send = call(
        back_expand_kernel,
        [shape((pixels, half_out), BF16), shape((pixels, half), BF16)],
        [mask, total_three, sums_three, first, outer_vectors, grad_summed, expanded, weight_three],
        name="back_expand", flops=rows * width * channels,
    )
    far = swap_core(send)
    (mine,) = call(
        functools.partial(back_part_kernel, 0), [shape((pixels, half), F32)], [flat_three, weight_three],
        name="back_part", flops=rows * width * channels,
    )
    dz_two, part = call(
        back_act_kernel,
        [shape((pixels, half), F32), shape((2, half), F32)],
        [total_two, first, inner_vectors, mine, far, grouped], name="back_act",
    )
    (expand_term,) = call(
        weight_expand_kernel, [shape((width, half_out), BF16)], [after(act_two, part), flat_three],
        name="weight_expand", flops=2 * rows * width * channels,
    )
    far_out = swap_core(after(send_out, part))
    middle = plane_sum(part)

    def expand_sums(places, arrived=()):
        return call(
            functools.partial(expand_sum_kernel, places, w_expand.shape[0]),
            [shape((w_expand.shape[0] * len(blocks), half_out), BF16) for blocks in places],
            [expand_term] + list(arrived), name="expand_sum",
        )

    if small:
        middle, *moving = together(middle, *expand_sums((((6, ()), (2, ())), ((7, ()), (4, ())))))
        moving = [swap_x(moving[0]), across(moving[1])]
        sums_two = line_sum(middle)
    else:
        sums_two = line_sum(middle)
        own_expand = lax.psum_scatter(expand_term, "fsdp", scatter_dimension=0, tiled=True)
    flat_two, dz_one, part = call(
        functools.partial(back_group_kernel, side),
        [shape((pixels, half), BF16), shape((pixels, half), F32), shape((2, half), F32)],
        [mask, total_two, sums_two, first, inner_vectors, dz_two, grouped, red, wide_turned],
        scratch=[pltpu.VMEM(pad_shape, BF16)], name="back_group", flops=2 * TAPS * rows * width * BLOCK,
    )
    (group_term,) = call(
        functools.partial(weight_group_kernel, side, inner),
        [shape((size, extra, half), BF16)],
        [pads, after(flat_two, part)], scratch=[pltpu.VMEM((TAPS * inner, half), F32)], name="weight_group",
        flops=2 * TAPS * rows * width * BLOCK,
    )
    middle, group_term = together(plane_sum(part), group_term)
    if small:
        middle, *moving = together(middle, *moving)
        middle, expand_first_other, expand_second = together(middle, *expand_sums((((5, ((0, 0),)),), ((3, ((1, 0),)),)), moving))
        expand_first_other, expand_second = across(expand_first_other), along(expand_second, -1)
    sums_one = line_sum(middle)
    if small:
        sums_one, expand_first_other, expand_second = together(sums_one, expand_first_other, expand_second)
        expand_passed, expand_other = moving
        (expand_first_own,) = expand_sums((((1, ((0, 1), (1, 0), (2, 0))),),), (expand_passed, expand_first_other, expand_second))
    tall = depth + extra
    places = (6, 7) if small else tuple(range(size))
    flat_one, *moving = call(
        functools.partial(back_reduce_kernel, small, places),
        [shape((pixels, half), BF16)] + [shape((tall, half), BF16)] * len(places),
        [mask, first, sums_one, inner_vectors, dz_one, red, turned, group_term],
        name="back_reduce", flops=2 * rows * depth * width * len(places),
    )

    def terms_of(places):
        return call(
            functools.partial(block_sum_kernel, small, places),
            [shape((tall, half), F32)] * len(places),
            [turned, group_term, flat_one],
            name="block_sum", flops=2 * rows * depth * width * len(places),
        )

    def sums(terms, *arrived):
        numbers = tuple(len(some) for some in arrived)
        return call(
            functools.partial(arrived_kernel, numbers), [shape((tall, half), BF16)] * len(terms),
            [*terms, *(value for some in arrived for value in some)], name="arrived",
        )

    def back_input(begin, flat, *far):
        out = shape(images.shape, BF16) if far else shape((rows, channels), BF16)
        return call(
            functools.partial(back_input_kernel, slots, slot_depth, begin),
            [out], [flat, grad_summed, *weights, *far],
            scratch=[pltpu.VMEM((rows, channels), F32)], name="back_input", flops=rows * width * channels,
        )[0]

    def own_shards(totals):
        near = jnp.concatenate(totals, axis=1)
        far = swap_core(near)
        lengths = (per, per, outer)
        if small:
            outs = call(
                functools.partial(own_kernel, lengths), [shape((1, n), F32) for n in lengths for _ in range(2)], [near, far],
                name="own",
            )
            return [out.reshape(-1) for out in outs]
        cut, at = [], 0
        for total, length in zip(totals, lengths):
            whole = both(total, far[:, at : at + total.shape[1]], core)
            at += total.shape[1]
            cut += [lax.dynamic_slice_in_dim(whole[row], position * length, length, 0) for row in (1, 0)]
        return cut

    def image_of(far_out):
        return call(image_kernel, [shape(images.shape, BF16)], [keep_out, far_out], name="image")[0]

    def join(own, far, outs):
        return call(
            join_kernel, [shape(out.shape, F32) for out in outs], [own, far, swap_core(own), swap_core(far)], name="join"
        )

    if small:
        moving[1], expand_first_own = together(moving[1], expand_first_own)
        moving = [swap_x(moving[0]), across(moving[1])]
        expand_first_own = along(expand_first_own, -1)
        terms = terms_of((5, 2, 3, 1, 4, 0))
        shards = own_shards([sums_one, sums_two, sums_three])
        moving[0], expand_first_own, *shards = together(moving[0], expand_first_own, *shards)
        (own_expand,) = expand_sums((((0, ((0, 0), (1, 1))),),), [expand_first_own, expand_other])
        first_other, passed, second = sums(terms[0:3], moving[0:1], (), moving[1:2])
        moving = [swap_x(passed), along(second, -1), across(first_other)]
        far_input = swap_core(after(back_input(rows, flat_one), second))
        output = pinned(image_of(after(far_out, second)))
        moving[0], output = together(moving[0], output)
        first_own, other = sums(terms[3:5], moving, ())
        moving = [along(first_own, -1), across(other)]
        grad_input, own_expand = pinned(back_input(0, after(flat_one, first_own), far_input)), after(own_expand, first_own)
        far_expand = swap_x(own_expand)
        moving[0], grad_input, far_expand = together(moving[0], grad_input, far_expand)
        (own_reduce,) = sums(terms[5:6], moving)
        own_expand, far_expand = after(own_expand, own_reduce), after(far_expand, own_reduce)
        (grad_w_expand,) = join(own_expand, far_expand, [w_expand])
        far_reduce, grad_w_expand = together(swap_x(own_reduce), grad_w_expand)
    else:
        grad_input, output = back_input(0, flat_one, swap_core(back_input(rows, flat_one))), image_of(far_out)
        shards = own_shards([sums_one, sums_two, sums_three])
        whole = jnp.stack(moving).reshape(size * tall, half)
        own_reduce = lax.psum_scatter(whole, "fsdp", scatter_dimension=0, tiled=True)
        (grad_w_expand,) = join(own_expand, swap_x(own_expand), [w_expand])
        far_reduce = swap_x(own_reduce)
    grad_w_reduce, grad_w_group = join(own_reduce, far_reduce, [w_reduce, w_group])
    return (output, grad_input, grad_w_reduce, grad_w_group, grad_w_expand) + tuple(shards)


def solution(mesh):
    fsdp, dp = mesh.shape["fsdp"], mesh.shape["dp"]
    split = Mesh(mesh.devices.reshape(fsdp, dp // 2, 2), ("fsdp", "x", "core"))
    images, rows, vector = P(("fsdp", "x", "core"), None, None, None), P("fsdp", None), P("fsdp")
    return jax.shard_map(
        per_device,
        mesh=split,
        in_specs=(
            images, P(("fsdp", "x", "core")), images,
            rows, vector, vector, rows, vector, vector, rows, vector, vector,
        ),
        out_specs=(images, images, rows, rows, rows) + (vector,) * 6,
        check_vma=False,
    )
```
